32 devices in a mesh: tok: 8 (over z, x), head: 4 (over y, core).
Axes of the slice: x: 2, y: 2, z: 4, core: 2. Of those that a mesh axis runs over, the one named last changes fastest.
Arguments:
- queries: bfloat16 [8192, 4096], P(('tok', 'head')), may hold values from -32 to 32
- key_states: bfloat16 [8192, 512], P(('tok', 'head')), may hold values from -10 to 10
- value_states: bfloat16 [8192, 512], P(('tok', 'head')), may hold values from -6 to 6
- out_grad: bfloat16 [8192, 4096], P(('tok', 'head')), may hold values from -15 to 15
- sink_logits: float32 [64], P('head'), may hold values from 0 to 5
- branch_start: int32 [16], replicated, may hold values from 0 to 8064, as said below
- branch_len: int32 [16], replicated, may hold values from 128 to 384, as said below
- parent_list: int32 [16, 2], replicated, may hold values from -1 to 256, as said below
Outputs:
- attn_out: bfloat16 [8192, 4096], P(('tok', 'head'))
- query_grad: bfloat16 [8192, 4096], P(('tok', 'head'))
- key_grad: bfloat16 [8192, 512], P(('tok', 'head'))
- value_grad: bfloat16 [8192, 512], P(('tok', 'head'))
- sink_grad: float32 [64], P('head')
The draws below stay inside these ranges and needn't reach their ends.
Inputs may be any that keep to these rules, and one draw needn't show every extreme that they name: `branch_start`: branch b lies within the tokens of index b // 2 of tok. The branches of one index follow one another in order, begin at multiples of 128 and do not intersect; tokens between them belong to no branch. `branch_len`: A multiple of 128. `parent_list`: row b is (parent branch, tail offset). The branches of index 0 of tok have parent -1 and offset 0; the parent of a branch on index d lies on index d - s for some s from 1 to min(3, d), and each s from 1 to 3 occurs. Branches 2m and 2m + 1 are siblings with equal rows. The offset is a multiple of 128 and the 128 tokens of the parent that begin there lie inside the parent.
All inputs are finite; a program needn't handle non-finite values.
Results may differ from the reference program's by a relative error of at most 0.02.
Values may be sent and summed in bfloat16 or wider, within the bound.
No kernel may reach another device: no remote copies, remote signals or barrier semaphores. Data moves between devices by JAX's collectives and lax.ppermute only.
A program may use at most 64 MiB of HBM per device.

```python
import math
import jax
import jax.numpy as jnp
from jax import lax

HEAD_DIM = 64
Q_HEADS = 64
KV_HEADS = 8
WINDOW = 128
LAG = 3
BLK_DEV = 8
BR_DEV = 2
PAIRS = 1
BRANCHES = 16
TOKENS = 8192
N_TOK = 8


def tree_layout(key):
    length_key, gap_key = jax.random.split(key, 2)
    spans = jax.random.randint(length_key, (N_TOK, BR_DEV), 1, 4)
    last_col = jnp.arange(BR_DEV)[None, :] == BR_DEV - 1
    spans = jnp.where(last_col, 3, spans)
    gaps = jax.random.randint(gap_key, (N_TOK, BR_DEV), 0, 2)
    ends = jnp.cumsum(spans + gaps, axis=1)
    offsets = ends - spans + jnp.arange(N_TOK)[:, None] * BLK_DEV
    return ((offsets * WINDOW).reshape(-1).astype(jnp.int32), (spans * WINDOW).reshape(-1).astype(jnp.int32), spans.reshape(-1))


def scaled_rows(value_key, scale_key, heads, low, high):
    scales = jnp.exp(jax.random.uniform(scale_key, (TOKENS, heads, 1), minval=math.log(low), maxval=math.log(high)))
    values = jnp.clip(jax.random.normal(value_key, (TOKENS, heads, HEAD_DIM)), -4.0, 4.0)
    return (values * scales).reshape(TOKENS, heads * HEAD_DIM)


def draw_branch_start(key, part):
    starts, lengths, spans = tree_layout(key)
    return starts


def draw_branch_len(key, part):
    starts, lengths, spans = tree_layout(key)
    return lengths


def draw_parent_list(key, part):
    starts, lengths, spans = tree_layout(key)
    key = jax.random.fold_in(key, 3)
    lag_key, pick_key, offset_key = jax.random.split(key, 3)
    count = N_TOK * BR_DEV
    device_ids = jnp.arange(N_TOK, dtype=jnp.int32)[:, None]
    pair_ids = jnp.arange(PAIRS, dtype=jnp.int32)[None, :]
    pinned = (device_ids == N_TOK - 1) & (pair_ids == 0)
    reach = jnp.maximum(jnp.minimum(device_ids, LAG), 1)
    rolls = jax.random.randint(lag_key, (N_TOK, PAIRS), 0, 36)
    distance = jnp.where(pair_ids == 0, 1 + device_ids % reach, 1 + rolls % reach)
    distance = jnp.where(pinned, 1, distance)
    owner = device_ids - distance
    picks_branch = jax.random.randint(pick_key, (N_TOK, PAIRS), 0, BR_DEV)
    picks_branch = jnp.where(pinned, BR_DEV - 1, picks_branch)
    parents = owner * BR_DEV + picks_branch
    rooted = device_ids == 0
    parents = jnp.where(rooted, -1, parents)
    parent_spans = spans[jnp.maximum(parents, 0)]
    picks = jax.random.randint(offset_key, (N_TOK, PAIRS), 0, 168)
    offsets = jnp.where(rooted, 0, picks % parent_spans * WINDOW)
    offsets = jnp.where(pinned, 2 * WINDOW, offsets)
    both = jnp.stack([parents, offsets], axis=-1)
    return jnp.repeat(both, 2, axis=1).reshape(count, 2).astype(jnp.int32)


def draw_key_states(key, part):
    key = jax.random.fold_in(key, 11)
    value_key, scale_key = jax.random.split(key)
    return scaled_rows(value_key, scale_key, KV_HEADS, 0.4, 2.5).astype(jnp.bfloat16)


def draw_queries(key, part):
    key = jax.random.fold_in(key, 13)
    value_key, scale_key = jax.random.split(key)
    return scaled_rows(value_key, scale_key, Q_HEADS, 0.4, 2.5).astype(jnp.bfloat16)


def draw_out_grad(key, part):
    key = jax.random.fold_in(key, 5)
    ramp = jnp.arange(TOKENS, dtype=jnp.float32)[:, None] / TOKENS
    values = jnp.clip(jax.random.normal(key, (TOKENS, Q_HEADS * HEAD_DIM)), -5.0, 5.0)
    return (values * (1.0 + 2.0 * ramp)).astype(jnp.bfloat16)


def level_of(own_key, extent, cuts, smallest, high):
    def one(position, shards_of):
        steps = jax.random.uniform(jax.random.fold_in(jax.random.fold_in(own_key, 6), position), (shards_of,), jnp.float32, smallest / len(cuts), high / len(cuts))
        return jnp.repeat(jnp.exp(steps), extent[position] // shards_of).reshape((-1,) + (1,) * (len(extent) - position - 1))

    loudness = one(*cuts[0])
    for cut in cuts[1:]:
        loudness = loudness * one(*cut)
    return loudness


def normal_values(stream_key, dims, deviation, most, cuts=(), kind=jnp.bfloat16):
    values = deviation * jax.random.normal(stream_key, dims, jnp.float32)
    if cuts:
        values = values * level_of(stream_key, dims, cuts, -0.22, 0.18)
    return jnp.clip(values, -most, most).astype(kind)


def setup_inputs(seed: int = 0) -> dict:
    key_list = jax.random.split(jax.random.key(seed), 9)
    queries = draw_queries(jax.random.fold_in(key_list[8], 71), 0)
    key_states = draw_key_states(jax.random.fold_in(key_list[8], 71), 0)
    value_states = normal_values(key_list[2], (TOKENS, KV_HEADS * HEAD_DIM), 1.0, 6.0, ((0, 32),))
    out_grad = draw_out_grad(jax.random.fold_in(key_list[8], 71), 0)
    sink_logits = jnp.clip(5.0 * jax.random.uniform(key_list[4], (Q_HEADS,), jnp.float32) ** level_of(key_list[4], (Q_HEADS,), ((0, 4),), -0.2, 0.2), 0.0, 5.0)
    branch_start = draw_branch_start(jax.random.fold_in(key_list[8], 71), 0)
    branch_len = draw_branch_len(jax.random.fold_in(key_list[8], 71), 0)
    parent_list = draw_parent_list(jax.random.fold_in(key_list[8], 71), 0)
    return dict(queries=queries, key_states=key_states, value_states=value_states, out_grad=out_grad, sink_logits=sink_logits, branch_start=branch_start, branch_len=branch_len, parent_list=parent_list)


def product(spec, left, right):
    return jnp.einsum(spec, left.astype(jnp.float32), right.astype(jnp.float32))

def attend(query_rows, key_own, value_own, key_prev, value_prev, grad_rows, prev_ok, alive, sink_table):
    window_len = query_rows.shape[1]
    factor = 1.0 / math.sqrt(query_rows.shape[-1])
    offsets = jnp.arange(window_len)
    causal = offsets[None, :] <= offsets[:, None]
    behind = (offsets[None, :] > offsets[:, None])[None, None, None] & prev_ok[:, None, None, None, None]
    own_scores = jnp.where(causal, product('bqkgd,bjkd->bkgqj', query_rows, key_own) * factor, -jnp.inf)
    prev_scores = jnp.where(behind, product('bqkgd,bjkd->bkgqj', query_rows, key_prev) * factor, -jnp.inf)
    sink_col = sink_table[None, :, :, None]
    peak = jnp.maximum(jnp.maximum(lax.optimization_barrier(jnp.max(own_scores, axis=-1)), lax.optimization_barrier(jnp.max(prev_scores, axis=-1))), sink_col)
    own_exp = jnp.exp(own_scores - peak[..., None])
    prev_exp = jnp.exp(prev_scores - peak[..., None])
    sink_exp = jnp.exp(sink_col - peak)
    summed = lax.optimization_barrier(jnp.sum(own_exp, axis=-1)) + lax.optimization_barrier(jnp.sum(prev_exp, axis=-1)) + sink_exp
    own_prob = own_exp / summed[..., None]
    prev_prob = prev_exp / summed[..., None]
    own_half = own_prob.astype(jnp.bfloat16)
    prev_half = prev_prob.astype(jnp.bfloat16)
    blended = product('bkgqj,bjkd->bqkgd', own_half, value_own) + product('bkgqj,bjkd->bqkgd', prev_half, value_prev)
    alive_rows = alive[:, None, None, None, None]
    attended = jnp.where(alive_rows, blended, 0.0).astype(jnp.bfloat16)
    grad_rows = jnp.where(alive_rows, grad_rows, jnp.zeros_like(grad_rows))
    row_delta = jnp.moveaxis(lax.optimization_barrier(jnp.sum(grad_rows.astype(jnp.float32) * attended.astype(jnp.float32), axis=-1)), 1, -1)
    own_slope = (own_prob * (product('bqkgd,bjkd->bkgqj', grad_rows, value_own) - row_delta[..., None])).astype(jnp.bfloat16)
    prev_slope = (prev_prob * (product('bqkgd,bjkd->bkgqj', grad_rows, value_prev) - row_delta[..., None])).astype(jnp.bfloat16)
    query_grad = ((product('bkgqj,bjkd->bqkgd', own_slope, key_own) + product('bkgqj,bjkd->bqkgd', prev_slope, key_prev)) * factor).astype(jnp.bfloat16)
    key_own_grad = product('bkgqj,bqkgd->bjkd', own_slope, query_rows) * factor
    key_prev_grad = product('bkgqj,bqkgd->bjkd', prev_slope, query_rows) * factor
    value_own_grad = product('bkgqj,bqkgd->bjkd', own_half, grad_rows)
    value_prev_grad = product('bkgqj,bqkgd->bjkd', prev_half, grad_rows)
    sink_grad = -lax.optimization_barrier(jnp.sum(sink_exp / summed * row_delta, axis=(0, 3)))
    return (attended, query_grad, key_own_grad, value_own_grad, key_prev_grad, value_prev_grad, sink_grad)

def reference(queries, key_states, value_states, out_grad, sink_logits, branch_start, branch_len, parent_list):
    blocks = TOKENS // WINDOW
    branch_ids = jnp.arange(BRANCHES, dtype=jnp.int32)
    block_pos = jnp.arange(blocks, dtype=jnp.int32) * WINDOW
    branch_end = branch_start + branch_len
    covers = (branch_start[None, :] <= block_pos[:, None]) & (block_pos[:, None] < branch_end[None, :])
    alive = jnp.any(covers, axis=1)
    opening = jnp.any(covers & (branch_start[None, :] == block_pos[:, None]), axis=1)
    holder = lax.optimization_barrier(jnp.sum(jnp.where(covers, branch_ids[None, :], 0), axis=1)).astype(jnp.int32)
    parent = parent_list[:, 0]
    parent_start = lax.optimization_barrier(jnp.sum(jnp.where(branch_ids[None, :] == parent[:, None], branch_start[None, :], 0), axis=1))
    tail_block = ((parent_start + parent_list[:, 1]) // WINDOW).astype(jnp.int32)
    has_tail = parent >= 0
    prev_block = jnp.where(opening, tail_block[holder], jnp.arange(blocks, dtype=jnp.int32) - 1)
    prev_ok = alive & (jnp.logical_not(opening) | has_tail[holder])
    prev_block = jnp.where(prev_ok, prev_block, 0).astype(jnp.int32)
    group_size = Q_HEADS // KV_HEADS
    query_blocks = queries.reshape(blocks, WINDOW, KV_HEADS, group_size, HEAD_DIM)
    grad_blocks = out_grad.reshape(blocks, WINDOW, KV_HEADS, group_size, HEAD_DIM)
    key_blocks = key_states.reshape(blocks, WINDOW, KV_HEADS, HEAD_DIM)
    value_blocks = value_states.reshape(blocks, WINDOW, KV_HEADS, HEAD_DIM)
    key_before = key_blocks[prev_block]
    value_before = value_blocks[prev_block]
    sink_table = sink_logits.reshape(KV_HEADS, group_size).astype(jnp.float32)
    per_stretch = blocks // N_TOK

    def split_stretches(array):
        return array.reshape((N_TOK, per_stretch) + array.shape[1:])

    def attend_stretch(pieces):
        return attend(*pieces, sink_table)
    results = lax.map(attend_stretch, (split_stretches(query_blocks), split_stretches(key_blocks), split_stretches(value_blocks), split_stretches(key_before), split_stretches(value_before), split_stretches(grad_blocks), split_stretches(prev_ok), split_stretches(alive)))
    attended, query_grad, key_own, value_own, key_prev, value_prev, sink_parts = results

    def merge_stretches(array):
        return array.reshape((blocks,) + array.shape[2:])
    keep = prev_ok[:, None, None, None]
    key_total = merge_stretches(key_own).at[prev_block].add(jnp.where(keep, merge_stretches(key_prev), 0.0))
    value_total = merge_stretches(value_own).at[prev_block].add(jnp.where(keep, merge_stretches(value_prev), 0.0))
    return (merge_stretches(attended).reshape(TOKENS, Q_HEADS * HEAD_DIM), merge_stretches(query_grad).reshape(TOKENS, Q_HEADS * HEAD_DIM), key_total.astype(jnp.bfloat16).reshape(TOKENS, KV_HEADS * HEAD_DIM), value_total.astype(jnp.bfloat16).reshape(TOKENS, KV_HEADS * HEAD_DIM), lax.optimization_barrier(jnp.sum(sink_parts, axis=0)).reshape(Q_HEADS))
```

```python
import functools

import jax
import jax.numpy as jnp
from jax import lax
from jax.experimental import pallas as pl
from jax.experimental.pallas import tpu as pltpu
from jax.sharding import PartitionSpec as P

HEAD_DIM = 64
KV_HEADS = 8
GROUP = 8
WINDOW = 128
LAG = 3
BR_DEV = 2
PAIRS = KV_HEADS // 2
FACTOR = 0.125
LOW = -1e30
EXTRA = 16
BF16 = jnp.bfloat16
F32 = jnp.float32

SMEM = pl.BlockSpec(memory_space=pltpu.SMEM)
VMEM = pl.BlockSpec(memory_space=pltpu.VMEM)
PARAMS = pltpu.CompilerParams(vmem_limit_bytes=24 * 1024 * 1024)


def shift(value, axis, steps):
    count = lax.axis_size(axis)
    leading, last = (max(0, -steps), min(count, count - steps))
    return lax.ppermute(value, axis, [(source, source + steps) for source in range(leading, last)])


def ring(value, axis, steps):
    count = lax.axis_size(axis)
    return lax.ppermute(value, axis, [(source, (source + steps) % count) for source in range(count)])


def row_split(row, dims):
    high = row.astype(BF16).astype(F32)
    middle = (row - high).astype(BF16).astype(F32)
    low = row - high - middle
    place = lax.broadcasted_iota(jnp.int32, dims, 0)
    rest = jnp.where(place == 2, low, 0.0)
    return jnp.where(place == 0, high, jnp.where(place == 1, middle, rest)).astype(BF16)


def row_join(rows):
    rows = rows.astype(F32)
    return rows[0:1] + rows[1:2] + rows[2:3]


def child_tail(table, tok, distance, tok_count, blocks):
    branches = tok_count * BR_DEV
    child = jnp.minimum(tok + distance, tok_count - 1) * BR_DEV
    parent = table[2 * branches + child]
    safe = jnp.maximum(parent, 0)
    valid = (tok + distance < tok_count) & (parent >= 0) & (safe // BR_DEV == tok)
    place = (table[safe] + table[3 * branches + child]) // WINDOW - tok * blocks
    return valid, jnp.where(valid, place, 0)


def block_state(table, tok, tok_count, block):
    branches = tok_count * BR_DEV
    position = block * WINDOW
    alive, opening = jnp.bool_(False), jnp.bool_(False)
    for branch in range(BR_DEV):
        start = table[tok * BR_DEV + branch]
        length = table[branches + tok * BR_DEV + branch]
        alive = alive | ((start <= position) & (position < start + length))
        opening = opening | (start == position)
    has_tail = table[2 * branches + tok * BR_DEV] >= 0
    return alive, opening, jnp.logical_not(opening) | has_tail


def pack_kernel(sinks, key_ref, value_ref, slot_ref, halo_ref):
    slots, rows = slot_ref.shape[0], key_ref.shape[0]
    width = KV_HEADS * HEAD_DIM // slots
    lane = lax.broadcasted_iota(jnp.int32, (1, 2 * width), 1)
    sink_row = jnp.zeros((1, 2 * width), F32)
    for head in range(sinks.shape[0]):
        sink_row = jnp.where(lane == head, sinks[head], sink_row)
    extra = row_split(sink_row, (EXTRA, 2 * width))
    for slot in range(slots):
        lanes = slice(slot * width, (slot + 1) * width)
        slot_ref[slot, :rows] = jnp.concatenate([key_ref[:, lanes], value_ref[:, lanes]], axis=1)
        slot_ref[slot, rows:] = extra
    for pair in range(PAIRS):
        lanes = slice(pair * 128, (pair + 1) * 128)
        last = slice(rows - WINDOW, rows)
        halo_ref[pair] = jnp.concatenate([key_ref[last, lanes], value_ref[last, lanes]], axis=1)


def choose_kernel(tok_count, blocks, table, all_ref, *refs):
    tok = lax.axis_index("tok")
    *out_refs, sink_ref = refs
    slots = all_ref.shape[0]
    rows = all_ref.shape[1] - EXTRA
    blocks_here = rows // WINDOW
    heads = sink_ref.shape[0] // slots
    for distance, out_ref in enumerate(out_refs, 1):
        _, place = child_tail(table, tok, distance, tok_count, blocks)
        begin = pl.multiple_of(place % blocks_here * WINDOW, WINDOW)
        out_ref[...] = all_ref[place // blocks_here, pl.ds(begin, WINDOW), :]
    for slot in range(slots):
        sink_row = row_join(all_ref[slot, rows:, :])[:, :128]
        turned = jnp.broadcast_to(sink_row, (128, 128)).T
        sink_ref[slot * heads : (slot + 1) * heads, :] = turned[:heads]


def arrive_kernel(tok_count, table, *refs):
    tok = lax.axis_index("tok")
    *in_refs, out_ref = refs
    parent = table[2 * tok_count * BR_DEV + tok * BR_DEV]
    mine = jnp.where(parent >= 0, tok - jnp.maximum(parent, 0) // BR_DEV, 1)
    for distance, in_ref in enumerate(in_refs, 1):

        @pl.when(mine == distance)
        def _(in_ref=in_ref):
            out_ref[...] = in_ref[...]


def attend_kernel(
    tok_count,
    per_slot,
    blocks_here,
    table,
    sink_ref,
    q_ref,
    g_ref,
    k_ref,
    v_ref,
    halo_ref,
    tail_ref,
    o_ref,
    dq_ref,
    dk_ref,
    dv_ref,
    dhalo_ref,
    dtail_ref,
    tail_sum,
    sink_rows,
    q_turned,
    g_turned,
    prob2,
    slope2,
):
    pair, block = pl.program_id(0), pl.program_id(1)
    tok, head = lax.axis_index("tok"), lax.axis_index("head")
    number = (tok * lax.axis_size("head") + head) * blocks_here + block
    alive, opening, prev_ok = block_state(table, tok, tok_count, number)
    here = pl.ds(pl.multiple_of(block * WINDOW, WINDOW), WINDOW)
    before = pl.ds(pl.multiple_of(jnp.maximum(block - 1, 0) * WINDOW, WINDOW), WINDOW)
    first = block == 0

    @pl.when(first)
    def _():
        tail_sum[...] = jnp.zeros_like(tail_sum)
        dhalo_ref[...] = jnp.zeros_like(dhalo_ref)
        sink_rows[...] = jnp.zeros_like(sink_rows)

    @pl.when(jnp.logical_not(alive))
    def _():
        o_ref[...] = jnp.zeros_like(o_ref)
        dq_ref[...] = jnp.zeros_like(dq_ref)
        dk_ref[here, :] = jnp.zeros((WINDOW, 128), F32)
        dv_ref[here, :] = jnp.zeros((WINDOW, 128), F32)

    @pl.when(alive)
    def _():
        halo = halo_ref[0]
        if per_slot == 2:
            tail = tail_ref[0]
            tail_k, tail_v = tail[:, :128], tail[:, 128:]
        else:
            tail_k = jnp.concatenate([tail_ref[0][:, :64], tail_ref[1][:, :64]], axis=1)
            tail_v = jnp.concatenate([tail_ref[0][:, 64:], tail_ref[1][:, 64:]], axis=1)
        near_k = jnp.where(first, halo[:, :128], k_ref[before, :])
        near_v = jnp.where(first, halo[:, 128:], v_ref[before, :])
        prev_k = jnp.where(opening, tail_k, near_k)
        prev_v = jnp.where(opening, tail_v, near_v)
        both_k = jnp.concatenate([k_ref[here, :], prev_k], axis=0) * BF16(FACTOR)
        both_v = jnp.concatenate([v_ref[here, :], prev_v], axis=0)
        turned_k, turned_v = both_k.T, both_v.T
        bias = jnp.where(prev_ok, 0.0, LOW)
        key_place = lax.broadcasted_iota(jnp.int32, (WINDOW, WINDOW), 0)
        query_place = lax.broadcasted_iota(jnp.int32, (WINDOW, WINDOW), 1)
        own_one = key_place <= query_place
        own = jnp.concatenate([own_one, own_one], axis=1)
        own16 = own.astype(F32).astype(BF16)
        turn = (((1,), (1,)), ((), ()))
        couples = GROUP // 2

        def columns(index):
            return slice(index * 128, (index + 1) * 128)

        def wide(index):
            return slice(index * 256, (index + 1) * 256)

        def feats(index):
            unit = index // couples
            return slice(unit * HEAD_DIM, (unit + 1) * HEAD_DIM)

        def products(index):
            q_t, g_t = q_ref[:, columns(index)].T, g_ref[:, columns(index)].T
            q_t = jnp.concatenate([q_t[:64], q_t[64:]], axis=1)
            g_t = jnp.concatenate([g_t[:64], g_t[64:]], axis=1)
            q_turned[:, wide(index)] = q_t
            g_turned[:, wide(index)] = g_t
            score2 = jnp.dot(both_k[:, feats(index)], q_t, preferred_element_type=F32)
            dp2 = jnp.dot(both_v[:, feats(index)], g_t, preferred_element_type=F32)
            score = jnp.where(own, score2[:WINDOW], score2[WINDOW:] + bias)
            return score, jnp.where(own, dp2[:WINDOW], dp2[WINDOW:])

        def weigh(index, score, dp):
            row = index * 2
            sink = jnp.concatenate([sink_ref[row : row + 1], sink_ref[row + 1 : row + 2]], axis=1)
            peak = jnp.maximum(jnp.max(score, axis=0, keepdims=True), sink)
            weight = jnp.exp(score - peak)
            sink_weight = jnp.exp(sink - peak)
            inverse = 1.0 / (jnp.sum(weight, axis=0, keepdims=True) + sink_weight)
            prob = weight * inverse
            term = prob * dp
            delta = jnp.sum(term, axis=0, keepdims=True)
            prob16 = prob.astype(BF16)
            slope16 = (term - prob * delta).astype(BF16)
            prob_own, slope_own = prob16 * own16, slope16 * own16
            prob2[:WINDOW, wide(index)] = prob_own
            prob2[WINDOW:, wide(index)] = prob16 - prob_own
            slope2[:WINDOW, wide(index)] = slope_own
            slope2[WINDOW:, wide(index)] = slope16 - slope_own
            sink_term = sink_weight * inverse * delta
            sink_rows[row : row + 1] += sink_term[:, :WINDOW]
            sink_rows[row + 1 : row + 2] += sink_term[:, WINDOW:]

        def finish(index):
            for source, turned, out_ref in ((prob2, turned_v, o_ref), (slope2, turned_k, dq_ref)):
                out_t = jnp.dot(
                    turned[feats(index)], source[:, wide(index)], preferred_element_type=F32
                ).astype(BF16)
                out_ref[:, columns(index)] = jnp.concatenate(
                    [out_t[:, :128], out_t[:, 128:]], axis=0
                ).T

        def reduce(unit):
            lanes = slice(unit * couples * 256, (unit + 1) * couples * 256)
            dk = lax.dot_general(
                slope2[:, lanes], q_turned[:, lanes], turn, preferred_element_type=F32
            )
            dv = lax.dot_general(
                prob2[:, lanes], g_turned[:, lanes], turn, preferred_element_type=F32
            )
            return dk * FACTOR, dv

        total = 2 * couples
        ahead = {0: products(0)}
        grads = []
        for index in range(total):
            if index + 1 < total:
                ahead[index + 1] = products(index + 1)
            weigh(index, *ahead.pop(index))
            if index >= 1:
                finish(index - 1)
            if index == couples:
                grads.append(reduce(0))
        finish(total - 1)
        grads.append(reduce(1))
        dk = jnp.concatenate([grads[0][0], grads[1][0]], axis=1)
        dv = jnp.concatenate([grads[0][1], grads[1][1]], axis=1)
        dk_ref[here, :] = dk[:WINDOW]
        dv_ref[here, :] = dv[:WINDOW]

        @pl.when(opening & prev_ok)
        def _():
            tail_sum[:, :128] += dk[WINDOW:]
            tail_sum[:, 128:] += dv[WINDOW:]

        @pl.when(jnp.logical_not(opening) & first)
        def _():
            dhalo_ref[0, :, :128] = dk[WINDOW:].astype(BF16)
            dhalo_ref[0, :, 128:] = dv[WINDOW:].astype(BF16)

        @pl.when(jnp.logical_not(opening) & jnp.logical_not(first))
        def _():
            dk_ref[before, :] += dk[WINDOW:]
            dv_ref[before, :] += dv[WINDOW:]

    @pl.when(block == blocks_here - 1)
    def _():
        slots, width = dtail_ref.shape[0], dtail_ref.shape[2]
        heads = 2 * GROUP // slots
        total = tail_sum[...].astype(BF16)
        for slot in range(slots):
            feats = slice(slot * width // 2, (slot + 1) * width // 2)
            dtail_ref[slot, :WINDOW] = jnp.concatenate(
                [total[:, :128][:, feats], total[:, 128:][:, feats]], axis=1
            )
            rows = sink_rows[slot * heads : (slot + 1) * heads]
            rows = jnp.concatenate([rows, jnp.zeros((128 - heads, WINDOW), F32)], axis=0)
            sink_row = jnp.sum(rows.T, axis=0, keepdims=True)
            if width > 128:
                sink_row = jnp.concatenate([sink_row, jnp.zeros((1, width - 128), F32)], axis=1)
            dtail_ref[slot, WINDOW:] = row_split(sink_row, (EXTRA, width))


def gather_kernel(in_ref, out_ref):
    total = in_ref[0, :WINDOW].astype(F32)
    sink_row = row_join(in_ref[0, WINDOW:])
    for slot in range(1, in_ref.shape[0]):
        total = total + in_ref[slot, :WINDOW].astype(F32)
        sink_row = sink_row + row_join(in_ref[slot, WINDOW:])
    out_ref[:WINDOW] = total.astype(BF16)
    out_ref[WINDOW:] = row_split(sink_row, (EXTRA, in_ref.shape[2]))


def land_kernel(tok_count, blocks, table, here_ref, *refs):
    tok = lax.axis_index("tok")
    *in_refs, out_ref, sink_ref = refs
    state = [
        child_tail(table, tok, distance, tok_count, blocks) for distance in range(1, LAG + 1)
    ]
    out_ref[...] = jnp.zeros_like(out_ref)
    sink_row = row_join(here_ref[WINDOW:])
    for (valid, place), in_ref in zip(state, in_refs):
        sink_row = sink_row + row_join(in_ref[WINDOW:])

        @pl.when(valid)
        def _(place=place, in_ref=in_ref):
            total = out_ref[place].astype(F32) + in_ref[:WINDOW].astype(F32)
            out_ref[place] = total.astype(BF16)

    sink_ref[...] = jnp.broadcast_to(sink_row[:, :128], sink_ref.shape)


def total_kernel(
    dk_ref, dv_ref, halo_ref, tail_ref, sink_ref, far_ref, key_ref, value_ref, sink_grad
):
    rows = dk_ref.shape[0]
    slots, width = tail_ref.shape[0], tail_ref.shape[2] // 2
    halo_k = jnp.concatenate([halo_ref[pair][:, :128] for pair in range(PAIRS)], axis=1)
    halo_v = jnp.concatenate([halo_ref[pair][:, 128:] for pair in range(PAIRS)], axis=1)
    for in_ref, halo, at, out_ref in (
        (dk_ref, halo_k, 0, key_ref),
        (dv_ref, halo_v, width, value_ref),
    ):
        for begin in range(0, rows, WINDOW):
            here = slice(begin, begin + WINDOW)
            tails = [tail_ref[slot, here, at : at + width] for slot in range(slots)]
            total = in_ref[here, :] + jnp.concatenate(tails, axis=1).astype(F32)
            if begin == rows - WINDOW:
                total = total + halo.astype(F32)
            out_ref[here, :] = total.astype(BF16)
    sink_row = -(sink_ref[0:1] + far_ref[0:1])
    for head in range(sink_grad.shape[0]):
        sink_grad[head] = sink_row[0, head]


def local(
    queries, key_states, value_states, out_grad, sink_logits, branch_start, branch_len, parent_list
):
    tok_count, head_count = lax.axis_size("tok"), lax.axis_size("head")
    rows = queries.shape[0]
    blocks_here = rows // WINDOW
    blocks = blocks_here * head_count
    per_slot = KV_HEADS // head_count
    width = 2 * per_slot * HEAD_DIM

    def shape(dims, kind=BF16):
        return jax.ShapeDtypeStruct(dims, kind)

    table = jnp.concatenate([branch_start, branch_len, parent_list[:, 0], parent_list[:, 1]])
    slots, halo_out = pl.pallas_call(
        pack_kernel,
        out_shape=(shape((head_count, rows + EXTRA, width)), shape((PAIRS, WINDOW, 256))),
        in_specs=[SMEM, VMEM, VMEM],
        out_specs=(VMEM, VMEM),
        compiler_params=PARAMS,
        name="pack",
    )(sink_logits, key_states, value_states)
    halo = shift(halo_out, "head", 1)
    spread = lax.all_to_all(slots, "head", split_axis=0, concat_axis=0, tiled=True)
    *chosen, sinks = pl.pallas_call(
        functools.partial(choose_kernel, tok_count, blocks),
        out_shape=(shape((WINDOW, width)),) * LAG + (shape((KV_HEADS * GROUP, 128), F32),),
        in_specs=[SMEM, VMEM],
        out_specs=(VMEM,) * (LAG + 1),
        compiler_params=PARAMS,
        name="choose",
    )(table, spread)
    arrived = [shift(chosen[s - 1], "tok", s) for s in range(1, LAG + 1)]
    quarter = pl.pallas_call(
        functools.partial(arrive_kernel, tok_count),
        out_shape=shape((WINDOW, width)),
        in_specs=[SMEM] + [VMEM] * LAG,
        out_specs=VMEM,
        compiler_params=PARAMS,
        name="arrive",
    )(table, *arrived)
    tail = lax.all_gather(quarter, "head")
    slots_per_pair = 2 // per_slot
    big = pl.BlockSpec((WINDOW, 1024), lambda p, b: (b, p))
    small = pl.BlockSpec((rows, 128), lambda p, b: (0, p))
    near = pl.BlockSpec((1, WINDOW, 256), lambda p, b: (p, 0, 0))
    attended, query_grad, dk, dv, dhalo, dtail = pl.pallas_call(
        functools.partial(attend_kernel, tok_count, per_slot, blocks_here),
        grid=(PAIRS, blocks_here),
        out_shape=(
            shape(queries.shape),
            shape(queries.shape),
            shape(key_states.shape, F32),
            shape(key_states.shape, F32),
            shape((PAIRS, WINDOW, 256)),
            shape((head_count, WINDOW + EXTRA, width)),
        ),
        in_specs=[
            SMEM,
            pl.BlockSpec((2 * GROUP, 128), lambda p, b: (p, 0)),
            big,
            big,
            small,
            small,
            near,
            pl.BlockSpec((slots_per_pair, WINDOW, width), lambda p, b: (p, 0, 0)),
        ],
        out_specs=(
            big,
            big,
            small,
            small,
            near,
            pl.BlockSpec((slots_per_pair, WINDOW + EXTRA, width), lambda p, b: (p, 0, 0)),
        ),
        scratch_shapes=[
            pltpu.VMEM((WINDOW, 256), F32),
            pltpu.VMEM((2 * GROUP, WINDOW), F32),
            pltpu.VMEM((HEAD_DIM, 2048), BF16),
            pltpu.VMEM((HEAD_DIM, 2048), BF16),
            pltpu.VMEM((2 * WINDOW, 2048), BF16),
            pltpu.VMEM((2 * WINDOW, 2048), BF16),
        ],
        compiler_params=PARAMS,
        name="attend",
    )(table, sinks, queries, out_grad, key_states, value_states, halo, tail)
    halo_back = shift(dhalo, "head", -1)
    parts = lax.all_to_all(dtail, "head", split_axis=0, concat_axis=0, tiled=True)
    quarter_grad = pl.pallas_call(
        gather_kernel,
        out_shape=shape((WINDOW + EXTRA, width)),
        in_specs=[VMEM],
        out_specs=VMEM,
        compiler_params=PARAMS,
        name="gather",
    )(parts)
    returned = [ring(quarter_grad, "tok", -s) for s in range(1, LAG + 1)]
    landed, sink_near = pl.pallas_call(
        functools.partial(land_kernel, tok_count, blocks),
        out_shape=(shape((blocks, WINDOW, width)), shape((8, 128), F32)),
        in_specs=[SMEM] + [VMEM] * (LAG + 1),
        out_specs=(VMEM, VMEM),
        compiler_params=PARAMS,
        name="land",
    )(table, quarter_grad, *returned)
    tails_back = lax.all_to_all(
        landed.reshape(head_count, rows, width), "head", split_axis=0, concat_axis=0, tiled=True
    )
    span = LAG + 1
    while 2 * span < tok_count:
        sink_near = sink_near + ring(sink_near, "tok", -span)
        span *= 2
    sink_far = ring(sink_near, "tok", -span)
    key_grad, value_grad, sink_grad = pl.pallas_call(
        total_kernel,
        out_shape=(
            shape(key_states.shape),
            shape(value_states.shape),
            shape(sink_logits.shape, F32),
        ),
        in_specs=[VMEM] * 6,
        out_specs=(VMEM, VMEM, SMEM),
        compiler_params=PARAMS,
        name="total",
    )(dk, dv, halo_back, tails_back, sink_near, sink_far)
    return attended, query_grad, key_grad, value_grad, sink_grad


def solution(mesh):
    rows = P(("tok", "head"), None)
    return jax.shard_map(
        local,
        mesh=mesh,
        in_specs=(rows, rows, rows, rows, P("head"), P(), P(), P()),
        out_specs=(rows, rows, rows, rows, P("head")),
        check_vma=False,
    )
```

```python
import functools

import jax
import jax.numpy as jnp
from jax import lax
from jax.experimental import pallas as pl
from jax.experimental.pallas import tpu as pltpu
from jax.sharding import PartitionSpec as P

HEAD_DIM = 64
KV_HEADS = 8
GROUP = 8
WINDOW = 128
LAG = 3
BR_DEV = 2
PAIRS = KV_HEADS // 2
FACTOR = 0.125
LOW = -1e30
EXTRA = 16
BF16 = jnp.bfloat16
F32 = jnp.float32

SMEM = pl.BlockSpec(memory_space=pltpu.SMEM)
VMEM = pl.BlockSpec(memory_space=pltpu.VMEM)
HBM = pl.BlockSpec(memory_space=pltpu.HBM)
PARAMS = pltpu.CompilerParams(vmem_limit_bytes=24 * 1024 * 1024)


def shift(value, axis, steps):
    count = lax.axis_size(axis)
    leading, last = (max(0, -steps), min(count, count - steps))
    return lax.ppermute(value, axis, [(source, source + steps) for source in range(leading, last)])


def ring(value, axis, steps):
    count = lax.axis_size(axis)
    return lax.ppermute(value, axis, [(source, (source + steps) % count) for source in range(count)])


def row_split(row, dims):
    high = row.astype(BF16).astype(F32)
    middle = (row - high).astype(BF16).astype(F32)
    low = row - high - middle
    place = lax.broadcasted_iota(jnp.int32, dims, 0)
    rest = jnp.where(place == 2, low, 0.0)
    return jnp.where(place == 0, high, jnp.where(place == 1, middle, rest)).astype(BF16)


def row_join(rows):
    rows = rows.astype(F32)
    return rows[0:1] + rows[1:2] + rows[2:3]


def child_tail(table, tok, distance, tok_count, blocks):
    branches = tok_count * BR_DEV
    child = jnp.minimum(tok + distance, tok_count - 1) * BR_DEV
    parent = table[2 * branches + child]
    safe = jnp.maximum(parent, 0)
    valid = (tok + distance < tok_count) & (parent >= 0) & (safe // BR_DEV == tok)
    place = (table[safe] + table[3 * branches + child]) // WINDOW - tok * blocks
    return valid, jnp.where(valid, place, 0)


def block_state(table, tok, tok_count, block):
    branches = tok_count * BR_DEV
    position = block * WINDOW
    alive, opening = jnp.bool_(False), jnp.bool_(False)
    for branch in range(BR_DEV):
        start = table[tok * BR_DEV + branch]
        length = table[branches + tok * BR_DEV + branch]
        alive = alive | ((start <= position) & (position < start + length))
        opening = opening | (start == position)
    has_tail = table[2 * branches + tok * BR_DEV] >= 0
    return alive, opening, jnp.logical_not(opening) | has_tail


def take(ref, slot, width):
    if width % 128 == 0:
        return ref[:, pl.ds(pl.multiple_of(slot * width, width), width)]
    value = ref[:, :width]
    for other in range(1, ref.shape[1] // width):
        value = jnp.where(slot == other, ref[:, other * width : (other + 1) * width], value)
    return value


def pack_kernel(sink_hbm, key_hbm, value_hbm, *refs):
    *slot_refs, halo_ref, sinks, keys, values, sems = refs
    copies = [
        pltpu.make_async_copy(source, target, sems.at[place])
        for place, (source, target) in enumerate(
            ((sink_hbm, sinks), (key_hbm, keys), (value_hbm, values))
        )
    ]
    for copy in copies:
        copy.start()
    for copy in copies:
        copy.wait()
    slots, rows = len(slot_refs), keys.shape[0]
    head = lax.axis_index("head")
    width = KV_HEADS * HEAD_DIM // slots
    lane = lax.broadcasted_iota(jnp.int32, (1, 2 * width), 1)
    sink_row = jnp.zeros((1, 2 * width), F32)
    for place in range(sinks.shape[0]):
        sink_row = jnp.where(lane == place, sinks[place], sink_row)
    extra = row_split(sink_row, (EXTRA, 2 * width))
    for step, slot_ref in enumerate(slot_refs):
        slot = lax.rem(head + step, slots)
        slot_ref[:rows] = jnp.concatenate(
            [take(keys, slot, width), take(values, slot, width)], axis=1
        )
        slot_ref[rows:] = extra
    for pair in range(PAIRS):
        lanes = slice(pair * 128, (pair + 1) * 128)
        last = slice(rows - WINDOW, rows)
        halo_ref[pair] = jnp.concatenate([keys[last, lanes], values[last, lanes]], axis=1)


def choose_kernel(tok_count, blocks, table, *refs):
    slots = len(refs) - LAG - 1
    slot_refs, out_refs, sink_ref = refs[:slots], refs[slots:-1], refs[-1]
    tok, head = lax.axis_index("tok"), lax.axis_index("head")
    rows = slot_refs[0].shape[0] - EXTRA
    blocks_here = rows // WINDOW
    heads = sink_ref.shape[0] // slots
    for distance, out_ref in enumerate(out_refs, 1):
        _, place = child_tail(table, tok, distance, tok_count, blocks)
        begin = pl.multiple_of(place % blocks_here * WINDOW, WINDOW)
        wanted = lax.rem(head - place // blocks_here + slots, slots)
        for step, slot_ref in enumerate(slot_refs):

            @pl.when(wanted == step)
            def _(out_ref=out_ref, slot_ref=slot_ref, begin=begin):
                out_ref[...] = slot_ref[pl.ds(begin, WINDOW), :]

    for step, slot_ref in enumerate(slot_refs):
        source = lax.rem(head - step + slots, slots)
        sink_row = row_join(slot_ref[rows:, :])[:, :128]
        turned = jnp.broadcast_to(sink_row, (128, 128)).T
        sink_ref[pl.ds(pl.multiple_of(source * heads, heads), heads), :] = turned[:heads]


def arrive_kernel(tok_count, table, *refs):
    tok = lax.axis_index("tok")
    *in_refs, out_ref = refs
    parent = table[2 * tok_count * BR_DEV + tok * BR_DEV]
    mine = jnp.where(parent >= 0, tok - jnp.maximum(parent, 0) // BR_DEV, 1)
    for distance, in_ref in enumerate(in_refs, 1):

        @pl.when(mine == distance)
        def _(in_ref=in_ref):
            out_ref[...] = in_ref[...]


def attend_kernel(
    tok_count,
    blocks_here,
    slots,
    table,
    sink_ref,
    q_ref,
    g_ref,
    k_ref,
    v_ref,
    halo_ref,
    *refs,
):
    tail_refs, refs = refs[:slots], refs[slots:]
    o_ref, dq_ref, dk_ref, dv_ref, dhalo_ref = refs[:5]
    dtail_refs, refs = refs[5 : 5 + slots], refs[5 + slots :]
    tails, tail_sum, sink_rows, q_turned, g_turned, prob2, slope2 = refs
    per_slot = KV_HEADS // slots
    pair, block = pl.program_id(0), pl.program_id(1)
    tok, head = lax.axis_index("tok"), lax.axis_index("head")
    number = (tok * lax.axis_size("head") + head) * blocks_here + block
    alive, opening, prev_ok = block_state(table, tok, tok_count, number)
    here = pl.ds(pl.multiple_of(block * WINDOW, WINDOW), WINDOW)
    before = pl.ds(pl.multiple_of(jnp.maximum(block - 1, 0) * WINDOW, WINDOW), WINDOW)
    first = block == 0

    @pl.when(first & (pair == 0))
    def _():
        for step, tail_ref in enumerate(tail_refs):
            tails[lax.rem(head - step + slots, slots)] = tail_ref[...]

    @pl.when(first)
    def _():
        tail_sum[...] = jnp.zeros_like(tail_sum)
        dhalo_ref[...] = jnp.zeros_like(dhalo_ref)
        sink_rows[...] = jnp.zeros_like(sink_rows)

    @pl.when(jnp.logical_not(alive))
    def _():
        o_ref[...] = jnp.zeros_like(o_ref)
        dq_ref[...] = jnp.zeros_like(dq_ref)
        dk_ref[here, :] = jnp.zeros((WINDOW, 128), F32)
        dv_ref[here, :] = jnp.zeros((WINDOW, 128), F32)

    @pl.when(alive)
    def _():
        halo = halo_ref[0]
        if per_slot == 2:
            tail = tails[pair]
            tail_k, tail_v = tail[:, :128], tail[:, 128:]
        else:
            tail_a, tail_b = tails[2 * pair], tails[2 * pair + 1]
            tail_k = jnp.concatenate([tail_a[:, :64], tail_b[:, :64]], axis=1)
            tail_v = jnp.concatenate([tail_a[:, 64:], tail_b[:, 64:]], axis=1)
        near_k = jnp.where(first, halo[:, :128], k_ref[before, :])
        near_v = jnp.where(first, halo[:, 128:], v_ref[before, :])
        prev_k = jnp.where(opening, tail_k, near_k)
        prev_v = jnp.where(opening, tail_v, near_v)
        both_k = jnp.concatenate([k_ref[here, :], prev_k], axis=0) * BF16(FACTOR)
        both_v = jnp.concatenate([v_ref[here, :], prev_v], axis=0)
        turned_k, turned_v = both_k.T, both_v.T
        bias = jnp.where(prev_ok, 0.0, LOW)
        key_place = lax.broadcasted_iota(jnp.int32, (WINDOW, WINDOW), 0)
        query_place = lax.broadcasted_iota(jnp.int32, (WINDOW, WINDOW), 1)
        own_one = key_place <= query_place
        own = jnp.concatenate([own_one, own_one], axis=1)
        own16 = own.astype(F32).astype(BF16)
        turn = (((1,), (1,)), ((), ()))
        couples = GROUP // 2

        def columns(index):
            return slice(index * 128, (index + 1) * 128)

        def wide(index):
            return slice(index * 256, (index + 1) * 256)

        def feats(index):
            unit = index // couples
            return slice(unit * HEAD_DIM, (unit + 1) * HEAD_DIM)

        def products(index):
            q_t, g_t = q_ref[:, columns(index)].T, g_ref[:, columns(index)].T
            q_t = jnp.concatenate([q_t[:64], q_t[64:]], axis=1)
            g_t = jnp.concatenate([g_t[:64], g_t[64:]], axis=1)
            q_turned[:, wide(index)] = q_t
            g_turned[:, wide(index)] = g_t
            score2 = jnp.dot(both_k[:, feats(index)], q_t, preferred_element_type=F32)
            dp2 = jnp.dot(both_v[:, feats(index)], g_t, preferred_element_type=F32)
            score = jnp.where(own, score2[:WINDOW], score2[WINDOW:] + bias)
            return score, jnp.where(own, dp2[:WINDOW], dp2[WINDOW:])

        def weigh(index, score, dp):
            row = index * 2
            sink = jnp.concatenate([sink_ref[row : row + 1], sink_ref[row + 1 : row + 2]], axis=1)
            peak = jnp.maximum(jnp.max(score, axis=0, keepdims=True), sink)
            weight = jnp.exp(score - peak)
            sink_weight = jnp.exp(sink - peak)
            inverse = 1.0 / (jnp.sum(weight, axis=0, keepdims=True) + sink_weight)
            prob = weight * inverse
            term = prob * dp
            delta = jnp.sum(term, axis=0, keepdims=True)
            prob16 = prob.astype(BF16)
            slope16 = (term - prob * delta).astype(BF16)
            prob_own, slope_own = prob16 * own16, slope16 * own16
            prob2[:WINDOW, wide(index)] = prob_own
            prob2[WINDOW:, wide(index)] = prob16 - prob_own
            slope2[:WINDOW, wide(index)] = slope_own
            slope2[WINDOW:, wide(index)] = slope16 - slope_own
            sink_term = sink_weight * inverse * delta
            sink_rows[row : row + 1] += sink_term[:, :WINDOW]
            sink_rows[row + 1 : row + 2] += sink_term[:, WINDOW:]

        def finish(index):
            for source, turned, out_ref in ((prob2, turned_v, o_ref), (slope2, turned_k, dq_ref)):
                out_t = jnp.dot(
                    turned[feats(index)], source[:, wide(index)], preferred_element_type=F32
                ).astype(BF16)
                out_ref[:, columns(index)] = jnp.concatenate(
                    [out_t[:, :128], out_t[:, 128:]], axis=0
                ).T

        def reduce(unit):
            lanes = slice(unit * couples * 256, (unit + 1) * couples * 256)
            dk = lax.dot_general(
                slope2[:, lanes], q_turned[:, lanes], turn, preferred_element_type=F32
            )
            dv = lax.dot_general(
                prob2[:, lanes], g_turned[:, lanes], turn, preferred_element_type=F32
            )
            return dk * FACTOR, dv

        total = 2 * couples
        ahead = {0: products(0)}
        grads = []
        for index in range(total):
            if index + 1 < total:
                ahead[index + 1] = products(index + 1)
            weigh(index, *ahead.pop(index))
            if index >= 1:
                finish(index - 1)
            if index == couples:
                grads.append(reduce(0))
        finish(total - 1)
        grads.append(reduce(1))
        dk = jnp.concatenate([grads[0][0], grads[1][0]], axis=1)
        dv = jnp.concatenate([grads[0][1], grads[1][1]], axis=1)
        dk_ref[here, :] = dk[:WINDOW]
        dv_ref[here, :] = dv[:WINDOW]

        @pl.when(opening & prev_ok)
        def _():
            tail_sum[:, :128] += dk[WINDOW:]
            tail_sum[:, 128:] += dv[WINDOW:]

        @pl.when(jnp.logical_not(opening) & first)
        def _():
            dhalo_ref[0, :, :128] = dk[WINDOW:].astype(BF16)
            dhalo_ref[0, :, 128:] = dv[WINDOW:].astype(BF16)

        @pl.when(jnp.logical_not(opening) & jnp.logical_not(first))
        def _():
            dk_ref[before, :] += dk[WINDOW:]
            dv_ref[before, :] += dv[WINDOW:]

    @pl.when(block == blocks_here - 1)
    def _():
        width = dtail_refs[0].shape[1]
        heads = per_slot * GROUP
        total = tail_sum[...].astype(BF16)
        for part in range(2 // per_slot):
            feats = slice(part * width // 2, (part + 1) * width // 2)
            tail = jnp.concatenate([total[:, :128][:, feats], total[:, 128:][:, feats]], axis=1)
            rows = sink_rows[part * heads : (part + 1) * heads]
            rows = jnp.concatenate([rows, jnp.zeros((128 - heads, WINDOW), F32)], axis=0)
            sink_row = jnp.sum(rows.T, axis=0, keepdims=True)
            if width > 128:
                sink_row = jnp.concatenate([sink_row, jnp.zeros((1, width - 128), F32)], axis=1)
            extra = row_split(sink_row, (EXTRA, width))
            wanted = lax.rem(pair * (2 // per_slot) + part - head + slots, slots)
            for step, dtail_ref in enumerate(dtail_refs):

                @pl.when(wanted == step)
                def _(dtail_ref=dtail_ref, tail=tail, extra=extra):
                    dtail_ref[:WINDOW] = tail
                    dtail_ref[WINDOW:] = extra


def gather_kernel(*refs):
    *in_refs, out_ref = refs
    total, sink_row = 0.0, 0.0
    for in_ref in in_refs:
        total = total + in_ref[:WINDOW].astype(F32)
        sink_row = sink_row + row_join(in_ref[WINDOW:])
    out_ref[:WINDOW] = total.astype(BF16)
    out_ref[WINDOW:] = row_split(sink_row, (EXTRA, out_ref.shape[1]))


def land_kernel(tok_count, blocks, table, here_ref, *refs):
    tok, head = lax.axis_index("tok"), lax.axis_index("head")
    in_refs, out_refs, sink_ref = refs[:LAG], refs[LAG:-1], refs[-1]
    slots = len(out_refs)
    blocks_here = blocks // slots
    for out_ref in out_refs:
        out_ref[...] = jnp.zeros_like(out_ref)
    sink_row = row_join(here_ref[WINDOW:])
    for distance, in_ref in enumerate(in_refs, 1):
        valid, place = child_tail(table, tok, distance, tok_count, blocks)
        sink_row = sink_row + row_join(in_ref[WINDOW:])
        wanted = lax.rem(place // blocks_here - head + slots, slots)
        here = pl.ds(pl.multiple_of(place % blocks_here * WINDOW, WINDOW), WINDOW)
        for step, out_ref in enumerate(out_refs):

            @pl.when(valid & (wanted == step))
            def _(out_ref=out_ref, in_ref=in_ref, here=here):
                total = out_ref[here, :].astype(F32) + in_ref[:WINDOW].astype(F32)
                out_ref[here, :] = total.astype(BF16)

    sink_ref[...] = jnp.broadcast_to(sink_row[:, :128], sink_ref.shape)


def total_kernel(dk_ref, dv_ref, halo_ref, sink_ref, far_ref, *refs):
    *tail_refs, key_ref, value_ref, sink_grad, tails = refs
    slots, rows = len(tail_refs), dk_ref.shape[0]
    width = tails.shape[2] // 2
    head = lax.axis_index("head")
    for step, tail_ref in enumerate(tail_refs):
        tails[lax.rem(head - step + slots, slots)] = tail_ref[...]
    halo_k = jnp.concatenate([halo_ref[pair][:, :128] for pair in range(PAIRS)], axis=1)
    halo_v = jnp.concatenate([halo_ref[pair][:, 128:] for pair in range(PAIRS)], axis=1)
    for in_ref, halo, at, out_ref in (
        (dk_ref, halo_k, 0, key_ref),
        (dv_ref, halo_v, width, value_ref),
    ):
        for begin in range(0, rows, WINDOW):
            here = slice(begin, begin + WINDOW)
            parts = [tails[slot, here, at : at + width] for slot in range(slots)]
            total = in_ref[here, :] + jnp.concatenate(parts, axis=1).astype(F32)
            if begin == rows - WINDOW:
                total = total + halo.astype(F32)
            out_ref[here, :] = total.astype(BF16)
    sink_row = -(sink_ref[0:1] + far_ref[0:1])
    for place in range(sink_grad.shape[0]):
        sink_grad[place] = sink_row[0, place]


def swap(values, axis):
    return [values[0]] + [ring(values[step], axis, step) for step in range(1, len(values))]


def local(
    queries, key_states, value_states, out_grad, sink_logits, branch_start, branch_len, parent_list
):
    tok_count, head_count = lax.axis_size("tok"), lax.axis_size("head")
    rows = queries.shape[0]
    blocks_here = rows // WINDOW
    blocks = blocks_here * head_count
    per_slot = KV_HEADS // head_count
    width = 2 * per_slot * HEAD_DIM

    def shape(dims, kind=BF16):
        return jax.ShapeDtypeStruct(dims, kind)

    table = jnp.concatenate([branch_start, branch_len, parent_list[:, 0], parent_list[:, 1]])
    *slots, halo_out = pl.pallas_call(
        pack_kernel,
        out_shape=(shape((rows + EXTRA, width)),) * head_count + (shape((PAIRS, WINDOW, 256)),),
        in_specs=[HBM] * 3,
        out_specs=(VMEM,) * (head_count + 1),
        scratch_shapes=[
            pltpu.SMEM(sink_logits.shape, F32),
            pltpu.VMEM(key_states.shape, BF16),
            pltpu.VMEM(key_states.shape, BF16),
            pltpu.SemaphoreType.DMA((3,)),
        ],
        compiler_params=PARAMS,
        name="pack",
    )(sink_logits, key_states, value_states)
    spread = swap(slots, "head")
    *chosen, sinks = pl.pallas_call(
        functools.partial(choose_kernel, tok_count, blocks),
        out_shape=(shape((WINDOW, width)),) * LAG + (shape((KV_HEADS * GROUP, 128), F32),),
        in_specs=[SMEM] + [VMEM] * head_count,
        out_specs=(VMEM,) * (LAG + 1),
        compiler_params=PARAMS,
        name="choose",
    )(table, *spread)
    arrived = [shift(chosen[s - 1], "tok", s) for s in range(LAG, 0, -1)][::-1]
    halo_out, _ = lax.optimization_barrier((halo_out, chosen[0]))
    halo = shift(halo_out, "head", 1)
    quarter = pl.pallas_call(
        functools.partial(arrive_kernel, tok_count),
        out_shape=shape((WINDOW, width)),
        in_specs=[SMEM] + [VMEM] * LAG,
        out_specs=VMEM,
        compiler_params=PARAMS,
        name="arrive",
    )(table, *arrived)
    tails = swap([quarter] * head_count, "head")
    big = pl.BlockSpec((WINDOW, 1024), lambda p, b: (b, p))
    small = pl.BlockSpec((rows, 128), lambda p, b: (0, p))
    near = pl.BlockSpec((1, WINDOW, 256), lambda p, b: (p, 0, 0))
    whole = pl.BlockSpec((WINDOW, width), lambda p, b: (0, 0))
    whole_back = pl.BlockSpec((WINDOW + EXTRA, width), lambda p, b: (0, 0))
    attended, query_grad, dk, dv, dhalo, *dtail = pl.pallas_call(
        functools.partial(attend_kernel, tok_count, blocks_here, head_count),
        grid=(PAIRS, blocks_here),
        out_shape=(
            shape(queries.shape),
            shape(queries.shape),
            shape(key_states.shape, F32),
            shape(key_states.shape, F32),
            shape((PAIRS, WINDOW, 256)),
        )
        + (shape((WINDOW + EXTRA, width)),) * head_count,
        in_specs=[
            SMEM,
            pl.BlockSpec((2 * GROUP, 128), lambda p, b: (p, 0)),
            big,
            big,
            small,
            small,
            near,
        ]
        + [whole] * head_count,
        out_specs=(big, big, small, small, near) + (whole_back,) * head_count,
        scratch_shapes=[
            pltpu.VMEM((head_count, WINDOW, width), BF16),
            pltpu.VMEM((WINDOW, 256), F32),
            pltpu.VMEM((2 * GROUP, WINDOW), F32),
            pltpu.VMEM((HEAD_DIM, 2048), BF16),
            pltpu.VMEM((HEAD_DIM, 2048), BF16),
            pltpu.VMEM((2 * WINDOW, 2048), BF16),
            pltpu.VMEM((2 * WINDOW, 2048), BF16),
        ],
        compiler_params=PARAMS,
        name="attend",
    )(table, sinks, queries, out_grad, key_states, value_states, halo, *tails)
    parts = swap(dtail, "head")
    quarter_grad = pl.pallas_call(
        gather_kernel,
        out_shape=shape((WINDOW + EXTRA, width)),
        in_specs=[VMEM] * head_count,
        out_specs=VMEM,
        compiler_params=PARAMS,
        name="gather",
    )(*parts)
    returned = [ring(quarter_grad, "tok", -s) for s in range(LAG, 0, -1)][::-1]
    dhalo, _ = lax.optimization_barrier((dhalo, quarter_grad))
    halo_back = shift(dhalo, "head", -1)
    *landed, sink_near = pl.pallas_call(
        functools.partial(land_kernel, tok_count, blocks),
        out_shape=(shape((rows, width)),) * head_count + (shape((8, 128), F32),),
        in_specs=[SMEM] + [VMEM] * (LAG + 1),
        out_specs=(VMEM,) * (head_count + 1),
        compiler_params=PARAMS,
        name="land",
    )(table, quarter_grad, *returned)
    tails_back = swap(landed, "head")
    span = LAG + 1
    while 2 * span < tok_count:
        sink_near = sink_near + ring(sink_near, "tok", -span)
        span *= 2
    sink_far = ring(sink_near, "tok", -span)
    key_grad, value_grad, sink_grad = pl.pallas_call(
        total_kernel,
        out_shape=(
            shape(key_states.shape),
            shape(value_states.shape),
            shape(sink_logits.shape, F32),
        ),
        in_specs=[VMEM] * (5 + head_count),
        out_specs=(VMEM, VMEM, SMEM),
        scratch_shapes=[pltpu.VMEM((head_count, rows, width), BF16)],
        compiler_params=PARAMS,
        name="total",
    )(dk, dv, halo_back, sink_near, sink_far, *tails_back)
    return attended, query_grad, key_grad, value_grad, sink_grad


def solution(mesh):
    rows = P(("tok", "head"), None)
    return jax.shard_map(
        local,
        mesh=mesh,
        in_specs=(rows, rows, rows, rows, P("head"), P(), P(), P()),
        out_specs=(rows, rows, rows, rows, P("head")),
        check_vma=False,
    )
```

```python
import functools

import jax
import jax.numpy as jnp
from jax import lax
from jax.experimental import pallas as pl
from jax.experimental.pallas import tpu as pltpu
from jax.sharding import PartitionSpec as P

HEAD_DIM = 64
KV_HEADS = 8
GROUP = 8
WINDOW = 128
HALF = WINDOW // 2
LAG = 3
BR_DEV = 2
PAIRS = KV_HEADS // 2
FACTOR = 0.125
LOW = -1e30
EXTRA = 16
BF16 = jnp.bfloat16
F32 = jnp.float32

SMEM = pl.BlockSpec(memory_space=pltpu.SMEM)
VMEM = pl.BlockSpec(memory_space=pltpu.VMEM)
HBM = pl.BlockSpec(memory_space=pltpu.HBM)
PARAMS = pltpu.CompilerParams(vmem_limit_bytes=24 * 1024 * 1024)


def shift(value, axis, steps):
    count = lax.axis_size(axis)
    leading, last = (max(0, -steps), min(count, count - steps))
    return lax.ppermute(value, axis, [(source, source + steps) for source in range(leading, last)])


def ring(value, axis, steps):
    count = lax.axis_size(axis)
    return lax.ppermute(value, axis, [(source, (source + steps) % count) for source in range(count)])


def row_split(row, dims):
    high = row.astype(BF16).astype(F32)
    middle = (row - high).astype(BF16).astype(F32)
    low = row - high - middle
    place = lax.broadcasted_iota(jnp.int32, dims, 0)
    rest = jnp.where(place == 2, low, 0.0)
    return jnp.where(place == 0, high, jnp.where(place == 1, middle, rest)).astype(BF16)


def row_join(rows):
    rows = rows.astype(F32)
    return rows[0:1] + rows[1:2] + rows[2:3]


def child_tail(table, tok, distance, tok_count, blocks):
    branches = tok_count * BR_DEV
    child = jnp.minimum(tok + distance, tok_count - 1) * BR_DEV
    parent = table[2 * branches + child]
    safe = jnp.maximum(parent, 0)
    valid = (tok + distance < tok_count) & (parent >= 0) & (safe // BR_DEV == tok)
    place = (table[safe] + table[3 * branches + child]) // WINDOW - tok * blocks
    return valid, jnp.where(valid, place, 0)


def block_state(table, tok, tok_count, block):
    branches = tok_count * BR_DEV
    position = block * WINDOW
    alive, opening = jnp.bool_(False), jnp.bool_(False)
    for branch in range(BR_DEV):
        start = table[tok * BR_DEV + branch]
        length = table[branches + tok * BR_DEV + branch]
        alive = alive | ((start <= position) & (position < start + length))
        opening = opening | (start == position)
    has_tail = table[2 * branches + tok * BR_DEV] >= 0
    return alive, opening, jnp.logical_not(opening) | has_tail


def take(ref, slot, width):
    if width % 128 == 0:
        return ref[:, pl.ds(pl.multiple_of(slot * width, width), width)]
    value = ref[:, :width]
    for other in range(1, ref.shape[1] // width):
        value = jnp.where(slot == other, ref[:, other * width : (other + 1) * width], value)
    return value


def pack_kernel(sink_hbm, key_hbm, value_hbm, *refs):
    *slot_refs, halo_ref, sinks, keys, values, sems = refs
    copies = [
        pltpu.make_async_copy(source, target, sems.at[place])
        for place, (source, target) in enumerate(
            ((sink_hbm, sinks), (key_hbm, keys), (value_hbm, values))
        )
    ]
    for copy in copies:
        copy.start()
    for copy in copies:
        copy.wait()
    slots, rows = len(slot_refs), keys.shape[0]
    head = lax.axis_index("head")
    width = KV_HEADS * HEAD_DIM // slots
    lane = lax.broadcasted_iota(jnp.int32, (1, 2 * width), 1)
    sink_row = jnp.zeros((1, 2 * width), F32)
    for place in range(sinks.shape[0]):
        sink_row = jnp.where(lane == place, sinks[place], sink_row)
    extra = row_split(sink_row, (EXTRA, 2 * width))
    for step, slot_ref in enumerate(slot_refs):
        slot = lax.rem(head + step, slots)
        slot_ref[:rows] = jnp.concatenate(
            [take(keys, slot, width), take(values, slot, width)], axis=1
        )
        slot_ref[rows:] = extra
    for pair in range(PAIRS):
        lanes = slice(pair * 128, (pair + 1) * 128)
        last = slice(rows - WINDOW, rows)
        halo_ref[pair] = jnp.concatenate([keys[last, lanes], values[last, lanes]], axis=1)


def choose_kernel(tok_count, blocks, table, *refs):
    slots = len(refs) - LAG - 1
    slot_refs, out_refs, sink_ref = refs[:slots], refs[slots:-1], refs[-1]
    tok, head = lax.axis_index("tok"), lax.axis_index("head")
    rows = slot_refs[0].shape[0] - EXTRA
    blocks_here = rows // WINDOW
    heads = sink_ref.shape[0] // slots
    for distance, out_ref in enumerate(out_refs, 1):
        _, place = child_tail(table, tok, distance, tok_count, blocks)
        begin = pl.multiple_of(place % blocks_here * WINDOW, WINDOW)
        wanted = lax.rem(head - place // blocks_here + slots, slots)
        for step, slot_ref in enumerate(slot_refs):

            @pl.when(wanted == step)
            def _(out_ref=out_ref, slot_ref=slot_ref, begin=begin):
                out_ref[...] = slot_ref[pl.ds(begin, WINDOW), :]

    for step, slot_ref in enumerate(slot_refs):
        source = lax.rem(head - step + slots, slots)
        sink_row = row_join(slot_ref[rows:, :])[:, :128]
        turned = jnp.broadcast_to(sink_row, (128, 128)).T
        sink_ref[pl.ds(pl.multiple_of(source * heads, heads), heads), :] = turned[:heads]


def arrive_kernel(tok_count, table, *refs):
    tok = lax.axis_index("tok")
    *in_refs, out_ref = refs
    parent = table[2 * tok_count * BR_DEV + tok * BR_DEV]
    mine = jnp.where(parent >= 0, tok - jnp.maximum(parent, 0) // BR_DEV, 1)
    for distance, in_ref in enumerate(in_refs, 1):

        @pl.when(mine == distance)
        def _(in_ref=in_ref):
            out_ref[...] = in_ref[...]


def attend_kernel(
    tok_count,
    blocks_here,
    slots,
    table,
    sink_ref,
    q_ref,
    g_ref,
    k_ref,
    v_ref,
    halo_ref,
    *refs,
):
    tail_refs, refs = refs[:slots], refs[slots:]
    o_ref, dq_ref, dk_ref, dv_ref, dhalo_ref = refs[:5]
    dtail_refs, refs = refs[5 : 5 + slots], refs[5 + slots :]
    tails, tail_sum, sink_rows, q_turned, g_turned, prob2, slope2 = refs
    per_slot = KV_HEADS // slots
    pair, block = pl.program_id(0), pl.program_id(1)
    tok, head = lax.axis_index("tok"), lax.axis_index("head")
    number = (tok * lax.axis_size("head") + head) * blocks_here + block
    alive, opening, prev_ok = block_state(table, tok, tok_count, number)
    here = pl.ds(pl.multiple_of(block * WINDOW, WINDOW), WINDOW)
    before = pl.ds(pl.multiple_of(jnp.maximum(block - 1, 0) * WINDOW, WINDOW), WINDOW)
    first = block == 0

    @pl.when(first & (pair == 0))
    def _():
        for step, tail_ref in enumerate(tail_refs):
            tails[lax.rem(head - step + slots, slots)] = tail_ref[...]

    @pl.when(first)
    def _():
        tail_sum[...] = jnp.zeros_like(tail_sum)
        dhalo_ref[...] = jnp.zeros_like(dhalo_ref)
        sink_rows[...] = jnp.zeros_like(sink_rows)

    @pl.when(jnp.logical_not(alive))
    def _():
        o_ref[...] = jnp.zeros_like(o_ref)
        dq_ref[...] = jnp.zeros_like(dq_ref)
        dk_ref[here, :] = jnp.zeros((WINDOW, 128), F32)
        dv_ref[here, :] = jnp.zeros((WINDOW, 128), F32)

    @pl.when(alive)
    def _():
        halo = halo_ref[0]
        if per_slot == 2:
            tail = tails[pair]
            tail_k, tail_v = tail[:, :128], tail[:, 128:]
        else:
            tail_a, tail_b = tails[2 * pair], tails[2 * pair + 1]
            tail_k = jnp.concatenate([tail_a[:, :64], tail_b[:, :64]], axis=1)
            tail_v = jnp.concatenate([tail_a[:, 64:], tail_b[:, 64:]], axis=1)
        near_k = jnp.where(first, halo[:, :128], k_ref[before, :])
        near_v = jnp.where(first, halo[:, 128:], v_ref[before, :])
        prev_k = jnp.where(opening, tail_k, near_k)
        prev_v = jnp.where(opening, tail_v, near_v)
        own_k, own_v = k_ref[here, :], v_ref[here, :]

        def halves(own, prev):
            return (
                jnp.concatenate([own[:HALF], prev[:HALF], prev[HALF:]], axis=0),
                jnp.concatenate([own[HALF:], prev[HALF:], own[:HALF]], axis=0),
            )

        seen_k = halves(own_k * BF16(FACTOR), prev_k * BF16(FACTOR))
        seen_v = halves(own_v, prev_v)
        turned_k = tuple(value.T for value in seen_k)
        turned_v = tuple(value.T for value in seen_v)
        bias = jnp.where(prev_ok, 0.0, LOW)
        key_place = lax.broadcasted_iota(jnp.int32, (HALF, 4 * HALF), 0)
        query_place = lax.broadcasted_iota(jnp.int32, (HALF, 4 * HALF), 1) & (HALF - 1)
        own = key_place <= query_place
        own16 = own.astype(F32).astype(BF16)
        left = lax.broadcasted_iota(jnp.int32, (1, 128), 1) < HALF
        turn = (((1,), (1,)), ((), ()))
        items = [(unit, half, quad) for unit in range(2) for half in range(2) for quad in range(2)]

        def wide(index):
            return slice(index * 256, (index + 1) * 256)

        def feats(index):
            unit = items[index][0]
            return slice(unit * HEAD_DIM, (unit + 1) * HEAD_DIM)

        def corner(index):
            unit, half, quad = items[index]
            lane = unit * 512 + quad * 256
            rows = slice(half * HALF, (half + 1) * HALF)
            return rows, slice(lane, lane + 128), slice(lane + 128, lane + 256)

        def turned(ref, index):
            rows, left_lanes, right_lanes = corner(index)
            tile = jnp.concatenate([ref[rows, left_lanes], ref[rows, right_lanes]], axis=0).T
            return jnp.concatenate([tile[:64], tile[64:]], axis=1)

        def products(index):
            half = items[index][1]
            q_t, g_t = turned(q_ref, index), turned(g_ref, index)
            q_turned[:, wide(index)] = q_t
            g_turned[:, wide(index)] = g_t
            score = jnp.dot(seen_k[half][:, feats(index)], q_t, preferred_element_type=F32)
            dp = jnp.dot(seen_v[half][:, feats(index)], g_t, preferred_element_type=F32)
            edge = jnp.where(own, score[:HALF], score[HALF : 2 * HALF] + bias)
            whole = score[2 * HALF :] + bias if half == 0 else score[2 * HALF :]
            dp_edge = jnp.where(own, dp[:HALF], dp[HALF : 2 * HALF])
            return edge, whole, dp_edge, dp[2 * HALF :]

        def weigh(index, edge, whole, dp_edge, dp_whole):
            unit, half, quad = items[index]
            row = unit * GROUP + quad * 4
            sink = jnp.concatenate(
                [
                    jnp.where(left, sink_ref[row : row + 1], sink_ref[row + 2 : row + 3]),
                    jnp.where(left, sink_ref[row + 1 : row + 2], sink_ref[row + 3 : row + 4]),
                ],
                axis=1,
            )
            peak = jnp.max(jnp.maximum(edge, whole), axis=0, keepdims=True)
            peak = jnp.maximum(peak, sink)
            edge, whole = jnp.exp(edge - peak), jnp.exp(whole - peak)
            sink_weight = jnp.exp(sink - peak)
            inverse = 1.0 / (jnp.sum(edge + whole, axis=0, keepdims=True) + sink_weight)
            edge, whole = edge * inverse, whole * inverse
            term_edge, term_whole = edge * dp_edge, whole * dp_whole
            delta = jnp.sum(term_edge + term_whole, axis=0, keepdims=True)
            for target, at_edge, at_whole in (
                (prob2, edge, whole),
                (slope2, term_edge - edge * delta, term_whole - whole * delta),
            ):
                edge16 = at_edge.astype(BF16)
                edge_own = edge16 * own16
                target[:HALF, wide(index)] = edge_own
                target[HALF : 2 * HALF, wide(index)] = edge16 - edge_own
                target[2 * HALF :, wide(index)] = at_whole.astype(BF16)
            sink_term = sink_weight * inverse * delta
            for place, lanes in enumerate((slice(0, 128), slice(128, 256))):
                part = sink_term[:, lanes]
                sink_rows[row + place : row + place + 1] += jnp.where(left, part, 0.0)
                sink_rows[row + place + 2 : row + place + 3] += jnp.where(left, 0.0, part)

        def finish(index):
            half = items[index][1]
            rows, left_lanes, right_lanes = corner(index)
            for source, across, out_ref in ((prob2, turned_v, o_ref), (slope2, turned_k, dq_ref)):
                out_t = jnp.dot(
                    across[half][feats(index)], source[:, wide(index)], preferred_element_type=F32
                ).astype(BF16)
                out = jnp.concatenate([out_t[:, :128], out_t[:, 128:]], axis=0).T
                out_ref[rows, left_lanes] = out[:HALF]
                out_ref[rows, right_lanes] = out[HALF:]

        def reduce(unit):
            totals = []
            for weights, rows in ((slope2, q_turned), (prob2, g_turned)):
                first_half, second_half = (
                    lax.dot_general(
                        weights[:, at : at + 512],
                        rows[:, at : at + 512],
                        turn,
                        preferred_element_type=F32,
                    )
                    for at in (unit * 1024, unit * 1024 + 512)
                )
                totals.append(
                    jnp.concatenate(
                        [
                            first_half[:HALF] + second_half[2 * HALF :],
                            second_half[:HALF],
                            first_half[HALF : 2 * HALF],
                            first_half[2 * HALF :] + second_half[HALF : 2 * HALF],
                        ],
                        axis=0,
                    )
                )
            return totals[0] * FACTOR, totals[1]

        total = len(items)
        ahead = {0: products(0)}
        grads = []
        for index in range(total):
            if index + 1 < total:
                ahead[index + 1] = products(index + 1)
            weigh(index, *ahead.pop(index))
            if index >= 1:
                finish(index - 1)
            if index == total // 2:
                grads.append(reduce(0))
        finish(total - 1)
        grads.append(reduce(1))
        dk = jnp.concatenate([grads[0][0], grads[1][0]], axis=1)
        dv = jnp.concatenate([grads[0][1], grads[1][1]], axis=1)
        dk_ref[here, :] = dk[:WINDOW]
        dv_ref[here, :] = dv[:WINDOW]

        @pl.when(opening & prev_ok)
        def _():
            tail_sum[:, :128] += dk[WINDOW:]
            tail_sum[:, 128:] += dv[WINDOW:]

        @pl.when(jnp.logical_not(opening) & first)
        def _():
            dhalo_ref[0, :, :128] = dk[WINDOW:].astype(BF16)
            dhalo_ref[0, :, 128:] = dv[WINDOW:].astype(BF16)

        @pl.when(jnp.logical_not(opening) & jnp.logical_not(first))
        def _():
            dk_ref[before, :] += dk[WINDOW:]
            dv_ref[before, :] += dv[WINDOW:]

    @pl.when(block == blocks_here - 1)
    def _():
        width = dtail_refs[0].shape[1]
        heads = per_slot * GROUP
        total = tail_sum[...].astype(BF16)
        for part in range(2 // per_slot):
            feats = slice(part * width // 2, (part + 1) * width // 2)
            tail = jnp.concatenate([total[:, :128][:, feats], total[:, 128:][:, feats]], axis=1)
            rows = sink_rows[part * heads : (part + 1) * heads]
            rows = jnp.concatenate([rows, jnp.zeros((128 - heads, WINDOW), F32)], axis=0)
            sink_row = jnp.sum(rows.T, axis=0, keepdims=True)
            if width > 128:
                sink_row = jnp.concatenate([sink_row, jnp.zeros((1, width - 128), F32)], axis=1)
            extra = row_split(sink_row, (EXTRA, width))
            wanted = lax.rem(pair * (2 // per_slot) + part - head + slots, slots)
            for step, dtail_ref in enumerate(dtail_refs):

                @pl.when(wanted == step)
                def _(dtail_ref=dtail_ref, tail=tail, extra=extra):
                    dtail_ref[:WINDOW] = tail
                    dtail_ref[WINDOW:] = extra


def gather_kernel(*refs):
    *in_refs, out_ref = refs
    total, sink_row = 0.0, 0.0
    for in_ref in in_refs:
        total = total + in_ref[:WINDOW].astype(F32)
        sink_row = sink_row + row_join(in_ref[WINDOW:])
    out_ref[:WINDOW] = total.astype(BF16)
    out_ref[WINDOW:] = row_split(sink_row, (EXTRA, out_ref.shape[1]))


def land_kernel(tok_count, blocks, table, here_ref, *refs):
    tok, head = lax.axis_index("tok"), lax.axis_index("head")
    in_refs, out_refs, sink_ref = refs[:LAG], refs[LAG:-1], refs[-1]
    slots = len(out_refs)
    blocks_here = blocks // slots
    for out_ref in out_refs:
        out_ref[...] = jnp.zeros_like(out_ref)
    sink_row = row_join(here_ref[WINDOW:])
    for distance, in_ref in enumerate(in_refs, 1):
        valid, place = child_tail(table, tok, distance, tok_count, blocks)
        sink_row = sink_row + row_join(in_ref[WINDOW:])
        wanted = lax.rem(place // blocks_here - head + slots, slots)
        here = pl.ds(pl.multiple_of(place % blocks_here * WINDOW, WINDOW), WINDOW)
        for step, out_ref in enumerate(out_refs):

            @pl.when(valid & (wanted == step))
            def _(out_ref=out_ref, in_ref=in_ref, here=here):
                total = out_ref[here, :].astype(F32) + in_ref[:WINDOW].astype(F32)
                out_ref[here, :] = total.astype(BF16)

    sink_ref[...] = jnp.broadcast_to(sink_row[:, :128], sink_ref.shape)


def total_kernel(dk_ref, dv_ref, halo_ref, sink_ref, far_ref, *refs):
    *tail_refs, key_ref, value_ref, sink_grad, tails = refs
    slots, rows = len(tail_refs), dk_ref.shape[0]
    width = tails.shape[2] // 2
    head = lax.axis_index("head")
    for step, tail_ref in enumerate(tail_refs):
        tails[lax.rem(head - step + slots, slots)] = tail_ref[...]
    halo_k = jnp.concatenate([halo_ref[pair][:, :128] for pair in range(PAIRS)], axis=1)
    halo_v = jnp.concatenate([halo_ref[pair][:, 128:] for pair in range(PAIRS)], axis=1)
    for in_ref, halo, at, out_ref in (
        (dk_ref, halo_k, 0, key_ref),
        (dv_ref, halo_v, width, value_ref),
    ):
        for begin in range(0, rows, WINDOW):
            here = slice(begin, begin + WINDOW)
            parts = [tails[slot, here, at : at + width] for slot in range(slots)]
            total = in_ref[here, :] + jnp.concatenate(parts, axis=1).astype(F32)
            if begin == rows - WINDOW:
                total = total + halo.astype(F32)
            out_ref[here, :] = total.astype(BF16)
    sink_row = -(sink_ref[0:1] + far_ref[0:1])
    for place in range(sink_grad.shape[0]):
        sink_grad[place] = sink_row[0, place]


def swap(values, axis):
    return [values[0]] + [ring(values[step], axis, step) for step in range(1, len(values))]


def local(
    queries, key_states, value_states, out_grad, sink_logits, branch_start, branch_len, parent_list
):
    tok_count, head_count = lax.axis_size("tok"), lax.axis_size("head")
    rows = queries.shape[0]
    blocks_here = rows // WINDOW
    blocks = blocks_here * head_count
    per_slot = KV_HEADS // head_count
    width = 2 * per_slot * HEAD_DIM

    def shape(dims, kind=BF16):
        return jax.ShapeDtypeStruct(dims, kind)

    queries, out_grad, key_states, value_states, sink_logits = (
        pltpu.with_memory_space_constraint(value, pltpu.HBM)
        for value in (queries, out_grad, key_states, value_states, sink_logits)
    )
    table = jnp.concatenate([branch_start, branch_len, parent_list[:, 0], parent_list[:, 1]])
    *slots, halo_out = pl.pallas_call(
        pack_kernel,
        out_shape=(shape((rows + EXTRA, width)),) * head_count + (shape((PAIRS, WINDOW, 256)),),
        in_specs=[HBM] * 3,
        out_specs=(VMEM,) * (head_count + 1),
        scratch_shapes=[
            pltpu.SMEM(sink_logits.shape, F32),
            pltpu.VMEM(key_states.shape, BF16),
            pltpu.VMEM(key_states.shape, BF16),
            pltpu.SemaphoreType.DMA((3,)),
        ],
        compiler_params=PARAMS,
        name="pack",
    )(sink_logits, key_states, value_states)
    spread = swap(slots, "head")
    halo = shift(halo_out, "head", 1)
    *chosen, sinks = pl.pallas_call(
        functools.partial(choose_kernel, tok_count, blocks),
        out_shape=(shape((WINDOW, width)),) * LAG + (shape((KV_HEADS * GROUP, 128), F32),),
        in_specs=[SMEM] + [VMEM] * head_count,
        out_specs=(VMEM,) * (LAG + 1),
        compiler_params=PARAMS,
        name="choose",
    )(table, *spread)
    arrived = [shift(chosen[s - 1], "tok", s) for s in range(LAG, 0, -1)][::-1]
    quarter = pl.pallas_call(
        functools.partial(arrive_kernel, tok_count),
        out_shape=shape((WINDOW, width)),
        in_specs=[SMEM] + [VMEM] * LAG,
        out_specs=VMEM,
        compiler_params=PARAMS,
        name="arrive",
    )(table, *arrived)
    tails = swap([quarter] * head_count, "head")
    big = pl.BlockSpec((WINDOW, 1024), lambda p, b: (b, p))
    small = pl.BlockSpec((rows, 128), lambda p, b: (0, p))
    near = pl.BlockSpec((1, WINDOW, 256), lambda p, b: (p, 0, 0))
    whole = pl.BlockSpec((WINDOW, width), lambda p, b: (0, 0))
    whole_back = pl.BlockSpec((WINDOW + EXTRA, width), lambda p, b: (0, 0))
    attended, query_grad, dk, dv, dhalo, *dtail = pl.pallas_call(
        functools.partial(attend_kernel, tok_count, blocks_here, head_count),
        grid=(PAIRS, blocks_here),
        out_shape=(
            shape(queries.shape),
            shape(queries.shape),
            shape(key_states.shape, F32),
            shape(key_states.shape, F32),
            shape((PAIRS, WINDOW, 256)),
        )
        + (shape((WINDOW + EXTRA, width)),) * head_count,
        in_specs=[
            SMEM,
            pl.BlockSpec((2 * GROUP, 128), lambda p, b: (p, 0)),
            big,
            big,
            small,
            small,
            near,
        ]
        + [whole] * head_count,
        out_specs=(big, big, small, small, near) + (whole_back,) * head_count,
        scratch_shapes=[
            pltpu.VMEM((head_count, WINDOW, width), BF16),
            pltpu.VMEM((WINDOW, 256), F32),
            pltpu.VMEM((2 * GROUP, WINDOW), F32),
            pltpu.VMEM((HEAD_DIM, 2048), BF16),
            pltpu.VMEM((HEAD_DIM, 2048), BF16),
            pltpu.VMEM((3 * HALF, 2048), BF16),
            pltpu.VMEM((3 * HALF, 2048), BF16),
        ],
        compiler_params=PARAMS,
        name="attend",
    )(table, sinks, queries, out_grad, key_states, value_states, halo, *tails)
    parts = swap(dtail, "head")
    quarter_grad = pl.pallas_call(
        gather_kernel,
        out_shape=shape((WINDOW + EXTRA, width)),
        in_specs=[VMEM] * head_count,
        out_specs=VMEM,
        compiler_params=PARAMS,
        name="gather",
    )(*parts)
    returned = [ring(quarter_grad, "tok", -s) for s in range(LAG, 0, -1)][::-1]
    halo_back = shift(dhalo, "head", -1)
    *landed, sink_near = pl.pallas_call(
        functools.partial(land_kernel, tok_count, blocks),
        out_shape=(shape((rows, width)),) * head_count + (shape((8, 128), F32),),
        in_specs=[SMEM] + [VMEM] * (LAG + 1),
        out_specs=(VMEM,) * (head_count + 1),
        compiler_params=PARAMS,
        name="land",
    )(table, quarter_grad, *returned)
    tails_back = swap(landed, "head")
    span = LAG + 1
    while 2 * span < tok_count:
        sink_near = sink_near + ring(sink_near, "tok", -span)
        span *= 2
    sink_far = ring(sink_near, "tok", -span)
    key_grad, value_grad, sink_grad = pl.pallas_call(
        total_kernel,
        out_shape=(
            shape(key_states.shape),
            shape(value_states.shape),
            shape(sink_logits.shape, F32),
        ),
        in_specs=[VMEM] * (5 + head_count),
        out_specs=(VMEM, VMEM, SMEM),
        scratch_shapes=[pltpu.VMEM((head_count, rows, width), BF16)],
        compiler_params=PARAMS,
        name="total",
    )(dk, dv, halo_back, sink_near, sink_far, *tails_back)
    return attended, query_grad, key_grad, value_grad, sink_grad


def solution(mesh):
    rows = P(("tok", "head"), None)
    return jax.shard_map(
        local,
        mesh=mesh,
        in_specs=(rows, rows, rows, rows, P("head"), P(), P(), P()),
        out_specs=(rows, rows, rows, rows, P("head")),
        check_vma=False,
    )
```

```python
import functools

import jax
import jax.numpy as jnp
from jax import lax
from jax.experimental import pallas as pl
from jax.experimental.pallas import tpu as pltpu
from jax.sharding import PartitionSpec as P

HEAD_DIM = 64
KV_HEADS = 8
GROUP = 8
WINDOW = 128
HALF = WINDOW // 2
LAG = 3
BR_DEV = 2
PAIRS = KV_HEADS // 2
FACTOR = 0.125
LOW = -1e30
EXTRA = 16
BF16 = jnp.bfloat16
F32 = jnp.float32

SMEM = pl.BlockSpec(memory_space=pltpu.SMEM)
VMEM = pl.BlockSpec(memory_space=pltpu.VMEM)
HBM = pl.BlockSpec(memory_space=pltpu.HBM)
PARAMS = pltpu.CompilerParams(vmem_limit_bytes=24 * 1024 * 1024)


def shift(value, axis, steps):
    count = lax.axis_size(axis)
    leading, last = (max(0, -steps), min(count, count - steps))
    return lax.ppermute(value, axis, [(source, source + steps) for source in range(leading, last)])


def ring(value, axis, steps):
    count = lax.axis_size(axis)
    return lax.ppermute(value, axis, [(source, (source + steps) % count) for source in range(count)])


def row_split(row, dims):
    high = row.astype(BF16).astype(F32)
    middle = (row - high).astype(BF16).astype(F32)
    low = row - high - middle
    place = lax.broadcasted_iota(jnp.int32, dims, 0)
    rest = jnp.where(place == 2, low, 0.0)
    return jnp.where(place == 0, high, jnp.where(place == 1, middle, rest)).astype(BF16)


def row_join(rows):
    rows = rows.astype(F32)
    return rows[0:1] + rows[1:2] + rows[2:3]


def child_tail(table, tok, distance, tok_count, blocks):
    branches = tok_count * BR_DEV
    child = jnp.minimum(tok + distance, tok_count - 1) * BR_DEV
    parent = table[2 * branches + child]
    safe = jnp.maximum(parent, 0)
    valid = (tok + distance < tok_count) & (parent >= 0) & (safe // BR_DEV == tok)
    place = (table[safe] + table[3 * branches + child]) // WINDOW - tok * blocks
    return valid, jnp.where(valid, place, 0)


def block_state(table, tok, tok_count, block):
    branches = tok_count * BR_DEV
    position = block * WINDOW
    alive, opening = jnp.bool_(False), jnp.bool_(False)
    for branch in range(BR_DEV):
        start = table[tok * BR_DEV + branch]
        length = table[branches + tok * BR_DEV + branch]
        alive = alive | ((start <= position) & (position < start + length))
        opening = opening | (start == position)
    has_tail = table[2 * branches + tok * BR_DEV] >= 0
    return alive, opening, jnp.logical_not(opening) | has_tail


def take(ref, slot, width):
    if width % 128 == 0:
        return ref[:, pl.ds(pl.multiple_of(slot * width, width), width)]
    value = ref[:, :width]
    for other in range(1, ref.shape[1] // width):
        value = jnp.where(slot == other, ref[:, other * width : (other + 1) * width], value)
    return value


def pack_kernel(sink_hbm, key_hbm, value_hbm, *refs):
    *slot_refs, halo_ref, sinks, keys, values, sems = refs
    copies = [
        pltpu.make_async_copy(source, target, sems.at[place])
        for place, (source, target) in enumerate(
            ((sink_hbm, sinks), (key_hbm, keys), (value_hbm, values))
        )
    ]
    for copy in copies:
        copy.start()
    for copy in copies:
        copy.wait()
    slots, rows = len(slot_refs), keys.shape[0]
    head = lax.axis_index("head")
    width = KV_HEADS * HEAD_DIM // slots
    lane = lax.broadcasted_iota(jnp.int32, (1, 2 * width), 1)
    sink_row = jnp.zeros((1, 2 * width), F32)
    for place in range(sinks.shape[0]):
        sink_row = jnp.where(lane == place, sinks[place], sink_row)
    extra = row_split(sink_row, (EXTRA, 2 * width))
    for step, slot_ref in enumerate(slot_refs):
        slot = lax.rem(head + step, slots)
        slot_ref[:rows] = jnp.concatenate(
            [take(keys, slot, width), take(values, slot, width)], axis=1
        )
        slot_ref[rows:] = extra
    for pair in range(PAIRS):
        lanes = slice(pair * 128, (pair + 1) * 128)
        last = slice(rows - WINDOW, rows)
        halo_ref[pair] = jnp.concatenate([keys[last, lanes], values[last, lanes]], axis=1)


def choose_kernel(tok_count, blocks, table, *refs):
    slots = len(refs) - LAG - 1
    slot_refs, out_refs, sink_ref = refs[:slots], refs[slots:-1], refs[-1]
    tok, head = lax.axis_index("tok"), lax.axis_index("head")
    rows = slot_refs[0].shape[0] - EXTRA
    blocks_here = rows // WINDOW
    heads = sink_ref.shape[0] // slots
    for distance, out_ref in zip(range(LAG, 0, -1), out_refs):
        _, place = child_tail(table, tok, distance, tok_count, blocks)
        begin = pl.multiple_of(place % blocks_here * WINDOW, WINDOW)
        wanted = lax.rem(head - place // blocks_here + slots, slots)
        for step, slot_ref in enumerate(slot_refs):

            @pl.when(wanted == step)
            def _(out_ref=out_ref, slot_ref=slot_ref, begin=begin):
                out_ref[...] = slot_ref[pl.ds(begin, WINDOW), :]

    for step, slot_ref in enumerate(slot_refs):
        source = lax.rem(head - step + slots, slots)
        sink_row = row_join(slot_ref[rows:, :])[:, :128]
        turned = jnp.broadcast_to(sink_row, (128, 128)).T
        sink_ref[pl.ds(pl.multiple_of(source * heads, heads), heads), :] = turned[:heads]


def arrive_kernel(tok_count, table, *refs):
    tok = lax.axis_index("tok")
    *in_refs, out_ref = refs
    parent = table[2 * tok_count * BR_DEV + tok * BR_DEV]
    mine = jnp.where(parent >= 0, tok - jnp.maximum(parent, 0) // BR_DEV, 1)
    for distance, in_ref in enumerate(in_refs, 1):

        @pl.when(mine == distance)
        def _(in_ref=in_ref):
            out_ref[...] = in_ref[...]


def attend_kernel(
    tok_count,
    blocks_here,
    slots,
    table,
    sink_ref,
    q_ref,
    g_ref,
    k_ref,
    v_ref,
    halo_ref,
    *refs,
):
    tail_refs, refs = refs[:slots], refs[slots:]
    o_ref, dq_ref, dk_ref, dv_ref, dhalo_ref = refs[:5]
    dtail_refs, refs = refs[5 : 5 + slots], refs[5 + slots :]
    tails, tail_sum, sink_rows, prob2, slope2 = refs
    per_slot = KV_HEADS // slots
    pair, block = pl.program_id(0), pl.program_id(1)
    tok, head = lax.axis_index("tok"), lax.axis_index("head")
    number = (tok * lax.axis_size("head") + head) * blocks_here + block
    alive, opening, prev_ok = block_state(table, tok, tok_count, number)
    here = pl.ds(pl.multiple_of(block * WINDOW, WINDOW), WINDOW)
    before = pl.ds(pl.multiple_of(jnp.maximum(block - 1, 0) * WINDOW, WINDOW), WINDOW)
    first = block == 0

    @pl.when(first & (pair == 0))
    def _():
        for step, tail_ref in enumerate(tail_refs):
            tails[lax.rem(head - step + slots, slots)] = tail_ref[...]

    @pl.when(first)
    def _():
        tail_sum[...] = jnp.zeros_like(tail_sum)
        dhalo_ref[...] = jnp.zeros_like(dhalo_ref)
        sink_rows[...] = jnp.zeros_like(sink_rows)

    @pl.when(jnp.logical_not(alive))
    def _():
        o_ref[...] = jnp.zeros_like(o_ref)
        dq_ref[...] = jnp.zeros_like(dq_ref)
        dk_ref[here, :] = jnp.zeros((WINDOW, 128), F32)
        dv_ref[here, :] = jnp.zeros((WINDOW, 128), F32)

    @pl.when(alive)
    def _():
        halo = halo_ref[0]
        if per_slot == 2:
            tail = tails[pair]
            tail_k, tail_v = tail[:, :128], tail[:, 128:]
        else:
            tail_a, tail_b = tails[2 * pair], tails[2 * pair + 1]
            tail_k = jnp.concatenate([tail_a[:, :64], tail_b[:, :64]], axis=1)
            tail_v = jnp.concatenate([tail_a[:, 64:], tail_b[:, 64:]], axis=1)
        near_k = jnp.where(first, halo[:, :128], k_ref[before, :])
        near_v = jnp.where(first, halo[:, 128:], v_ref[before, :])
        prev_k = jnp.where(opening, tail_k, near_k)
        prev_v = jnp.where(opening, tail_v, near_v)
        own_k, own_v = k_ref[here, :], v_ref[here, :]

        def halves(own, prev):
            return (
                jnp.concatenate([own[:HALF], prev[:HALF], prev[HALF:]], axis=0),
                jnp.concatenate([own[HALF:], prev[HALF:], own[:HALF]], axis=0),
            )

        left = lax.broadcasted_iota(jnp.int32, (1, 128), 1) < HALF
        low16 = left.astype(F32).astype(BF16)
        high16 = BF16(1) - low16

        def padded(seen):
            swapped = jnp.concatenate([seen[:, 64:], seen[:, :64]], axis=1)
            return (
                jnp.concatenate([seen * low16, swapped * high16], axis=0),
                jnp.concatenate([swapped * low16, seen * high16], axis=0),
            )

        seen_k = halves(own_k * BF16(FACTOR), prev_k * BF16(FACTOR))
        seen_v = halves(own_v, prev_v)
        padded_k = tuple(padded(value) for value in seen_k)
        padded_v = tuple(padded(value) for value in seen_v)
        turned_k = tuple(value.T for value in seen_k)
        turned_v = tuple(value.T for value in seen_v)
        bias = jnp.where(prev_ok, 0.0, LOW)
        key_place = lax.broadcasted_iota(jnp.int32, (HALF, 4 * HALF), 0)
        query_place = lax.broadcasted_iota(jnp.int32, (HALF, 4 * HALF), 1) & (HALF - 1)
        own = key_place <= query_place
        own16 = own.astype(F32).astype(BF16)
        turn = (((1,), (1,)), ((), ()))
        items = [(unit, half) for unit in range(2) for half in range(2)]
        seen = 3 * HALF

        def wide(index):
            return slice(index * 256, (index + 1) * 256)

        def feats(index):
            unit = items[index][0]
            return slice(unit * HEAD_DIM, (unit + 1) * HEAD_DIM)

        def corners(unit, half):
            rows = slice(half * HALF, (half + 1) * HALF)
            return [
                (rows, slice(unit * 512 + at * 128, unit * 512 + (at + 1) * 128)) for at in range(4)
            ]

        def stacked(ref, unit, half):
            return jnp.concatenate([ref[corner] for corner in corners(unit, half)], axis=0)

        def products(index):
            unit, half = items[index]
            score, dp = (
                lax.dot_general(
                    padded[half][unit],
                    stacked(ref, unit, half),
                    turn,
                    preferred_element_type=F32,
                )
                for padded, ref in ((padded_k, q_ref), (padded_v, g_ref))
            )
            parts = []
            for base in (0, seen):
                near, far = slice(base, base + HALF), slice(base + HALF, base + 2 * HALF)
                rest = slice(base + 2 * HALF, base + 3 * HALF)
                edge = jnp.where(own, score[near], score[far] + bias)
                whole = score[rest] + bias if half == 0 else score[rest]
                parts.append((edge, whole, jnp.where(own, dp[near], dp[far]), dp[rest]))
            return parts

        def weigh(index, odd, edge, whole, dp_edge, dp_whole):
            unit, half = items[index]
            base = odd * seen
            row = unit * GROUP + odd
            sink = jnp.concatenate(
                [
                    jnp.where(left, sink_ref[at : at + 1], sink_ref[at + 2 : at + 3])
                    for at in (row, row + 4)
                ],
                axis=1,
            )
            peak = jnp.max(jnp.maximum(edge, whole), axis=0, keepdims=True)
            peak = jnp.maximum(peak, sink)
            edge, whole = jnp.exp(edge - peak), jnp.exp(whole - peak)
            sink_weight = jnp.exp(sink - peak)
            inverse = 1.0 / (jnp.sum(edge + whole, axis=0, keepdims=True) + sink_weight)
            edge, whole = edge * inverse, whole * inverse
            term_edge, term_whole = edge * dp_edge, whole * dp_whole
            delta = jnp.sum(term_edge + term_whole, axis=0, keepdims=True)
            for target, at_edge, at_whole in (
                (prob2, edge, whole),
                (slope2, term_edge - edge * delta, term_whole - whole * delta),
            ):
                edge16 = at_edge.astype(BF16)
                edge_own = edge16 * own16
                target[base : base + HALF, wide(index)] = edge_own
                target[base + HALF : base + 2 * HALF, wide(index)] = edge16 - edge_own
                target[base + 2 * HALF : base + seen, wide(index)] = at_whole.astype(BF16)
            sink_term = sink_weight * inverse * delta
            for at, lanes in ((row, slice(0, 128)), (row + 4, slice(128, 256))):
                part = sink_term[:, lanes]
                sink_rows[at : at + 1] += jnp.where(left, part, 0.0)
                sink_rows[at + 2 : at + 3] += jnp.where(left, 0.0, part)

        def finish(index):
            unit, half = items[index]
            for source, across, out_ref in ((prob2, turned_v, o_ref), (slope2, turned_k, dq_ref)):
                out_t = [
                    jnp.dot(
                        across[half][feats(index)],
                        source[base : base + seen, wide(index)],
                        preferred_element_type=F32,
                    ).astype(BF16)
                    for base in (0, seen)
                ]
                out = jnp.concatenate(out_t, axis=0).T
                for at, corner in enumerate(corners(unit, half)):
                    out_ref[corner] = out[at * HALF : (at + 1) * HALF]

        def reduce(index):
            unit, half = items[index]
            parts = []
            for weights, ref in ((slope2, q_ref), (prob2, g_ref)):
                part = jnp.dot(
                    weights[:, wide(index)], stacked(ref, unit, half), preferred_element_type=F32
                )
                parts.append(jnp.where(left, part[:seen], part[seen:]))
            return parts

        def join(first_half, second_half):
            total = jnp.concatenate(
                [
                    first_half[:HALF] + second_half[2 * HALF :],
                    second_half[:HALF],
                    first_half[HALF : 2 * HALF],
                    first_half[2 * HALF :] + second_half[HALF : 2 * HALF],
                ],
                axis=0,
            )
            return total + pltpu.roll(total, HEAD_DIM, 1)

        ahead, parts = products(0), []
        for index in range(len(items)):
            now = ahead
            weigh(index, 0, *now[0])
            if index + 1 < len(items):
                ahead = products(index + 1)
            weigh(index, 1, *now[1])
            if index >= 1:
                finish(index - 1)
            parts.append(reduce(index))
        finish(len(items) - 1)
        grads = [
            [join(parts[2 * unit][place], parts[2 * unit + 1][place]) for place in range(2)]
            for unit in range(2)
        ]
        dk = jnp.where(left, grads[0][0], grads[1][0]) * FACTOR
        dv = jnp.where(left, grads[0][1], grads[1][1])
        dk_ref[here, :] = dk[:WINDOW]
        dv_ref[here, :] = dv[:WINDOW]

        @pl.when(opening & prev_ok)
        def _():
            tail_sum[:, :128] += dk[WINDOW:]
            tail_sum[:, 128:] += dv[WINDOW:]

        @pl.when(jnp.logical_not(opening) & first)
        def _():
            dhalo_ref[0, :, :128] = dk[WINDOW:].astype(BF16)
            dhalo_ref[0, :, 128:] = dv[WINDOW:].astype(BF16)

        @pl.when(jnp.logical_not(opening) & jnp.logical_not(first))
        def _():
            dk_ref[before, :] += dk[WINDOW:]
            dv_ref[before, :] += dv[WINDOW:]

    @pl.when(block == blocks_here - 1)
    def _():
        width = dtail_refs[0].shape[1]
        heads = per_slot * GROUP
        total = tail_sum[...].astype(BF16)
        for part in range(2 // per_slot):
            feats = slice(part * width // 2, (part + 1) * width // 2)
            tail = jnp.concatenate([total[:, :128][:, feats], total[:, 128:][:, feats]], axis=1)
            rows = sink_rows[part * heads : (part + 1) * heads]
            rows = jnp.concatenate([rows, jnp.zeros((128 - heads, WINDOW), F32)], axis=0)
            sink_row = jnp.sum(rows.T, axis=0, keepdims=True)
            if width > 128:
                sink_row = jnp.concatenate([sink_row, jnp.zeros((1, width - 128), F32)], axis=1)
            extra = row_split(sink_row, (EXTRA, width))
            wanted = lax.rem(pair * (2 // per_slot) + part - head + slots, slots)
            for step, dtail_ref in enumerate(dtail_refs):

                @pl.when(wanted == step)
                def _(dtail_ref=dtail_ref, tail=tail, extra=extra):
                    dtail_ref[:WINDOW] = tail
                    dtail_ref[WINDOW:] = extra


def gather_kernel(*refs):
    *in_refs, out_ref = refs
    total, sink_row = 0.0, 0.0
    for in_ref in in_refs:
        total = total + in_ref[:WINDOW].astype(F32)
        sink_row = sink_row + row_join(in_ref[WINDOW:])
    out_ref[:WINDOW] = total.astype(BF16)
    out_ref[WINDOW:] = row_split(sink_row, (EXTRA, out_ref.shape[1]))


def land_kernel(tok_count, blocks, table, here_ref, *refs):
    tok, head = lax.axis_index("tok"), lax.axis_index("head")
    in_refs, out_refs, sink_ref = refs[:LAG], refs[LAG:-1], refs[-1]
    slots = len(out_refs)
    blocks_here = blocks // slots
    for out_ref in out_refs:
        out_ref[...] = jnp.zeros_like(out_ref)
    sink_row = row_join(here_ref[WINDOW:])
    for distance, in_ref in enumerate(in_refs, 1):
        valid, place = child_tail(table, tok, distance, tok_count, blocks)
        sink_row = sink_row + row_join(in_ref[WINDOW:])
        wanted = lax.rem(place // blocks_here - head + slots, slots)
        here = pl.ds(pl.multiple_of(place % blocks_here * WINDOW, WINDOW), WINDOW)
        for step, out_ref in enumerate(out_refs):

            @pl.when(valid & (wanted == step))
            def _(out_ref=out_ref, in_ref=in_ref, here=here):
                total = out_ref[here, :].astype(F32) + in_ref[:WINDOW].astype(F32)
                out_ref[here, :] = total.astype(BF16)

    sink_ref[...] = jnp.broadcast_to(sink_row[:, :128], sink_ref.shape)


def total_kernel(dk_ref, dv_ref, halo_ref, sink_ref, far_ref, *refs):
    *tail_refs, key_ref, value_ref, sink_grad, tails = refs
    slots, rows = len(tail_refs), dk_ref.shape[0]
    width = tails.shape[2] // 2
    head = lax.axis_index("head")
    for step, tail_ref in enumerate(tail_refs):
        tails[lax.rem(head - step + slots, slots)] = tail_ref[...]
    halo_k = jnp.concatenate([halo_ref[pair][:, :128] for pair in range(PAIRS)], axis=1)
    halo_v = jnp.concatenate([halo_ref[pair][:, 128:] for pair in range(PAIRS)], axis=1)
    for in_ref, halo, at, out_ref in (
        (dk_ref, halo_k, 0, key_ref),
        (dv_ref, halo_v, width, value_ref),
    ):
        for begin in range(0, rows, WINDOW):
            here = slice(begin, begin + WINDOW)
            parts = [tails[slot, here, at : at + width] for slot in range(slots)]
            total = in_ref[here, :] + jnp.concatenate(parts, axis=1).astype(F32)
            if begin == rows - WINDOW:
                total = total + halo.astype(F32)
            out_ref[here, :] = total.astype(BF16)
    sink_row = -(sink_ref[0:1] + far_ref[0:1])
    for place in range(sink_grad.shape[0]):
        sink_grad[place] = sink_row[0, place]


def swap(values, axis):
    return [values[0]] + [ring(values[step], axis, step) for step in range(1, len(values))]


def local(
    queries, key_states, value_states, out_grad, sink_logits, branch_start, branch_len, parent_list
):
    tok_count, head_count = lax.axis_size("tok"), lax.axis_size("head")
    rows = queries.shape[0]
    blocks_here = rows // WINDOW
    blocks = blocks_here * head_count
    per_slot = KV_HEADS // head_count
    width = 2 * per_slot * HEAD_DIM

    def shape(dims, kind=BF16):
        return jax.ShapeDtypeStruct(dims, kind)

    queries, out_grad, key_states, value_states, sink_logits = (
        pltpu.with_memory_space_constraint(value, pltpu.HBM)
        for value in (queries, out_grad, key_states, value_states, sink_logits)
    )
    table = jnp.concatenate([branch_start, branch_len, parent_list[:, 0], parent_list[:, 1]])
    *slots, halo_out = pl.pallas_call(
        pack_kernel,
        out_shape=(shape((rows + EXTRA, width)),) * head_count + (shape((PAIRS, WINDOW, 256)),),
        in_specs=[HBM] * 3,
        out_specs=(VMEM,) * (head_count + 1),
        scratch_shapes=[
            pltpu.SMEM(sink_logits.shape, F32),
            pltpu.VMEM(key_states.shape, BF16),
            pltpu.VMEM(key_states.shape, BF16),
            pltpu.SemaphoreType.DMA((3,)),
        ],
        compiler_params=PARAMS,
        name="pack",
    )(sink_logits, key_states, value_states)
    spread = swap(slots, "head")
    halo = shift(halo_out, "head", 1)
    *chosen, sinks = pl.pallas_call(
        functools.partial(choose_kernel, tok_count, blocks),
        out_shape=(shape((WINDOW, width)),) * LAG + (shape((KV_HEADS * GROUP, 128), F32),),
        in_specs=[SMEM] + [VMEM] * head_count,
        out_specs=(VMEM,) * (LAG + 1),
        compiler_params=PARAMS,
        name="choose",
    )(table, *spread)
    arrived = [ring(chosen[LAG - s], "tok", s) for s in range(1, LAG + 1)]
    quarter = pl.pallas_call(
        functools.partial(arrive_kernel, tok_count),
        out_shape=shape((WINDOW, width)),
        in_specs=[SMEM] + [VMEM] * LAG,
        out_specs=VMEM,
        compiler_params=PARAMS,
        name="arrive",
    )(table, *arrived)
    tails = swap([quarter] * head_count, "head")
    big = pl.BlockSpec((WINDOW, 1024), lambda p, b: (b, p))
    small = pl.BlockSpec((rows, 128), lambda p, b: (0, p))
    near = pl.BlockSpec((1, WINDOW, 256), lambda p, b: (p, 0, 0))
    whole = pl.BlockSpec((WINDOW, width), lambda p, b: (0, 0))
    whole_back = pl.BlockSpec((WINDOW + EXTRA, width), lambda p, b: (0, 0))
    attended, query_grad, dk, dv, dhalo, *dtail = pl.pallas_call(
        functools.partial(attend_kernel, tok_count, blocks_here, head_count),
        grid=(PAIRS, blocks_here),
        out_shape=(
            shape(queries.shape),
            shape(queries.shape),
            shape(key_states.shape, F32),
            shape(key_states.shape, F32),
            shape((PAIRS, WINDOW, 256)),
        )
        + (shape((WINDOW + EXTRA, width)),) * head_count,
        in_specs=[
            SMEM,
            pl.BlockSpec((2 * GROUP, 128), lambda p, b: (p, 0)),
            big,
            big,
            small,
            small,
            near,
        ]
        + [whole] * head_count,
        out_specs=(big, big, small, small, near) + (whole_back,) * head_count,
        scratch_shapes=[
            pltpu.VMEM((head_count, WINDOW, width), BF16),
            pltpu.VMEM((WINDOW, 256), F32),
            pltpu.VMEM((2 * GROUP, WINDOW), F32),
            pltpu.VMEM((6 * HALF, 1024), BF16),
            pltpu.VMEM((6 * HALF, 1024), BF16),
        ],
        compiler_params=PARAMS,
        name="attend",
    )(table, sinks, queries, out_grad, key_states, value_states, halo, *tails)
    parts = swap(dtail, "head")
    quarter_grad = pl.pallas_call(
        gather_kernel,
        out_shape=shape((WINDOW + EXTRA, width)),
        in_specs=[VMEM] * head_count,
        out_specs=VMEM,
        compiler_params=PARAMS,
        name="gather",
    )(*parts)
    returned = [ring(quarter_grad, "tok", -s) for s in range(LAG, 0, -1)][::-1]
    halo_back = shift(dhalo, "head", -1)
    *landed, sink_near = pl.pallas_call(
        functools.partial(land_kernel, tok_count, blocks),
        out_shape=(shape((rows, width)),) * head_count + (shape((8, 128), F32),),
        in_specs=[SMEM] + [VMEM] * (LAG + 1),
        out_specs=(VMEM,) * (head_count + 1),
        compiler_params=PARAMS,
        name="land",
    )(table, quarter_grad, *returned)
    tails_back = swap(landed, "head")
    span = LAG + 1
    while 2 * span < tok_count:
        sink_near = sink_near + ring(sink_near, "tok", -span)
        span *= 2
    sink_far = ring(sink_near, "tok", -span)
    key_grad, value_grad, sink_grad = pl.pallas_call(
        total_kernel,
        out_shape=(
            shape(key_states.shape),
            shape(value_states.shape),
            shape(sink_logits.shape, F32),
        ),
        in_specs=[VMEM] * (5 + head_count),
        out_specs=(VMEM, VMEM, SMEM),
        scratch_shapes=[pltpu.VMEM((head_count, rows, width), BF16)],
        compiler_params=PARAMS,
        name="total",
    )(dk, dv, halo_back, sink_near, sink_far, *tails_back)
    return attended, query_grad, key_grad, value_grad, sink_grad


def solution(mesh):
    rows = P(("tok", "head"), None)
    return jax.shard_map(
        local,
        mesh=mesh,
        in_specs=(rows, rows, rows, rows, P("head"), P(), P(), P()),
        out_specs=(rows, rows, rows, rows, P("head")),
        check_vma=False,
    )
```

```python
import functools

import jax
import jax.numpy as jnp
from jax import lax
from jax.experimental import pallas as pl
from jax.experimental.pallas import tpu as pltpu
from jax.sharding import PartitionSpec as P

HEAD_DIM = 64
KV_HEADS = 8
GROUP = 8
WINDOW = 128
HALF = WINDOW // 2
LAG = 3
BR_DEV = 2
PAIRS = KV_HEADS // 2
FACTOR = 0.125
LOW = -1e30
EXTRA = 16
BF16 = jnp.bfloat16
F32 = jnp.float32

SMEM = pl.BlockSpec(memory_space=pltpu.SMEM)
VMEM = pl.BlockSpec(memory_space=pltpu.VMEM)
HBM = pl.BlockSpec(memory_space=pltpu.HBM)
PARAMS = pltpu.CompilerParams(vmem_limit_bytes=24 * 1024 * 1024)


def shift(value, axis, steps):
    count = lax.axis_size(axis)
    leading, last = (max(0, -steps), min(count, count - steps))
    return lax.ppermute(value, axis, [(source, source + steps) for source in range(leading, last)])


def ring(value, axis, steps):
    count = lax.axis_size(axis)
    return lax.ppermute(value, axis, [(source, (source + steps) % count) for source in range(count)])


def row_split(row, dims):
    high = row.astype(BF16).astype(F32)
    middle = (row - high).astype(BF16).astype(F32)
    low = row - high - middle
    place = lax.broadcasted_iota(jnp.int32, dims, 0)
    rest = jnp.where(place == 2, low, 0.0)
    return jnp.where(place == 0, high, jnp.where(place == 1, middle, rest)).astype(BF16)


def row_join(rows):
    rows = rows.astype(F32)
    return rows[0:1] + rows[1:2] + rows[2:3]


def child_tail(table, tok, distance, tok_count, blocks):
    branches = tok_count * BR_DEV
    child = jnp.minimum(tok + distance, tok_count - 1) * BR_DEV
    parent = table[2 * branches + child]
    safe = jnp.maximum(parent, 0)
    valid = (tok + distance < tok_count) & (parent >= 0) & (safe // BR_DEV == tok)
    place = (table[safe] + table[3 * branches + child]) // WINDOW - tok * blocks
    return valid, jnp.where(valid, place, 0)


def block_state(table, tok, tok_count, block):
    branches = tok_count * BR_DEV
    position = block * WINDOW
    alive, opening = jnp.bool_(False), jnp.bool_(False)
    for branch in range(BR_DEV):
        start = table[tok * BR_DEV + branch]
        length = table[branches + tok * BR_DEV + branch]
        alive = alive | ((start <= position) & (position < start + length))
        opening = opening | (start == position)
    has_tail = table[2 * branches + tok * BR_DEV] >= 0
    return alive, opening, jnp.logical_not(opening) | has_tail


def take(ref, slot, width):
    if width % 128 == 0:
        return ref[:, pl.ds(pl.multiple_of(slot * width, width), width)]
    value = ref[:, :width]
    for other in range(1, ref.shape[1] // width):
        value = jnp.where(slot == other, ref[:, other * width : (other + 1) * width], value)
    return value


def pack_kernel(sink_hbm, key_hbm, value_hbm, *refs):
    *slot_refs, halo_ref, sinks, keys, values, sems = refs
    copies = [
        pltpu.make_async_copy(source, target, sems.at[place])
        for place, (source, target) in enumerate(
            ((sink_hbm, sinks), (key_hbm, keys), (value_hbm, values))
        )
    ]
    for copy in copies:
        copy.start()
    for copy in copies:
        copy.wait()
    slots, rows = len(slot_refs), keys.shape[0]
    head = lax.axis_index("head")
    width = KV_HEADS * HEAD_DIM // slots
    lane = lax.broadcasted_iota(jnp.int32, (1, 2 * width), 1)
    sink_row = jnp.zeros((1, 2 * width), F32)
    for place in range(sinks.shape[0]):
        sink_row = jnp.where(lane == place, sinks[place], sink_row)
    extra = row_split(sink_row, (EXTRA, 2 * width))
    for step, slot_ref in enumerate(slot_refs):
        slot = lax.rem(head + step, slots)
        slot_ref[:rows] = jnp.concatenate(
            [take(keys, slot, width), take(values, slot, width)], axis=1
        )
        slot_ref[rows:] = extra
    for pair in range(PAIRS):
        lanes = slice(pair * 128, (pair + 1) * 128)
        last = slice(rows - WINDOW, rows)
        halo_ref[pair] = jnp.concatenate([keys[last, lanes], values[last, lanes]], axis=1)


def choose_kernel(tok_count, blocks, table, *refs):
    slots = len(refs) - LAG - 1
    slot_refs, out_refs, sink_ref = refs[:slots], refs[slots:-1], refs[-1]
    tok, head = lax.axis_index("tok"), lax.axis_index("head")
    rows = slot_refs[0].shape[0] - EXTRA
    blocks_here = rows // WINDOW
    heads = sink_ref.shape[0] // slots
    for distance, out_ref in zip(range(LAG, 0, -1), out_refs):
        _, place = child_tail(table, tok, distance, tok_count, blocks)
        begin = pl.multiple_of(place % blocks_here * WINDOW, WINDOW)
        wanted = lax.rem(head - place // blocks_here + slots, slots)
        for step, slot_ref in enumerate(slot_refs):

            @pl.when(wanted == step)
            def _(out_ref=out_ref, slot_ref=slot_ref, begin=begin):
                out_ref[...] = slot_ref[pl.ds(begin, WINDOW), :]

    for step, slot_ref in enumerate(slot_refs):
        source = lax.rem(head - step + slots, slots)
        sink_row = row_join(slot_ref[rows:, :])[:, :128]
        turned = jnp.broadcast_to(sink_row, (128, 128)).T
        sink_ref[pl.ds(pl.multiple_of(source * heads, heads), heads), :] = turned[:heads]


def arrive_kernel(tok_count, table, *refs):
    tok = lax.axis_index("tok")
    *in_refs, out_ref = refs
    parent = table[2 * tok_count * BR_DEV + tok * BR_DEV]
    mine = jnp.where(parent >= 0, tok - jnp.maximum(parent, 0) // BR_DEV, 1)
    for distance, in_ref in zip(range(LAG, 0, -1), in_refs):

        @pl.when(mine == distance)
        def _(in_ref=in_ref):
            out_ref[...] = in_ref[...]


def own_pair(turn_of, offset):
    return lax.rem(lax.axis_index("head") + turn_of + offset, PAIRS)


def attend_kernel(
    tok_count,
    blocks_here,
    slots,
    steps,
    offset,
    joins,
    table,
    sink_ref,
    q_ref,
    g_ref,
    k_ref,
    v_ref,
    halo_ref,
    *refs,
):
    tail_refs, refs = refs[: len(steps)], refs[len(steps) + joins :]
    o_ref, dq_ref, dk_ref, dv_ref, dhalo_ref = refs[:5]
    dtail_refs, refs = refs[5 : 5 + len(steps)], refs[5 + len(steps) :]
    tails, tail_sum, sink_rows, prob2, slope2 = refs
    per_slot = KV_HEADS // slots
    turn_of, block = pl.program_id(0), pl.program_id(1)
    pair = turn_of if offset is None else own_pair(turn_of, offset)
    tok, head = lax.axis_index("tok"), lax.axis_index("head")
    number = (tok * lax.axis_size("head") + head) * blocks_here + block
    alive, opening, prev_ok = block_state(table, tok, tok_count, number)
    here = pl.ds(pl.multiple_of(block * WINDOW, WINDOW), WINDOW)
    before = pl.ds(pl.multiple_of(jnp.maximum(block - 1, 0) * WINDOW, WINDOW), WINDOW)
    first = block == 0

    @pl.when(first & (turn_of == 0))
    def _():
        for step, tail_ref in zip(steps, tail_refs):
            tails[lax.rem(head - step + slots, slots)] = tail_ref[...]

    @pl.when(first)
    def _():
        tail_sum[...] = jnp.zeros_like(tail_sum)
        dhalo_ref[...] = jnp.zeros_like(dhalo_ref)
        sink_rows[...] = jnp.zeros_like(sink_rows)

    @pl.when(jnp.logical_not(alive))
    def _():
        o_ref[...] = jnp.zeros_like(o_ref)
        dq_ref[...] = jnp.zeros_like(dq_ref)
        dk_ref[here, :] = jnp.zeros((WINDOW, 128), F32)
        dv_ref[here, :] = jnp.zeros((WINDOW, 128), F32)

    @pl.when(alive)
    def _():
        halo = halo_ref[...] if len(halo_ref.shape) == 2 else halo_ref[0]
        if per_slot == 2:
            tail = tails[pair]
            tail_k, tail_v = tail[:, :128], tail[:, 128:]
        else:
            tail_a, tail_b = tails[2 * pair], tails[2 * pair + 1]
            tail_k = jnp.concatenate([tail_a[:, :64], tail_b[:, :64]], axis=1)
            tail_v = jnp.concatenate([tail_a[:, 64:], tail_b[:, 64:]], axis=1)
        near_k = jnp.where(first, halo[:, :128], k_ref[before, :])
        near_v = jnp.where(first, halo[:, 128:], v_ref[before, :])
        prev_k = jnp.where(opening, tail_k, near_k)
        prev_v = jnp.where(opening, tail_v, near_v)
        own_k, own_v = k_ref[here, :], v_ref[here, :]

        def halves(own, prev):
            return (
                jnp.concatenate([own[:HALF], prev[:HALF], prev[HALF:]], axis=0),
                jnp.concatenate([own[HALF:], prev[HALF:], own[:HALF]], axis=0),
            )

        left = lax.broadcasted_iota(jnp.int32, (1, 128), 1) < HALF
        low16 = left.astype(F32).astype(BF16)
        high16 = BF16(1) - low16

        def padded(seen):
            swapped = jnp.concatenate([seen[:, 64:], seen[:, :64]], axis=1)
            return (
                jnp.concatenate([seen * low16, swapped * high16], axis=0),
                jnp.concatenate([swapped * low16, seen * high16], axis=0),
            )

        seen_k = halves(own_k * BF16(FACTOR), prev_k * BF16(FACTOR))
        seen_v = halves(own_v, prev_v)
        padded_k = tuple(padded(value) for value in seen_k)
        padded_v = tuple(padded(value) for value in seen_v)
        turned_k = tuple(value.T for value in seen_k)
        turned_v = tuple(value.T for value in seen_v)
        bias = jnp.where(prev_ok, 0.0, LOW)
        key_place = lax.broadcasted_iota(jnp.int32, (HALF, 4 * HALF), 0)
        query_place = lax.broadcasted_iota(jnp.int32, (HALF, 4 * HALF), 1) & (HALF - 1)
        own = key_place <= query_place
        own16 = own.astype(F32).astype(BF16)
        turn = (((1,), (1,)), ((), ()))
        items = [(unit, half) for unit in range(2) for half in range(2)]
        seen = 3 * HALF

        def wide(index):
            return slice(index * 256, (index + 1) * 256)

        def feats(index):
            unit = items[index][0]
            return slice(unit * HEAD_DIM, (unit + 1) * HEAD_DIM)

        def corners(unit, half):
            rows = slice(half * HALF, (half + 1) * HALF)
            return [
                (rows, slice(unit * 512 + at * 128, unit * 512 + (at + 1) * 128)) for at in range(4)
            ]

        def stacked(ref, unit, half):
            return jnp.concatenate([ref[corner] for corner in corners(unit, half)], axis=0)

        def products(index):
            unit, half = items[index]
            score, dp = (
                lax.dot_general(
                    padded[half][unit],
                    stacked(ref, unit, half),
                    turn,
                    preferred_element_type=F32,
                )
                for padded, ref in ((padded_k, q_ref), (padded_v, g_ref))
            )
            parts = []
            for base in (0, seen):
                near, far = slice(base, base + HALF), slice(base + HALF, base + 2 * HALF)
                rest = slice(base + 2 * HALF, base + 3 * HALF)
                edge = jnp.where(own, score[near], score[far] + bias)
                whole = score[rest] + bias if half == 0 else score[rest]
                parts.append((edge, whole, jnp.where(own, dp[near], dp[far]), dp[rest]))
            return parts

        def weigh(index, odd, edge, whole, dp_edge, dp_whole):
            unit, half = items[index]
            base = odd * seen
            row = unit * GROUP + odd
            sink = jnp.concatenate(
                [
                    jnp.where(left, sink_ref[at : at + 1], sink_ref[at + 2 : at + 3])
                    for at in (row, row + 4)
                ],
                axis=1,
            )
            peak = jnp.max(jnp.maximum(edge, whole), axis=0, keepdims=True)
            peak = jnp.maximum(peak, sink)
            edge, whole = jnp.exp(edge - peak), jnp.exp(whole - peak)
            sink_weight = jnp.exp(sink - peak)
            inverse = 1.0 / (jnp.sum(edge + whole, axis=0, keepdims=True) + sink_weight)
            edge, whole = edge * inverse, whole * inverse
            term_edge, term_whole = edge * dp_edge, whole * dp_whole
            delta = jnp.sum(term_edge + term_whole, axis=0, keepdims=True)
            for target, at_edge, at_whole in (
                (prob2, edge, whole),
                (slope2, term_edge - edge * delta, term_whole - whole * delta),
            ):
                edge16 = at_edge.astype(BF16)
                edge_own = edge16 * own16
                target[base : base + HALF, wide(index)] = edge_own
                target[base + HALF : base + 2 * HALF, wide(index)] = edge16 - edge_own
                target[base + 2 * HALF : base + seen, wide(index)] = at_whole.astype(BF16)
            sink_term = sink_weight * inverse * delta
            for at, lanes in ((row, slice(0, 128)), (row + 4, slice(128, 256))):
                part = sink_term[:, lanes]
                sink_rows[at : at + 1] += jnp.where(left, part, 0.0)
                sink_rows[at + 2 : at + 3] += jnp.where(left, 0.0, part)

        def finish(index):
            unit, half = items[index]
            for source, across, out_ref in ((prob2, turned_v, o_ref), (slope2, turned_k, dq_ref)):
                out_t = [
                    jnp.dot(
                        across[half][feats(index)],
                        source[base : base + seen, wide(index)],
                        preferred_element_type=F32,
                    ).astype(BF16)
                    for base in (0, seen)
                ]
                out = jnp.concatenate(out_t, axis=0).T
                for at, corner in enumerate(corners(unit, half)):
                    out_ref[corner] = out[at * HALF : (at + 1) * HALF]

        def reduce(index):
            unit, half = items[index]
            parts = []
            for weights, ref in ((slope2, q_ref), (prob2, g_ref)):
                part = jnp.dot(
                    weights[:, wide(index)], stacked(ref, unit, half), preferred_element_type=F32
                )
                parts.append(jnp.where(left, part[:seen], part[seen:]))
            return parts

        def join(first_half, second_half):
            total = jnp.concatenate(
                [
                    first_half[:HALF] + second_half[2 * HALF :],
                    second_half[:HALF],
                    first_half[HALF : 2 * HALF],
                    first_half[2 * HALF :] + second_half[HALF : 2 * HALF],
                ],
                axis=0,
            )
            return total + pltpu.roll(total, HEAD_DIM, 1)

        ahead, parts = products(0), []
        for index in range(len(items)):
            now = ahead
            weigh(index, 0, *now[0])
            if index + 1 < len(items):
                ahead = products(index + 1)
            weigh(index, 1, *now[1])
            if index >= 1:
                finish(index - 1)
            parts.append(reduce(index))
        finish(len(items) - 1)
        grads = [
            [join(parts[2 * unit][place], parts[2 * unit + 1][place]) for place in range(2)]
            for unit in range(2)
        ]
        dk = jnp.where(left, grads[0][0], grads[1][0]) * FACTOR
        dv = jnp.where(left, grads[0][1], grads[1][1])
        dk_ref[here, :] = dk[:WINDOW]
        dv_ref[here, :] = dv[:WINDOW]

        @pl.when(opening & prev_ok)
        def _():
            tail_sum[:, :128] += dk[WINDOW:]
            tail_sum[:, 128:] += dv[WINDOW:]

        @pl.when(jnp.logical_not(opening) & first)
        def _():
            dhalo_ref[0, :, :128] = dk[WINDOW:].astype(BF16)
            dhalo_ref[0, :, 128:] = dv[WINDOW:].astype(BF16)

        @pl.when(jnp.logical_not(opening) & jnp.logical_not(first))
        def _():
            dk_ref[before, :] += dk[WINDOW:]
            dv_ref[before, :] += dv[WINDOW:]

    @pl.when(block == blocks_here - 1)
    def _():
        width = dtail_refs[0].shape[1]
        heads = per_slot * GROUP
        total = tail_sum[...].astype(BF16)
        for part in range(2 // per_slot):
            feats = slice(part * width // 2, (part + 1) * width // 2)
            tail = jnp.concatenate([total[:, :128][:, feats], total[:, 128:][:, feats]], axis=1)
            rows = sink_rows[part * heads : (part + 1) * heads]
            rows = jnp.concatenate([rows, jnp.zeros((128 - heads, WINDOW), F32)], axis=0)
            sink_row = jnp.sum(rows.T, axis=0, keepdims=True)
            if width > 128:
                sink_row = jnp.concatenate([sink_row, jnp.zeros((1, width - 128), F32)], axis=1)
            extra = row_split(sink_row, (EXTRA, width))
            wanted = lax.rem(pair * (2 // per_slot) + part - head + slots, slots)
            for step, dtail_ref in zip(steps, dtail_refs):

                @pl.when(wanted == step)
                def _(dtail_ref=dtail_ref, tail=tail, extra=extra):
                    dtail_ref[:WINDOW] = tail
                    dtail_ref[WINDOW:] = extra


def gather_kernel(*refs):
    *in_refs, out_ref = refs
    total, sink_row = 0.0, 0.0
    for in_ref in in_refs:
        total = total + in_ref[:WINDOW].astype(F32)
        sink_row = sink_row + row_join(in_ref[WINDOW:])
    out_ref[:WINDOW] = total.astype(BF16)
    out_ref[WINDOW:] = row_split(sink_row, (EXTRA, out_ref.shape[1]))


def land_kernel(tok_count, blocks, table, here_ref, *refs):
    tok, head = lax.axis_index("tok"), lax.axis_index("head")
    in_refs, out_refs, sink_ref = refs[:LAG], refs[LAG:-1], refs[-1]
    slots = len(out_refs)
    blocks_here = blocks // slots
    for out_ref in out_refs:
        out_ref[...] = jnp.zeros_like(out_ref)
    sink_row = row_join(here_ref[WINDOW:])
    for distance, in_ref in enumerate(in_refs, 1):
        valid, place = child_tail(table, tok, distance, tok_count, blocks)
        sink_row = sink_row + row_join(in_ref[WINDOW:])
        wanted = lax.rem(place // blocks_here - head + slots, slots)
        here = pl.ds(pl.multiple_of(place % blocks_here * WINDOW, WINDOW), WINDOW)
        for step, out_ref in enumerate(out_refs):

            @pl.when(valid & (wanted == step))
            def _(out_ref=out_ref, in_ref=in_ref, here=here):
                total = out_ref[here, :].astype(F32) + in_ref[:WINDOW].astype(F32)
                out_ref[here, :] = total.astype(BF16)

    sink_ref[...] = jnp.broadcast_to(sink_row[:, :128], sink_ref.shape)


def total_kernel(dk_ref, dv_ref, halo_ref, sink_ref, far_ref, *refs):
    *tail_refs, key_ref, value_ref, sink_grad, tails = refs
    slots, rows = len(tail_refs), dk_ref.shape[0]
    width = tails.shape[2] // 2
    head = lax.axis_index("head")
    for step, tail_ref in enumerate(tail_refs):
        tails[lax.rem(head - step + slots, slots)] = tail_ref[...]
    halo_k = jnp.concatenate([halo_ref[pair][:, :128] for pair in range(PAIRS)], axis=1)
    halo_v = jnp.concatenate([halo_ref[pair][:, 128:] for pair in range(PAIRS)], axis=1)
    for in_ref, halo, at, out_ref in (
        (dk_ref, halo_k, 0, key_ref),
        (dv_ref, halo_v, width, value_ref),
    ):
        for begin in range(0, rows, WINDOW):
            here = slice(begin, begin + WINDOW)
            parts = [tails[slot, here, at : at + width] for slot in range(slots)]
            total = in_ref[here, :] + jnp.concatenate(parts, axis=1).astype(F32)
            if begin == rows - WINDOW:
                total = total + halo.astype(F32)
            out_ref[here, :] = total.astype(BF16)
    sink_row = -(sink_ref[0:1] + far_ref[0:1])
    for place in range(sink_grad.shape[0]):
        sink_grad[place] = sink_row[0, place]


def swap(values, axis):
    return [values[0]] + [ring(values[step], axis, step) for step in range(1, len(values))]


def local(
    queries, key_states, value_states, out_grad, sink_logits, branch_start, branch_len, parent_list
):
    tok_count, head_count = lax.axis_size("tok"), lax.axis_size("head")
    rows = queries.shape[0]
    blocks_here = rows // WINDOW
    blocks = blocks_here * head_count
    per_slot = KV_HEADS // head_count
    width = 2 * per_slot * HEAD_DIM

    def shape(dims, kind=BF16):
        return jax.ShapeDtypeStruct(dims, kind)

    queries, out_grad, key_states, value_states, sink_logits = (
        pltpu.with_memory_space_constraint(value, pltpu.HBM)
        for value in (queries, out_grad, key_states, value_states, sink_logits)
    )
    table = jnp.concatenate([branch_start, branch_len, parent_list[:, 0], parent_list[:, 1]])
    *slots, halo_out = pl.pallas_call(
        pack_kernel,
        out_shape=(shape((rows + EXTRA, width)),) * head_count + (shape((PAIRS, WINDOW, 256)),),
        in_specs=[HBM] * 3,
        out_specs=(VMEM,) * (head_count + 1),
        scratch_shapes=[
            pltpu.SMEM(sink_logits.shape, F32),
            pltpu.VMEM(key_states.shape, BF16),
            pltpu.VMEM(key_states.shape, BF16),
            pltpu.SemaphoreType.DMA((3,)),
        ],
        compiler_params=PARAMS,
        name="pack",
    )(sink_logits, key_states, value_states)
    spread = swap(slots, "head")
    *chosen, sinks = pl.pallas_call(
        functools.partial(choose_kernel, tok_count, blocks),
        out_shape=(shape((WINDOW, width)),) * LAG + (shape((KV_HEADS * GROUP, 128), F32),),
        in_specs=[SMEM] + [VMEM] * head_count,
        out_specs=(VMEM,) * (LAG + 1),
        compiler_params=PARAMS,
        name="choose",
    )(table, *spread)
    arrived = [ring(chosen[LAG - s], "tok", s) for s in range(LAG, 0, -1)]
    quarter = pl.pallas_call(
        functools.partial(arrive_kernel, tok_count),
        out_shape=shape((WINDOW, width)),
        in_specs=[SMEM] + [VMEM] * LAG,
        out_specs=VMEM,
        compiler_params=PARAMS,
        name="arrive",
    )(table, *arrived)
    tails = swap([quarter] * head_count, "head")
    halo_out, _ = lax.optimization_barrier((halo_out, quarter))
    halo = shift(halo_out, "head", 1)

    def attend(steps, pairs, offset, halo, joined):
        def at(index):
            def place(p, b):
                return index(p if offset is None else own_pair(p, offset), b)

            return place

        big = pl.BlockSpec((WINDOW, 1024), at(lambda p, b: (b, p)))
        small = pl.BlockSpec((rows, 128), at(lambda p, b: (0, p)))
        near = pl.BlockSpec((1, WINDOW, 256), at(lambda p, b: (p, 0, 0)))
        last = pl.BlockSpec((WINDOW, width), lambda p, b: (blocks_here - 1, 0))
        whole = pl.BlockSpec((WINDOW, width), lambda p, b: (0, 0))
        whole_back = pl.BlockSpec((WINDOW + EXTRA, width), lambda p, b: (0, 0))
        inputs = (
            (table, SMEM),
            (sinks, pl.BlockSpec((2 * GROUP, 128), at(lambda p, b: (p, 0)))),
            (queries, big),
            (out_grad, big),
            (key_states, small),
            (value_states, small),
            (halo, near if halo.ndim == 3 else last),
            *((tails[step], whole) for step in steps),
            *((value, pl.BlockSpec(memory_space=pl.ANY)) for value in joined),
        )
        base = len(inputs) - len(joined)
        return pl.pallas_call(
            functools.partial(
                attend_kernel, tok_count, blocks_here, head_count, steps, offset, len(joined)
            ),
            grid=(pairs, blocks_here),
            out_shape=(
                shape(queries.shape),
                shape(queries.shape),
                shape(key_states.shape, F32),
                shape(key_states.shape, F32),
                shape((PAIRS, WINDOW, 256)),
            )
            + (shape((WINDOW + EXTRA, width)),) * len(steps),
            in_specs=[spec for _, spec in inputs],
            out_specs=(big, big, small, small, near) + (whole_back,) * len(steps),
            scratch_shapes=[
                pltpu.VMEM((head_count, WINDOW, width), BF16),
                pltpu.VMEM((WINDOW, 256), F32),
                pltpu.VMEM((2 * GROUP, WINDOW), F32),
                pltpu.VMEM((6 * HALF, 1024), BF16),
                pltpu.VMEM((6 * HALF, 1024), BF16),
            ],
            input_output_aliases={base + place: place for place in range(len(joined))},
            compiler_params=PARAMS,
            name="attend",
        )(*(value for value, _ in inputs))

    if per_slot == 2:
        *joined, own_tail = attend((0,), 1, 0, spread[1], ())
        *results, tail_1, tail_2, tail_3 = attend((1, 2, 3), PAIRS - 1, 1, halo, joined)
        dtail = [own_tail, tail_1, tail_2, tail_3]
    else:
        results = attend(tuple(range(head_count)), PAIRS, None, halo, ())
        results, dtail = results[:5], list(results[5:])
    attended, query_grad, dk, dv, dhalo = results
    parts = swap(dtail, "head")
    quarter_grad = pl.pallas_call(
        gather_kernel,
        out_shape=shape((WINDOW + EXTRA, width)),
        in_specs=[VMEM] * head_count,
        out_specs=VMEM,
        compiler_params=PARAMS,
        name="gather",
    )(*parts)
    returned = [ring(quarter_grad, "tok", -s) for s in range(LAG, 0, -1)][::-1]
    halo_back = shift(dhalo, "head", -1)
    *landed, sink_near = pl.pallas_call(
        functools.partial(land_kernel, tok_count, blocks),
        out_shape=(shape((rows, width)),) * head_count + (shape((8, 128), F32),),
        in_specs=[SMEM] + [VMEM] * (LAG + 1),
        out_specs=(VMEM,) * (head_count + 1),
        compiler_params=PARAMS,
        name="land",
    )(table, quarter_grad, *returned)
    tails_back = swap(landed, "head")
    span = LAG + 1
    while 2 * span < tok_count:
        sink_near = sink_near + ring(sink_near, "tok", -span)
        span *= 2
    sink_far = ring(sink_near, "tok", -span)
    key_grad, value_grad, sink_grad = pl.pallas_call(
        total_kernel,
        out_shape=(
            shape(key_states.shape),
            shape(value_states.shape),
            shape(sink_logits.shape, F32),
        ),
        in_specs=[VMEM] * (5 + head_count),
        out_specs=(VMEM, VMEM, SMEM),
        scratch_shapes=[pltpu.VMEM((head_count, rows, width), BF16)],
        compiler_params=PARAMS,
        name="total",
    )(dk, dv, halo_back, sink_near, sink_far, *tails_back)
    return attended, query_grad, key_grad, value_grad, sink_grad


def solution(mesh):
    rows = P(("tok", "head"), None)
    return jax.shard_map(
        local,
        mesh=mesh,
        in_specs=(rows, rows, rows, rows, P("head"), P(), P(), P()),
        out_specs=(rows, rows, rows, rows, P("head")),
        check_vma=False,
    )
```

```python
import functools

import jax
import jax.numpy as jnp
from jax import lax
from jax.experimental import pallas as pl
from jax.experimental.pallas import tpu as pltpu
from jax.sharding import PartitionSpec as P

HEAD_DIM = 64
KV_HEADS = 8
GROUP = 8
WINDOW = 128
HALF = WINDOW // 2
LAG = 3
BR_DEV = 2
PAIRS = KV_HEADS // 2
FACTOR = 0.125
LOW = -1e30
EXTRA = 16
BF16 = jnp.bfloat16
F32 = jnp.float32

SMEM = pl.BlockSpec(memory_space=pltpu.SMEM)
VMEM = pl.BlockSpec(memory_space=pltpu.VMEM)
HBM = pl.BlockSpec(memory_space=pltpu.HBM)
PARAMS = pltpu.CompilerParams(vmem_limit_bytes=24 * 1024 * 1024)


def shift(value, axis, steps):
    count = lax.axis_size(axis)
    leading, last = (max(0, -steps), min(count, count - steps))
    return lax.ppermute(value, axis, [(source, source + steps) for source in range(leading, last)])


def ring(value, axis, steps):
    count = lax.axis_size(axis)
    return lax.ppermute(value, axis, [(source, (source + steps) % count) for source in range(count)])


def row_split(row, dims):
    high = row.astype(BF16).astype(F32)
    middle = (row - high).astype(BF16).astype(F32)
    low = row - high - middle
    place = lax.broadcasted_iota(jnp.int32, dims, 0)
    rest = jnp.where(place == 2, low, 0.0)
    return jnp.where(place == 0, high, jnp.where(place == 1, middle, rest)).astype(BF16)


def row_join(rows):
    rows = rows.astype(F32)
    return rows[0:1] + rows[1:2] + rows[2:3]


def child_tail(table, tok, distance, tok_count, blocks):
    branches = tok_count * BR_DEV
    child = jnp.minimum(tok + distance, tok_count - 1) * BR_DEV
    parent = table[2 * branches + child]
    safe = jnp.maximum(parent, 0)
    valid = (tok + distance < tok_count) & (parent >= 0) & (safe // BR_DEV == tok)
    place = (table[safe] + table[3 * branches + child]) // WINDOW - tok * blocks
    return valid, jnp.where(valid, place, 0)


def block_state(table, tok, tok_count, block):
    branches = tok_count * BR_DEV
    position = block * WINDOW
    alive, opening = jnp.bool_(False), jnp.bool_(False)
    for branch in range(BR_DEV):
        start = table[tok * BR_DEV + branch]
        length = table[branches + tok * BR_DEV + branch]
        alive = alive | ((start <= position) & (position < start + length))
        opening = opening | (start == position)
    has_tail = table[2 * branches + tok * BR_DEV] >= 0
    return alive, opening, jnp.logical_not(opening) | has_tail


def take(ref, slot, width):
    if width % 128 == 0:
        return ref[:, pl.ds(pl.multiple_of(slot * width, width), width)]
    value = ref[:, :width]
    for other in range(1, ref.shape[1] // width):
        value = jnp.where(slot == other, ref[:, other * width : (other + 1) * width], value)
    return value


def pack_kernel(sink_hbm, key_hbm, value_hbm, *refs):
    *slot_refs, halo_ref, keys, values, sinks, sems = refs
    copies = [
        pltpu.make_async_copy(source, target, sems.at[place])
        for place, (source, target) in enumerate(
            ((sink_hbm, sinks), (key_hbm, keys), (value_hbm, values))
        )
    ]
    for copy in copies:
        copy.start()
    for copy in copies:
        copy.wait()
    slots, rows = len(slot_refs), keys.shape[0]
    head = lax.axis_index("head")
    width = KV_HEADS * HEAD_DIM // slots
    lane = lax.broadcasted_iota(jnp.int32, (1, 2 * width), 1)
    sink_row = jnp.zeros((1, 2 * width), F32)
    for place in range(sinks.shape[0]):
        sink_row = jnp.where(lane == place, sinks[place], sink_row)
    extra = row_split(sink_row, (EXTRA, 2 * width))
    for step, slot_ref in enumerate(slot_refs):
        slot = lax.rem(head + step, slots)
        slot_ref[:rows] = jnp.concatenate(
            [take(keys, slot, width), take(values, slot, width)], axis=1
        )
        slot_ref[rows:] = extra
    for pair in range(PAIRS):
        lanes = slice(pair * 128, (pair + 1) * 128)
        last = slice(rows - WINDOW, rows)
        halo_ref[pair] = jnp.concatenate([keys[last, lanes], values[last, lanes]], axis=1)


def choose_kernel(tok_count, blocks, table, *refs):
    slots = len(refs) - LAG - 1
    slot_refs, out_refs, sink_ref = refs[:slots], refs[slots:-1], refs[-1]
    tok, head = lax.axis_index("tok"), lax.axis_index("head")
    rows = slot_refs[0].shape[0] - EXTRA
    blocks_here = rows // WINDOW
    heads = sink_ref.shape[0] // slots
    for distance, out_ref in zip(range(LAG, 0, -1), out_refs):
        _, place = child_tail(table, tok, distance, tok_count, blocks)
        begin = pl.multiple_of(place % blocks_here * WINDOW, WINDOW)
        wanted = lax.rem(head - place // blocks_here + slots, slots)
        for step, slot_ref in enumerate(slot_refs):

            @pl.when(wanted == step)
            def _(out_ref=out_ref, slot_ref=slot_ref, begin=begin):
                out_ref[...] = slot_ref[pl.ds(begin, WINDOW), :]

    for step, slot_ref in enumerate(slot_refs):
        source = lax.rem(head - step + slots, slots)
        sink_row = row_join(slot_ref[rows:, :])[:, :128]
        turned = jnp.broadcast_to(sink_row, (128, 128)).T
        sink_ref[pl.ds(pl.multiple_of(source * heads, heads), heads), :] = turned[:heads]


def arrive_kernel(tok_count, table, *refs):
    tok = lax.axis_index("tok")
    *in_refs, out_ref = refs
    parent = table[2 * tok_count * BR_DEV + tok * BR_DEV]
    mine = jnp.where(parent >= 0, tok - jnp.maximum(parent, 0) // BR_DEV, 1)
    for distance, in_ref in zip(range(LAG, 0, -1), in_refs):

        @pl.when(mine == distance)
        def _(in_ref=in_ref):
            out_ref[...] = in_ref[...]


def stage_kernel(*refs):
    *arrays, sems = refs
    half = len(arrays) // 2
    copies = [
        pltpu.make_async_copy(source, target, sems.at[place])
        for place, (source, target) in enumerate(zip(arrays[:half], arrays[half:]))
    ]
    for copy in copies:
        copy.start()
    for copy in copies:
        copy.wait()


def attend_kernel(tok_count, blocks_here, slots, steps, offset, pairs, joins, *refs):
    inputs, refs = refs[:7], refs[7:]
    tail_refs, refs = refs[: len(steps)], refs[len(steps) + joins :]
    outputs, refs = refs[:5], refs[5:]
    dtail_refs, refs = refs[: len(steps)], refs[len(steps) :]
    tails, *scratch = refs
    head = lax.axis_index("head")
    for step, tail_ref in zip(steps, tail_refs):
        tails[lax.rem(head - step + slots, slots)] = tail_ref[...]

    def step(place, carry):
        pair = place // blocks_here
        if offset is not None:
            pair = lax.rem(head + pair + offset, PAIRS)
        attend_block(
            tok_count,
            blocks_here,
            slots,
            pair,
            place % blocks_here,
            inputs,
            outputs,
            tails,
            tuple(zip(steps, dtail_refs)),
            scratch,
        )
        return carry

    lax.fori_loop(0, pairs * blocks_here, step, 0)


def attend_block(
    tok_count, blocks_here, slots, pair, block, inputs, outputs, tails, dtails, scratch
):
    table, sink_ref, q_ref, g_ref, k_ref, v_ref, halo_ref = inputs
    o_ref, dq_ref, dk_ref, dv_ref, dhalo_ref = outputs
    tail_sum, sink_rows, prob2, slope2 = scratch
    per_slot = KV_HEADS // slots
    tok, head = lax.axis_index("tok"), lax.axis_index("head")
    number = (tok * lax.axis_size("head") + head) * blocks_here + block
    alive, opening, prev_ok = block_state(table, tok, tok_count, number)
    here = pl.ds(pl.multiple_of(block * WINDOW, WINDOW), WINDOW)
    before = pl.ds(pl.multiple_of(jnp.maximum(block - 1, 0) * WINDOW, WINDOW), WINDOW)
    first = block == 0
    near = pl.ds(pl.multiple_of(pair * 128, 128), 128)
    big = pl.ds(pl.multiple_of(pair * 1024, 1024), 1024)
    q_ref, g_ref, o_ref, dq_ref = (ref.at[here, big] for ref in (q_ref, g_ref, o_ref, dq_ref))
    k_ref, v_ref, dk_ref, dv_ref = (ref.at[:, near] for ref in (k_ref, v_ref, dk_ref, dv_ref))
    sink_ref = sink_ref.at[pl.ds(pl.multiple_of(pair * 16, 16), 16)]
    dhalo_ref = dhalo_ref.at[pair]

    @pl.when(first)
    def _():
        tail_sum[...] = jnp.zeros_like(tail_sum)
        dhalo_ref[...] = jnp.zeros((WINDOW, 256), BF16)
        sink_rows[...] = jnp.zeros_like(sink_rows)

    @pl.when(jnp.logical_not(alive))
    def _():
        o_ref[...] = jnp.zeros((WINDOW, 1024), BF16)
        dq_ref[...] = jnp.zeros((WINDOW, 1024), BF16)
        dk_ref[here, :] = jnp.zeros((WINDOW, 128), F32)
        dv_ref[here, :] = jnp.zeros((WINDOW, 128), F32)

    @pl.when(alive)
    def _():
        if len(halo_ref.shape) == 2:
            last = halo_ref.shape[0] - EXTRA
            halo = halo_ref[last - WINDOW : last]
        else:
            halo = halo_ref[pair]
        if per_slot == 2:
            tail = tails[pair]
            tail_k, tail_v = tail[:, :128], tail[:, 128:]
        else:
            tail_a, tail_b = tails[2 * pair], tails[2 * pair + 1]
            tail_k = jnp.concatenate([tail_a[:, :64], tail_b[:, :64]], axis=1)
            tail_v = jnp.concatenate([tail_a[:, 64:], tail_b[:, 64:]], axis=1)
        near_k = jnp.where(first, halo[:, :128], k_ref[before, :])
        near_v = jnp.where(first, halo[:, 128:], v_ref[before, :])
        prev_k = jnp.where(opening, tail_k, near_k)
        prev_v = jnp.where(opening, tail_v, near_v)
        own_k, own_v = k_ref[here, :], v_ref[here, :]

        def halves(own, prev):
            return (
                jnp.concatenate([own[:HALF], prev[:HALF], prev[HALF:]], axis=0),
                jnp.concatenate([own[HALF:], prev[HALF:], own[:HALF]], axis=0),
            )

        left = lax.broadcasted_iota(jnp.int32, (1, 128), 1) < HALF
        low16 = left.astype(F32).astype(BF16)
        high16 = BF16(1) - low16

        def padded(seen):
            swapped = jnp.concatenate([seen[:, 64:], seen[:, :64]], axis=1)
            return (
                jnp.concatenate([seen * low16, swapped * high16], axis=0),
                jnp.concatenate([swapped * low16, seen * high16], axis=0),
            )

        seen_k = halves(own_k * BF16(FACTOR), prev_k * BF16(FACTOR))
        seen_v = halves(own_v, prev_v)
        padded_k = tuple(padded(value) for value in seen_k)
        padded_v = tuple(padded(value) for value in seen_v)
        turned_k = tuple(value.T for value in seen_k)
        turned_v = tuple(value.T for value in seen_v)
        bias = jnp.where(prev_ok, 0.0, LOW)
        key_place = lax.broadcasted_iota(jnp.int32, (HALF, 4 * HALF), 0)
        query_place = lax.broadcasted_iota(jnp.int32, (HALF, 4 * HALF), 1) & (HALF - 1)
        own = key_place <= query_place
        own16 = own.astype(F32).astype(BF16)
        turn = (((1,), (1,)), ((), ()))
        items = [(unit, half) for unit in range(2) for half in range(2)]
        seen = 3 * HALF

        def wide(index):
            return slice(index * 256, (index + 1) * 256)

        def feats(index):
            unit = items[index][0]
            return slice(unit * HEAD_DIM, (unit + 1) * HEAD_DIM)

        def corners(unit, half):
            rows = slice(half * HALF, (half + 1) * HALF)
            return [
                (rows, slice(unit * 512 + at * 128, unit * 512 + (at + 1) * 128)) for at in range(4)
            ]

        def stacked(ref, unit, half):
            return jnp.concatenate([ref[corner] for corner in corners(unit, half)], axis=0)

        def products(index):
            unit, half = items[index]
            score, dp = (
                lax.dot_general(
                    padded[half][unit],
                    stacked(ref, unit, half),
                    turn,
                    preferred_element_type=F32,
                )
                for padded, ref in ((padded_k, q_ref), (padded_v, g_ref))
            )
            parts = []
            for base in (0, seen):
                near, far = slice(base, base + HALF), slice(base + HALF, base + 2 * HALF)
                rest = slice(base + 2 * HALF, base + 3 * HALF)
                edge = jnp.where(own, score[near], score[far] + bias)
                whole = score[rest] + bias if half == 0 else score[rest]
                parts.append((edge, whole, jnp.where(own, dp[near], dp[far]), dp[rest]))
            return parts

        def weigh(index, odd, edge, whole, dp_edge, dp_whole):
            unit, half = items[index]
            base = odd * seen
            row = unit * GROUP + odd
            sink = jnp.concatenate(
                [
                    jnp.where(left, sink_ref[at : at + 1], sink_ref[at + 2 : at + 3])
                    for at in (row, row + 4)
                ],
                axis=1,
            )
            peak = jnp.max(jnp.maximum(edge, whole), axis=0, keepdims=True)
            peak = jnp.maximum(peak, sink)
            edge, whole = jnp.exp(edge - peak), jnp.exp(whole - peak)
            sink_weight = jnp.exp(sink - peak)
            inverse = 1.0 / (jnp.sum(edge + whole, axis=0, keepdims=True) + sink_weight)
            edge, whole = edge * inverse, whole * inverse
            term_edge, term_whole = edge * dp_edge, whole * dp_whole
            delta = jnp.sum(term_edge + term_whole, axis=0, keepdims=True)
            for target, at_edge, at_whole in (
                (prob2, edge, whole),
                (slope2, term_edge - edge * delta, term_whole - whole * delta),
            ):
                edge16 = at_edge.astype(BF16)
                edge_own = edge16 * own16
                target[base : base + HALF, wide(index)] = edge_own
                target[base + HALF : base + 2 * HALF, wide(index)] = edge16 - edge_own
                target[base + 2 * HALF : base + seen, wide(index)] = at_whole.astype(BF16)
            sink_term = sink_weight * inverse * delta
            for at, lanes in ((row, slice(0, 128)), (row + 4, slice(128, 256))):
                part = sink_term[:, lanes]
                sink_rows[at : at + 1] += jnp.where(left, part, 0.0)
                sink_rows[at + 2 : at + 3] += jnp.where(left, 0.0, part)

        def finish(index):
            unit, half = items[index]
            for source, across, out_ref in ((prob2, turned_v, o_ref), (slope2, turned_k, dq_ref)):
                out_t = [
                    jnp.dot(
                        across[half][feats(index)],
                        source[base : base + seen, wide(index)],
                        preferred_element_type=F32,
                    ).astype(BF16)
                    for base in (0, seen)
                ]
                out = jnp.concatenate(out_t, axis=0).T
                for at, corner in enumerate(corners(unit, half)):
                    out_ref[corner] = out[at * HALF : (at + 1) * HALF]

        def reduce(index):
            unit, half = items[index]
            parts = []
            for weights, ref in ((slope2, q_ref), (prob2, g_ref)):
                part = jnp.dot(
                    weights[:, wide(index)], stacked(ref, unit, half), preferred_element_type=F32
                )
                parts.append(jnp.where(left, part[:seen], part[seen:]))
            return parts

        def join(first_half, second_half):
            total = jnp.concatenate(
                [
                    first_half[:HALF] + second_half[2 * HALF :],
                    second_half[:HALF],
                    first_half[HALF : 2 * HALF],
                    first_half[2 * HALF :] + second_half[HALF : 2 * HALF],
                ],
                axis=0,
            )
            return total + pltpu.roll(total, HEAD_DIM, 1)

        ahead, parts = products(0), []
        for index in range(len(items)):
            now = ahead
            weigh(index, 0, *now[0])
            if index + 1 < len(items):
                ahead = products(index + 1)
            weigh(index, 1, *now[1])
            if index >= 1:
                finish(index - 1)
            parts.append(reduce(index))
        finish(len(items) - 1)
        grads = [
            [join(parts[2 * unit][place], parts[2 * unit + 1][place]) for place in range(2)]
            for unit in range(2)
        ]
        dk = jnp.where(left, grads[0][0], grads[1][0]) * FACTOR
        dv = jnp.where(left, grads[0][1], grads[1][1])
        dk_ref[here, :] = dk[:WINDOW]
        dv_ref[here, :] = dv[:WINDOW]

        @pl.when(opening & prev_ok)
        def _():
            tail_sum[:, :128] += dk[WINDOW:]
            tail_sum[:, 128:] += dv[WINDOW:]

        @pl.when(jnp.logical_not(opening) & first)
        def _():
            dhalo_ref[:, :128] = dk[WINDOW:].astype(BF16)
            dhalo_ref[:, 128:] = dv[WINDOW:].astype(BF16)

        @pl.when(jnp.logical_not(opening) & jnp.logical_not(first))
        def _():
            dk_ref[before, :] += dk[WINDOW:]
            dv_ref[before, :] += dv[WINDOW:]

    @pl.when(block == blocks_here - 1)
    def _():
        width = 2 * per_slot * HEAD_DIM
        heads = per_slot * GROUP
        total = tail_sum[...].astype(BF16)
        for part in range(2 // per_slot):
            feats = slice(part * width // 2, (part + 1) * width // 2)
            tail = jnp.concatenate([total[:, :128][:, feats], total[:, 128:][:, feats]], axis=1)
            rows = sink_rows[part * heads : (part + 1) * heads]
            rows = jnp.concatenate([rows, jnp.zeros((128 - heads, WINDOW), F32)], axis=0)
            sink_row = jnp.sum(rows.T, axis=0, keepdims=True)
            if width > 128:
                sink_row = jnp.concatenate([sink_row, jnp.zeros((1, width - 128), F32)], axis=1)
            extra = row_split(sink_row, (EXTRA, width))
            wanted = lax.rem(pair * (2 // per_slot) + part - head + slots, slots)
            for step, dtail_ref in dtails:

                @pl.when(wanted == step)
                def _(dtail_ref=dtail_ref, tail=tail, extra=extra):
                    dtail_ref[:WINDOW] = tail
                    dtail_ref[WINDOW:] = extra


def gather_kernel(*refs):
    *in_refs, out_ref = refs
    total, sink_row = 0.0, 0.0
    for in_ref in in_refs:
        total = total + in_ref[:WINDOW].astype(F32)
        sink_row = sink_row + row_join(in_ref[WINDOW:])
    out_ref[:WINDOW] = total.astype(BF16)
    out_ref[WINDOW:] = row_split(sink_row, (EXTRA, out_ref.shape[1]))


def land_kernel(tok_count, blocks, table, here_ref, *refs):
    tok, head = lax.axis_index("tok"), lax.axis_index("head")
    in_refs, out_refs, sink_ref = refs[:LAG], refs[LAG:-1], refs[-1]
    slots = len(out_refs)
    blocks_here = blocks // slots
    for out_ref in out_refs:
        out_ref[...] = jnp.zeros_like(out_ref)
    sink_row = row_join(here_ref[WINDOW:])
    for distance, in_ref in enumerate(in_refs, 1):
        valid, place = child_tail(table, tok, distance, tok_count, blocks)
        sink_row = sink_row + row_join(in_ref[WINDOW:])
        wanted = lax.rem(place // blocks_here - head + slots, slots)
        here = pl.ds(pl.multiple_of(place % blocks_here * WINDOW, WINDOW), WINDOW)
        for step, out_ref in enumerate(out_refs):

            @pl.when(valid & (wanted == step))
            def _(out_ref=out_ref, in_ref=in_ref, here=here):
                total = out_ref[here, :].astype(F32) + in_ref[:WINDOW].astype(F32)
                out_ref[here, :] = total.astype(BF16)

    sink_ref[...] = jnp.broadcast_to(sink_row[:, :128], sink_ref.shape)


def total_kernel(dk_ref, dv_ref, halo_ref, sink_ref, far_ref, *refs):
    *tail_refs, key_ref, value_ref, sink_grad, tails = refs
    slots, rows = len(tail_refs), dk_ref.shape[0]
    width = tails.shape[2] // 2
    head = lax.axis_index("head")
    for step, tail_ref in enumerate(tail_refs):
        tails[lax.rem(head - step + slots, slots)] = tail_ref[...]
    halo_k = jnp.concatenate([halo_ref[pair][:, :128] for pair in range(PAIRS)], axis=1)
    halo_v = jnp.concatenate([halo_ref[pair][:, 128:] for pair in range(PAIRS)], axis=1)
    for in_ref, halo, at, out_ref in (
        (dk_ref, halo_k, 0, key_ref),
        (dv_ref, halo_v, width, value_ref),
    ):
        for begin in range(0, rows, WINDOW):
            here = slice(begin, begin + WINDOW)
            parts = [tails[slot, here, at : at + width] for slot in range(slots)]
            total = in_ref[here, :] + jnp.concatenate(parts, axis=1).astype(F32)
            if begin == rows - WINDOW:
                total = total + halo.astype(F32)
            out_ref[here, :] = total.astype(BF16)
    sink_row = -(sink_ref[0:1] + far_ref[0:1])
    for place in range(sink_grad.shape[0]):
        sink_grad[place] = sink_row[0, place]


def swap(values, axis):
    return [values[0]] + [ring(values[step], axis, step) for step in range(1, len(values))]


def local(
    queries, key_states, value_states, out_grad, sink_logits, branch_start, branch_len, parent_list
):
    tok_count, head_count = lax.axis_size("tok"), lax.axis_size("head")
    rows = queries.shape[0]
    blocks_here = rows // WINDOW
    blocks = blocks_here * head_count
    per_slot = KV_HEADS // head_count
    width = 2 * per_slot * HEAD_DIM

    def shape(dims, kind=BF16):
        return jax.ShapeDtypeStruct(dims, kind)

    def far(value):
        return pltpu.with_memory_space_constraint(value, pltpu.HBM)

    def close(value):
        return pltpu.with_memory_space_constraint(value, pltpu.VMEM)

    table = jnp.concatenate([branch_start, branch_len, parent_list[:, 0], parent_list[:, 1]])
    *slots, halo_out, keys, values = pl.pallas_call(
        pack_kernel,
        out_shape=(shape((rows + EXTRA, width)),) * head_count
        + (shape((PAIRS, WINDOW, 256)),)
        + (pltpu.VMEM(key_states.shape, BF16),) * 2,
        in_specs=[HBM] * 3,
        out_specs=(VMEM,) * (head_count + 3),
        scratch_shapes=[
            pltpu.SMEM(sink_logits.shape, F32),
            pltpu.SemaphoreType.DMA((3,)),
        ],
        compiler_params=PARAMS,
        name="pack",
    )(far(sink_logits), far(key_states), far(value_states))
    spread = swap(slots, "head")
    *chosen, sinks = pl.pallas_call(
        functools.partial(choose_kernel, tok_count, blocks),
        out_shape=(shape((WINDOW, width)),) * LAG + (shape((KV_HEADS * GROUP, 128), F32),),
        in_specs=[SMEM] + [VMEM] * head_count,
        out_specs=(VMEM,) * (LAG + 1),
        compiler_params=PARAMS,
        name="choose",
    )(table, *spread)
    arrived = [ring(chosen[LAG - s], "tok", s) for s in range(LAG, 0, -1)]
    queries, out_grad, _ = lax.optimization_barrier((queries, out_grad, sinks))
    near_queries, near_grad = pl.pallas_call(
        stage_kernel,
        out_shape=(pltpu.VMEM(queries.shape, BF16),) * 2,
        in_specs=[HBM] * 2,
        out_specs=(VMEM,) * 2,
        scratch_shapes=[pltpu.SemaphoreType.DMA((2,))],
        compiler_params=PARAMS,
        name="stage",
    )(far(queries), far(out_grad))
    *arrived, near_queries, near_grad = lax.optimization_barrier(
        (*arrived, near_queries, near_grad)
    )
    quarter = pl.pallas_call(
        functools.partial(arrive_kernel, tok_count),
        out_shape=shape((WINDOW, width)),
        in_specs=[SMEM] + [VMEM] * LAG,
        out_specs=VMEM,
        compiler_params=PARAMS,
        name="arrive",
    )(table, *arrived)
    tails = swap([quarter] * head_count, "head")
    halo_out, _ = lax.optimization_barrier((halo_out, quarter))
    halo = shift(halo_out, "head", 1)

    def attend(steps, pairs, offset, halo, joined):
        inputs = (
            sinks,
            close(near_queries),
            close(near_grad),
            close(keys),
            close(values),
            halo,
            *(tails[step] for step in steps),
            *(close(value) for value in joined),
        )
        base = 1 + len(inputs) - len(joined)
        return pl.pallas_call(
            functools.partial(
                attend_kernel,
                tok_count,
                blocks_here,
                head_count,
                steps,
                offset,
                pairs,
                len(joined),
            ),
            out_shape=(
                pltpu.VMEM(queries.shape, BF16),
                pltpu.VMEM(queries.shape, BF16),
                pltpu.VMEM(key_states.shape, F32),
                pltpu.VMEM(key_states.shape, F32),
                pltpu.VMEM((PAIRS, WINDOW, 256), BF16),
            )
            + (shape((WINDOW + EXTRA, width)),) * len(steps),
            in_specs=[SMEM] + [VMEM] * len(inputs),
            out_specs=(VMEM,) * (5 + len(steps)),
            scratch_shapes=[
                pltpu.VMEM((head_count, WINDOW, width), BF16),
                pltpu.VMEM((WINDOW, 256), F32),
                pltpu.VMEM((2 * GROUP, WINDOW), F32),
                pltpu.VMEM((6 * HALF, 1024), BF16),
                pltpu.VMEM((6 * HALF, 1024), BF16),
            ],
            input_output_aliases={base + place: place for place in range(len(joined))},
            compiler_params=PARAMS,
            name="attend",
        )(table, *inputs)

    if per_slot == 2:
        *joined, own_tail = attend((0,), 1, 0, spread[1], ())
        *results, tail_1, tail_2, tail_3 = attend((1, 2, 3), PAIRS - 1, 1, halo, joined)
        dtail = [own_tail, tail_1, tail_2, tail_3]
    else:
        results = attend(tuple(range(head_count)), PAIRS, None, halo, ())
        results, dtail = results[:5], list(results[5:])
    attended, query_grad, dk, dv, dhalo = results
    parts = swap(dtail, "head")
    quarter_grad = pl.pallas_call(
        gather_kernel,
        out_shape=shape((WINDOW + EXTRA, width)),
        in_specs=[VMEM] * head_count,
        out_specs=VMEM,
        compiler_params=PARAMS,
        name="gather",
    )(*parts)
    attended, query_grad, _ = lax.optimization_barrier((attended, query_grad, quarter_grad))
    attended, query_grad = pl.pallas_call(
        stage_kernel,
        out_shape=(pltpu.HBM(queries.shape, BF16),) * 2,
        in_specs=[VMEM] * 2,
        out_specs=(HBM,) * 2,
        scratch_shapes=[pltpu.SemaphoreType.DMA((2,))],
        compiler_params=PARAMS,
        name="flush",
    )(close(attended), close(query_grad))
    returned = [ring(quarter_grad, "tok", -s) for s in range(LAG, 0, -1)][::-1]
    halo_back = shift(dhalo, "head", -1)
    *landed, sink_near = pl.pallas_call(
        functools.partial(land_kernel, tok_count, blocks),
        out_shape=(shape((rows, width)),) * head_count + (shape((8, 128), F32),),
        in_specs=[SMEM] + [VMEM] * (LAG + 1),
        out_specs=(VMEM,) * (head_count + 1),
        compiler_params=PARAMS,
        name="land",
    )(table, quarter_grad, *returned)
    tails_back = swap(landed, "head")
    span = LAG + 1
    while 2 * span < tok_count:
        sink_near = sink_near + ring(sink_near, "tok", -span)
        span *= 2
    sink_far = ring(sink_near, "tok", -span)
    key_grad, value_grad, sink_grad = pl.pallas_call(
        total_kernel,
        out_shape=(
            shape(key_states.shape),
            shape(value_states.shape),
            shape(sink_logits.shape, F32),
        ),
        in_specs=[VMEM] * (5 + head_count),
        out_specs=(VMEM, VMEM, SMEM),
        scratch_shapes=[pltpu.VMEM((head_count, rows, width), BF16)],
        compiler_params=PARAMS,
        name="total",
    )(dk, dv, halo_back, sink_near, sink_far, *tails_back)
    return attended, query_grad, key_grad, value_grad, sink_grad


def solution(mesh):
    rows = P(("tok", "head"), None)
    return jax.shard_map(
        local,
        mesh=mesh,
        in_specs=(rows, rows, rows, rows, P("head"), P(), P(), P()),
        out_specs=(rows, rows, rows, rows, P("head")),
        check_vma=False,
    )
```

```python
import functools

import jax
import jax.numpy as jnp
from jax import lax
from jax.experimental import pallas as pl
from jax.experimental.pallas import tpu as pltpu
from jax.sharding import PartitionSpec as P

HEAD_DIM = 64
KV_HEADS = 8
GROUP = 8
WINDOW = 128
HALF = WINDOW // 2
LAG = 3
BR_DEV = 2
PAIRS = KV_HEADS // 2
FACTOR = 0.125
LOW = -1e30
EXTRA = 16
BF16 = jnp.bfloat16
F32 = jnp.float32

SMEM = pl.BlockSpec(memory_space=pltpu.SMEM)
VMEM = pl.BlockSpec(memory_space=pltpu.VMEM)
HBM = pl.BlockSpec(memory_space=pltpu.HBM)
PARAMS = pltpu.CompilerParams(vmem_limit_bytes=24 * 1024 * 1024)


def shift(value, axis, steps):
    count = lax.axis_size(axis)
    leading, last = (max(0, -steps), min(count, count - steps))
    return lax.ppermute(value, axis, [(source, source + steps) for source in range(leading, last)])


def ring(value, axis, steps):
    count = lax.axis_size(axis)
    return lax.ppermute(value, axis, [(source, (source + steps) % count) for source in range(count)])


def row_split(row, dims):
    high = row.astype(BF16).astype(F32)
    middle = (row - high).astype(BF16).astype(F32)
    low = row - high - middle
    place = lax.broadcasted_iota(jnp.int32, dims, 0)
    rest = jnp.where(place == 2, low, 0.0)
    return jnp.where(place == 0, high, jnp.where(place == 1, middle, rest)).astype(BF16)


def row_join(rows):
    rows = rows.astype(F32)
    return rows[0:1] + rows[1:2] + rows[2:3]


def child_tail(table, tok, distance, tok_count, blocks):
    branches = tok_count * BR_DEV
    child = jnp.minimum(tok + distance, tok_count - 1) * BR_DEV
    parent = table[2 * branches + child]
    safe = jnp.maximum(parent, 0)
    valid = (tok + distance < tok_count) & (parent >= 0) & (safe // BR_DEV == tok)
    place = (table[safe] + table[3 * branches + child]) // WINDOW - tok * blocks
    return valid, jnp.where(valid, place, 0)


def block_state(table, tok, tok_count, block):
    branches = tok_count * BR_DEV
    position = block * WINDOW
    alive, opening = jnp.bool_(False), jnp.bool_(False)
    for branch in range(BR_DEV):
        start = table[tok * BR_DEV + branch]
        length = table[branches + tok * BR_DEV + branch]
        alive = alive | ((start <= position) & (position < start + length))
        opening = opening | (start == position)
    has_tail = table[2 * branches + tok * BR_DEV] >= 0
    return alive, opening, jnp.logical_not(opening) | has_tail


def plan_kernel(tok_count, blocks, blocks_here, table, plan_ref):
    tok, head = lax.axis_index("tok"), lax.axis_index("head")
    values = []
    for distance in range(1, LAG + 1):
        values += child_tail(table, tok, distance, tok_count, blocks)
    parent = table[2 * tok_count * BR_DEV + tok * BR_DEV]
    values.append(jnp.where(parent >= 0, tok - jnp.maximum(parent, 0) // BR_DEV, 1))
    for block in range(blocks_here):
        number = tok * blocks + head * blocks_here + block
        values += block_state(table, tok, tok_count, number)
    lane = lax.broadcasted_iota(jnp.int32, plan_ref.shape, 1)
    plan = jnp.zeros(plan_ref.shape, jnp.int32)
    for place, value in enumerate(values):
        plan = jnp.where(lane == place, value.astype(jnp.int32), plan)
    plan_ref[...] = plan


def planned_tail(plan_ref, distance):
    row = plan_ref[0:1, :]
    return row[0, 2 * distance - 2] != 0, row[0, 2 * distance - 1]


def planned_source(plan_ref):
    return plan_ref[0:1, :][0, 2 * LAG]


def planned_block(plan_ref, block):
    row = plan_ref[0:1, :]
    return tuple(row[0, 2 * LAG + 1 + 3 * block + place] for place in range(3))


def take(ref, slot, width):
    if width % 128 == 0:
        return ref[:, pl.ds(pl.multiple_of(slot * width, width), width)]
    value = ref[:, :width]
    for other in range(1, ref.shape[1] // width):
        value = jnp.where(slot == other, ref[:, other * width : (other + 1) * width], value)
    return value


def pack_kernel(sink_hbm, key_hbm, value_hbm, *refs):
    *slot_refs, halo_ref, keys, values, sinks, sems = refs
    copies = [
        pltpu.make_async_copy(source, target, sems.at[place])
        for place, (source, target) in enumerate(
            ((sink_hbm, sinks), (key_hbm, keys), (value_hbm, values))
        )
    ]
    for copy in copies:
        copy.start()
    for copy in copies:
        copy.wait()
    slots, rows = len(slot_refs), keys.shape[0]
    head = lax.axis_index("head")
    width = KV_HEADS * HEAD_DIM // slots
    lane = lax.broadcasted_iota(jnp.int32, (1, 2 * width), 1)
    sink_row = jnp.zeros((1, 2 * width), F32)
    for place in range(sinks.shape[0]):
        sink_row = jnp.where(lane == place, sinks[place], sink_row)
    extra = row_split(sink_row, (EXTRA, 2 * width))
    for step, slot_ref in enumerate(slot_refs):
        slot = lax.rem(head + step, slots)
        slot_ref[:rows] = jnp.concatenate(
            [take(keys, slot, width), take(values, slot, width)], axis=1
        )
        slot_ref[rows:] = extra
    for pair in range(PAIRS):
        lanes = slice(pair * 128, (pair + 1) * 128)
        last = slice(rows - WINDOW, rows)
        halo_ref[pair] = jnp.concatenate([keys[last, lanes], values[last, lanes]], axis=1)


def choose_kernel(plan_ref, *refs):
    slots = len(refs) - LAG - 1
    slot_refs, out_refs, sink_ref = refs[:slots], refs[slots:-1], refs[-1]
    head = lax.axis_index("head")
    rows = slot_refs[0].shape[0] - EXTRA
    blocks_here = rows // WINDOW
    heads = sink_ref.shape[0] // slots
    for distance, out_ref in zip(range(LAG, 0, -1), out_refs):
        _, place = planned_tail(plan_ref, distance)
        begin = pl.multiple_of(place % blocks_here * WINDOW, WINDOW)
        wanted = lax.rem(head - place // blocks_here + slots, slots)
        for step, slot_ref in enumerate(slot_refs):

            @pl.when(wanted == step)
            def _(out_ref=out_ref, slot_ref=slot_ref, begin=begin):
                out_ref[...] = slot_ref[pl.ds(begin, WINDOW), :]

    for step, slot_ref in enumerate(slot_refs):
        source = lax.rem(head - step + slots, slots)
        sink_row = row_join(slot_ref[rows:, :])[:, :128]
        turned = jnp.broadcast_to(sink_row, (128, 128)).T
        sink_ref[pl.ds(pl.multiple_of(source * heads, heads), heads), :] = turned[:heads]


def arrive_kernel(plan_ref, *refs):
    *in_refs, out_ref = refs
    mine = planned_source(plan_ref)
    for distance, in_ref in zip(range(LAG, 0, -1), in_refs):

        @pl.when(mine == distance)
        def _(in_ref=in_ref):
            out_ref[...] = in_ref[...]


def stage_kernel(*refs):
    *arrays, sems = refs
    half = len(arrays) // 2
    copies = [
        pltpu.make_async_copy(source, target, sems.at[place])
        for place, (source, target) in enumerate(zip(arrays[:half], arrays[half:]))
    ]
    for copy in copies:
        copy.start()
    for copy in copies:
        copy.wait()


def attend_kernel(blocks_here, slots, steps, offset, pairs, joins, *refs):
    inputs, refs = refs[:7], refs[7:]
    tail_refs, refs = refs[: len(steps)], refs[len(steps) + joins :]
    outputs, refs = refs[:5], refs[5:]
    dtail_refs, refs = refs[: len(steps)], refs[len(steps) :]
    tails, *scratch = refs
    head = lax.axis_index("head")
    states = [planned_block(inputs[0], block) for block in range(blocks_here)]
    for step, tail_ref in zip(steps, tail_refs):
        tails[lax.rem(head - step + slots, slots)] = tail_ref[...]

    def step(place, carry):
        pair = place // blocks_here
        if offset is not None:
            pair = lax.rem(head + pair + offset, PAIRS)
        block = place % blocks_here
        state = states[0]
        for other in range(1, blocks_here):
            state = [jnp.where(block == other, *two) for two in zip(states[other], state)]
        attend_block(
            blocks_here,
            slots,
            pair,
            block,
            [value != 0 for value in state],
            inputs,
            outputs,
            tails,
            tuple(zip(steps, dtail_refs)),
            scratch,
        )
        return carry

    lax.fori_loop(0, pairs * blocks_here, step, 0)


def attend_block(
    blocks_here, slots, pair, block, state, inputs, outputs, tails, dtails, scratch
):
    _, sink_ref, q_ref, g_ref, k_ref, v_ref, halo_ref = inputs
    o_ref, dq_ref, dk_ref, dv_ref, dhalo_ref = outputs
    tail_sum, sink_rows, prob2, slope2 = scratch
    per_slot = KV_HEADS // slots
    head = lax.axis_index("head")
    alive, opening, prev_ok = state
    here = pl.ds(pl.multiple_of(block * WINDOW, WINDOW), WINDOW)
    before = pl.ds(pl.multiple_of(jnp.maximum(block - 1, 0) * WINDOW, WINDOW), WINDOW)
    first = block == 0
    near = pl.ds(pl.multiple_of(pair * 128, 128), 128)
    big = pl.ds(pl.multiple_of(pair * 1024, 1024), 1024)
    q_ref, g_ref, o_ref, dq_ref = (ref.at[here, big] for ref in (q_ref, g_ref, o_ref, dq_ref))
    k_ref, v_ref, dk_ref, dv_ref = (ref.at[:, near] for ref in (k_ref, v_ref, dk_ref, dv_ref))
    sink_ref = sink_ref.at[pl.ds(pl.multiple_of(pair * 16, 16), 16)]
    dhalo_ref = dhalo_ref.at[pair]

    @pl.when(first)
    def _():
        tail_sum[...] = jnp.zeros_like(tail_sum)
        dhalo_ref[...] = jnp.zeros((WINDOW, 256), BF16)
        sink_rows[...] = jnp.zeros_like(sink_rows)

    @pl.when(jnp.logical_not(alive))
    def _():
        o_ref[...] = jnp.zeros((WINDOW, 1024), BF16)
        dq_ref[...] = jnp.zeros((WINDOW, 1024), BF16)
        dk_ref[here, :] = jnp.zeros((WINDOW, 128), F32)
        dv_ref[here, :] = jnp.zeros((WINDOW, 128), F32)

    @pl.when(alive)
    def _():
        if len(halo_ref.shape) == 2:
            last = halo_ref.shape[0] - EXTRA
            halo = halo_ref[last - WINDOW : last]
        else:
            halo = halo_ref[pair]
        if per_slot == 2:
            tail = tails[pair]
            tail_k, tail_v = tail[:, :128], tail[:, 128:]
        else:
            tail_a, tail_b = tails[2 * pair], tails[2 * pair + 1]
            tail_k = jnp.concatenate([tail_a[:, :64], tail_b[:, :64]], axis=1)
            tail_v = jnp.concatenate([tail_a[:, 64:], tail_b[:, 64:]], axis=1)
        near_k = jnp.where(first, halo[:, :128], k_ref[before, :])
        near_v = jnp.where(first, halo[:, 128:], v_ref[before, :])
        prev_k = jnp.where(opening, tail_k, near_k)
        prev_v = jnp.where(opening, tail_v, near_v)
        own_k, own_v = k_ref[here, :], v_ref[here, :]

        def halves(own, prev):
            return (
                jnp.concatenate([own[:HALF], prev[:HALF], prev[HALF:]], axis=0),
                jnp.concatenate([own[HALF:], prev[HALF:], own[:HALF]], axis=0),
            )

        left = lax.broadcasted_iota(jnp.int32, (1, 128), 1) < HALF
        low16 = left.astype(F32).astype(BF16)
        high16 = BF16(1) - low16

        def padded(seen):
            swapped = jnp.concatenate([seen[:, 64:], seen[:, :64]], axis=1)
            return (
                jnp.concatenate([seen * low16, swapped * high16], axis=0),
                jnp.concatenate([swapped * low16, seen * high16], axis=0),
            )

        seen_k = halves(own_k * BF16(FACTOR), prev_k * BF16(FACTOR))
        seen_v = halves(own_v, prev_v)
        padded_k = tuple(padded(value) for value in seen_k)
        padded_v = tuple(padded(value) for value in seen_v)
        turned_k = tuple(value.T for value in seen_k)
        turned_v = tuple(value.T for value in seen_v)
        bias = jnp.where(prev_ok, 0.0, LOW)
        key_place = lax.broadcasted_iota(jnp.int32, (HALF, 4 * HALF), 0)
        query_place = lax.broadcasted_iota(jnp.int32, (HALF, 4 * HALF), 1) & (HALF - 1)
        own = key_place <= query_place
        own16 = own.astype(F32).astype(BF16)
        turn = (((1,), (1,)), ((), ()))
        items = [(unit, half) for unit in range(2) for half in range(2)]
        seen = 3 * HALF

        def wide(index):
            return slice(index * 256, (index + 1) * 256)

        def feats(index):
            unit = items[index][0]
            return slice(unit * HEAD_DIM, (unit + 1) * HEAD_DIM)

        def corners(unit, half):
            rows = slice(half * HALF, (half + 1) * HALF)
            return [
                (rows, slice(unit * 512 + at * 128, unit * 512 + (at + 1) * 128)) for at in range(4)
            ]

        def stacked(ref, unit, half):
            return jnp.concatenate([ref[corner] for corner in corners(unit, half)], axis=0)

        def products(index):
            unit, half = items[index]
            score, dp = (
                lax.dot_general(
                    padded[half][unit],
                    stacked(ref, unit, half),
                    turn,
                    preferred_element_type=F32,
                )
                for padded, ref in ((padded_k, q_ref), (padded_v, g_ref))
            )
            parts = []
            for base in (0, seen):
                near, far = slice(base, base + HALF), slice(base + HALF, base + 2 * HALF)
                rest = slice(base + 2 * HALF, base + 3 * HALF)
                edge = jnp.where(own, score[near], score[far] + bias)
                whole = score[rest] + bias if half == 0 else score[rest]
                parts.append((edge, whole, jnp.where(own, dp[near], dp[far]), dp[rest]))
            return parts

        def weigh(index, odd, edge, whole, dp_edge, dp_whole):
            unit, half = items[index]
            base = odd * seen
            row = unit * GROUP + odd
            sink = jnp.concatenate(
                [
                    jnp.where(left, sink_ref[at : at + 1], sink_ref[at + 2 : at + 3])
                    for at in (row, row + 4)
                ],
                axis=1,
            )
            peak = jnp.max(jnp.maximum(edge, whole), axis=0, keepdims=True)
            peak = jnp.maximum(peak, sink)
            edge, whole = jnp.exp(edge - peak), jnp.exp(whole - peak)
            sink_weight = jnp.exp(sink - peak)
            inverse = 1.0 / (jnp.sum(edge + whole, axis=0, keepdims=True) + sink_weight)
            edge, whole = edge * inverse, whole * inverse
            term_edge, term_whole = edge * dp_edge, whole * dp_whole
            delta = jnp.sum(term_edge + term_whole, axis=0, keepdims=True)
            for target, at_edge, at_whole in (
                (prob2, edge, whole),
                (slope2, term_edge - edge * delta, term_whole - whole * delta),
            ):
                edge16 = at_edge.astype(BF16)
                edge_own = edge16 * own16
                target[base : base + HALF, wide(index)] = edge_own
                target[base + HALF : base + 2 * HALF, wide(index)] = edge16 - edge_own
                target[base + 2 * HALF : base + seen, wide(index)] = at_whole.astype(BF16)
            sink_term = sink_weight * inverse * delta
            for at, lanes in ((row, slice(0, 128)), (row + 4, slice(128, 256))):
                part = sink_term[:, lanes]
                sink_rows[at : at + 1] += jnp.where(left, part, 0.0)
                sink_rows[at + 2 : at + 3] += jnp.where(left, 0.0, part)

        def finish(index):
            unit, half = items[index]
            for source, across, out_ref in ((prob2, turned_v, o_ref), (slope2, turned_k, dq_ref)):
                out_t = [
                    jnp.dot(
                        across[half][feats(index)],
                        source[base : base + seen, wide(index)],
                        preferred_element_type=F32,
                    ).astype(BF16)
                    for base in (0, seen)
                ]
                out = jnp.concatenate(out_t, axis=0).T
                for at, corner in enumerate(corners(unit, half)):
                    out_ref[corner] = out[at * HALF : (at + 1) * HALF]

        def reduce(index):
            unit, half = items[index]
            parts = []
            for weights, ref in ((slope2, q_ref), (prob2, g_ref)):
                part = jnp.dot(
                    weights[:, wide(index)], stacked(ref, unit, half), preferred_element_type=F32
                )
                parts.append(jnp.where(left, part[:seen], part[seen:]))
            return parts

        def join(first_half, second_half):
            total = jnp.concatenate(
                [
                    first_half[:HALF] + second_half[2 * HALF :],
                    second_half[:HALF],
                    first_half[HALF : 2 * HALF],
                    first_half[2 * HALF :] + second_half[HALF : 2 * HALF],
                ],
                axis=0,
            )
            return total + pltpu.roll(total, HEAD_DIM, 1)

        ahead, parts = products(0), []
        for index in range(len(items)):
            now = ahead
            weigh(index, 0, *now[0])
            if index + 1 < len(items):
                ahead = products(index + 1)
            weigh(index, 1, *now[1])
            if index >= 1:
                finish(index - 1)
            parts.append(reduce(index))
        finish(len(items) - 1)
        grads = [
            [join(parts[2 * unit][place], parts[2 * unit + 1][place]) for place in range(2)]
            for unit in range(2)
        ]
        dk = jnp.where(left, grads[0][0], grads[1][0]) * FACTOR
        dv = jnp.where(left, grads[0][1], grads[1][1])
        dk_ref[here, :] = dk[:WINDOW]
        dv_ref[here, :] = dv[:WINDOW]

        @pl.when(opening & prev_ok)
        def _():
            tail_sum[:, :128] += dk[WINDOW:]
            tail_sum[:, 128:] += dv[WINDOW:]

        @pl.when(jnp.logical_not(opening) & first)
        def _():
            dhalo_ref[:, :128] = dk[WINDOW:].astype(BF16)
            dhalo_ref[:, 128:] = dv[WINDOW:].astype(BF16)

        @pl.when(jnp.logical_not(opening) & jnp.logical_not(first))
        def _():
            dk_ref[before, :] += dk[WINDOW:]
            dv_ref[before, :] += dv[WINDOW:]

    @pl.when(block == blocks_here - 1)
    def _():
        width = 2 * per_slot * HEAD_DIM
        heads = per_slot * GROUP
        total = tail_sum[...].astype(BF16)
        for part in range(2 // per_slot):
            feats = slice(part * width // 2, (part + 1) * width // 2)
            tail = jnp.concatenate([total[:, :128][:, feats], total[:, 128:][:, feats]], axis=1)
            rows = sink_rows[part * heads : (part + 1) * heads]
            rows = jnp.concatenate([rows, jnp.zeros((128 - heads, WINDOW), F32)], axis=0)
            sink_row = jnp.sum(rows.T, axis=0, keepdims=True)
            if width > 128:
                sink_row = jnp.concatenate([sink_row, jnp.zeros((1, width - 128), F32)], axis=1)
            extra = row_split(sink_row, (EXTRA, width))
            wanted = lax.rem(pair * (2 // per_slot) + part - head + slots, slots)
            for step, dtail_ref in dtails:

                @pl.when(wanted == step)
                def _(dtail_ref=dtail_ref, tail=tail, extra=extra):
                    dtail_ref[:WINDOW] = tail
                    dtail_ref[WINDOW:] = extra


def gather_kernel(*refs):
    *in_refs, out_ref = refs
    total, sink_row = 0.0, 0.0
    for in_ref in in_refs:
        total = total + in_ref[:WINDOW].astype(F32)
        sink_row = sink_row + row_join(in_ref[WINDOW:])
    out_ref[:WINDOW] = total.astype(BF16)
    out_ref[WINDOW:] = row_split(sink_row, (EXTRA, out_ref.shape[1]))


def land_kernel(blocks, plan_ref, here_ref, *refs):
    head = lax.axis_index("head")
    in_refs, out_refs, sink_ref = refs[:LAG], refs[LAG:-1], refs[-1]
    slots = len(out_refs)
    blocks_here = blocks // slots
    for out_ref in out_refs:
        out_ref[...] = jnp.zeros_like(out_ref)
    sink_row = row_join(here_ref[WINDOW:])
    for distance, in_ref in enumerate(in_refs, 1):
        valid, place = planned_tail(plan_ref, distance)
        sink_row = sink_row + row_join(in_ref[WINDOW:])
        wanted = lax.rem(place // blocks_here - head + slots, slots)
        here = pl.ds(pl.multiple_of(place % blocks_here * WINDOW, WINDOW), WINDOW)
        for step, out_ref in enumerate(out_refs):

            @pl.when(valid & (wanted == step))
            def _(out_ref=out_ref, in_ref=in_ref, here=here):
                total = out_ref[here, :].astype(F32) + in_ref[:WINDOW].astype(F32)
                out_ref[here, :] = total.astype(BF16)

    sink_ref[...] = jnp.broadcast_to(sink_row[:, :128], sink_ref.shape)


def total_kernel(dk_ref, dv_ref, halo_ref, sink_ref, far_ref, *refs):
    *tail_refs, key_ref, value_ref, sink_grad, tails = refs
    slots, rows = len(tail_refs), dk_ref.shape[0]
    width = tails.shape[2] // 2
    head = lax.axis_index("head")
    for step, tail_ref in enumerate(tail_refs):
        tails[lax.rem(head - step + slots, slots)] = tail_ref[...]
    halo_k = jnp.concatenate([halo_ref[pair][:, :128] for pair in range(PAIRS)], axis=1)
    halo_v = jnp.concatenate([halo_ref[pair][:, 128:] for pair in range(PAIRS)], axis=1)
    for in_ref, halo, at, out_ref in (
        (dk_ref, halo_k, 0, key_ref),
        (dv_ref, halo_v, width, value_ref),
    ):
        for begin in range(0, rows, WINDOW):
            here = slice(begin, begin + WINDOW)
            parts = [tails[slot, here, at : at + width] for slot in range(slots)]
            total = in_ref[here, :] + jnp.concatenate(parts, axis=1).astype(F32)
            if begin == rows - WINDOW:
                total = total + halo.astype(F32)
            out_ref[here, :] = total.astype(BF16)
    sink_row = -(sink_ref[0:1] + far_ref[0:1])
    for place in range(sink_grad.shape[0]):
        sink_grad[place] = sink_row[0, place]


def swap(values, axis):
    return [values[0]] + [ring(values[step], axis, step) for step in range(1, len(values))]


def local(
    queries, key_states, value_states, out_grad, sink_logits, branch_start, branch_len, parent_list
):
    tok_count, head_count = lax.axis_size("tok"), lax.axis_size("head")
    rows = queries.shape[0]
    blocks_here = rows // WINDOW
    blocks = blocks_here * head_count
    per_slot = KV_HEADS // head_count
    width = 2 * per_slot * HEAD_DIM

    def shape(dims, kind=BF16):
        return jax.ShapeDtypeStruct(dims, kind)

    def far(value):
        return pltpu.with_memory_space_constraint(value, pltpu.HBM)

    def close(value):
        return pltpu.with_memory_space_constraint(value, pltpu.VMEM)

    table = jnp.concatenate([branch_start, branch_len, parent_list[:, 0], parent_list[:, 1]])
    *slots, halo_out, keys, values = pl.pallas_call(
        pack_kernel,
        out_shape=(shape((rows + EXTRA, width)),) * head_count
        + (shape((PAIRS, WINDOW, 256)),)
        + (pltpu.VMEM(key_states.shape, BF16),) * 2,
        in_specs=[HBM] * 3,
        out_specs=(VMEM,) * (head_count + 3),
        scratch_shapes=[
            pltpu.SMEM(sink_logits.shape, F32),
            pltpu.SemaphoreType.DMA((3,)),
        ],
        compiler_params=PARAMS,
        name="pack",
    )(far(sink_logits), far(key_states), far(value_states))
    spread = swap(slots, "head")
    halo = shift(halo_out, "head", 1)
    plan = pl.pallas_call(
        functools.partial(plan_kernel, tok_count, blocks, blocks_here),
        out_shape=pltpu.VMEM((8, 128), jnp.int32),
        in_specs=[SMEM],
        out_specs=VMEM,
        compiler_params=PARAMS,
        name="plan",
    )(table)
    plan = close(plan)
    *chosen, sinks = pl.pallas_call(
        choose_kernel,
        out_shape=(shape((WINDOW, width)),) * LAG + (shape((KV_HEADS * GROUP, 128), F32),),
        in_specs=[VMEM] * (1 + head_count),
        out_specs=(VMEM,) * (LAG + 1),
        compiler_params=PARAMS,
        name="choose",
    )(plan, *spread)
    arrived = [ring(chosen[LAG - s], "tok", s) for s in range(LAG, 0, -1)]
    queries, out_grad, _ = lax.optimization_barrier((queries, out_grad, sinks))
    near_queries, near_grad = pl.pallas_call(
        stage_kernel,
        out_shape=(pltpu.VMEM(queries.shape, BF16),) * 2,
        in_specs=[HBM] * 2,
        out_specs=(VMEM,) * 2,
        scratch_shapes=[pltpu.SemaphoreType.DMA((2,))],
        compiler_params=PARAMS,
        name="stage",
    )(far(queries), far(out_grad))
    *arrived, near_queries, near_grad = lax.optimization_barrier(
        (*arrived, near_queries, near_grad)
    )
    quarter = pl.pallas_call(
        arrive_kernel,
        out_shape=shape((WINDOW, width)),
        in_specs=[VMEM] * (1 + LAG),
        out_specs=VMEM,
        compiler_params=PARAMS,
        name="arrive",
    )(plan, *arrived)
    tails = swap([quarter] * head_count, "head")

    def attend(steps, pairs, offset, halo, joined):
        inputs = (
            sinks,
            close(near_queries),
            close(near_grad),
            close(keys),
            close(values),
            halo,
            *(tails[step] for step in steps),
            *(close(value) for value in joined),
        )
        base = 1 + len(inputs) - len(joined)
        return pl.pallas_call(
            functools.partial(
                attend_kernel,
                blocks_here,
                head_count,
                steps,
                offset,
                pairs,
                len(joined),
            ),
            out_shape=(
                pltpu.VMEM(queries.shape, BF16),
                pltpu.VMEM(queries.shape, BF16),
                pltpu.VMEM(key_states.shape, F32),
                pltpu.VMEM(key_states.shape, F32),
                pltpu.VMEM((PAIRS, WINDOW, 256), BF16),
            )
            + (shape((WINDOW + EXTRA, width)),) * len(steps),
            in_specs=[VMEM] * (1 + len(inputs)),
            out_specs=(VMEM,) * (5 + len(steps)),
            scratch_shapes=[
                pltpu.VMEM((head_count, WINDOW, width), BF16),
                pltpu.VMEM((WINDOW, 256), F32),
                pltpu.VMEM((2 * GROUP, WINDOW), F32),
                pltpu.VMEM((6 * HALF, 1024), BF16),
                pltpu.VMEM((6 * HALF, 1024), BF16),
            ],
            input_output_aliases={base + place: place for place in range(len(joined))},
            compiler_params=PARAMS,
            name="attend",
        )(plan, *inputs)

    if per_slot == 2:
        *joined, own_tail = attend((0,), 1, 0, spread[1], ())
        *results, tail_1, tail_2, tail_3 = attend((1, 2, 3), PAIRS - 1, 1, halo, joined)
        dtail = [own_tail, tail_1, tail_2, tail_3]
    else:
        results = attend(tuple(range(head_count)), PAIRS, None, halo, ())
        results, dtail = results[:5], list(results[5:])
    attended, query_grad, dk, dv, dhalo = results
    parts = swap(dtail, "head")
    quarter_grad = pl.pallas_call(
        gather_kernel,
        out_shape=shape((WINDOW + EXTRA, width)),
        in_specs=[VMEM] * head_count,
        out_specs=VMEM,
        compiler_params=PARAMS,
        name="gather",
    )(*parts)
    def flush(value):
        return pl.pallas_call(
            stage_kernel,
            out_shape=pltpu.HBM(value.shape, BF16),
            in_specs=[VMEM],
            out_specs=HBM,
            scratch_shapes=[pltpu.SemaphoreType.DMA((1,))],
            compiler_params=PARAMS,
            name="flush",
        )(close(value))

    returned = [ring(quarter_grad, "tok", -s) for s in range(LAG, 0, -1)][::-1]
    attended, _ = lax.optimization_barrier((attended, quarter_grad))
    attended = flush(attended)
    attended, *returned = lax.optimization_barrier((attended, *returned))
    halo_back = shift(dhalo, "head", -1)
    *landed, sink_near = pl.pallas_call(
        functools.partial(land_kernel, blocks),
        out_shape=(shape((rows, width)),) * head_count + (shape((8, 128), F32),),
        in_specs=[VMEM] * (LAG + 2),
        out_specs=(VMEM,) * (head_count + 1),
        compiler_params=PARAMS,
        name="land",
    )(plan, quarter_grad, *returned)
    tails_back = swap(landed, "head")
    query_grad, _ = lax.optimization_barrier((query_grad, sink_near))
    query_grad = flush(query_grad)
    span = LAG + 1
    while 2 * span < tok_count:
        sink_near = sink_near + ring(sink_near, "tok", -span)
        span *= 2
    sink_far = ring(sink_near, "tok", -span)
    key_grad, value_grad, sink_grad = pl.pallas_call(
        total_kernel,
        out_shape=(
            shape(key_states.shape),
            shape(value_states.shape),
            shape(sink_logits.shape, F32),
        ),
        in_specs=[VMEM] * (5 + head_count),
        out_specs=(VMEM, VMEM, SMEM),
        scratch_shapes=[pltpu.VMEM((head_count, rows, width), BF16)],
        compiler_params=PARAMS,
        name="total",
    )(dk, dv, halo_back, sink_near, sink_far, *tails_back)
    return attended, query_grad, key_grad, value_grad, sink_grad


def solution(mesh):
    rows = P(("tok", "head"), None)
    return jax.shard_map(
        local,
        mesh=mesh,
        in_specs=(rows, rows, rows, rows, P("head"), P(), P(), P()),
        out_specs=(rows, rows, rows, rows, P("head")),
        check_vma=False,
    )
```

```python
import functools

import jax
import jax.numpy as jnp
from jax import lax
from jax.experimental import pallas as pl
from jax.experimental.pallas import tpu as pltpu
from jax.sharding import PartitionSpec as P

HEAD_DIM = 64
KV_HEADS = 8
GROUP = 8
WINDOW = 128
HALF = WINDOW // 2
LAG = 3
BR_DEV = 2
PAIRS = KV_HEADS // 2
FACTOR = 0.125
LOW = -1e30
BF16 = jnp.bfloat16
F32 = jnp.float32

SMEM = pl.BlockSpec(memory_space=pltpu.SMEM)
VMEM = pl.BlockSpec(memory_space=pltpu.VMEM)
HBM = pl.BlockSpec(memory_space=pltpu.HBM)
PARAMS = pltpu.CompilerParams(vmem_limit_bytes=24 * 1024 * 1024)


def shift(value, axis, steps):
    count = lax.axis_size(axis)
    leading, last = (max(0, -steps), min(count, count - steps))
    return lax.ppermute(value, axis, [(source, source + steps) for source in range(leading, last)])


def ring(value, axis, steps):
    count = lax.axis_size(axis)
    return lax.ppermute(value, axis, [(source, (source + steps) % count) for source in range(count)])


def with_row(tile, row):
    high = row.astype(BF16).astype(F32)
    middle = (row - high).astype(BF16).astype(F32)
    low = row - high - middle
    packed = high + pltpu.roll(middle, 32, 1) + pltpu.roll(low, 64, 1)
    place = lax.broadcasted_iota(jnp.int32, (16, 128), 0)
    top = jnp.where(place == 0, packed, tile[:16, :128].astype(F32)).astype(BF16)
    if tile.shape[1] > 128:
        top = jnp.concatenate([top, tile[:16, 128:]], axis=1)
    return jnp.concatenate([top, tile[16:]], axis=0)


def row_join(top):
    packed = top[0:1, :128].astype(F32)
    row = packed + pltpu.roll(packed, 96, 1) + pltpu.roll(packed, 64, 1)
    return jnp.where(lax.broadcasted_iota(jnp.int32, (1, 128), 1) < 32, row, 0.0)


def child_tail(table, tok, distance, tok_count, blocks):
    branches = tok_count * BR_DEV
    child = jnp.minimum(tok + distance, tok_count - 1) * BR_DEV
    parent = table[2 * branches + child]
    safe = jnp.maximum(parent, 0)
    valid = (tok + distance < tok_count) & (parent >= 0) & (safe // BR_DEV == tok)
    place = (table[safe] + table[3 * branches + child]) // WINDOW - tok * blocks
    return valid, jnp.where(valid, place, 0)


def block_state(table, tok, tok_count, block):
    branches = tok_count * BR_DEV
    position = block * WINDOW
    alive, opening = jnp.bool_(False), jnp.bool_(False)
    for branch in range(BR_DEV):
        start = table[tok * BR_DEV + branch]
        length = table[branches + tok * BR_DEV + branch]
        alive = alive | ((start <= position) & (position < start + length))
        opening = opening | (start == position)
    has_tail = table[2 * branches + tok * BR_DEV] >= 0
    return alive, opening, jnp.logical_not(opening) | has_tail


def plan_kernel(tok_count, blocks, blocks_here, table, plan_ref):
    tok, head = lax.axis_index("tok"), lax.axis_index("head")
    values = []
    for distance in range(1, LAG + 1):
        values += child_tail(table, tok, distance, tok_count, blocks)
    parent = table[2 * tok_count * BR_DEV + tok * BR_DEV]
    values.append(jnp.where(parent >= 0, tok - jnp.maximum(parent, 0) // BR_DEV, 1))
    for block in range(blocks_here):
        number = tok * blocks + head * blocks_here + block
        values += block_state(table, tok, tok_count, number)
    lane = lax.broadcasted_iota(jnp.int32, plan_ref.shape, 1)
    plan = jnp.zeros(plan_ref.shape, jnp.int32)
    for place, value in enumerate(values):
        plan = jnp.where(lane == place, value.astype(jnp.int32), plan)
    plan_ref[...] = plan


def planned_tail(plan_ref, distance):
    row = plan_ref[0:1, :]
    return row[0, 2 * distance - 2] != 0, row[0, 2 * distance - 1]


def planned_source(plan_ref):
    return plan_ref[0:1, :][0, 2 * LAG]


def planned_block(plan_ref, block):
    row = plan_ref[0:1, :]
    return tuple(row[0, 2 * LAG + 1 + 3 * block + place] for place in range(3))


def take(ref, slot, width):
    if width % 128 == 0:
        return ref[:, pl.ds(pl.multiple_of(slot * width, width), width)]
    value = ref[:, :width]
    for other in range(1, ref.shape[1] // width):
        value = jnp.where(slot == other, ref[:, other * width : (other + 1) * width], value)
    return value


def pack_kernel(sink_hbm, key_hbm, value_hbm, *refs):
    *slot_refs, halo_ref, keys, values, sinks, sems = refs
    copies = [
        pltpu.make_async_copy(source, target, sems.at[place])
        for place, (source, target) in enumerate(
            ((sink_hbm, sinks), (key_hbm, keys), (value_hbm, values))
        )
    ]
    for copy in copies:
        copy.start()
    for copy in copies:
        copy.wait()
    slots, rows = len(slot_refs), keys.shape[0]
    head = lax.axis_index("head")
    width = KV_HEADS * HEAD_DIM // slots
    lane = lax.broadcasted_iota(jnp.int32, (1, 128), 1)
    sink_row = jnp.zeros((1, 128), F32)
    for place in range(sinks.shape[0]):
        sink_row = jnp.where(lane == place, sinks[place], sink_row)
    for step, slot_ref in enumerate(slot_refs):
        slot = lax.rem(head + step, slots)
        both = jnp.concatenate([take(keys, slot, width), take(values, slot, width)], axis=1)
        slot_ref[...] = with_row(both, sink_row)
    for pair in range(PAIRS):
        lanes = slice(pair * 128, (pair + 1) * 128)
        last = slice(rows - WINDOW, rows)
        halo_ref[pair] = jnp.concatenate([keys[last, lanes], values[last, lanes]], axis=1)


def choose_kernel(plan_ref, *refs):
    slots = len(refs) - LAG - 1
    slot_refs, out_refs, sink_ref = refs[:slots], refs[slots:-1], refs[-1]
    head = lax.axis_index("head")
    rows = slot_refs[0].shape[0]
    blocks_here = rows // WINDOW
    heads = sink_ref.shape[0] // slots
    for distance, out_ref in zip(range(LAG, 0, -1), out_refs):
        _, place = planned_tail(plan_ref, distance)
        begin = pl.multiple_of(place % blocks_here * WINDOW, WINDOW)
        wanted = lax.rem(head - place // blocks_here + slots, slots)
        for step, slot_ref in enumerate(slot_refs):

            @pl.when(wanted == step)
            def _(out_ref=out_ref, slot_ref=slot_ref, begin=begin):
                out_ref[...] = slot_ref[pl.ds(begin, WINDOW), :]

    for step, slot_ref in enumerate(slot_refs):
        source = lax.rem(head - step + slots, slots)
        sink_row = row_join(slot_ref[:16])
        turned = jnp.broadcast_to(sink_row, (128, 128)).T
        sink_ref[pl.ds(pl.multiple_of(source * heads, heads), heads), :] = turned[:heads]


def arrive_kernel(plan_ref, *refs):
    *in_refs, out_ref = refs
    mine = planned_source(plan_ref)
    for distance, in_ref in zip(range(LAG, 0, -1), in_refs):

        @pl.when(mine == distance)
        def _(in_ref=in_ref):
            out_ref[...] = in_ref[...]


def stage_kernel(*refs):
    *arrays, sems = refs
    half = len(arrays) // 2
    copies = [
        pltpu.make_async_copy(source, target, sems.at[place])
        for place, (source, target) in enumerate(zip(arrays[:half], arrays[half:]))
    ]
    for copy in copies:
        copy.start()
    for copy in copies:
        copy.wait()


def attend_kernel(blocks_here, slots, steps, offset, pairs, joins, *refs):
    inputs, refs = refs[:7], refs[7:]
    tail_refs, refs = refs[: len(steps)], refs[len(steps) + joins :]
    outputs, refs = refs[:5], refs[5:]
    dtail_refs, refs = refs[: len(steps)], refs[len(steps) :]
    tails, *scratch = refs
    head = lax.axis_index("head")
    states = [planned_block(inputs[0], block) for block in range(blocks_here)]
    for step, tail_ref in zip(steps, tail_refs):
        tails[lax.rem(head - step + slots, slots)] = tail_ref[...]

    def step(place, carry):
        pair = place // blocks_here
        if offset is not None:
            pair = lax.rem(head + pair + offset, PAIRS)
        block = place % blocks_here
        state = states[0]
        for other in range(1, blocks_here):
            state = [jnp.where(block == other, *two) for two in zip(states[other], state)]
        attend_block(
            blocks_here,
            slots,
            pair,
            block,
            [value != 0 for value in state],
            inputs,
            outputs,
            tails,
            tuple(zip(steps, dtail_refs)),
            scratch,
        )
        return carry

    lax.fori_loop(0, pairs * blocks_here, step, 0)


def attend_block(
    blocks_here, slots, pair, block, state, inputs, outputs, tails, dtails, scratch
):
    _, sink_ref, q_ref, g_ref, k_ref, v_ref, halo_ref = inputs
    o_ref, dq_ref, dk_ref, dv_ref, dhalo_ref = outputs
    tail_sum, sink_rows, prob2, slope2 = scratch
    per_slot = KV_HEADS // slots
    head = lax.axis_index("head")
    alive, opening, prev_ok = state
    here = pl.ds(pl.multiple_of(block * WINDOW, WINDOW), WINDOW)
    before = pl.ds(pl.multiple_of(jnp.maximum(block - 1, 0) * WINDOW, WINDOW), WINDOW)
    first = block == 0
    near = pl.ds(pl.multiple_of(pair * 128, 128), 128)
    big = pl.ds(pl.multiple_of(pair * 1024, 1024), 1024)
    q_ref, g_ref, o_ref, dq_ref = (ref.at[here, big] for ref in (q_ref, g_ref, o_ref, dq_ref))
    k_ref, v_ref, dk_ref, dv_ref = (ref.at[:, near] for ref in (k_ref, v_ref, dk_ref, dv_ref))
    sink_ref = sink_ref.at[pl.ds(pl.multiple_of(pair * 16, 16), 16)]
    dhalo_ref = dhalo_ref.at[pair]

    @pl.when(first)
    def _():
        tail_sum[...] = jnp.zeros_like(tail_sum)
        dhalo_ref[...] = jnp.zeros((WINDOW, 256), BF16)
        sink_rows[...] = jnp.zeros_like(sink_rows)

    @pl.when(jnp.logical_not(alive))
    def _():
        o_ref[...] = jnp.zeros((WINDOW, 1024), BF16)
        dq_ref[...] = jnp.zeros((WINDOW, 1024), BF16)
        dk_ref[here, :] = jnp.zeros((WINDOW, 128), F32)
        dv_ref[here, :] = jnp.zeros((WINDOW, 128), F32)

    @pl.when(alive)
    def _():
        if len(halo_ref.shape) == 2:
            halo = halo_ref[halo_ref.shape[0] - WINDOW :]
        else:
            halo = halo_ref[pair]
        if per_slot == 2:
            tail = tails[pair]
            tail_k, tail_v = tail[:, :128], tail[:, 128:]
        else:
            tail_a, tail_b = tails[2 * pair], tails[2 * pair + 1]
            tail_k = jnp.concatenate([tail_a[:, :64], tail_b[:, :64]], axis=1)
            tail_v = jnp.concatenate([tail_a[:, 64:], tail_b[:, 64:]], axis=1)
        near_k = jnp.where(first, halo[:, :128], k_ref[before, :])
        near_v = jnp.where(first, halo[:, 128:], v_ref[before, :])
        prev_k = jnp.where(opening, tail_k, near_k)
        prev_v = jnp.where(opening, tail_v, near_v)
        own_k, own_v = k_ref[here, :], v_ref[here, :]

        def halves(own, prev):
            return (
                jnp.concatenate([own[:HALF], prev[:HALF], prev[HALF:]], axis=0),
                jnp.concatenate([own[HALF:], prev[HALF:], own[:HALF]], axis=0),
            )

        left = lax.broadcasted_iota(jnp.int32, (1, 128), 1) < HALF
        low16 = left.astype(F32).astype(BF16)
        high16 = BF16(1) - low16

        def padded(seen):
            swapped = jnp.concatenate([seen[:, 64:], seen[:, :64]], axis=1)
            return (
                jnp.concatenate([seen * low16, swapped * high16], axis=0),
                jnp.concatenate([swapped * low16, seen * high16], axis=0),
            )

        seen_k = halves(own_k * BF16(FACTOR), prev_k * BF16(FACTOR))
        seen_v = halves(own_v, prev_v)
        padded_k = tuple(padded(value) for value in seen_k)
        padded_v = tuple(padded(value) for value in seen_v)
        turned_k = tuple(value.T for value in seen_k)
        turned_v = tuple(value.T for value in seen_v)
        bias = jnp.where(prev_ok, 0.0, LOW)
        key_place = lax.broadcasted_iota(jnp.int32, (HALF, 4 * HALF), 0)
        query_place = lax.broadcasted_iota(jnp.int32, (HALF, 4 * HALF), 1) & (HALF - 1)
        own = key_place <= query_place
        own16 = own.astype(F32).astype(BF16)
        turn = (((1,), (1,)), ((), ()))
        items = [(unit, half) for unit in range(2) for half in range(2)]
        seen = 3 * HALF

        def wide(index):
            return slice(index * 256, (index + 1) * 256)

        def feats(index):
            unit = items[index][0]
            return slice(unit * HEAD_DIM, (unit + 1) * HEAD_DIM)

        def corners(unit, half):
            rows = slice(half * HALF, (half + 1) * HALF)
            return [
                (rows, slice(unit * 512 + at * 128, unit * 512 + (at + 1) * 128)) for at in range(4)
            ]

        def stacked(ref, unit, half):
            return jnp.concatenate([ref[corner] for corner in corners(unit, half)], axis=0)

        def products(index):
            unit, half = items[index]
            score, dp = (
                lax.dot_general(
                    padded[half][unit],
                    stacked(ref, unit, half),
                    turn,
                    preferred_element_type=F32,
                )
                for padded, ref in ((padded_k, q_ref), (padded_v, g_ref))
            )
            parts = []
            for base in (0, seen):
                near, far = slice(base, base + HALF), slice(base + HALF, base + 2 * HALF)
                rest = slice(base + 2 * HALF, base + 3 * HALF)
                edge = jnp.where(own, score[near], score[far] + bias)
                whole = score[rest] + bias if half == 0 else score[rest]
                parts.append((edge, whole, jnp.where(own, dp[near], dp[far]), dp[rest]))
            return parts

        def weigh(index, odd, edge, whole, dp_edge, dp_whole):
            unit, half = items[index]
            base = odd * seen
            row = unit * GROUP + odd
            sink = jnp.concatenate(
                [
                    jnp.where(left, sink_ref[at : at + 1], sink_ref[at + 2 : at + 3])
                    for at in (row, row + 4)
                ],
                axis=1,
            )
            peak = jnp.max(jnp.maximum(edge, whole), axis=0, keepdims=True)
            peak = jnp.maximum(peak, sink)
            edge, whole = jnp.exp(edge - peak), jnp.exp(whole - peak)
            sink_weight = jnp.exp(sink - peak)
            inverse = 1.0 / (jnp.sum(edge + whole, axis=0, keepdims=True) + sink_weight)
            edge, whole = edge * inverse, whole * inverse
            term_edge, term_whole = edge * dp_edge, whole * dp_whole
            delta = jnp.sum(term_edge + term_whole, axis=0, keepdims=True)
            for target, at_edge, at_whole in (
                (prob2, edge, whole),
                (slope2, term_edge - edge * delta, term_whole - whole * delta),
            ):
                edge16 = at_edge.astype(BF16)
                edge_own = edge16 * own16
                target[base : base + HALF, wide(index)] = edge_own
                target[base + HALF : base + 2 * HALF, wide(index)] = edge16 - edge_own
                target[base + 2 * HALF : base + seen, wide(index)] = at_whole.astype(BF16)
            sink_term = sink_weight * inverse * delta
            for at, lanes in ((row, slice(0, 128)), (row + 4, slice(128, 256))):
                part = sink_term[:, lanes]
                sink_rows[at : at + 1] += jnp.where(left, part, 0.0)
                sink_rows[at + 2 : at + 3] += jnp.where(left, 0.0, part)

        def finish(index):
            unit, half = items[index]
            for source, across, out_ref in ((prob2, turned_v, o_ref), (slope2, turned_k, dq_ref)):
                out_t = [
                    jnp.dot(
                        across[half][feats(index)],
                        source[base : base + seen, wide(index)],
                        preferred_element_type=F32,
                    ).astype(BF16)
                    for base in (0, seen)
                ]
                out = jnp.concatenate(out_t, axis=0).T
                for at, corner in enumerate(corners(unit, half)):
                    out_ref[corner] = out[at * HALF : (at + 1) * HALF]

        def reduce(index):
            unit, half = items[index]
            parts = []
            for weights, ref in ((slope2, q_ref), (prob2, g_ref)):
                part = jnp.dot(
                    weights[:, wide(index)], stacked(ref, unit, half), preferred_element_type=F32
                )
                parts.append(jnp.where(left, part[:seen], part[seen:]))
            return parts

        def join(first_half, second_half):
            total = jnp.concatenate(
                [
                    first_half[:HALF] + second_half[2 * HALF :],
                    second_half[:HALF],
                    first_half[HALF : 2 * HALF],
                    first_half[2 * HALF :] + second_half[HALF : 2 * HALF],
                ],
                axis=0,
            )
            return total + pltpu.roll(total, HEAD_DIM, 1)

        ahead, parts = products(0), []
        for index in range(len(items)):
            now = ahead
            weigh(index, 0, *now[0])
            if index + 1 < len(items):
                ahead = products(index + 1)
            weigh(index, 1, *now[1])
            if index >= 1:
                finish(index - 1)
            parts.append(reduce(index))
        finish(len(items) - 1)
        grads = [
            [join(parts[2 * unit][place], parts[2 * unit + 1][place]) for place in range(2)]
            for unit in range(2)
        ]
        dk = jnp.where(left, grads[0][0], grads[1][0]) * FACTOR
        dv = jnp.where(left, grads[0][1], grads[1][1])
        dk_ref[here, :] = dk[:WINDOW]
        dv_ref[here, :] = dv[:WINDOW]

        @pl.when(opening & prev_ok)
        def _():
            tail_sum[:, :128] += dk[WINDOW:]
            tail_sum[:, 128:] += dv[WINDOW:]

        @pl.when(jnp.logical_not(opening) & first)
        def _():
            dhalo_ref[:, :128] = dk[WINDOW:].astype(BF16)
            dhalo_ref[:, 128:] = dv[WINDOW:].astype(BF16)

        @pl.when(jnp.logical_not(opening) & jnp.logical_not(first))
        def _():
            dk_ref[before, :] += dk[WINDOW:]
            dv_ref[before, :] += dv[WINDOW:]

    @pl.when(block == blocks_here - 1)
    def _():
        width = 2 * per_slot * HEAD_DIM
        heads = per_slot * GROUP
        total = tail_sum[...].astype(BF16)
        for part in range(2 // per_slot):
            feats = slice(part * width // 2, (part + 1) * width // 2)
            tail = jnp.concatenate([total[:, :128][:, feats], total[:, 128:][:, feats]], axis=1)
            rows = sink_rows[part * heads : (part + 1) * heads]
            rows = jnp.concatenate([rows, jnp.zeros((128 - heads, WINDOW), F32)], axis=0)
            sink_row = jnp.sum(rows.T, axis=0, keepdims=True)
            tail = with_row(tail, sink_row)
            wanted = lax.rem(pair * (2 // per_slot) + part - head + slots, slots)
            for step, dtail_ref in dtails:

                @pl.when(wanted == step)
                def _(dtail_ref=dtail_ref, tail=tail):
                    dtail_ref[...] = tail


def gather_kernel(*refs):
    *in_refs, out_ref = refs
    total, sink_row = 0.0, 0.0
    for in_ref in in_refs:
        total = total + in_ref[...].astype(F32)
        sink_row = sink_row + row_join(in_ref[:16])
    out_ref[...] = with_row(total.astype(BF16), sink_row)


def land_kernel(blocks, plan_ref, here_ref, *refs):
    head = lax.axis_index("head")
    in_refs, out_refs, sink_ref = refs[:LAG], refs[LAG:-1], refs[-1]
    slots = len(out_refs)
    blocks_here = blocks // slots
    for out_ref in out_refs:
        out_ref[...] = jnp.zeros_like(out_ref)
    sink_row = row_join(here_ref[:16])
    seen = lax.broadcasted_iota(jnp.int32, here_ref.shape, 0) > 0
    for distance, in_ref in enumerate(in_refs, 1):
        valid, place = planned_tail(plan_ref, distance)
        sink_row = sink_row + row_join(in_ref[:16])
        wanted = lax.rem(place // blocks_here - head + slots, slots)
        here = pl.ds(pl.multiple_of(place % blocks_here * WINDOW, WINDOW), WINDOW)
        for step, out_ref in enumerate(out_refs):

            @pl.when(valid & (wanted == step))
            def _(out_ref=out_ref, in_ref=in_ref, here=here):
                total = out_ref[here, :].astype(F32) + in_ref[...].astype(F32)
                out_ref[here, :] = jnp.where(seen, total, 0.0).astype(BF16)

    sink_ref[...] = jnp.broadcast_to(sink_row, sink_ref.shape)


def total_kernel(dk_ref, dv_ref, halo_ref, sink_ref, far_ref, *refs):
    *tail_refs, key_ref, value_ref, sink_grad, tails = refs
    slots, rows = len(tail_refs), dk_ref.shape[0]
    width = tails.shape[2] // 2
    head = lax.axis_index("head")
    for step, tail_ref in enumerate(tail_refs):
        tails[lax.rem(head - step + slots, slots)] = tail_ref[...]
    halo_k = jnp.concatenate([halo_ref[pair][:, :128] for pair in range(PAIRS)], axis=1)
    halo_v = jnp.concatenate([halo_ref[pair][:, 128:] for pair in range(PAIRS)], axis=1)
    for in_ref, halo, at, out_ref in (
        (dk_ref, halo_k, 0, key_ref),
        (dv_ref, halo_v, width, value_ref),
    ):
        for begin in range(0, rows, WINDOW):
            here = slice(begin, begin + WINDOW)
            parts = [tails[slot, here, at : at + width] for slot in range(slots)]
            total = in_ref[here, :] + jnp.concatenate(parts, axis=1).astype(F32)
            if begin == rows - WINDOW:
                total = total + halo.astype(F32)
            out_ref[here, :] = total.astype(BF16)
    sink_row = -(sink_ref[0:1] + far_ref[0:1])
    for place in range(sink_grad.shape[0]):
        sink_grad[place] = sink_row[0, place]


def swap(values, axis):
    return [values[0]] + [ring(values[step], axis, step) for step in range(1, len(values))]


def local(
    queries, key_states, value_states, out_grad, sink_logits, branch_start, branch_len, parent_list
):
    tok_count, head_count = lax.axis_size("tok"), lax.axis_size("head")
    rows = queries.shape[0]
    blocks_here = rows // WINDOW
    blocks = blocks_here * head_count
    per_slot = KV_HEADS // head_count
    width = 2 * per_slot * HEAD_DIM

    def shape(dims, kind=BF16):
        return jax.ShapeDtypeStruct(dims, kind)

    def far(value):
        return pltpu.with_memory_space_constraint(value, pltpu.HBM)

    def close(value):
        return pltpu.with_memory_space_constraint(value, pltpu.VMEM)

    table = jnp.concatenate([branch_start, branch_len, parent_list[:, 0], parent_list[:, 1]])
    *slots, halo_out, keys, values = pl.pallas_call(
        pack_kernel,
        out_shape=(shape((rows, width)),) * head_count
        + (shape((PAIRS, WINDOW, 256)),)
        + (pltpu.VMEM(key_states.shape, BF16),) * 2,
        in_specs=[HBM] * 3,
        out_specs=(VMEM,) * (head_count + 3),
        scratch_shapes=[
            pltpu.SMEM(sink_logits.shape, F32),
            pltpu.SemaphoreType.DMA((3,)),
        ],
        compiler_params=PARAMS,
        name="pack",
    )(far(sink_logits), far(key_states), far(value_states))
    spread = swap(slots, "head")
    halo = shift(halo_out, "head", 1)
    plan = pl.pallas_call(
        functools.partial(plan_kernel, tok_count, blocks, blocks_here),
        out_shape=pltpu.VMEM((8, 128), jnp.int32),
        in_specs=[SMEM],
        out_specs=VMEM,
        compiler_params=PARAMS,
        name="plan",
    )(table)
    plan = close(plan)
    *chosen, sinks = pl.pallas_call(
        choose_kernel,
        out_shape=(shape((WINDOW, width)),) * LAG + (shape((KV_HEADS * GROUP, 128), F32),),
        in_specs=[VMEM] * (1 + head_count),
        out_specs=(VMEM,) * (LAG + 1),
        compiler_params=PARAMS,
        name="choose",
    )(plan, *spread)
    arrived = [ring(chosen[LAG - s], "tok", s) for s in range(LAG, 0, -1)]
    queries, out_grad, _ = lax.optimization_barrier((queries, out_grad, sinks))
    near_queries, near_grad = pl.pallas_call(
        stage_kernel,
        out_shape=(pltpu.VMEM(queries.shape, BF16),) * 2,
        in_specs=[HBM] * 2,
        out_specs=(VMEM,) * 2,
        scratch_shapes=[pltpu.SemaphoreType.DMA((2,))],
        compiler_params=PARAMS,
        name="stage",
    )(far(queries), far(out_grad))
    *arrived, near_queries, near_grad = lax.optimization_barrier(
        (*arrived, near_queries, near_grad)
    )
    quarter = pl.pallas_call(
        arrive_kernel,
        out_shape=shape((WINDOW, width)),
        in_specs=[VMEM] * (1 + LAG),
        out_specs=VMEM,
        compiler_params=PARAMS,
        name="arrive",
    )(plan, *arrived)
    tails = swap([quarter] * head_count, "head")

    def attend(steps, pairs, offset, halo, joined):
        inputs = (
            sinks,
            close(near_queries),
            close(near_grad),
            close(keys),
            close(values),
            halo,
            *(tails[step] for step in steps),
            *(close(value) for value in joined),
        )
        base = 1 + len(inputs) - len(joined)
        return pl.pallas_call(
            functools.partial(
                attend_kernel,
                blocks_here,
                head_count,
                steps,
                offset,
                pairs,
                len(joined),
            ),
            out_shape=(
                pltpu.VMEM(queries.shape, BF16),
                pltpu.VMEM(queries.shape, BF16),
                pltpu.VMEM(key_states.shape, F32),
                pltpu.VMEM(key_states.shape, F32),
                pltpu.VMEM((PAIRS, WINDOW, 256), BF16),
            )
            + (shape((WINDOW, width)),) * len(steps),
            in_specs=[VMEM] * (1 + len(inputs)),
            out_specs=(VMEM,) * (5 + len(steps)),
            scratch_shapes=[
                pltpu.VMEM((head_count, WINDOW, width), BF16),
                pltpu.VMEM((WINDOW, 256), F32),
                pltpu.VMEM((2 * GROUP, WINDOW), F32),
                pltpu.VMEM((6 * HALF, 1024), BF16),
                pltpu.VMEM((6 * HALF, 1024), BF16),
            ],
            input_output_aliases={base + place: place for place in range(len(joined))},
            compiler_params=PARAMS,
            name="attend",
        )(plan, *inputs)

    if per_slot == 2:
        *joined, own_tail = attend((0,), 1, 0, spread[1], ())
        *results, tail_1, tail_2, tail_3 = attend((1, 2, 3), PAIRS - 1, 1, halo, joined)
        dtail = [own_tail, tail_1, tail_2, tail_3]
    else:
        results = attend(tuple(range(head_count)), PAIRS, None, halo, ())
        results, dtail = results[:5], list(results[5:])
    attended, query_grad, dk, dv, dhalo = results
    parts = swap(dtail, "head")
    quarter_grad = pl.pallas_call(
        gather_kernel,
        out_shape=shape((WINDOW, width)),
        in_specs=[VMEM] * head_count,
        out_specs=VMEM,
        compiler_params=PARAMS,
        name="gather",
    )(*parts)
    def flush(value):
        return pl.pallas_call(
            stage_kernel,
            out_shape=pltpu.HBM(value.shape, BF16),
            in_specs=[VMEM],
            out_specs=HBM,
            scratch_shapes=[pltpu.SemaphoreType.DMA((1,))],
            compiler_params=PARAMS,
            name="flush",
        )(close(value))

    returned = [ring(quarter_grad, "tok", -s) for s in range(LAG, 0, -1)][::-1]
    attended, _ = lax.optimization_barrier((attended, quarter_grad))
    attended = flush(attended)
    attended, *returned = lax.optimization_barrier((attended, *returned))
    halo_back = shift(dhalo, "head", -1)
    *landed, sink_near = pl.pallas_call(
        functools.partial(land_kernel, blocks),
        out_shape=(shape((rows, width)),) * head_count + (shape((8, 128), F32),),
        in_specs=[VMEM] * (LAG + 2),
        out_specs=(VMEM,) * (head_count + 1),
        compiler_params=PARAMS,
        name="land",
    )(plan, quarter_grad, *returned)
    tails_back = swap(landed, "head")
    query_grad, _ = lax.optimization_barrier((query_grad, sink_near))
    query_grad = flush(query_grad)
    span = LAG + 1
    while 2 * span < tok_count:
        sink_near = sink_near + ring(sink_near, "tok", -span)
        span *= 2
    sink_far = ring(sink_near, "tok", -span)
    key_grad, value_grad, sink_grad = pl.pallas_call(
        total_kernel,
        out_shape=(
            shape(key_states.shape),
            shape(value_states.shape),
            shape(sink_logits.shape, F32),
        ),
        in_specs=[VMEM] * (5 + head_count),
        out_specs=(VMEM, VMEM, SMEM),
        scratch_shapes=[pltpu.VMEM((head_count, rows, width), BF16)],
        compiler_params=PARAMS,
        name="total",
    )(dk, dv, halo_back, sink_near, sink_far, *tails_back)
    return attended, query_grad, key_grad, value_grad, sink_grad


def solution(mesh):
    rows = P(("tok", "head"), None)
    return jax.shard_map(
        local,
        mesh=mesh,
        in_specs=(rows, rows, rows, rows, P("head"), P(), P(), P()),
        out_specs=(rows, rows, rows, rows, P("head")),
        check_vma=False,
    )
```

```python
import functools

import jax
import jax.numpy as jnp
from jax import lax
from jax.experimental import pallas as pl
from jax.experimental.pallas import tpu as pltpu
from jax.sharding import PartitionSpec as P

HEAD_DIM = 64
KV_HEADS = 8
GROUP = 8
WINDOW = 128
HALF = WINDOW // 2
LAG = 3
BR_DEV = 2
PAIRS = KV_HEADS // 2
FACTOR = 0.125
LOW = -1e30
BF16 = jnp.bfloat16
F32 = jnp.float32

SMEM = pl.BlockSpec(memory_space=pltpu.SMEM)
VMEM = pl.BlockSpec(memory_space=pltpu.VMEM)
HBM = pl.BlockSpec(memory_space=pltpu.HBM)
PARAMS = pltpu.CompilerParams(vmem_limit_bytes=24 * 1024 * 1024)


def shift(value, axis, steps):
    count = lax.axis_size(axis)
    leading, last = (max(0, -steps), min(count, count - steps))
    return lax.ppermute(value, axis, [(source, source + steps) for source in range(leading, last)])


def ring(value, axis, steps):
    count = lax.axis_size(axis)
    return lax.ppermute(value, axis, [(source, (source + steps) % count) for source in range(count)])


def with_row(tile, row):
    high = row.astype(BF16).astype(F32)
    middle = (row - high).astype(BF16).astype(F32)
    low = row - high - middle
    packed = high + pltpu.roll(middle, 32, 1) + pltpu.roll(low, 64, 1)
    place = lax.broadcasted_iota(jnp.int32, (16, 128), 0)
    top = jnp.where(place == 0, packed, tile[:16, :128].astype(F32)).astype(BF16)
    if tile.shape[1] > 128:
        top = jnp.concatenate([top, tile[:16, 128:]], axis=1)
    return jnp.concatenate([top, tile[16:]], axis=0)


def row_join(top):
    packed = top[0:1, :128].astype(F32)
    row = packed + pltpu.roll(packed, 96, 1) + pltpu.roll(packed, 64, 1)
    return jnp.where(lax.broadcasted_iota(jnp.int32, (1, 128), 1) < 32, row, 0.0)


def child_tail(starts, parents, tok, distance, tok_count, blocks):
    child = jnp.minimum(tok + distance, tok_count - 1) * BR_DEV
    parent = parents[0, child]
    safe = jnp.maximum(parent, 0)
    valid = (tok + distance < tok_count) & (parent >= 0) & (safe // BR_DEV == tok)
    place = (starts[safe] + parents[1, child]) // WINDOW - tok * blocks
    return valid, jnp.where(valid, place, 0)


def block_state(starts, lengths, parents, tok, block):
    position = block * WINDOW
    alive, opening = jnp.bool_(False), jnp.bool_(False)
    for branch in range(BR_DEV):
        start = starts[tok * BR_DEV + branch]
        length = lengths[tok * BR_DEV + branch]
        alive = alive | ((start <= position) & (position < start + length))
        opening = opening | (start == position)
    has_tail = parents[0, tok * BR_DEV] >= 0
    return alive, opening, jnp.logical_not(opening) | has_tail


def plan_kernel(tok_count, blocks, blocks_here, starts, lengths, parents, plan_ref):
    tok, head = lax.axis_index("tok"), lax.axis_index("head")
    values = []
    for distance in range(1, LAG + 1):
        values += child_tail(starts, parents, tok, distance, tok_count, blocks)
    parent = parents[0, tok * BR_DEV]
    values.append(jnp.where(parent >= 0, tok - jnp.maximum(parent, 0) // BR_DEV, 1))
    for block in range(blocks_here):
        number = tok * blocks + head * blocks_here + block
        values += block_state(starts, lengths, parents, tok, number)
    lane = lax.broadcasted_iota(jnp.int32, plan_ref.shape, 1)
    plan = jnp.zeros(plan_ref.shape, jnp.int32)
    for place, value in enumerate(values):
        plan = jnp.where(lane == place, value.astype(jnp.int32), plan)
    plan_ref[...] = plan


def planned_tail(plan_ref, distance):
    row = plan_ref[0:1, :]
    return row[0, 2 * distance - 2] != 0, row[0, 2 * distance - 1]


def planned_source(plan_ref):
    return plan_ref[0:1, :][0, 2 * LAG]


def planned_block(plan_ref, block):
    row = plan_ref[0:1, :]
    return tuple(row[0, 2 * LAG + 1 + 3 * block + place] for place in range(3))


def take(ref, slot, width):
    if width % 128 == 0:
        return ref[:, pl.ds(pl.multiple_of(slot * width, width), width)]
    value = ref[:, :width]
    for other in range(1, ref.shape[1] // width):
        value = jnp.where(slot == other, ref[:, other * width : (other + 1) * width], value)
    return value


def pack_kernel(sink_hbm, key_hbm, value_hbm, *refs):
    *slot_refs, halo_ref, keys, values, sinks, sems = refs
    copies = [
        pltpu.make_async_copy(source, target, sems.at[place])
        for place, (source, target) in enumerate(
            ((sink_hbm, sinks), (key_hbm, keys), (value_hbm, values))
        )
    ]
    for copy in copies:
        copy.start()
    for copy in copies:
        copy.wait()
    slots, rows = len(slot_refs), keys.shape[0]
    head = lax.axis_index("head")
    width = KV_HEADS * HEAD_DIM // slots
    lane = lax.broadcasted_iota(jnp.int32, (1, 128), 1)
    sink_row = jnp.zeros((1, 128), F32)
    for place in range(sinks.shape[0]):
        sink_row = jnp.where(lane == place, sinks[place], sink_row)
    for step, slot_ref in enumerate(slot_refs):
        slot = lax.rem(head + step, slots)
        both = jnp.concatenate([take(keys, slot, width), take(values, slot, width)], axis=1)
        slot_ref[...] = with_row(both, sink_row)
    for pair in range(PAIRS):
        lanes = slice(pair * 128, (pair + 1) * 128)
        last = slice(rows - WINDOW, rows)
        halo_ref[pair] = jnp.concatenate([keys[last, lanes], values[last, lanes]], axis=1)


def choose_kernel(plan_ref, *refs):
    slots = len(refs) - LAG - 1
    slot_refs, out_refs, sink_ref = refs[:slots], refs[slots:-1], refs[-1]
    head = lax.axis_index("head")
    rows = slot_refs[0].shape[0]
    blocks_here = rows // WINDOW
    heads = sink_ref.shape[0] // slots
    for distance, out_ref in zip(range(LAG, 0, -1), out_refs):
        _, place = planned_tail(plan_ref, distance)
        begin = pl.multiple_of(place % blocks_here * WINDOW, WINDOW)
        wanted = lax.rem(head - place // blocks_here + slots, slots)
        for step, slot_ref in enumerate(slot_refs):

            @pl.when(wanted == step)
            def _(out_ref=out_ref, slot_ref=slot_ref, begin=begin):
                out_ref[...] = slot_ref[pl.ds(begin, WINDOW), :]

    for step, slot_ref in enumerate(slot_refs):
        source = lax.rem(head - step + slots, slots)
        sink_row = row_join(slot_ref[:16])
        turned = jnp.broadcast_to(sink_row, (128, 128)).T
        sink_ref[pl.ds(pl.multiple_of(source * heads, heads), heads), :] = turned[:heads]


def arrive_kernel(plan_ref, *refs):
    *in_refs, out_ref = refs
    mine = planned_source(plan_ref)
    for distance, in_ref in zip(range(LAG, 0, -1), in_refs):

        @pl.when(mine == distance)
        def _(in_ref=in_ref):
            out_ref[...] = in_ref[...]


def stage_kernel(*refs):
    *arrays, sems = refs
    half = len(arrays) // 2
    copies = [
        pltpu.make_async_copy(source, target, sems.at[place])
        for place, (source, target) in enumerate(zip(arrays[:half], arrays[half:]))
    ]
    for copy in copies:
        copy.start()
    for copy in copies:
        copy.wait()


def attend_kernel(blocks_here, slots, steps, offset, pairs, joins, *refs):
    inputs, refs = refs[:7], refs[7:]
    tail_refs, refs = refs[: len(steps)], refs[len(steps) + joins :]
    outputs, refs = refs[:5], refs[5:]
    dtail_refs, refs = refs[: len(steps)], refs[len(steps) :]
    tails, *scratch = refs
    head = lax.axis_index("head")
    states = [planned_block(inputs[0], block) for block in range(blocks_here)]
    for step, tail_ref in zip(steps, tail_refs):
        tails[lax.rem(head - step + slots, slots)] = tail_ref[...]

    def step(place, carry):
        pair = place if offset is None else lax.rem(head + place + offset, PAIRS)
        attend_pair(
            slots, pair, states, inputs, outputs, tails, tuple(zip(steps, dtail_refs)), scratch
        )
        return carry

    lax.fori_loop(0, pairs, step, 0)


def attend_pair(slots, pair, states, inputs, outputs, tails, dtails, scratch):
    _, sink_ref, q_ref, g_ref, k_ref, v_ref, halo_ref = inputs
    o_ref, dq_ref, dk_ref, dv_ref, dhalo_ref = outputs
    tail_sum, sink_rows, prob2, slope2 = scratch
    per_slot = KV_HEADS // slots
    head = lax.axis_index("head")
    near = pl.ds(pl.multiple_of(pair * 128, 128), 128)
    big = pl.ds(pl.multiple_of(pair * 1024, 1024), 1024)
    dhalo_ref = dhalo_ref.at[pair]
    tail_sum[...] = jnp.zeros_like(tail_sum)
    dhalo_ref[...] = jnp.zeros((WINDOW, 256), BF16)
    sink_rows[...] = jnp.zeros_like(sink_rows)
    if len(halo_ref.shape) == 2:
        halo_ref = halo_ref.at[halo_ref.shape[0] - WINDOW :]
    else:
        halo_ref = halo_ref.at[pair]
    if per_slot == 2:
        tail_refs = (tails.at[pair],)
    else:
        tail_refs = (tails.at[2 * pair], tails.at[2 * pair + 1])

    def attend(blocks, blocks_state):
        attend_blocks(
            blocks,
            blocks_state,
            [ref.at[:, big] for ref in (q_ref, g_ref, o_ref, dq_ref)],
            [ref.at[:, near] for ref in (k_ref, v_ref, dk_ref, dv_ref)],
            sink_ref.at[pl.ds(pl.multiple_of(pair * 16, 16), 16)],
            halo_ref,
            tail_refs,
            dhalo_ref,
            scratch,
        )

    for block, (alive, _, _) in enumerate(states):
        here = slice(block * WINDOW, (block + 1) * WINDOW)

        @pl.when(alive == 0)
        def _(here=here):
            o_ref[here, big] = jnp.zeros((WINDOW, 1024), BF16)
            dq_ref[here, big] = jnp.zeros((WINDOW, 1024), BF16)
            dk_ref[here, near] = jnp.zeros((WINDOW, 128), F32)
            dv_ref[here, near] = jnp.zeros((WINDOW, 128), F32)

    count = len(states)
    living = sum(alive for alive, _, _ in states)
    if count > 1:

        @pl.when(living == count)
        def _():
            attend(tuple(range(count)), states)

    @pl.when((living > 0) & ((living < count) | (count == 1)))
    def _():
        def single(block, carry):
            state = states[0]
            for other in range(1, count):
                state = [jnp.where(block == other, *two) for two in zip(states[other], state)]

            @pl.when(state[0] != 0)
            def _():
                attend((block,), (state,))

            return carry

        lax.fori_loop(0, count, single, 0)

    width = 2 * per_slot * HEAD_DIM
    heads = per_slot * GROUP
    total = tail_sum[...].astype(BF16)
    for part in range(2 // per_slot):
        feats = slice(part * width // 2, (part + 1) * width // 2)
        tail = jnp.concatenate([total[:, :128][:, feats], total[:, 128:][:, feats]], axis=1)
        rows = sink_rows[part * heads : (part + 1) * heads]
        rows = jnp.concatenate([rows, jnp.zeros((128 - heads, WINDOW), F32)], axis=0)
        sink_row = jnp.sum(rows.T, axis=0, keepdims=True)
        tail = with_row(tail, sink_row)
        wanted = lax.rem(pair * (2 // per_slot) + part - head + slots, slots)
        for step, dtail_ref in dtails:

            @pl.when(wanted == step)
            def _(dtail_ref=dtail_ref, tail=tail):
                dtail_ref[...] = tail


def attend_blocks(
    blocks, states, bigs, smalls, sink_ref, halo_ref, tail_refs, dhalo_ref, scratch
):
    q_ref, g_ref, o_ref, dq_ref = bigs
    k_ref, v_ref, dk_ref, dv_ref = smalls
    tail_sum, sink_rows, prob2, slope2 = scratch
    left = lax.broadcasted_iota(jnp.int32, (1, 128), 1) < HALF
    low16 = left.astype(F32).astype(BF16)
    high16 = BF16(1) - low16
    key_place = lax.broadcasted_iota(jnp.int32, (HALF, 4 * HALF), 0)
    query_place = lax.broadcasted_iota(jnp.int32, (HALF, 4 * HALF), 1) & (HALF - 1)
    own = key_place <= query_place
    own16 = own.astype(F32).astype(BF16)
    turn = (((1,), (1,)), ((), ()))
    seen = 3 * HALF

    def at(block, begin=0, count=WINDOW):
        start = block * WINDOW + begin
        if isinstance(start, int):
            return pl.ds(start, count)
        return pl.ds(pl.multiple_of(start, HALF), count)

    def before(block):
        return at(max(block - 1, 0) if isinstance(block, int) else jnp.maximum(block - 1, 0))

    def halves(own, prev):
        return (
            jnp.concatenate([own[:HALF], prev[:HALF], prev[HALF:]], axis=0),
            jnp.concatenate([own[HALF:], prev[HALF:], own[:HALF]], axis=0),
        )

    def padded(rows):
        swapped = jnp.concatenate([rows[:, 64:], rows[:, :64]], axis=1)
        return (
            jnp.concatenate([rows * low16, swapped * high16], axis=0),
            jnp.concatenate([swapped * low16, rows * high16], axis=0),
        )

    def prepare(block, opening):
        halo = halo_ref[...]
        if len(tail_refs) == 1:
            tail = tail_refs[0][...]
            tail_k, tail_v = tail[:, :128], tail[:, 128:]
        else:
            tail_a, tail_b = (ref[...] for ref in tail_refs)
            tail_k = jnp.concatenate([tail_a[:, :64], tail_b[:, :64]], axis=1)
            tail_v = jnp.concatenate([tail_a[:, 64:], tail_b[:, 64:]], axis=1)
        near_k = jnp.where(block == 0, halo[:, :128], k_ref[before(block), :])
        near_v = jnp.where(block == 0, halo[:, 128:], v_ref[before(block), :])
        prev_k = jnp.where(opening != 0, tail_k, near_k)
        prev_v = jnp.where(opening != 0, tail_v, near_v)
        seen_k = halves(k_ref[at(block), :] * BF16(FACTOR), prev_k * BF16(FACTOR))
        seen_v = halves(v_ref[at(block), :], prev_v)
        return (
            tuple(padded(value) for value in seen_k),
            tuple(padded(value) for value in seen_v),
            tuple(value.T for value in seen_k),
            tuple(value.T for value in seen_v),
        )

    keys = [prepare(block, opening) for block, (_, opening, _) in zip(blocks, states)]
    biases = [jnp.where(prev_ok != 0, 0.0, LOW) for _, _, prev_ok in states]
    items = [
        (place, unit, half)
        for place in range(len(blocks))
        for unit in range(2)
        for half in range(2)
    ]

    def wide(index):
        return slice(index * 256, (index + 1) * 256)

    def feats(index):
        unit = items[index][1]
        return slice(unit * HEAD_DIM, (unit + 1) * HEAD_DIM)

    def corners(index):
        place, unit, half = items[index]
        rows = at(blocks[place], half * HALF, HALF)
        return [(rows, slice(unit * 512 + by * 128, unit * 512 + (by + 1) * 128)) for by in range(4)]

    def stacked(ref, index):
        return jnp.concatenate([ref[corner] for corner in corners(index)], axis=0)

    def products(index):
        place, unit, half = items[index]
        padded_k, padded_v, _, _ = keys[place]
        bias = biases[place]
        score, dp = (
            lax.dot_general(
                rows[half][unit], stacked(ref, index), turn, preferred_element_type=F32
            )
            for rows, ref in ((padded_k, q_ref), (padded_v, g_ref))
        )
        parts = []
        for base in (0, seen):
            near, far = slice(base, base + HALF), slice(base + HALF, base + 2 * HALF)
            rest = slice(base + 2 * HALF, base + 3 * HALF)
            edge = jnp.where(own, score[near], score[far] + bias)
            whole = score[rest] + bias if half == 0 else score[rest]
            parts.append((edge, whole, jnp.where(own, dp[near], dp[far]), dp[rest]))
        return parts

    def weigh(index, odd, edge, whole, dp_edge, dp_whole):
        unit = items[index][1]
        base = odd * seen
        row = unit * GROUP + odd
        sink = jnp.concatenate(
            [
                jnp.where(left, sink_ref[by : by + 1], sink_ref[by + 2 : by + 3])
                for by in (row, row + 4)
            ],
            axis=1,
        )
        peak = jnp.max(jnp.maximum(edge, whole), axis=0, keepdims=True)
        peak = jnp.maximum(peak, sink)
        edge, whole = jnp.exp(edge - peak), jnp.exp(whole - peak)
        sink_weight = jnp.exp(sink - peak)
        inverse = 1.0 / (jnp.sum(edge + whole, axis=0, keepdims=True) + sink_weight)
        edge, whole = edge * inverse, whole * inverse
        term_edge, term_whole = edge * dp_edge, whole * dp_whole
        delta = jnp.sum(term_edge + term_whole, axis=0, keepdims=True)
        for target, at_edge, at_whole in (
            (prob2, edge, whole),
            (slope2, term_edge - edge * delta, term_whole - whole * delta),
        ):
            edge16 = at_edge.astype(BF16)
            edge_own = edge16 * own16
            target[base : base + HALF, wide(index)] = edge_own
            target[base + HALF : base + 2 * HALF, wide(index)] = edge16 - edge_own
            target[base + 2 * HALF : base + seen, wide(index)] = at_whole.astype(BF16)
        sink_term = sink_weight * inverse * delta
        for by, lanes in ((row, slice(0, 128)), (row + 4, slice(128, 256))):
            part = sink_term[:, lanes]
            sink_rows[by : by + 1] += jnp.where(left, part, 0.0)
            sink_rows[by + 2 : by + 3] += jnp.where(left, 0.0, part)

    def finish(index):
        place, _, half = items[index]
        _, _, turned_k, turned_v = keys[place]
        for source, across, out_ref in ((prob2, turned_v, o_ref), (slope2, turned_k, dq_ref)):
            out_t = [
                jnp.dot(
                    across[half][feats(index)],
                    source[base : base + seen, wide(index)],
                    preferred_element_type=F32,
                ).astype(BF16)
                for base in (0, seen)
            ]
            out = jnp.concatenate(out_t, axis=0).T
            for by, corner in enumerate(corners(index)):
                out_ref[corner] = out[by * HALF : (by + 1) * HALF]

    def reduce(index):
        parts = []
        for weights, ref in ((slope2, q_ref), (prob2, g_ref)):
            part = jnp.dot(
                weights[:, wide(index)], stacked(ref, index), preferred_element_type=F32
            )
            parts.append(jnp.where(left, part[:seen], part[seen:]))
        return parts

    def join(first_half, second_half):
        total = jnp.concatenate(
            [
                first_half[:HALF] + second_half[2 * HALF :],
                second_half[:HALF],
                first_half[HALF : 2 * HALF],
                first_half[2 * HALF :] + second_half[HALF : 2 * HALF],
            ],
            axis=0,
        )
        return total + pltpu.roll(total, HEAD_DIM, 1)

    ahead, parts, grads = products(0), [], []
    for index in range(len(items)):
        now = ahead
        weigh(index, 0, *now[0])
        if index + 1 < len(items):
            ahead = products(index + 1)
        weigh(index, 1, *now[1])
        if index >= 1:
            finish(index - 1)
        parts.append(reduce(index))
        if len(parts) == 4:
            joined = [
                [join(parts[2 * unit][which], parts[2 * unit + 1][which]) for unit in range(2)]
                for which in range(2)
            ]
            dk, dv = (jnp.where(left, *both) for both in joined)
            grads.append((dk * FACTOR, dv))
            parts = []
    finish(len(items) - 1)
    for block, (dk, dv) in zip(blocks, grads):
        dk_ref[at(block), :] = dk[:WINDOW]
        dv_ref[at(block), :] = dv[:WINDOW]
    for block, (_, opening, prev_ok), (dk, dv) in zip(blocks, states, grads):

        @pl.when((opening != 0) & (prev_ok != 0))
        def _(dk=dk, dv=dv):
            tail_sum[:, :128] += dk[WINDOW:]
            tail_sum[:, 128:] += dv[WINDOW:]

        @pl.when((opening == 0) & (block == 0))
        def _(dk=dk, dv=dv):
            dhalo_ref[:, :128] = dk[WINDOW:].astype(BF16)
            dhalo_ref[:, 128:] = dv[WINDOW:].astype(BF16)

        @pl.when((opening == 0) & (block != 0))
        def _(dk=dk, dv=dv, block=block):
            dk_ref[before(block), :] += dk[WINDOW:]
            dv_ref[before(block), :] += dv[WINDOW:]


def gather_kernel(*refs):
    *in_refs, out_ref = refs
    total, sink_row = 0.0, 0.0
    for in_ref in in_refs:
        total = total + in_ref[...].astype(F32)
        sink_row = sink_row + row_join(in_ref[:16])
    out_ref[...] = with_row(total.astype(BF16), sink_row)


def land_kernel(blocks, plan_ref, here_ref, *refs):
    head = lax.axis_index("head")
    in_refs, out_refs, sink_ref = refs[:LAG], refs[LAG:-1], refs[-1]
    slots = len(out_refs)
    blocks_here = blocks // slots
    for out_ref in out_refs:
        out_ref[...] = jnp.zeros_like(out_ref)
    sink_row = row_join(here_ref[:16])
    seen = lax.broadcasted_iota(jnp.int32, here_ref.shape, 0) > 0
    for distance, in_ref in enumerate(in_refs, 1):
        valid, place = planned_tail(plan_ref, distance)
        sink_row = sink_row + row_join(in_ref[:16])
        wanted = lax.rem(place // blocks_here - head + slots, slots)
        here = pl.ds(pl.multiple_of(place % blocks_here * WINDOW, WINDOW), WINDOW)
        for step, out_ref in enumerate(out_refs):

            @pl.when(valid & (wanted == step))
            def _(out_ref=out_ref, in_ref=in_ref, here=here):
                total = out_ref[here, :].astype(F32) + in_ref[...].astype(F32)
                out_ref[here, :] = jnp.where(seen, total, 0.0).astype(BF16)

    sink_ref[...] = jnp.broadcast_to(sink_row, sink_ref.shape)


def total_kernel(dk_ref, dv_ref, halo_ref, sink_ref, far_ref, *refs):
    *tail_refs, key_ref, value_ref, sink_grad, tails = refs
    slots, rows = len(tail_refs), dk_ref.shape[0]
    width = tails.shape[2] // 2
    head = lax.axis_index("head")
    for step, tail_ref in enumerate(tail_refs):
        tails[lax.rem(head - step + slots, slots)] = tail_ref[...]
    halo_k = jnp.concatenate([halo_ref[pair][:, :128] for pair in range(PAIRS)], axis=1)
    halo_v = jnp.concatenate([halo_ref[pair][:, 128:] for pair in range(PAIRS)], axis=1)
    for in_ref, halo, at, out_ref in (
        (dk_ref, halo_k, 0, key_ref),
        (dv_ref, halo_v, width, value_ref),
    ):
        for begin in range(0, rows, WINDOW):
            here = slice(begin, begin + WINDOW)
            parts = [tails[slot, here, at : at + width] for slot in range(slots)]
            total = in_ref[here, :] + jnp.concatenate(parts, axis=1).astype(F32)
            if begin == rows - WINDOW:
                total = total + halo.astype(F32)
            out_ref[here, :] = total.astype(BF16)
    sink_row = -(sink_ref[0:1] + far_ref[0:1])
    for place in range(sink_grad.shape[0]):
        sink_grad[place] = sink_row[0, place]


def swap(values, axis):
    return [values[0]] + [ring(values[step], axis, step) for step in range(1, len(values))]


def local(
    queries, key_states, value_states, out_grad, sink_logits, branch_start, branch_len, parent_list
):
    tok_count, head_count = lax.axis_size("tok"), lax.axis_size("head")
    rows = queries.shape[0]
    blocks_here = rows // WINDOW
    blocks = blocks_here * head_count
    per_slot = KV_HEADS // head_count
    width = 2 * per_slot * HEAD_DIM

    def shape(dims, kind=BF16):
        return jax.ShapeDtypeStruct(dims, kind)

    def far(value):
        return pltpu.with_memory_space_constraint(value, pltpu.HBM)

    def close(value):
        return pltpu.with_memory_space_constraint(value, pltpu.VMEM)

    *slots, halo_out, keys, values = pl.pallas_call(
        pack_kernel,
        out_shape=(shape((rows, width)),) * head_count
        + (shape((PAIRS, WINDOW, 256)),)
        + (pltpu.VMEM(key_states.shape, BF16),) * 2,
        in_specs=[HBM] * 3,
        out_specs=(VMEM,) * (head_count + 3),
        scratch_shapes=[
            pltpu.SMEM(sink_logits.shape, F32),
            pltpu.SemaphoreType.DMA((3,)),
        ],
        compiler_params=PARAMS,
        name="pack",
    )(far(sink_logits), far(key_states), far(value_states))
    spread = swap(slots, "head")
    halo = shift(halo_out, "head", 1)
    plan = pl.pallas_call(
        functools.partial(plan_kernel, tok_count, blocks, blocks_here),
        out_shape=pltpu.VMEM((8, 128), jnp.int32),
        in_specs=[SMEM] * 3,
        out_specs=VMEM,
        compiler_params=PARAMS,
        name="plan",
    )(far(branch_start), far(branch_len), far(parent_list.T))
    plan = close(plan)
    *chosen, sinks = pl.pallas_call(
        choose_kernel,
        out_shape=(shape((WINDOW, width)),) * LAG + (shape((KV_HEADS * GROUP, 128), F32),),
        in_specs=[VMEM] * (1 + head_count),
        out_specs=(VMEM,) * (LAG + 1),
        compiler_params=PARAMS,
        name="choose",
    )(plan, *spread)
    arrived = [ring(chosen[LAG - s], "tok", s) for s in range(LAG, 0, -1)]
    queries, out_grad, _ = lax.optimization_barrier((queries, out_grad, sinks))
    near_queries, near_grad = pl.pallas_call(
        stage_kernel,
        out_shape=(pltpu.VMEM(queries.shape, BF16),) * 2,
        in_specs=[HBM] * 2,
        out_specs=(VMEM,) * 2,
        scratch_shapes=[pltpu.SemaphoreType.DMA((2,))],
        compiler_params=PARAMS,
        name="stage",
    )(far(queries), far(out_grad))
    *arrived, near_queries, near_grad = lax.optimization_barrier(
        (*arrived, near_queries, near_grad)
    )
    quarter = pl.pallas_call(
        arrive_kernel,
        out_shape=shape((WINDOW, width)),
        in_specs=[VMEM] * (1 + LAG),
        out_specs=VMEM,
        compiler_params=PARAMS,
        name="arrive",
    )(plan, *arrived)
    tails = swap([quarter] * head_count, "head")

    def attend(steps, pairs, offset, halo, joined):
        inputs = (
            sinks,
            close(near_queries),
            close(near_grad),
            close(keys),
            close(values),
            halo,
            *(tails[step] for step in steps),
            *(close(value) for value in joined),
        )
        base = 1 + len(inputs) - len(joined)
        return pl.pallas_call(
            functools.partial(
                attend_kernel,
                blocks_here,
                head_count,
                steps,
                offset,
                pairs,
                len(joined),
            ),
            out_shape=(
                pltpu.VMEM(queries.shape, BF16),
                pltpu.VMEM(queries.shape, BF16),
                pltpu.VMEM(key_states.shape, F32),
                pltpu.VMEM(key_states.shape, F32),
                pltpu.VMEM((PAIRS, WINDOW, 256), BF16),
            )
            + (shape((WINDOW, width)),) * len(steps),
            in_specs=[VMEM] * (1 + len(inputs)),
            out_specs=(VMEM,) * (5 + len(steps)),
            scratch_shapes=[
                pltpu.VMEM((head_count, WINDOW, width), BF16),
                pltpu.VMEM((WINDOW, 256), F32),
                pltpu.VMEM((2 * GROUP, WINDOW), F32),
                pltpu.VMEM((6 * HALF, 1024 * blocks_here), BF16),
                pltpu.VMEM((6 * HALF, 1024 * blocks_here), BF16),
            ],
            input_output_aliases={base + place: place for place in range(len(joined))},
            compiler_params=PARAMS,
            name="attend",
        )(plan, *inputs)

    if per_slot == 2:
        *joined, own_tail = attend((0,), 1, 0, spread[1], ())
        *results, tail_1, tail_2, tail_3 = attend((1, 2, 3), PAIRS - 1, 1, halo, joined)
        dtail = [own_tail, tail_1, tail_2, tail_3]
    else:
        results = attend(tuple(range(head_count)), PAIRS, None, halo, ())
        results, dtail = results[:5], list(results[5:])
    attended, query_grad, dk, dv, dhalo = results
    parts = swap(dtail, "head")
    quarter_grad = pl.pallas_call(
        gather_kernel,
        out_shape=shape((WINDOW, width)),
        in_specs=[VMEM] * head_count,
        out_specs=VMEM,
        compiler_params=PARAMS,
        name="gather",
    )(*parts)
    def flush(value):
        return pl.pallas_call(
            stage_kernel,
            out_shape=pltpu.HBM(value.shape, BF16),
            in_specs=[VMEM],
            out_specs=HBM,
            scratch_shapes=[pltpu.SemaphoreType.DMA((1,))],
            compiler_params=PARAMS,
            name="flush",
        )(close(value))

    returned = [ring(quarter_grad, "tok", -s) for s in range(LAG, 0, -1)][::-1]
    attended, _ = lax.optimization_barrier((attended, quarter_grad))
    attended = flush(attended)
    attended, *returned = lax.optimization_barrier((attended, *returned))
    halo_back = shift(dhalo, "head", -1)
    *landed, sink_near = pl.pallas_call(
        functools.partial(land_kernel, blocks),
        out_shape=(shape((rows, width)),) * head_count + (shape((8, 128), F32),),
        in_specs=[VMEM] * (LAG + 2),
        out_specs=(VMEM,) * (head_count + 1),
        compiler_params=PARAMS,
        name="land",
    )(plan, quarter_grad, *returned)
    tails_back = swap(landed, "head")
    query_grad, _ = lax.optimization_barrier((query_grad, sink_near))
    query_grad = flush(query_grad)
    span = LAG + 1
    while 2 * span < tok_count:
        sink_near = sink_near + ring(sink_near, "tok", -span)
        span *= 2
    sink_far = ring(sink_near, "tok", -span)
    key_grad, value_grad, sink_grad = pl.pallas_call(
        total_kernel,
        out_shape=(
            shape(key_states.shape),
            shape(value_states.shape),
            shape(sink_logits.shape, F32),
        ),
        in_specs=[VMEM] * (5 + head_count),
        out_specs=(VMEM, VMEM, SMEM),
        scratch_shapes=[pltpu.VMEM((head_count, rows, width), BF16)],
        compiler_params=PARAMS,
        name="total",
    )(dk, dv, halo_back, sink_near, sink_far, *tails_back)
    return attended, query_grad, key_grad, value_grad, sink_grad


def solution(mesh):
    rows = P(("tok", "head"), None)
    return jax.shard_map(
        local,
        mesh=mesh,
        in_specs=(rows, rows, rows, rows, P("head"), P(), P(), P()),
        out_specs=(rows, rows, rows, rows, P("head")),
        check_vma=False,
    )
```

```python
import functools

import jax
import jax.numpy as jnp
from jax import lax
from jax.experimental import pallas as pl
from jax.experimental.pallas import tpu as pltpu
from jax.sharding import PartitionSpec as P

HEAD_DIM = 64
KV_HEADS = 8
GROUP = 8
WINDOW = 128
HALF = WINDOW // 2
LAG = 3
BR_DEV = 2
PAIRS = KV_HEADS // 2
FACTOR = 0.125
LOW = -1e30
BF16 = jnp.bfloat16
F32 = jnp.float32

SMEM = pl.BlockSpec(memory_space=pltpu.SMEM)
VMEM = pl.BlockSpec(memory_space=pltpu.VMEM)
HBM = pl.BlockSpec(memory_space=pltpu.HBM)
PARAMS = pltpu.CompilerParams(vmem_limit_bytes=24 * 1024 * 1024)


def shift(value, axis, steps):
    count = lax.axis_size(axis)
    leading, last = (max(0, -steps), min(count, count - steps))
    return lax.ppermute(value, axis, [(source, source + steps) for source in range(leading, last)])


def ring(value, axis, steps):
    count = lax.axis_size(axis)
    return lax.ppermute(value, axis, [(source, (source + steps) % count) for source in range(count)])


def with_row(tile, row):
    high = row.astype(BF16).astype(F32)
    middle = (row - high).astype(BF16).astype(F32)
    low = row - high - middle
    packed = high + pltpu.roll(middle, 32, 1) + pltpu.roll(low, 64, 1)
    place = lax.broadcasted_iota(jnp.int32, (16, 128), 0)
    top = jnp.where(place == 0, packed, tile[:16, :128].astype(F32)).astype(BF16)
    if tile.shape[1] > 128:
        top = jnp.concatenate([top, tile[:16, 128:]], axis=1)
    return jnp.concatenate([top, tile[16:]], axis=0)


def row_join(top):
    packed = top[0:1, :128].astype(F32)
    row = packed + pltpu.roll(packed, 96, 1) + pltpu.roll(packed, 64, 1)
    return jnp.where(lax.broadcasted_iota(jnp.int32, (1, 128), 1) < 32, row, 0.0)


def child_tail(starts, parents, tok, distance, tok_count, blocks):
    child = jnp.minimum(tok + distance, tok_count - 1) * BR_DEV
    parent = parents[0, child]
    safe = jnp.maximum(parent, 0)
    valid = (tok + distance < tok_count) & (parent >= 0) & (safe // BR_DEV == tok)
    place = (starts[safe] + parents[1, child]) // WINDOW - tok * blocks
    return valid, jnp.where(valid, place, 0)


def block_state(starts, lengths, parents, tok, block):
    position = block * WINDOW
    alive, opening = jnp.bool_(False), jnp.bool_(False)
    for branch in range(BR_DEV):
        start = starts[tok * BR_DEV + branch]
        length = lengths[tok * BR_DEV + branch]
        alive = alive | ((start <= position) & (position < start + length))
        opening = opening | (start == position)
    has_tail = parents[0, tok * BR_DEV] >= 0
    return alive, opening, jnp.logical_not(opening) | has_tail


def plan_kernel(tok_count, blocks, blocks_here, starts, lengths, parents, plan_ref):
    tok, head = lax.axis_index("tok"), lax.axis_index("head")
    values = []
    for distance in range(1, LAG + 1):
        values += child_tail(starts, parents, tok, distance, tok_count, blocks)
    parent = parents[0, tok * BR_DEV]
    values.append(jnp.where(parent >= 0, tok - jnp.maximum(parent, 0) // BR_DEV, 1))
    for block in range(blocks_here):
        number = tok * blocks + head * blocks_here + block
        values += block_state(starts, lengths, parents, tok, number)
    lane = lax.broadcasted_iota(jnp.int32, plan_ref.shape, 1)
    plan = jnp.zeros(plan_ref.shape, jnp.int32)
    for place, value in enumerate(values):
        plan = jnp.where(lane == place, value.astype(jnp.int32), plan)
    plan_ref[...] = plan


def planned_tail(plan_ref, distance):
    row = plan_ref[0:1, :]
    return row[0, 2 * distance - 2] != 0, row[0, 2 * distance - 1]


def planned_source(plan_ref):
    return plan_ref[0:1, :][0, 2 * LAG]


def planned_block(plan_ref, block):
    row = plan_ref[0:1, :]
    return tuple(row[0, 2 * LAG + 1 + 3 * block + place] for place in range(3))


def take(ref, slot, width):
    if width % 128 == 0:
        return ref[:, pl.ds(pl.multiple_of(slot * width, width), width)]
    value = ref[:, :width]
    for other in range(1, ref.shape[1] // width):
        value = jnp.where(slot == other, ref[:, other * width : (other + 1) * width], value)
    return value


def pack_kernel(sink_hbm, key_hbm, value_hbm, *refs):
    *slot_refs, halo_ref, keys, values, sinks, sems = refs
    copies = [
        pltpu.make_async_copy(source, target, sems.at[place])
        for place, (source, target) in enumerate(
            ((sink_hbm, sinks), (key_hbm, keys), (value_hbm, values))
        )
    ]
    for copy in copies:
        copy.start()
    for copy in copies:
        copy.wait()
    slots, rows = len(slot_refs), keys.shape[0]
    head = lax.axis_index("head")
    width = KV_HEADS * HEAD_DIM // slots
    lane = lax.broadcasted_iota(jnp.int32, (1, 128), 1)
    sink_row = jnp.zeros((1, 128), F32)
    for place in range(sinks.shape[0]):
        sink_row = jnp.where(lane == place, sinks[place], sink_row)
    for step, slot_ref in enumerate(slot_refs):
        slot = lax.rem(head + step, slots)
        both = jnp.concatenate([take(keys, slot, width), take(values, slot, width)], axis=1)
        slot_ref[...] = with_row(both, sink_row)
    for pair in range(PAIRS):
        lanes = slice(pair * 128, (pair + 1) * 128)
        last = slice(rows - WINDOW, rows)
        halo_ref[pair] = jnp.concatenate([keys[last, lanes], values[last, lanes]], axis=1)


def choose_kernel(plan_ref, *refs):
    slots = len(refs) - LAG - 1
    slot_refs, out_refs, sink_ref = refs[:slots], refs[slots:-1], refs[-1]
    head = lax.axis_index("head")
    rows = slot_refs[0].shape[0]
    blocks_here = rows // WINDOW
    heads = sink_ref.shape[0] // slots
    for distance, out_ref in zip(range(LAG, 0, -1), out_refs):
        _, place = planned_tail(plan_ref, distance)
        begin = pl.multiple_of(place % blocks_here * WINDOW, WINDOW)
        wanted = lax.rem(head - place // blocks_here + slots, slots)
        for step, slot_ref in enumerate(slot_refs):

            @pl.when(wanted == step)
            def _(out_ref=out_ref, slot_ref=slot_ref, begin=begin):
                out_ref[...] = slot_ref[pl.ds(begin, WINDOW), :]

    for step, slot_ref in enumerate(slot_refs):
        source = lax.rem(head - step + slots, slots)
        sink_row = row_join(slot_ref[:16])
        turned = jnp.broadcast_to(sink_row, (128, 128)).T
        sink_ref[pl.ds(pl.multiple_of(source * heads, heads), heads), :] = turned[:heads]


def arrive_kernel(plan_ref, *refs):
    *in_refs, out_ref = refs
    mine = planned_source(plan_ref)
    for distance, in_ref in zip(range(LAG, 0, -1), in_refs):

        @pl.when(mine == distance)
        def _(in_ref=in_ref):
            out_ref[...] = in_ref[...]


def stage_kernel(*refs):
    *arrays, sems = refs
    half = len(arrays) // 2
    copies = [
        pltpu.make_async_copy(source, target, sems.at[place])
        for place, (source, target) in enumerate(zip(arrays[:half], arrays[half:]))
    ]
    for copy in copies:
        copy.start()
    for copy in copies:
        copy.wait()


def attend_kernel(blocks_here, slots, steps, offset, pairs, joins, *refs):
    inputs, refs = refs[:7], refs[7:]
    tail_refs, refs = refs[: len(steps)], refs[len(steps) + joins :]
    outputs, refs = refs[:5], refs[5:]
    dtail_refs, refs = refs[: len(steps)], refs[len(steps) :]
    tails, *scratch = refs
    head = lax.axis_index("head")
    states = [planned_block(inputs[0], block) for block in range(blocks_here)]
    for step, tail_ref in zip(steps, tail_refs):
        tails[lax.rem(head - step + slots, slots)] = tail_ref[...]

    def step(place, carry):
        pair = place // blocks_here
        if offset is not None:
            pair = lax.rem(head + pair + offset, PAIRS)
        block = place % blocks_here
        state = states[0]
        for other in range(1, blocks_here):
            state = [jnp.where(block == other, *two) for two in zip(states[other], state)]
        attend_block(
            blocks_here,
            slots,
            pair,
            block,
            [value != 0 for value in state],
            inputs,
            outputs,
            tails,
            tuple(zip(steps, dtail_refs)),
            scratch,
        )
        return carry

    lax.fori_loop(0, pairs * blocks_here, step, 0)


def attend_block(
    blocks_here, slots, pair, block, state, inputs, outputs, tails, dtails, scratch
):
    _, sink_ref, q_ref, g_ref, k_ref, v_ref, halo_ref = inputs
    o_ref, dq_ref, dk_ref, dv_ref, dhalo_ref = outputs
    tail_sum, sink_rows, prob2, slope2 = scratch
    per_slot = KV_HEADS // slots
    head = lax.axis_index("head")
    alive, opening, prev_ok = state
    here = pl.ds(pl.multiple_of(block * WINDOW, WINDOW), WINDOW)
    before = pl.ds(pl.multiple_of(jnp.maximum(block - 1, 0) * WINDOW, WINDOW), WINDOW)
    first = block == 0
    near = pl.ds(pl.multiple_of(pair * 128, 128), 128)
    big = pl.ds(pl.multiple_of(pair * 1024, 1024), 1024)
    q_ref, g_ref, o_ref, dq_ref = (ref.at[here, big] for ref in (q_ref, g_ref, o_ref, dq_ref))
    k_ref, v_ref, dk_ref, dv_ref = (ref.at[:, near] for ref in (k_ref, v_ref, dk_ref, dv_ref))
    sink_ref = sink_ref.at[pl.ds(pl.multiple_of(pair * 16, 16), 16)]
    dhalo_ref = dhalo_ref.at[pair]

    @pl.when(first)
    def _():
        tail_sum[...] = jnp.zeros_like(tail_sum)
        dhalo_ref[...] = jnp.zeros((WINDOW, 256), BF16)
        sink_rows[...] = jnp.zeros_like(sink_rows)

    @pl.when(jnp.logical_not(alive))
    def _():
        o_ref[...] = jnp.zeros((WINDOW, 1024), BF16)
        dq_ref[...] = jnp.zeros((WINDOW, 1024), BF16)
        dk_ref[here, :] = jnp.zeros((WINDOW, 128), F32)
        dv_ref[here, :] = jnp.zeros((WINDOW, 128), F32)

    @pl.when(alive)
    def _():
        if len(halo_ref.shape) == 2:
            halo = halo_ref[halo_ref.shape[0] - WINDOW :]
        else:
            halo = halo_ref[pair]
        if per_slot == 2:
            tail = tails[pair]
            tail_k, tail_v = tail[:, :128], tail[:, 128:]
        else:
            tail_a, tail_b = tails[2 * pair], tails[2 * pair + 1]
            tail_k = jnp.concatenate([tail_a[:, :64], tail_b[:, :64]], axis=1)
            tail_v = jnp.concatenate([tail_a[:, 64:], tail_b[:, 64:]], axis=1)
        near_k = jnp.where(first, halo[:, :128], k_ref[before, :])
        near_v = jnp.where(first, halo[:, 128:], v_ref[before, :])
        prev_k = jnp.where(opening, tail_k, near_k)
        prev_v = jnp.where(opening, tail_v, near_v)
        own_k, own_v = k_ref[here, :], v_ref[here, :]

        def halves(own, prev):
            return (
                jnp.concatenate([own[:HALF], prev[:HALF], prev[HALF:]], axis=0),
                jnp.concatenate([own[HALF:], prev[HALF:], own[:HALF]], axis=0),
            )

        left = lax.broadcasted_iota(jnp.int32, (1, 128), 1) < HALF
        low16 = left.astype(F32).astype(BF16)
        high16 = BF16(1) - low16

        def padded(seen):
            seen = jnp.concatenate(
                [
                    seen[start + by : start + by + 16]
                    for by in range(0, HALF, 16)
                    for start in (0, HALF)
                ]
                + [seen[2 * HALF :]],
                axis=0,
            )
            swapped = jnp.concatenate([seen[:, 64:], seen[:, :64]], axis=1)
            return (
                jnp.concatenate([seen * low16, swapped * high16], axis=0),
                jnp.concatenate([swapped * low16, seen * high16], axis=0),
            )

        seen_k = halves(own_k * BF16(FACTOR), prev_k * BF16(FACTOR))
        seen_v = halves(own_v, prev_v)
        padded_k = tuple(padded(value) for value in seen_k)
        padded_v = tuple(padded(value) for value in seen_v)
        turned_k = tuple(value.T for value in seen_k)
        turned_v = tuple(value.T for value in seen_v)
        bias = jnp.where(prev_ok, 0.0, LOW)
        key_place = lax.broadcasted_iota(jnp.int32, (HALF, 4 * HALF), 0)
        query_place = lax.broadcasted_iota(jnp.int32, (HALF, 4 * HALF), 1) & (HALF - 1)
        own = key_place <= query_place
        own16 = own.astype(F32).astype(BF16)
        turn = (((1,), (1,)), ((), ()))
        items = [(unit, half) for unit in range(2) for half in range(2)]
        seen = 3 * HALF

        def wide(index):
            return slice(index * 256, (index + 1) * 256)

        def feats(index):
            unit = items[index][0]
            return slice(unit * HEAD_DIM, (unit + 1) * HEAD_DIM)

        def corners(unit, half):
            rows = slice(half * HALF, (half + 1) * HALF)
            return [
                (rows, slice(unit * 512 + at * 128, unit * 512 + (at + 1) * 128)) for at in range(4)
            ]

        def stacked(ref, unit, half):
            return jnp.concatenate([ref[corner] for corner in corners(unit, half)], axis=0)

        def products(index):
            unit, half = items[index]
            score, dp = (
                lax.dot_general(
                    padded[half][unit],
                    stacked(ref, unit, half),
                    turn,
                    preferred_element_type=F32,
                )
                for padded, ref in ((padded_k, q_ref), (padded_v, g_ref))
            )
            parts = []
            for base in (0, seen):
                edge, dp_edge = [], []
                for by in range(0, HALF, 16):
                    start = base + 2 * by
                    near, far = slice(start, start + 16), slice(start + 16, start + 32)
                    edge.append(jnp.where(own[by : by + 16], score[near], score[far] + bias))
                    dp_edge.append(jnp.where(own[by : by + 16], dp[near], dp[far]))
                edge, dp_edge = (jnp.concatenate(value, axis=0) for value in (edge, dp_edge))
                rest = slice(base + 2 * HALF, base + 3 * HALF)
                whole = score[rest] + bias if half == 0 else score[rest]
                parts.append((edge, whole, dp_edge, dp[rest]))
            return parts

        def weigh(index, odd, edge, whole, dp_edge, dp_whole):
            unit, half = items[index]
            base = odd * seen
            row = unit * GROUP + odd
            sink = jnp.concatenate(
                [
                    jnp.where(left, sink_ref[at : at + 1], sink_ref[at + 2 : at + 3])
                    for at in (row, row + 4)
                ],
                axis=1,
            )
            peak = jnp.max(jnp.maximum(edge, whole), axis=0, keepdims=True)
            peak = jnp.maximum(peak, sink)
            edge, whole = jnp.exp(edge - peak), jnp.exp(whole - peak)
            sink_weight = jnp.exp(sink - peak)
            inverse = 1.0 / (jnp.sum(edge + whole, axis=0, keepdims=True) + sink_weight)
            edge, whole = edge * inverse, whole * inverse
            term_edge, term_whole = edge * dp_edge, whole * dp_whole
            delta = jnp.sum(term_edge + term_whole, axis=0, keepdims=True)
            for target, at_edge, at_whole in (
                (prob2, edge, whole),
                (slope2, term_edge - edge * delta, term_whole - whole * delta),
            ):
                edge16 = at_edge.astype(BF16)
                edge_own = edge16 * own16
                target[base : base + HALF, wide(index)] = edge_own
                target[base + HALF : base + 2 * HALF, wide(index)] = edge16 - edge_own
                target[base + 2 * HALF : base + seen, wide(index)] = at_whole.astype(BF16)
            sink_term = sink_weight * inverse * delta
            for at, lanes in ((row, slice(0, 128)), (row + 4, slice(128, 256))):
                part = sink_term[:, lanes]
                sink_rows[at : at + 1] += jnp.where(left, part, 0.0)
                sink_rows[at + 2 : at + 3] += jnp.where(left, 0.0, part)

        def finish(index):
            unit, half = items[index]
            for source, across, out_ref in ((prob2, turned_v, o_ref), (slope2, turned_k, dq_ref)):
                out_t = [
                    jnp.dot(
                        across[half][feats(index)],
                        source[base : base + seen, wide(index)],
                        preferred_element_type=F32,
                    ).astype(BF16)
                    for base in (0, seen)
                ]
                out = jnp.concatenate(out_t, axis=0).T
                for at, corner in enumerate(corners(unit, half)):
                    out_ref[corner] = out[at * HALF : (at + 1) * HALF]

        def reduce(index):
            unit, half = items[index]
            parts = []
            for weights, ref in ((slope2, q_ref), (prob2, g_ref)):
                part = jnp.dot(
                    weights[:, wide(index)], stacked(ref, unit, half), preferred_element_type=F32
                )
                parts.append(jnp.where(left, part[:seen], part[seen:]))
            return parts

        def join(first_half, second_half):
            total = jnp.concatenate(
                [
                    first_half[:HALF] + second_half[2 * HALF :],
                    second_half[:HALF],
                    first_half[HALF : 2 * HALF],
                    first_half[2 * HALF :] + second_half[HALF : 2 * HALF],
                ],
                axis=0,
            )
            return total + pltpu.roll(total, HEAD_DIM, 1)

        parts = []
        for index in range(len(items)):
            now = products(index)
            if index >= 1:
                finish(index - 1)
                parts.append(reduce(index - 1))
            weigh(index, 0, *now[0])
            weigh(index, 1, *now[1])
        finish(len(items) - 1)
        parts.append(reduce(len(items) - 1))
        grads = [
            [join(parts[2 * unit][place], parts[2 * unit + 1][place]) for place in range(2)]
            for unit in range(2)
        ]
        dk = jnp.where(left, grads[0][0], grads[1][0]) * FACTOR
        dv = jnp.where(left, grads[0][1], grads[1][1])
        dk_ref[here, :] = dk[:WINDOW]
        dv_ref[here, :] = dv[:WINDOW]

        @pl.when(opening & prev_ok)
        def _():
            tail_sum[:, :128] += dk[WINDOW:]
            tail_sum[:, 128:] += dv[WINDOW:]

        @pl.when(jnp.logical_not(opening) & first)
        def _():
            dhalo_ref[:, :128] = dk[WINDOW:].astype(BF16)
            dhalo_ref[:, 128:] = dv[WINDOW:].astype(BF16)

        @pl.when(jnp.logical_not(opening) & jnp.logical_not(first))
        def _():
            dk_ref[before, :] += dk[WINDOW:]
            dv_ref[before, :] += dv[WINDOW:]

    @pl.when(block == blocks_here - 1)
    def _():
        width = 2 * per_slot * HEAD_DIM
        heads = per_slot * GROUP
        total = tail_sum[...].astype(BF16)
        for part in range(2 // per_slot):
            feats = slice(part * width // 2, (part + 1) * width // 2)
            tail = jnp.concatenate([total[:, :128][:, feats], total[:, 128:][:, feats]], axis=1)
            rows = sink_rows[part * heads : (part + 1) * heads]
            rows = jnp.concatenate([rows, jnp.zeros((128 - heads, WINDOW), F32)], axis=0)
            sink_row = jnp.sum(rows.T, axis=0, keepdims=True)
            tail = with_row(tail, sink_row)
            wanted = lax.rem(pair * (2 // per_slot) + part - head + slots, slots)
            for step, dtail_ref in dtails:

                @pl.when(wanted == step)
                def _(dtail_ref=dtail_ref, tail=tail):
                    dtail_ref[...] = tail


def gather_kernel(*refs):
    *in_refs, out_ref = refs
    total, sink_row = 0.0, 0.0
    for in_ref in in_refs:
        total = total + in_ref[...].astype(F32)
        sink_row = sink_row + row_join(in_ref[:16])
    out_ref[...] = with_row(total.astype(BF16), sink_row)


def land_kernel(blocks, plan_ref, here_ref, *refs):
    head = lax.axis_index("head")
    in_refs, out_refs, sink_ref = refs[:LAG], refs[LAG:-1], refs[-1]
    slots = len(out_refs)
    blocks_here = blocks // slots
    for out_ref in out_refs:
        out_ref[...] = jnp.zeros_like(out_ref)
    sink_row = row_join(here_ref[:16])
    seen = lax.broadcasted_iota(jnp.int32, here_ref.shape, 0) > 0
    for distance, in_ref in enumerate(in_refs, 1):
        valid, place = planned_tail(plan_ref, distance)
        sink_row = sink_row + row_join(in_ref[:16])
        wanted = lax.rem(place // blocks_here - head + slots, slots)
        here = pl.ds(pl.multiple_of(place % blocks_here * WINDOW, WINDOW), WINDOW)
        for step, out_ref in enumerate(out_refs):

            @pl.when(valid & (wanted == step))
            def _(out_ref=out_ref, in_ref=in_ref, here=here):
                total = out_ref[here, :].astype(F32) + in_ref[...].astype(F32)
                out_ref[here, :] = jnp.where(seen, total, 0.0).astype(BF16)

    sink_ref[...] = jnp.broadcast_to(sink_row, sink_ref.shape)


def total_kernel(dk_ref, dv_ref, halo_ref, sink_ref, far_ref, *refs):
    *tail_refs, key_ref, value_ref, sink_grad, tails = refs
    slots, rows = len(tail_refs), dk_ref.shape[0]
    width = tails.shape[2] // 2
    head = lax.axis_index("head")
    for step, tail_ref in enumerate(tail_refs):
        tails[lax.rem(head - step + slots, slots)] = tail_ref[...]
    halo_k = jnp.concatenate([halo_ref[pair][:, :128] for pair in range(PAIRS)], axis=1)
    halo_v = jnp.concatenate([halo_ref[pair][:, 128:] for pair in range(PAIRS)], axis=1)
    for in_ref, halo, at, out_ref in (
        (dk_ref, halo_k, 0, key_ref),
        (dv_ref, halo_v, width, value_ref),
    ):
        for begin in range(0, rows, WINDOW):
            here = slice(begin, begin + WINDOW)
            parts = [tails[slot, here, at : at + width] for slot in range(slots)]
            total = in_ref[here, :] + jnp.concatenate(parts, axis=1).astype(F32)
            if begin == rows - WINDOW:
                total = total + halo.astype(F32)
            out_ref[here, :] = total.astype(BF16)
    sink_row = -(sink_ref[0:1] + far_ref[0:1])
    for place in range(sink_grad.shape[0]):
        sink_grad[place] = sink_row[0, place]


def swap(values, axis):
    return [values[0]] + [ring(values[step], axis, step) for step in range(1, len(values))]


def local(
    queries, key_states, value_states, out_grad, sink_logits, branch_start, branch_len, parent_list
):
    tok_count, head_count = lax.axis_size("tok"), lax.axis_size("head")
    rows = queries.shape[0]
    blocks_here = rows // WINDOW
    blocks = blocks_here * head_count
    per_slot = KV_HEADS // head_count
    width = 2 * per_slot * HEAD_DIM

    def shape(dims, kind=BF16):
        return jax.ShapeDtypeStruct(dims, kind)

    def far(value):
        return pltpu.with_memory_space_constraint(value, pltpu.HBM)

    def close(value):
        return pltpu.with_memory_space_constraint(value, pltpu.VMEM)

    *slots, halo_out, keys, values = pl.pallas_call(
        pack_kernel,
        out_shape=(shape((rows, width)),) * head_count
        + (shape((PAIRS, WINDOW, 256)),)
        + (pltpu.VMEM(key_states.shape, BF16),) * 2,
        in_specs=[HBM] * 3,
        out_specs=(VMEM,) * (head_count + 3),
        scratch_shapes=[
            pltpu.SMEM(sink_logits.shape, F32),
            pltpu.SemaphoreType.DMA((3,)),
        ],
        compiler_params=PARAMS,
        name="pack",
    )(far(sink_logits), far(key_states), far(value_states))
    spread = swap(slots, "head")
    halo = shift(halo_out, "head", 1)
    plan = pl.pallas_call(
        functools.partial(plan_kernel, tok_count, blocks, blocks_here),
        out_shape=pltpu.VMEM((8, 128), jnp.int32),
        in_specs=[SMEM] * 3,
        out_specs=VMEM,
        compiler_params=PARAMS,
        name="plan",
    )(far(branch_start), far(branch_len), far(parent_list.T))
    plan = close(plan)
    *chosen, sinks = pl.pallas_call(
        choose_kernel,
        out_shape=(shape((WINDOW, width)),) * LAG + (shape((KV_HEADS * GROUP, 128), F32),),
        in_specs=[VMEM] * (1 + head_count),
        out_specs=(VMEM,) * (LAG + 1),
        compiler_params=PARAMS,
        name="choose",
    )(plan, *spread)
    arrived = [ring(chosen[LAG - s], "tok", s) for s in range(LAG, 0, -1)]
    queries, out_grad, _ = lax.optimization_barrier((queries, out_grad, sinks))
    near_queries, near_grad = pl.pallas_call(
        stage_kernel,
        out_shape=(pltpu.VMEM(queries.shape, BF16),) * 2,
        in_specs=[HBM] * 2,
        out_specs=(VMEM,) * 2,
        scratch_shapes=[pltpu.SemaphoreType.DMA((2,))],
        compiler_params=PARAMS,
        name="stage",
    )(far(queries), far(out_grad))
    *arrived, near_queries, near_grad = lax.optimization_barrier(
        (*arrived, near_queries, near_grad)
    )
    quarter = pl.pallas_call(
        arrive_kernel,
        out_shape=shape((WINDOW, width)),
        in_specs=[VMEM] * (1 + LAG),
        out_specs=VMEM,
        compiler_params=PARAMS,
        name="arrive",
    )(plan, *arrived)
    tails = swap([quarter] * head_count, "head")

    def attend(steps, pairs, offset, halo, joined):
        inputs = (
            sinks,
            close(near_queries),
            close(near_grad),
            close(keys),
            close(values),
            halo,
            *(tails[step] for step in steps),
            *(close(value) for value in joined),
        )
        base = 1 + len(inputs) - len(joined)
        return pl.pallas_call(
            functools.partial(
                attend_kernel,
                blocks_here,
                head_count,
                steps,
                offset,
                pairs,
                len(joined),
            ),
            out_shape=(
                pltpu.VMEM(queries.shape, BF16),
                pltpu.VMEM(queries.shape, BF16),
                pltpu.VMEM(key_states.shape, F32),
                pltpu.VMEM(key_states.shape, F32),
                pltpu.VMEM((PAIRS, WINDOW, 256), BF16),
            )
            + (shape((WINDOW, width)),) * len(steps),
            in_specs=[VMEM] * (1 + len(inputs)),
            out_specs=(VMEM,) * (5 + len(steps)),
            scratch_shapes=[
                pltpu.VMEM((head_count, WINDOW, width), BF16),
                pltpu.VMEM((WINDOW, 256), F32),
                pltpu.VMEM((2 * GROUP, WINDOW), F32),
                pltpu.VMEM((6 * HALF, 1024), BF16),
                pltpu.VMEM((6 * HALF, 1024), BF16),
            ],
            input_output_aliases={base + place: place for place in range(len(joined))},
            compiler_params=PARAMS,
            name="attend",
        )(plan, *inputs)

    if per_slot == 2:
        *joined, own_tail = attend((0,), 1, 0, spread[1], ())
        *results, tail_1, tail_2, tail_3 = attend((1, 2, 3), PAIRS - 1, 1, halo, joined)
        dtail = [own_tail, tail_1, tail_2, tail_3]
    else:
        results = attend(tuple(range(head_count)), PAIRS, None, halo, ())
        results, dtail = results[:5], list(results[5:])
    attended, query_grad, dk, dv, dhalo = results
    parts = swap(dtail, "head")
    quarter_grad = pl.pallas_call(
        gather_kernel,
        out_shape=shape((WINDOW, width)),
        in_specs=[VMEM] * head_count,
        out_specs=VMEM,
        compiler_params=PARAMS,
        name="gather",
    )(*parts)
    def flush(value):
        return pl.pallas_call(
            stage_kernel,
            out_shape=pltpu.HBM(value.shape, BF16),
            in_specs=[VMEM],
            out_specs=HBM,
            scratch_shapes=[pltpu.SemaphoreType.DMA((1,))],
            compiler_params=PARAMS,
            name="flush",
        )(close(value))

    returned = [ring(quarter_grad, "tok", -s) for s in range(LAG, 0, -1)][::-1]
    attended, _ = lax.optimization_barrier((attended, quarter_grad))
    attended = flush(attended)
    attended, *returned = lax.optimization_barrier((attended, *returned))
    halo_back = shift(dhalo, "head", -1)
    *landed, sink_near = pl.pallas_call(
        functools.partial(land_kernel, blocks),
        out_shape=(shape((rows, width)),) * head_count + (shape((8, 128), F32),),
        in_specs=[VMEM] * (LAG + 2),
        out_specs=(VMEM,) * (head_count + 1),
        compiler_params=PARAMS,
        name="land",
    )(plan, quarter_grad, *returned)
    tails_back = swap(landed, "head")
    query_grad, _ = lax.optimization_barrier((query_grad, sink_near))
    query_grad = flush(query_grad)
    span = LAG + 1
    while 2 * span < tok_count:
        sink_near = sink_near + ring(sink_near, "tok", -span)
        span *= 2
    sink_far = ring(sink_near, "tok", -span)
    key_grad, value_grad, sink_grad = pl.pallas_call(
        total_kernel,
        out_shape=(
            shape(key_states.shape),
            shape(value_states.shape),
            shape(sink_logits.shape, F32),
        ),
        in_specs=[VMEM] * (5 + head_count),
        out_specs=(VMEM, VMEM, SMEM),
        scratch_shapes=[pltpu.VMEM((head_count, rows, width), BF16)],
        compiler_params=PARAMS,
        name="total",
    )(dk, dv, halo_back, sink_near, sink_far, *tails_back)
    return attended, query_grad, key_grad, value_grad, sink_grad


def solution(mesh):
    rows = P(("tok", "head"), None)
    return jax.shard_map(
        local,
        mesh=mesh,
        in_specs=(rows, rows, rows, rows, P("head"), P(), P(), P()),
        out_specs=(rows, rows, rows, rows, P("head")),
        check_vma=False,
    )
```

```python
import functools

import jax
import jax.numpy as jnp
from jax import lax
from jax.experimental import pallas as pl
from jax.experimental.pallas import tpu as pltpu
from jax.sharding import PartitionSpec as P

HEAD_DIM = 64
KV_HEADS = 8
GROUP = 8
WINDOW = 128
HALF = WINDOW // 2
LAG = 3
BR_DEV = 2
PAIRS = KV_HEADS // 2
FACTOR = 0.125
LOW = -1e30
BF16 = jnp.bfloat16
F32 = jnp.float32

SMEM = pl.BlockSpec(memory_space=pltpu.SMEM)
VMEM = pl.BlockSpec(memory_space=pltpu.VMEM)
HBM = pl.BlockSpec(memory_space=pltpu.HBM)
PARAMS = pltpu.CompilerParams(vmem_limit_bytes=24 * 1024 * 1024)


def shift(value, axis, steps):
    count = lax.axis_size(axis)
    leading, last = (max(0, -steps), min(count, count - steps))
    return lax.ppermute(value, axis, [(source, source + steps) for source in range(leading, last)])


def ring(value, axis, steps):
    count = lax.axis_size(axis)
    return lax.ppermute(value, axis, [(source, (source + steps) % count) for source in range(count)])


def with_row(tile, row):
    high = row.astype(BF16).astype(F32)
    middle = (row - high).astype(BF16).astype(F32)
    low = row - high - middle
    packed = high + pltpu.roll(middle, 32, 1) + pltpu.roll(low, 64, 1)
    place = lax.broadcasted_iota(jnp.int32, (16, 128), 0)
    top = jnp.where(place == 0, packed, tile[:16, :128].astype(F32)).astype(BF16)
    if tile.shape[1] > 128:
        top = jnp.concatenate([top, tile[:16, 128:]], axis=1)
    return jnp.concatenate([top, tile[16:]], axis=0)


def row_join(top):
    packed = top[0:1, :128].astype(F32)
    row = packed + pltpu.roll(packed, 96, 1) + pltpu.roll(packed, 64, 1)
    return jnp.where(lax.broadcasted_iota(jnp.int32, (1, 128), 1) < 32, row, 0.0)


def child_tail(starts, parents, tok, distance, tok_count, blocks):
    child = jnp.minimum(tok + distance, tok_count - 1) * BR_DEV
    parent = parents[0, child]
    safe = jnp.maximum(parent, 0)
    valid = (tok + distance < tok_count) & (parent >= 0) & (safe // BR_DEV == tok)
    place = (starts[safe] + parents[1, child]) // WINDOW - tok * blocks
    return valid, jnp.where(valid, place, 0)


def block_state(starts, lengths, parents, tok, block):
    position = block * WINDOW
    alive, opening = jnp.bool_(False), jnp.bool_(False)
    for branch in range(BR_DEV):
        start = starts[tok * BR_DEV + branch]
        length = lengths[tok * BR_DEV + branch]
        alive = alive | ((start <= position) & (position < start + length))
        opening = opening | (start == position)
    has_tail = parents[0, tok * BR_DEV] >= 0
    return alive, opening, jnp.logical_not(opening) | has_tail


def plan_kernel(tok_count, blocks, blocks_here, starts, lengths, parents, plan_ref):
    tok, head = lax.axis_index("tok"), lax.axis_index("head")
    values = []
    for distance in range(1, LAG + 1):
        values += child_tail(starts, parents, tok, distance, tok_count, blocks)
    parent = parents[0, tok * BR_DEV]
    values.append(jnp.where(parent >= 0, tok - jnp.maximum(parent, 0) // BR_DEV, 1))
    for block in range(blocks_here):
        number = tok * blocks + head * blocks_here + block
        values += block_state(starts, lengths, parents, tok, number)
    lane = lax.broadcasted_iota(jnp.int32, plan_ref.shape, 1)
    plan = jnp.zeros(plan_ref.shape, jnp.int32)
    for place, value in enumerate(values):
        plan = jnp.where(lane == place, value.astype(jnp.int32), plan)
    plan_ref[...] = plan


def planned_tail(plan_ref, distance):
    row = plan_ref[0:1, :]
    return row[0, 2 * distance - 2] != 0, row[0, 2 * distance - 1]


def planned_source(plan_ref):
    return plan_ref[0:1, :][0, 2 * LAG]


def planned_block(plan_ref, block):
    row = plan_ref[0:1, :]
    return tuple(row[0, 2 * LAG + 1 + 3 * block + place] for place in range(3))


def take(ref, slot, width):
    if width % 128 == 0:
        return ref[:, pl.ds(pl.multiple_of(slot * width, width), width)]
    value = ref[:, :width]
    for other in range(1, ref.shape[1] // width):
        value = jnp.where(slot == other, ref[:, other * width : (other + 1) * width], value)
    return value


def pack_kernel(sink_hbm, key_hbm, value_hbm, *refs):
    *slot_refs, halo_ref, keys, values, sinks, sems = refs
    copies = [
        pltpu.make_async_copy(source, target, sems.at[place])
        for place, (source, target) in enumerate(
            ((sink_hbm, sinks), (key_hbm, keys), (value_hbm, values))
        )
    ]
    for copy in copies:
        copy.start()
    for copy in copies:
        copy.wait()
    slots, rows = len(slot_refs), keys.shape[0]
    head = lax.axis_index("head")
    width = KV_HEADS * HEAD_DIM // slots
    lane = lax.broadcasted_iota(jnp.int32, (1, 128), 1)
    sink_row = jnp.zeros((1, 128), F32)
    for place in range(sinks.shape[0]):
        sink_row = jnp.where(lane == place, sinks[place], sink_row)
    for step, slot_ref in enumerate(slot_refs):
        slot = lax.rem(head + step, slots)
        both = jnp.concatenate([take(keys, slot, width), take(values, slot, width)], axis=1)
        slot_ref[...] = with_row(both, sink_row)
    for pair in range(PAIRS):
        lanes = slice(pair * 128, (pair + 1) * 128)
        last = slice(rows - WINDOW, rows)
        halo_ref[pair] = jnp.concatenate([keys[last, lanes], values[last, lanes]], axis=1)


def choose_kernel(plan_ref, *refs):
    slots = len(refs) - LAG - 1
    slot_refs, out_refs, sink_ref = refs[:slots], refs[slots:-1], refs[-1]
    head = lax.axis_index("head")
    rows = slot_refs[0].shape[0]
    blocks_here = rows // WINDOW
    heads = sink_ref.shape[0] // slots
    for distance, out_ref in zip(range(LAG, 0, -1), out_refs):
        _, place = planned_tail(plan_ref, distance)
        begin = pl.multiple_of(place % blocks_here * WINDOW, WINDOW)
        wanted = lax.rem(head - place // blocks_here + slots, slots)
        for step, slot_ref in enumerate(slot_refs):

            @pl.when(wanted == step)
            def _(out_ref=out_ref, slot_ref=slot_ref, begin=begin):
                out_ref[...] = slot_ref[pl.ds(begin, WINDOW), :]

    for step, slot_ref in enumerate(slot_refs):
        source = lax.rem(head - step + slots, slots)
        sink_row = row_join(slot_ref[:16])
        turned = jnp.broadcast_to(sink_row, (128, 128)).T
        sink_ref[pl.ds(pl.multiple_of(source * heads, heads), heads), :] = turned[:heads]


def arrive_kernel(plan_ref, *refs):
    *in_refs, out_ref = refs
    mine = planned_source(plan_ref)
    for distance, in_ref in zip(range(LAG, 0, -1), in_refs):

        @pl.when(mine == distance)
        def _(in_ref=in_ref):
            out_ref[...] = in_ref[...]


def stage_kernel(*refs):
    *arrays, sems = refs
    half = len(arrays) // 2
    copies = [
        pltpu.make_async_copy(source, target, sems.at[place])
        for place, (source, target) in enumerate(zip(arrays[:half], arrays[half:]))
    ]
    for copy in copies:
        copy.start()
    for copy in copies:
        copy.wait()


def attend_kernel(blocks_here, slots, steps, offset, pairs, joins, *refs):
    inputs, refs = refs[:7], refs[7:]
    tail_refs, refs = refs[: len(steps)], refs[len(steps) + joins :]
    outputs, refs = refs[:5], refs[5:]
    dtail_refs, refs = refs[: len(steps)], refs[len(steps) :]
    tails, *scratch = refs
    head = lax.axis_index("head")
    states = [planned_block(inputs[0], block) for block in range(blocks_here)]
    for step, tail_ref in zip(steps, tail_refs):
        tails[lax.rem(head - step + slots, slots)] = tail_ref[...]

    def step(place, carry):
        pair = place // blocks_here
        if offset is not None:
            pair = lax.rem(head + pair + offset, PAIRS)
        block = place % blocks_here
        state = states[0]
        for other in range(1, blocks_here):
            state = [jnp.where(block == other, *two) for two in zip(states[other], state)]
        attend_block(
            blocks_here,
            slots,
            pair,
            block,
            [value != 0 for value in state],
            inputs,
            outputs,
            tails,
            tuple(zip(steps, dtail_refs)),
            scratch,
        )
        return carry

    lax.fori_loop(0, pairs * blocks_here, step, 0)


def attend_block(
    blocks_here, slots, pair, block, state, inputs, outputs, tails, dtails, scratch
):
    _, sink_ref, q_ref, g_ref, k_ref, v_ref, halo_ref = inputs
    o_ref, dq_ref, dk_ref, dv_ref, dhalo_ref = outputs
    tail_sum, sink_rows, prob2, slope2 = scratch
    per_slot = KV_HEADS // slots
    head = lax.axis_index("head")
    alive, opening, prev_ok = state
    here = pl.ds(pl.multiple_of(block * WINDOW, WINDOW), WINDOW)
    before = pl.ds(pl.multiple_of(jnp.maximum(block - 1, 0) * WINDOW, WINDOW), WINDOW)
    first = block == 0
    near = pl.ds(pl.multiple_of(pair * 128, 128), 128)
    big = pl.ds(pl.multiple_of(pair * 1024, 1024), 1024)
    q_ref, g_ref, o_ref, dq_ref = (ref.at[here, big] for ref in (q_ref, g_ref, o_ref, dq_ref))
    k_ref, v_ref, dk_ref, dv_ref = (ref.at[:, near] for ref in (k_ref, v_ref, dk_ref, dv_ref))
    sink_ref = sink_ref.at[pl.ds(pl.multiple_of(pair * 16, 16), 16)]
    dhalo_ref = dhalo_ref.at[pair]

    @pl.when(first)
    def _():
        tail_sum[...] = jnp.zeros_like(tail_sum)
        dhalo_ref[...] = jnp.zeros((WINDOW, 256), BF16)
        sink_rows[...] = jnp.zeros_like(sink_rows)

    @pl.when(jnp.logical_not(alive))
    def _():
        o_ref[...] = jnp.zeros((WINDOW, 1024), BF16)
        dq_ref[...] = jnp.zeros((WINDOW, 1024), BF16)
        dk_ref[here, :] = jnp.zeros((WINDOW, 128), F32)
        dv_ref[here, :] = jnp.zeros((WINDOW, 128), F32)

    @pl.when(alive)
    def _():
        if len(halo_ref.shape) == 2:
            halo = halo_ref[halo_ref.shape[0] - WINDOW :]
        else:
            halo = halo_ref[pair]
        if per_slot == 2:
            tail = tails[pair]
            tail_k, tail_v = tail[:, :128], tail[:, 128:]
        else:
            tail_a, tail_b = tails[2 * pair], tails[2 * pair + 1]
            tail_k = jnp.concatenate([tail_a[:, :64], tail_b[:, :64]], axis=1)
            tail_v = jnp.concatenate([tail_a[:, 64:], tail_b[:, 64:]], axis=1)
        near_k = jnp.where(first, halo[:, :128], k_ref[before, :])
        near_v = jnp.where(first, halo[:, 128:], v_ref[before, :])
        prev_k = jnp.where(opening, tail_k, near_k)
        prev_v = jnp.where(opening, tail_v, near_v)
        own_k, own_v = k_ref[here, :], v_ref[here, :]

        def halves(own, prev):
            return (
                jnp.concatenate([own[:HALF], prev[:HALF], prev[HALF:]], axis=0),
                jnp.concatenate([own[HALF:], prev[HALF:], own[:HALF]], axis=0),
            )

        left = lax.broadcasted_iota(jnp.int32, (1, 128), 1) < HALF
        low16 = left.astype(F32).astype(BF16)
        high16 = BF16(1) - low16

        def padded(seen):
            swapped = jnp.concatenate([seen[:, 64:], seen[:, :64]], axis=1)
            return (
                jnp.concatenate([seen * low16, swapped * high16], axis=0),
                jnp.concatenate([swapped * low16, seen * high16], axis=0),
            )

        seen_k = halves(own_k * BF16(FACTOR), prev_k * BF16(FACTOR))
        seen_v = halves(own_v, prev_v)
        padded_k = tuple(padded(value) for value in seen_k)
        padded_v = tuple(padded(value) for value in seen_v)
        turned_k = tuple(value.T for value in seen_k)
        turned_v = tuple(value.T for value in seen_v)
        bias = jnp.where(prev_ok, 0.0, LOW)
        key_place = lax.broadcasted_iota(jnp.int32, (HALF, 4 * HALF), 0)
        query_place = lax.broadcasted_iota(jnp.int32, (HALF, 4 * HALF), 1) & (HALF - 1)
        own = key_place <= query_place
        own16 = own.astype(F32).astype(BF16)
        turn = (((1,), (1,)), ((), ()))
        items = [(unit, half) for unit in range(2) for half in range(2)]
        seen = 3 * HALF

        def wide(index):
            return slice(index * 256, (index + 1) * 256)

        def feats(index):
            unit = items[index][0]
            return slice(unit * HEAD_DIM, (unit + 1) * HEAD_DIM)

        def corners(unit, half):
            rows = slice(half * HALF, (half + 1) * HALF)
            return [
                (rows, slice(unit * 512 + at * 128, unit * 512 + (at + 1) * 128)) for at in range(4)
            ]

        def stacked(ref, unit, half):
            return jnp.concatenate([ref[corner] for corner in corners(unit, half)], axis=0)

        def products(index):
            unit, half = items[index]
            score, dp = (
                lax.dot_general(
                    padded[half][unit],
                    stacked(ref, unit, half),
                    turn,
                    preferred_element_type=F32,
                )
                for padded, ref in ((padded_k, q_ref), (padded_v, g_ref))
            )
            parts = []
            for base in (0, seen):
                near, far = slice(base, base + HALF), slice(base + HALF, base + 2 * HALF)
                rest = slice(base + 2 * HALF, base + 3 * HALF)
                edge = jnp.where(own, score[near], score[far] + bias)
                whole = score[rest] + bias if half == 0 else score[rest]
                parts.append((edge, whole, jnp.where(own, dp[near], dp[far]), dp[rest]))
            return parts

        def weigh(index, odd, edge, whole, dp_edge, dp_whole):
            unit, half = items[index]
            base = odd * seen
            row = unit * GROUP + odd
            sink = jnp.concatenate(
                [
                    jnp.where(left, sink_ref[at : at + 1], sink_ref[at + 2 : at + 3])
                    for at in (row, row + 4)
                ],
                axis=1,
            )
            peak = jnp.max(jnp.maximum(edge, whole), axis=0, keepdims=True)
            peak = jnp.maximum(peak, sink)
            edge, whole = jnp.exp(edge - peak), jnp.exp(whole - peak)
            sink_weight = jnp.exp(sink - peak)
            inverse = 1.0 / (jnp.sum(edge + whole, axis=0, keepdims=True) + sink_weight)
            edge, whole = edge * inverse, whole * inverse
            term_edge, term_whole = edge * dp_edge, whole * dp_whole
            delta = jnp.sum(term_edge + term_whole, axis=0, keepdims=True)
            for target, at_edge, at_whole in (
                (prob2, edge, whole),
                (slope2, term_edge - edge * delta, term_whole - whole * delta),
            ):
                edge16 = at_edge.astype(BF16)
                edge_own = edge16 * own16
                target[base : base + HALF, wide(index)] = edge_own
                target[base + HALF : base + 2 * HALF, wide(index)] = edge16 - edge_own
                target[base + 2 * HALF : base + seen, wide(index)] = at_whole.astype(BF16)
            sink_term = sink_weight * inverse * delta
            for at, lanes in ((row, slice(0, 128)), (row + 4, slice(128, 256))):
                part = sink_term[:, lanes]
                sink_rows[at : at + 1] += jnp.where(left, part, 0.0)
                sink_rows[at + 2 : at + 3] += jnp.where(left, 0.0, part)

        def finish(index):
            unit, half = items[index]
            for source, across, out_ref in ((prob2, turned_v, o_ref), (slope2, turned_k, dq_ref)):
                out_t = [
                    jnp.dot(
                        across[half][feats(index)],
                        source[base : base + seen, wide(index)],
                        preferred_element_type=F32,
                    ).astype(BF16)
                    for base in (0, seen)
                ]
                out = jnp.concatenate(out_t, axis=0).T
                for at, corner in enumerate(corners(unit, half)):
                    out_ref[corner] = out[at * HALF : (at + 1) * HALF]

        def reduce(index):
            unit, half = items[index]
            parts = []
            for weights, ref in ((slope2, q_ref), (prob2, g_ref)):
                part = jnp.dot(
                    weights[:, wide(index)], stacked(ref, unit, half), preferred_element_type=F32
                )
                parts.append(jnp.where(left, part[:seen], part[seen:]))
            return parts

        def join(first_half, second_half):
            total = jnp.concatenate(
                [
                    first_half[:HALF] + second_half[2 * HALF :],
                    second_half[:HALF],
                    first_half[HALF : 2 * HALF],
                    first_half[2 * HALF :] + second_half[HALF : 2 * HALF],
                ],
                axis=0,
            )
            return total + pltpu.roll(total, HEAD_DIM, 1)

        ahead, parts = products(0), []
        for index in range(len(items)):
            now = ahead
            if index + 1 < len(items):
                ahead = products(index + 1)
            weigh(index, 0, *now[0])
            if index >= 1:
                finish(index - 1)
            weigh(index, 1, *now[1])
            parts.append(reduce(index))
        finish(len(items) - 1)
        grads = [
            [join(parts[2 * unit][place], parts[2 * unit + 1][place]) for place in range(2)]
            for unit in range(2)
        ]
        dk = jnp.where(left, grads[0][0], grads[1][0]) * FACTOR
        dv = jnp.where(left, grads[0][1], grads[1][1])
        dk_ref[here, :] = dk[:WINDOW]
        dv_ref[here, :] = dv[:WINDOW]

        @pl.when(opening & prev_ok)
        def _():
            tail_sum[:, :128] += dk[WINDOW:]
            tail_sum[:, 128:] += dv[WINDOW:]

        @pl.when(jnp.logical_not(opening) & first)
        def _():
            dhalo_ref[:, :128] = dk[WINDOW:].astype(BF16)
            dhalo_ref[:, 128:] = dv[WINDOW:].astype(BF16)

        @pl.when(jnp.logical_not(opening) & jnp.logical_not(first))
        def _():
            dk_ref[before, :] += dk[WINDOW:]
            dv_ref[before, :] += dv[WINDOW:]

    @pl.when(block == blocks_here - 1)
    def _():
        width = 2 * per_slot * HEAD_DIM
        heads = per_slot * GROUP
        total = tail_sum[...].astype(BF16)
        for part in range(2 // per_slot):
            feats = slice(part * width // 2, (part + 1) * width // 2)
            tail = jnp.concatenate([total[:, :128][:, feats], total[:, 128:][:, feats]], axis=1)
            rows = sink_rows[part * heads : (part + 1) * heads]
            rows = jnp.concatenate([rows, jnp.zeros((128 - heads, WINDOW), F32)], axis=0)
            sink_row = jnp.sum(rows.T, axis=0, keepdims=True)
            tail = with_row(tail, sink_row)
            wanted = lax.rem(pair * (2 // per_slot) + part - head + slots, slots)
            for step, dtail_ref in dtails:

                @pl.when(wanted == step)
                def _(dtail_ref=dtail_ref, tail=tail):
                    dtail_ref[...] = tail


def gather_kernel(*refs):
    *in_refs, out_ref = refs
    total, sink_row = 0.0, 0.0
    for in_ref in in_refs:
        total = total + in_ref[...].astype(F32)
        sink_row = sink_row + row_join(in_ref[:16])
    out_ref[...] = with_row(total.astype(BF16), sink_row)


def land_kernel(blocks, plan_ref, here_ref, *refs):
    head = lax.axis_index("head")
    in_refs, out_refs, sink_ref = refs[:LAG], refs[LAG:-1], refs[-1]
    slots = len(out_refs)
    blocks_here = blocks // slots
    for out_ref in out_refs:
        out_ref[...] = jnp.zeros_like(out_ref)
    sink_row = row_join(here_ref[:16])
    seen = lax.broadcasted_iota(jnp.int32, here_ref.shape, 0) > 0
    for distance, in_ref in enumerate(in_refs, 1):
        valid, place = planned_tail(plan_ref, distance)
        sink_row = sink_row + row_join(in_ref[:16])
        wanted = lax.rem(place // blocks_here - head + slots, slots)
        here = pl.ds(pl.multiple_of(place % blocks_here * WINDOW, WINDOW), WINDOW)
        for step, out_ref in enumerate(out_refs):

            @pl.when(valid & (wanted == step))
            def _(out_ref=out_ref, in_ref=in_ref, here=here):
                total = out_ref[here, :].astype(F32) + in_ref[...].astype(F32)
                out_ref[here, :] = jnp.where(seen, total, 0.0).astype(BF16)

    sink_ref[...] = jnp.broadcast_to(sink_row, sink_ref.shape)


def total_kernel(dk_ref, dv_ref, halo_ref, sink_ref, far_ref, *refs):
    *tail_refs, key_ref, value_ref, sink_grad, tails = refs
    slots, rows = len(tail_refs), dk_ref.shape[0]
    width = tails.shape[2] // 2
    head = lax.axis_index("head")
    for step, tail_ref in enumerate(tail_refs):
        tails[lax.rem(head - step + slots, slots)] = tail_ref[...]
    halo_k = jnp.concatenate([halo_ref[pair][:, :128] for pair in range(PAIRS)], axis=1)
    halo_v = jnp.concatenate([halo_ref[pair][:, 128:] for pair in range(PAIRS)], axis=1)
    for in_ref, halo, at, out_ref in (
        (dk_ref, halo_k, 0, key_ref),
        (dv_ref, halo_v, width, value_ref),
    ):
        for begin in range(0, rows, WINDOW):
            here = slice(begin, begin + WINDOW)
            parts = [tails[slot, here, at : at + width] for slot in range(slots)]
            total = in_ref[here, :] + jnp.concatenate(parts, axis=1).astype(F32)
            if begin == rows - WINDOW:
                total = total + halo.astype(F32)
            out_ref[here, :] = total.astype(BF16)
    sink_row = -(sink_ref[0:1] + far_ref[0:1])
    sink_grad[...] = sink_row[0, : sink_grad.shape[0]]


def swap(values, axis):
    return [values[0]] + [ring(values[step], axis, step) for step in range(1, len(values))]


def local(
    queries, key_states, value_states, out_grad, sink_logits, branch_start, branch_len, parent_list
):
    tok_count, head_count = lax.axis_size("tok"), lax.axis_size("head")
    rows = queries.shape[0]
    blocks_here = rows // WINDOW
    blocks = blocks_here * head_count
    per_slot = KV_HEADS // head_count
    width = 2 * per_slot * HEAD_DIM

    def shape(dims, kind=BF16):
        return jax.ShapeDtypeStruct(dims, kind)

    def far(value):
        return pltpu.with_memory_space_constraint(value, pltpu.HBM)

    def close(value):
        return pltpu.with_memory_space_constraint(value, pltpu.VMEM)

    *slots, halo_out, keys, values = pl.pallas_call(
        pack_kernel,
        out_shape=(shape((rows, width)),) * head_count
        + (shape((PAIRS, WINDOW, 256)),)
        + (pltpu.VMEM(key_states.shape, BF16),) * 2,
        in_specs=[HBM] * 3,
        out_specs=(VMEM,) * (head_count + 3),
        scratch_shapes=[
            pltpu.SMEM(sink_logits.shape, F32),
            pltpu.SemaphoreType.DMA((3,)),
        ],
        compiler_params=PARAMS,
        name="pack",
    )(far(sink_logits), far(key_states), far(value_states))
    spread = swap(slots, "head")
    halo = shift(halo_out, "head", 1)
    plan = pl.pallas_call(
        functools.partial(plan_kernel, tok_count, blocks, blocks_here),
        out_shape=pltpu.VMEM((8, 128), jnp.int32),
        in_specs=[SMEM] * 3,
        out_specs=VMEM,
        compiler_params=PARAMS,
        name="plan",
    )(far(branch_start), far(branch_len), far(parent_list.T))
    plan = close(plan)
    *chosen, sinks = pl.pallas_call(
        choose_kernel,
        out_shape=(shape((WINDOW, width)),) * LAG + (shape((KV_HEADS * GROUP, 128), F32),),
        in_specs=[VMEM] * (1 + head_count),
        out_specs=(VMEM,) * (LAG + 1),
        compiler_params=PARAMS,
        name="choose",
    )(plan, *spread)
    arrived = [ring(chosen[LAG - s], "tok", s) for s in range(LAG, 0, -1)]
    queries, out_grad, _ = lax.optimization_barrier((queries, out_grad, sinks))
    near_queries, near_grad = pl.pallas_call(
        stage_kernel,
        out_shape=(pltpu.VMEM(queries.shape, BF16),) * 2,
        in_specs=[HBM] * 2,
        out_specs=(VMEM,) * 2,
        scratch_shapes=[pltpu.SemaphoreType.DMA((2,))],
        compiler_params=PARAMS,
        name="stage",
    )(far(queries), far(out_grad))
    *arrived, near_queries, near_grad = lax.optimization_barrier(
        (*arrived, near_queries, near_grad)
    )
    quarter = pl.pallas_call(
        arrive_kernel,
        out_shape=shape((WINDOW, width)),
        in_specs=[VMEM] * (1 + LAG),
        out_specs=VMEM,
        compiler_params=PARAMS,
        name="arrive",
    )(plan, *arrived)
    tails = swap([quarter] * head_count, "head")

    def attend(steps, pairs, offset, halo, joined):
        inputs = (
            sinks,
            close(near_queries),
            close(near_grad),
            close(keys),
            close(values),
            halo,
            *(tails[step] for step in steps),
            *(close(value) for value in joined),
        )
        base = 1 + len(inputs) - len(joined)
        return pl.pallas_call(
            functools.partial(
                attend_kernel,
                blocks_here,
                head_count,
                steps,
                offset,
                pairs,
                len(joined),
            ),
            out_shape=(
                pltpu.VMEM(queries.shape, BF16),
                pltpu.VMEM(queries.shape, BF16),
                pltpu.VMEM(key_states.shape, F32),
                pltpu.VMEM(key_states.shape, F32),
                pltpu.VMEM((PAIRS, WINDOW, 256), BF16),
            )
            + (shape((WINDOW, width)),) * len(steps),
            in_specs=[VMEM] * (1 + len(inputs)),
            out_specs=(VMEM,) * (5 + len(steps)),
            scratch_shapes=[
                pltpu.VMEM((head_count, WINDOW, width), BF16),
                pltpu.VMEM((WINDOW, 256), F32),
                pltpu.VMEM((2 * GROUP, WINDOW), F32),
                pltpu.VMEM((6 * HALF, 1024), BF16),
                pltpu.VMEM((6 * HALF, 1024), BF16),
            ],
            input_output_aliases={base + place: place for place in range(len(joined))},
            compiler_params=PARAMS,
            name="attend",
        )(plan, *inputs)

    if per_slot == 2:
        *joined, own_tail = attend((0,), 1, 0, spread[1], ())
        *results, tail_1, tail_2, tail_3 = attend((1, 2, 3), PAIRS - 1, 1, halo, joined)
        dtail = [own_tail, tail_1, tail_2, tail_3]
    else:
        results = attend(tuple(range(head_count)), PAIRS, None, halo, ())
        results, dtail = results[:5], list(results[5:])
    attended, query_grad, dk, dv, dhalo = results
    parts = swap(dtail, "head")
    quarter_grad = pl.pallas_call(
        gather_kernel,
        out_shape=shape((WINDOW, width)),
        in_specs=[VMEM] * head_count,
        out_specs=VMEM,
        compiler_params=PARAMS,
        name="gather",
    )(*parts)
    def flush(value):
        return pl.pallas_call(
            stage_kernel,
            out_shape=pltpu.HBM(value.shape, BF16),
            in_specs=[VMEM],
            out_specs=HBM,
            scratch_shapes=[pltpu.SemaphoreType.DMA((1,))],
            compiler_params=PARAMS,
            name="flush",
        )(close(value))

    returned = [ring(quarter_grad, "tok", -s) for s in range(LAG, 0, -1)][::-1]
    attended, _ = lax.optimization_barrier((attended, quarter_grad))
    attended = flush(attended)
    attended, *returned = lax.optimization_barrier((attended, *returned))
    halo_back = shift(dhalo, "head", -1)
    *landed, sink_near = pl.pallas_call(
        functools.partial(land_kernel, blocks),
        out_shape=(shape((rows, width)),) * head_count + (shape((8, 128), F32),),
        in_specs=[VMEM] * (LAG + 2),
        out_specs=(VMEM,) * (head_count + 1),
        compiler_params=PARAMS,
        name="land",
    )(plan, quarter_grad, *returned)
    tails_back = swap(landed, "head")
    query_grad, _ = lax.optimization_barrier((query_grad, sink_near))
    query_grad = flush(query_grad)
    span = LAG + 1
    while 2 * span < tok_count:
        sink_near = sink_near + ring(sink_near, "tok", -span)
        span *= 2
    sink_far = ring(sink_near, "tok", -span)
    key_grad, value_grad, sink_grad = pl.pallas_call(
        total_kernel,
        out_shape=(
            shape(key_states.shape),
            shape(value_states.shape),
            shape(sink_logits.shape, F32),
        ),
        in_specs=[VMEM] * (5 + head_count),
        out_specs=(VMEM,) * 3,
        scratch_shapes=[pltpu.VMEM((head_count, rows, width), BF16)],
        compiler_params=PARAMS,
        name="total",
    )(dk, dv, halo_back, sink_near, sink_far, *tails_back)
    return attended, query_grad, key_grad, value_grad, sink_grad


def solution(mesh):
    rows = P(("tok", "head"), None)
    return jax.shard_map(
        local,
        mesh=mesh,
        in_specs=(rows, rows, rows, rows, P("head"), P(), P(), P()),
        out_specs=(rows, rows, rows, rows, P("head")),
        check_vma=False,
    )
```

```python
import functools

import jax
import jax.numpy as jnp
from jax import lax
from jax.experimental import pallas as pl
from jax.experimental.pallas import tpu as pltpu
from jax.sharding import PartitionSpec as P

HEAD_DIM = 64
KV_HEADS = 8
GROUP = 8
WINDOW = 128
HALF = WINDOW // 2
LAG = 3
BR_DEV = 2
PAIRS = KV_HEADS // 2
FACTOR = 0.125
LOW = -1e30
BF16 = jnp.bfloat16
F32 = jnp.float32

SMEM = pl.BlockSpec(memory_space=pltpu.SMEM)
VMEM = pl.BlockSpec(memory_space=pltpu.VMEM)
HBM = pl.BlockSpec(memory_space=pltpu.HBM)
PARAMS = pltpu.CompilerParams(vmem_limit_bytes=24 * 1024 * 1024)


def shift(value, axis, steps):
    count = lax.axis_size(axis)
    leading, last = (max(0, -steps), min(count, count - steps))
    return lax.ppermute(value, axis, [(source, source + steps) for source in range(leading, last)])


def ring(value, axis, steps):
    count = lax.axis_size(axis)
    return lax.ppermute(value, axis, [(source, (source + steps) % count) for source in range(count)])


def with_row(tile, row):
    high = row.astype(BF16).astype(F32)
    middle = (row - high).astype(BF16).astype(F32)
    low = row - high - middle
    packed = high + pltpu.roll(middle, 32, 1) + pltpu.roll(low, 64, 1)
    place = lax.broadcasted_iota(jnp.int32, (16, 128), 0)
    top = jnp.where(place == 0, packed, tile[:16, :128].astype(F32)).astype(BF16)
    if tile.shape[1] > 128:
        top = jnp.concatenate([top, tile[:16, 128:]], axis=1)
    return jnp.concatenate([top, tile[16:]], axis=0)


def row_join(top):
    packed = top[0:1, :128].astype(F32)
    row = packed + pltpu.roll(packed, 96, 1) + pltpu.roll(packed, 64, 1)
    return jnp.where(lax.broadcasted_iota(jnp.int32, (1, 128), 1) < 32, row, 0.0)


def child_tail(starts, parents, tok, distance, tok_count, blocks):
    child = jnp.minimum(tok + distance, tok_count - 1) * BR_DEV
    parent = parents[0, child]
    safe = jnp.maximum(parent, 0)
    valid = (tok + distance < tok_count) & (parent >= 0) & (safe // BR_DEV == tok)
    place = (starts[safe] + parents[1, child]) // WINDOW - tok * blocks
    return valid, jnp.where(valid, place, 0)


def block_state(starts, lengths, parents, tok, block):
    position = block * WINDOW
    alive, opening = jnp.bool_(False), jnp.bool_(False)
    for branch in range(BR_DEV):
        start = starts[tok * BR_DEV + branch]
        length = lengths[tok * BR_DEV + branch]
        alive = alive | ((start <= position) & (position < start + length))
        opening = opening | (start == position)
    has_tail = parents[0, tok * BR_DEV] >= 0
    return alive, opening, jnp.logical_not(opening) | has_tail


def plan_kernel(tok_count, blocks, blocks_here, starts, lengths, parents, plan_ref):
    tok, head = lax.axis_index("tok"), lax.axis_index("head")
    values = []
    for distance in range(1, LAG + 1):
        values += child_tail(starts, parents, tok, distance, tok_count, blocks)
    parent = parents[0, tok * BR_DEV]
    values.append(jnp.where(parent >= 0, tok - jnp.maximum(parent, 0) // BR_DEV, 1))
    for block in range(blocks_here):
        number = tok * blocks + head * blocks_here + block
        values += block_state(starts, lengths, parents, tok, number)
    lane = lax.broadcasted_iota(jnp.int32, plan_ref.shape, 1)
    plan = jnp.zeros(plan_ref.shape, jnp.int32)
    for place, value in enumerate(values):
        plan = jnp.where(lane == place, value.astype(jnp.int32), plan)
    plan_ref[...] = plan


def planned_tail(plan_ref, distance):
    row = plan_ref[0:1, :]
    return row[0, 2 * distance - 2] != 0, row[0, 2 * distance - 1]


def planned_source(plan_ref):
    return plan_ref[0:1, :][0, 2 * LAG]


def planned_block(plan_ref, block):
    row = plan_ref[0:1, :]
    return tuple(row[0, 2 * LAG + 1 + 3 * block + place] for place in range(3))


def take(ref, slot, width):
    if width % 128 == 0:
        return ref[:, pl.ds(pl.multiple_of(slot * width, width), width)]
    value = ref[:, :width]
    for other in range(1, ref.shape[1] // width):
        value = jnp.where(slot == other, ref[:, other * width : (other + 1) * width], value)
    return value


def pack_kernel(sink_hbm, key_hbm, value_hbm, *refs):
    *slot_refs, halo_ref, keys, values, sinks, sems = refs
    copies = [
        pltpu.make_async_copy(source, target, sems.at[place])
        for place, (source, target) in enumerate(
            ((sink_hbm, sinks), (key_hbm, keys), (value_hbm, values))
        )
    ]
    for copy in copies:
        copy.start()
    for copy in copies:
        copy.wait()
    slots, rows = len(slot_refs), keys.shape[0]
    head = lax.axis_index("head")
    width = KV_HEADS * HEAD_DIM // slots
    lane = lax.broadcasted_iota(jnp.int32, (1, 128), 1)
    sink_row = jnp.zeros((1, 128), F32)
    for place in range(sinks.shape[0]):
        sink_row = jnp.where(lane == place, sinks[place], sink_row)
    for step, slot_ref in enumerate(slot_refs):
        slot = lax.rem(head + step, slots)
        both = jnp.concatenate([take(keys, slot, width), take(values, slot, width)], axis=1)
        slot_ref[...] = with_row(both, sink_row)
    for pair in range(PAIRS):
        lanes = slice(pair * 128, (pair + 1) * 128)
        last = slice(rows - WINDOW, rows)
        halo_ref[pair] = jnp.concatenate([keys[last, lanes], values[last, lanes]], axis=1)


def choose_kernel(plan_ref, *refs):
    slots = len(refs) - LAG
    slot_refs, out_refs = refs[:slots], refs[slots:]
    head = lax.axis_index("head")
    rows = slot_refs[0].shape[0]
    blocks_here = rows // WINDOW
    for distance, out_ref in zip(range(LAG, 0, -1), out_refs):
        _, place = planned_tail(plan_ref, distance)
        begin = pl.multiple_of(place % blocks_here * WINDOW, WINDOW)
        wanted = lax.rem(head - place // blocks_here + slots, slots)
        for step, slot_ref in enumerate(slot_refs):

            @pl.when(wanted == step)
            def _(out_ref=out_ref, slot_ref=slot_ref, begin=begin):
                out_ref[...] = slot_ref[pl.ds(begin, WINDOW), :]


def sinks_kernel(*refs):
    *slot_refs, sink_ref = refs
    slots = len(slot_refs)
    head = lax.axis_index("head")
    heads = sink_ref.shape[0] // slots
    for step, slot_ref in enumerate(slot_refs):
        source = lax.rem(head - step + slots, slots)
        sink_row = row_join(slot_ref[:16])
        turned = jnp.broadcast_to(sink_row, (128, 128)).T
        sink_ref[pl.ds(pl.multiple_of(source * heads, heads), heads), :] = turned[:heads]


def arrive_kernel(plan_ref, *refs):
    *in_refs, out_ref = refs
    mine = planned_source(plan_ref)
    for distance, in_ref in zip(range(LAG, 0, -1), in_refs):

        @pl.when(mine == distance)
        def _(in_ref=in_ref):
            out_ref[...] = in_ref[...]


def stage_kernel(*refs):
    *arrays, sems = refs
    half = len(arrays) // 2
    copies = [
        pltpu.make_async_copy(source, target, sems.at[place])
        for place, (source, target) in enumerate(zip(arrays[:half], arrays[half:]))
    ]
    for copy in copies:
        copy.start()
    for copy in copies:
        copy.wait()


def attend_kernel(blocks_here, slots, steps, offset, pairs, joins, *refs):
    inputs, refs = refs[:7], refs[7:]
    tail_refs, refs = refs[: len(steps)], refs[len(steps) + joins :]
    outputs, refs = refs[:5], refs[5:]
    dtail_refs, refs = refs[: len(steps)], refs[len(steps) :]
    tails, *scratch = refs
    head = lax.axis_index("head")
    states = [planned_block(inputs[0], block) for block in range(blocks_here)]
    for step, tail_ref in zip(steps, tail_refs):
        tails[lax.rem(head - step + slots, slots)] = tail_ref[...]

    def step(place, carry):
        pair = place // blocks_here
        if offset is not None:
            pair = lax.rem(head + pair + offset, PAIRS)
        block = place % blocks_here
        state = states[0]
        for other in range(1, blocks_here):
            state = [jnp.where(block == other, *two) for two in zip(states[other], state)]
        attend_block(
            blocks_here,
            slots,
            pair,
            block,
            [value != 0 for value in state],
            inputs,
            outputs,
            tails,
            tuple(zip(steps, dtail_refs)),
            scratch,
        )
        return carry

    lax.fori_loop(0, pairs * blocks_here, step, 0)


def attend_block(
    blocks_here, slots, pair, block, state, inputs, outputs, tails, dtails, scratch
):
    _, sink_ref, q_ref, g_ref, k_ref, v_ref, halo_ref = inputs
    o_ref, dq_ref, dk_ref, dv_ref, dhalo_ref = outputs
    tail_sum, sink_rows, prob2, slope2 = scratch
    per_slot = KV_HEADS // slots
    head = lax.axis_index("head")
    alive, opening, prev_ok = state
    here = pl.ds(pl.multiple_of(block * WINDOW, WINDOW), WINDOW)
    before = pl.ds(pl.multiple_of(jnp.maximum(block - 1, 0) * WINDOW, WINDOW), WINDOW)
    first = block == 0
    near = pl.ds(pl.multiple_of(pair * 128, 128), 128)
    big = pl.ds(pl.multiple_of(pair * 1024, 1024), 1024)
    q_ref, g_ref, o_ref, dq_ref = (ref.at[here, big] for ref in (q_ref, g_ref, o_ref, dq_ref))
    k_ref, v_ref, dk_ref, dv_ref = (ref.at[:, near] for ref in (k_ref, v_ref, dk_ref, dv_ref))
    sink_ref = sink_ref.at[pl.ds(pl.multiple_of(pair * 16, 16), 16)]
    dhalo_ref = dhalo_ref.at[pair]

    @pl.when(first)
    def _():
        tail_sum[...] = jnp.zeros_like(tail_sum)
        dhalo_ref[...] = jnp.zeros((WINDOW, 256), BF16)
        sink_rows[...] = jnp.zeros_like(sink_rows)

    @pl.when(jnp.logical_not(alive))
    def _():
        o_ref[...] = jnp.zeros((WINDOW, 1024), BF16)
        dq_ref[...] = jnp.zeros((WINDOW, 1024), BF16)
        dk_ref[here, :] = jnp.zeros((WINDOW, 128), F32)
        dv_ref[here, :] = jnp.zeros((WINDOW, 128), F32)

    @pl.when(alive)
    def _():
        if len(halo_ref.shape) == 2:
            halo = halo_ref[halo_ref.shape[0] - WINDOW :]
        else:
            halo = halo_ref[pair]
        if per_slot == 2:
            tail = tails[pair]
            tail_k, tail_v = tail[:, :128], tail[:, 128:]
        else:
            tail_a, tail_b = tails[2 * pair], tails[2 * pair + 1]
            tail_k = jnp.concatenate([tail_a[:, :64], tail_b[:, :64]], axis=1)
            tail_v = jnp.concatenate([tail_a[:, 64:], tail_b[:, 64:]], axis=1)
        near_k = jnp.where(first, halo[:, :128], k_ref[before, :])
        near_v = jnp.where(first, halo[:, 128:], v_ref[before, :])
        prev_k = jnp.where(opening, tail_k, near_k)
        prev_v = jnp.where(opening, tail_v, near_v)
        own_k, own_v = k_ref[here, :], v_ref[here, :]

        def halves(own, prev):
            return (
                jnp.concatenate([own[:HALF], prev[:HALF], prev[HALF:]], axis=0),
                jnp.concatenate([own[HALF:], prev[HALF:], own[:HALF]], axis=0),
            )

        left = lax.broadcasted_iota(jnp.int32, (1, 128), 1) < HALF
        low16 = left.astype(F32).astype(BF16)
        high16 = BF16(1) - low16

        def padded(seen):
            swapped = jnp.concatenate([seen[:, 64:], seen[:, :64]], axis=1)
            return (
                jnp.concatenate([seen * low16, swapped * high16], axis=0),
                jnp.concatenate([swapped * low16, seen * high16], axis=0),
            )

        seen_k = halves(own_k * BF16(FACTOR), prev_k * BF16(FACTOR))
        seen_v = halves(own_v, prev_v)
        padded_k = tuple(padded(value) for value in seen_k)
        padded_v = tuple(padded(value) for value in seen_v)
        turned_k = tuple(value.T for value in seen_k)
        turned_v = tuple(value.T for value in seen_v)
        bias = jnp.where(prev_ok, 0.0, LOW)
        key_place = lax.broadcasted_iota(jnp.int32, (HALF, 4 * HALF), 0)
        query_place = lax.broadcasted_iota(jnp.int32, (HALF, 4 * HALF), 1) & (HALF - 1)
        own = key_place <= query_place
        own16 = own.astype(F32).astype(BF16)
        turn = (((1,), (1,)), ((), ()))
        items = [(unit, half) for unit in range(2) for half in range(2)]
        seen = 3 * HALF

        def wide(index):
            return slice(index * 256, (index + 1) * 256)

        def feats(index):
            unit = items[index][0]
            return slice(unit * HEAD_DIM, (unit + 1) * HEAD_DIM)

        def corners(unit, half):
            rows = slice(half * HALF, (half + 1) * HALF)
            return [
                (rows, slice(unit * 512 + at * 128, unit * 512 + (at + 1) * 128)) for at in range(4)
            ]

        def stacked(ref, unit, half):
            return jnp.concatenate([ref[corner] for corner in corners(unit, half)], axis=0)

        def products(index):
            unit, half = items[index]
            score, dp = (
                lax.dot_general(
                    padded[half][unit],
                    stacked(ref, unit, half),
                    turn,
                    preferred_element_type=F32,
                )
                for padded, ref in ((padded_k, q_ref), (padded_v, g_ref))
            )
            parts = []
            for base in (0, seen):
                near, far = slice(base, base + HALF), slice(base + HALF, base + 2 * HALF)
                rest = slice(base + 2 * HALF, base + 3 * HALF)
                edge = jnp.where(own, score[near], score[far] + bias)
                whole = score[rest] + bias if half == 0 else score[rest]
                parts.append((edge, whole, jnp.where(own, dp[near], dp[far]), dp[rest]))
            return parts

        def weigh(index, odd, edge, whole, dp_edge, dp_whole):
            unit, half = items[index]
            base = odd * seen
            row = unit * GROUP + odd
            sink = jnp.concatenate(
                [
                    jnp.where(left, sink_ref[at : at + 1], sink_ref[at + 2 : at + 3])
                    for at in (row, row + 4)
                ],
                axis=1,
            )
            peak = jnp.max(jnp.maximum(edge, whole), axis=0, keepdims=True)
            peak = jnp.maximum(peak, sink)
            edge, whole = jnp.exp(edge - peak), jnp.exp(whole - peak)
            sink_weight = jnp.exp(sink - peak)
            inverse = 1.0 / (jnp.sum(edge + whole, axis=0, keepdims=True) + sink_weight)
            edge, whole = edge * inverse, whole * inverse
            term_edge, term_whole = edge * dp_edge, whole * dp_whole
            delta = jnp.sum(term_edge + term_whole, axis=0, keepdims=True)
            for target, at_edge, at_whole in (
                (prob2, edge, whole),
                (slope2, term_edge - edge * delta, term_whole - whole * delta),
            ):
                edge16 = at_edge.astype(BF16)
                edge_own = edge16 * own16
                target[base : base + HALF, wide(index)] = edge_own
                target[base + HALF : base + 2 * HALF, wide(index)] = edge16 - edge_own
                target[base + 2 * HALF : base + seen, wide(index)] = at_whole.astype(BF16)
            sink_term = sink_weight * inverse * delta
            for at, lanes in ((row, slice(0, 128)), (row + 4, slice(128, 256))):
                part = sink_term[:, lanes]
                sink_rows[at : at + 1] += jnp.where(left, part, 0.0)
                sink_rows[at + 2 : at + 3] += jnp.where(left, 0.0, part)

        def finish(index):
            unit, half = items[index]
            for source, across, out_ref in ((prob2, turned_v, o_ref), (slope2, turned_k, dq_ref)):
                out_t = [
                    jnp.dot(
                        across[half][feats(index)],
                        source[base : base + seen, wide(index)],
                        preferred_element_type=F32,
                    ).astype(BF16)
                    for base in (0, seen)
                ]
                out = jnp.concatenate(out_t, axis=0).T
                for at, corner in enumerate(corners(unit, half)):
                    out_ref[corner] = out[at * HALF : (at + 1) * HALF]

        def reduce(index):
            unit, half = items[index]
            parts = []
            for weights, ref in ((slope2, q_ref), (prob2, g_ref)):
                part = jnp.dot(
                    weights[:, wide(index)], stacked(ref, unit, half), preferred_element_type=F32
                )
                parts.append(jnp.where(left, part[:seen], part[seen:]))
            return parts

        def join(first_half, second_half):
            total = jnp.concatenate(
                [
                    first_half[:HALF] + second_half[2 * HALF :],
                    second_half[:HALF],
                    first_half[HALF : 2 * HALF],
                    first_half[2 * HALF :] + second_half[HALF : 2 * HALF],
                ],
                axis=0,
            )
            return total + pltpu.roll(total, HEAD_DIM, 1)

        ahead, parts = products(0), []
        for index in range(len(items)):
            now = ahead
            weigh(index, 0, *now[0])
            if index + 1 < len(items):
                ahead = products(index + 1)
            weigh(index, 1, *now[1])
            if index >= 1:
                finish(index - 1)
            parts.append(reduce(index))
        finish(len(items) - 1)
        grads = [
            [join(parts[2 * unit][place], parts[2 * unit + 1][place]) for place in range(2)]
            for unit in range(2)
        ]
        dk = jnp.where(left, grads[0][0], grads[1][0]) * FACTOR
        dv = jnp.where(left, grads[0][1], grads[1][1])
        dk_ref[here, :] = dk[:WINDOW]
        dv_ref[here, :] = dv[:WINDOW]

        @pl.when(opening & prev_ok)
        def _():
            tail_sum[:, :128] += dk[WINDOW:]
            tail_sum[:, 128:] += dv[WINDOW:]

        @pl.when(jnp.logical_not(opening) & first)
        def _():
            dhalo_ref[:, :128] = dk[WINDOW:].astype(BF16)
            dhalo_ref[:, 128:] = dv[WINDOW:].astype(BF16)

        @pl.when(jnp.logical_not(opening) & jnp.logical_not(first))
        def _():
            dk_ref[before, :] += dk[WINDOW:]
            dv_ref[before, :] += dv[WINDOW:]

    @pl.when(block == blocks_here - 1)
    def _():
        width = 2 * per_slot * HEAD_DIM
        heads = per_slot * GROUP
        total = tail_sum[...].astype(BF16)
        for part in range(2 // per_slot):
            feats = slice(part * width // 2, (part + 1) * width // 2)
            tail = jnp.concatenate([total[:, :128][:, feats], total[:, 128:][:, feats]], axis=1)
            rows = sink_rows[part * heads : (part + 1) * heads]
            rows = jnp.concatenate([rows, jnp.zeros((128 - heads, WINDOW), F32)], axis=0)
            sink_row = jnp.sum(rows.T, axis=0, keepdims=True)
            tail = with_row(tail, sink_row)
            wanted = lax.rem(pair * (2 // per_slot) + part - head + slots, slots)
            for step, dtail_ref in dtails:

                @pl.when(wanted == step)
                def _(dtail_ref=dtail_ref, tail=tail):
                    dtail_ref[...] = tail


def gather_kernel(*refs):
    *in_refs, out_ref = refs
    total, sink_row = 0.0, 0.0
    for in_ref in in_refs:
        total = total + in_ref[...].astype(F32)
        sink_row = sink_row + row_join(in_ref[:16])
    out_ref[...] = with_row(total.astype(BF16), sink_row)


def land_kernel(blocks, plan_ref, here_ref, *refs):
    head = lax.axis_index("head")
    in_refs, out_refs, sink_ref = refs[:LAG], refs[LAG:-1], refs[-1]
    slots = len(out_refs)
    blocks_here = blocks // slots
    for out_ref in out_refs:
        out_ref[...] = jnp.zeros_like(out_ref)
    sink_row = row_join(here_ref[:16])
    seen = lax.broadcasted_iota(jnp.int32, here_ref.shape, 0) > 0
    for distance, in_ref in enumerate(in_refs, 1):
        valid, place = planned_tail(plan_ref, distance)
        sink_row = sink_row + row_join(in_ref[:16])
        wanted = lax.rem(place // blocks_here - head + slots, slots)
        here = pl.ds(pl.multiple_of(place % blocks_here * WINDOW, WINDOW), WINDOW)
        for step, out_ref in enumerate(out_refs):

            @pl.when(valid & (wanted == step))
            def _(out_ref=out_ref, in_ref=in_ref, here=here):
                total = out_ref[here, :].astype(F32) + in_ref[...].astype(F32)
                out_ref[here, :] = jnp.where(seen, total, 0.0).astype(BF16)

    sink_ref[...] = jnp.broadcast_to(sink_row, sink_ref.shape)


def total_kernel(halo_ref, dk_ref, dv_ref, sink_ref, far_ref, *refs):
    *tail_refs, key_ref, value_ref, sink_grad, tails = refs
    slots, rows = len(tail_refs), dk_ref.shape[0]
    width = tails.shape[2] // 2
    head = lax.axis_index("head")
    for step, tail_ref in enumerate(tail_refs):
        tails[lax.rem(head - step + slots, slots)] = tail_ref[...]
    halo_k = jnp.concatenate([halo_ref[pair][:, :128] for pair in range(PAIRS)], axis=1)
    halo_v = jnp.concatenate([halo_ref[pair][:, 128:] for pair in range(PAIRS)], axis=1)
    for in_ref, halo, at, out_ref in (
        (dk_ref, halo_k, 0, key_ref),
        (dv_ref, halo_v, width, value_ref),
    ):
        for begin in range(0, rows, WINDOW):
            here = slice(begin, begin + WINDOW)
            parts = [tails[slot, here, at : at + width] for slot in range(slots)]
            total = in_ref[here, :] + jnp.concatenate(parts, axis=1).astype(F32)
            if begin == rows - WINDOW:
                total = total + halo.astype(F32)
            out_ref[here, :] = total.astype(BF16)
    sink_row = -(sink_ref[0:1] + far_ref[0:1])
    sink_grad[...] = sink_row[0, : sink_grad.shape[0]]


def swap(values, axis):
    return [values[0]] + [ring(values[step], axis, step) for step in range(1, len(values))]


def local(
    queries, key_states, value_states, out_grad, sink_logits, branch_start, branch_len, parent_list
):
    tok_count, head_count = lax.axis_size("tok"), lax.axis_size("head")
    rows = queries.shape[0]
    blocks_here = rows // WINDOW
    blocks = blocks_here * head_count
    per_slot = KV_HEADS // head_count
    width = 2 * per_slot * HEAD_DIM

    def shape(dims, kind=BF16):
        return jax.ShapeDtypeStruct(dims, kind)

    def far(value):
        return pltpu.with_memory_space_constraint(value, pltpu.HBM)

    def close(value):
        return pltpu.with_memory_space_constraint(value, pltpu.VMEM)

    *slots, halo_out, keys, values = pl.pallas_call(
        pack_kernel,
        out_shape=(shape((rows, width)),) * head_count
        + (shape((PAIRS, WINDOW, 256)),)
        + (pltpu.VMEM(key_states.shape, BF16),) * 2,
        in_specs=[HBM] * 3,
        out_specs=(VMEM,) * (head_count + 3),
        scratch_shapes=[
            pltpu.SMEM(sink_logits.shape, F32),
            pltpu.SemaphoreType.DMA((3,)),
        ],
        compiler_params=PARAMS,
        name="pack",
    )(far(sink_logits), far(key_states), far(value_states))
    spread = swap(slots, "head")
    halo = shift(halo_out, "head", 1)
    plan = pl.pallas_call(
        functools.partial(plan_kernel, tok_count, blocks, blocks_here),
        out_shape=pltpu.VMEM((8, 128), jnp.int32),
        in_specs=[SMEM] * 3,
        out_specs=VMEM,
        compiler_params=PARAMS,
        name="plan",
    )(far(branch_start), far(branch_len), far(parent_list.T))
    plan = close(plan)
    chosen = pl.pallas_call(
        choose_kernel,
        out_shape=(shape((WINDOW, width)),) * LAG,
        in_specs=[VMEM] * (1 + head_count),
        out_specs=(VMEM,) * LAG,
        compiler_params=PARAMS,
        name="choose",
    )(plan, *spread)
    late_slots = lax.optimization_barrier((*spread, *chosen))
    late_slots, chosen = late_slots[:head_count], late_slots[head_count:]
    sinks = pl.pallas_call(
        sinks_kernel,
        out_shape=shape((KV_HEADS * GROUP, 128), F32),
        in_specs=[VMEM] * head_count,
        out_specs=VMEM,
        compiler_params=PARAMS,
        name="sinks",
    )(*late_slots)
    arrived = [ring(chosen[LAG - s], "tok", s) for s in range(LAG, 0, -1)]
    queries, out_grad, _ = lax.optimization_barrier((queries, out_grad, sinks))
    near_queries, near_grad = pl.pallas_call(
        stage_kernel,
        out_shape=(pltpu.VMEM(queries.shape, BF16),) * 2,
        in_specs=[HBM] * 2,
        out_specs=(VMEM,) * 2,
        scratch_shapes=[pltpu.SemaphoreType.DMA((2,))],
        compiler_params=PARAMS,
        name="stage",
    )(far(queries), far(out_grad))
    *arrived, near_queries, near_grad = lax.optimization_barrier(
        (*arrived, near_queries, near_grad)
    )
    quarter = pl.pallas_call(
        arrive_kernel,
        out_shape=shape((WINDOW, width)),
        in_specs=[VMEM] * (1 + LAG),
        out_specs=VMEM,
        compiler_params=PARAMS,
        name="arrive",
    )(plan, *arrived)
    tails = swap([quarter] * head_count, "head")

    def attend(steps, pairs, offset, halo, joined):
        inputs = (
            sinks,
            close(near_queries),
            close(near_grad),
            close(keys),
            close(values),
            halo,
            *(tails[step] for step in steps),
            *(close(value) for value in joined),
        )
        base = 1 + len(inputs) - len(joined)
        return pl.pallas_call(
            functools.partial(
                attend_kernel,
                blocks_here,
                head_count,
                steps,
                offset,
                pairs,
                len(joined),
            ),
            out_shape=(
                pltpu.VMEM(queries.shape, BF16),
                pltpu.VMEM(queries.shape, BF16),
                pltpu.VMEM(key_states.shape, F32),
                pltpu.VMEM(key_states.shape, F32),
                pltpu.VMEM((PAIRS, WINDOW, 256), BF16),
            )
            + (shape((WINDOW, width)),) * len(steps),
            in_specs=[VMEM] * (1 + len(inputs)),
            out_specs=(VMEM,) * (5 + len(steps)),
            scratch_shapes=[
                pltpu.VMEM((head_count, WINDOW, width), BF16),
                pltpu.VMEM((WINDOW, 256), F32),
                pltpu.VMEM((2 * GROUP, WINDOW), F32),
                pltpu.VMEM((6 * HALF, 1024), BF16),
                pltpu.VMEM((6 * HALF, 1024), BF16),
            ],
            input_output_aliases={base + place: place for place in range(len(joined))},
            compiler_params=PARAMS,
            name="attend",
        )(plan, *inputs)

    if per_slot == 2:
        *joined, own_tail = attend((0,), 1, 0, spread[1], ())
        *results, tail_1, tail_2, tail_3 = attend((1, 2, 3), PAIRS - 1, 1, halo, joined)
        dtail = [own_tail, tail_1, tail_2, tail_3]
    else:
        results = attend(tuple(range(head_count)), PAIRS, None, halo, ())
        results, dtail = results[:5], list(results[5:])
    attended, query_grad, dk, dv, dhalo = results
    parts = swap(dtail, "head")
    quarter_grad = pl.pallas_call(
        gather_kernel,
        out_shape=shape((WINDOW, width)),
        in_specs=[VMEM] * head_count,
        out_specs=VMEM,
        compiler_params=PARAMS,
        name="gather",
    )(*parts)
    def flush(value):
        return pl.pallas_call(
            stage_kernel,
            out_shape=pltpu.HBM(value.shape, BF16),
            in_specs=[VMEM],
            out_specs=HBM,
            scratch_shapes=[pltpu.SemaphoreType.DMA((1,))],
            compiler_params=PARAMS,
            name="flush",
        )(close(value))

    returned = [ring(quarter_grad, "tok", -s) for s in range(LAG, 0, -1)][::-1]
    attended, _ = lax.optimization_barrier((attended, quarter_grad))
    attended = flush(attended)
    attended, *returned = lax.optimization_barrier((attended, *returned))
    dhalo, _ = lax.optimization_barrier((dhalo, quarter_grad))
    halo_back = shift(dhalo, "head", -1)
    *landed, sink_near = pl.pallas_call(
        functools.partial(land_kernel, blocks),
        out_shape=(shape((rows, width)),) * head_count + (shape((8, 128), F32),),
        in_specs=[VMEM] * (LAG + 2),
        out_specs=(VMEM,) * (head_count + 1),
        compiler_params=PARAMS,
        name="land",
    )(plan, quarter_grad, *returned)
    tails_back = swap(landed, "head")
    query_grad, _ = lax.optimization_barrier((query_grad, sink_near))
    query_grad = flush(query_grad)
    span = LAG + 1
    while 2 * span < tok_count:
        sink_near = sink_near + ring(sink_near, "tok", -span)
        span *= 2
    sink_far = ring(sink_near, "tok", -span)
    key_grad, value_grad, sink_grad = pl.pallas_call(
        total_kernel,
        out_shape=(
            shape(key_states.shape),
            shape(value_states.shape),
            shape(sink_logits.shape, F32),
        ),
        in_specs=[VMEM] * (5 + head_count),
        out_specs=(VMEM,) * 3,
        scratch_shapes=[pltpu.VMEM((head_count, rows, width), BF16)],
        compiler_params=PARAMS,
        name="total",
    )(halo_back, dk, dv, sink_near, sink_far, *tails_back)
    return attended, query_grad, key_grad, value_grad, sink_grad


def solution(mesh):
    rows = P(("tok", "head"), None)
    return jax.shard_map(
        local,
        mesh=mesh,
        in_specs=(rows, rows, rows, rows, P("head"), P(), P(), P()),
        out_specs=(rows, rows, rows, rows, P("head")),
        check_vma=False,
    )
```

```python
import functools

import jax
import jax.numpy as jnp
from jax import lax
from jax.experimental import pallas as pl
from jax.experimental.pallas import tpu as pltpu
from jax.sharding import PartitionSpec as P

HEAD_DIM = 64
KV_HEADS = 8
GROUP = 8
WINDOW = 128
HALF = WINDOW // 2
LAG = 3
BR_DEV = 2
PAIRS = KV_HEADS // 2
FACTOR = 0.125
LOW = -1e30
BF16 = jnp.bfloat16
F32 = jnp.float32

SMEM = pl.BlockSpec(memory_space=pltpu.SMEM)
VMEM = pl.BlockSpec(memory_space=pltpu.VMEM)
HBM = pl.BlockSpec(memory_space=pltpu.HBM)
PARAMS = pltpu.CompilerParams(vmem_limit_bytes=24 * 1024 * 1024)


def shift(value, axis, steps):
    count = lax.axis_size(axis)
    leading, last = (max(0, -steps), min(count, count - steps))
    return lax.ppermute(value, axis, [(source, source + steps) for source in range(leading, last)])


def ring(value, axis, steps):
    count = lax.axis_size(axis)
    return lax.ppermute(value, axis, [(source, (source + steps) % count) for source in range(count)])


def with_row(tile, row):
    high = row.astype(BF16).astype(F32)
    middle = (row - high).astype(BF16).astype(F32)
    low = row - high - middle
    packed = high + pltpu.roll(middle, 32, 1) + pltpu.roll(low, 64, 1)
    place = lax.broadcasted_iota(jnp.int32, (16, 128), 0)
    top = jnp.where(place == 0, packed, tile[:16, :128].astype(F32)).astype(BF16)
    if tile.shape[1] > 128:
        top = jnp.concatenate([top, tile[:16, 128:]], axis=1)
    return jnp.concatenate([top, tile[16:]], axis=0)


def row_join(top):
    packed = top[0:1, :128].astype(F32)
    row = packed + pltpu.roll(packed, 96, 1) + pltpu.roll(packed, 64, 1)
    return jnp.where(lax.broadcasted_iota(jnp.int32, (1, 128), 1) < 32, row, 0.0)


def child_tail(starts, parents, tok, distance, tok_count, blocks):
    child = jnp.minimum(tok + distance, tok_count - 1) * BR_DEV
    parent = parents[0, child]
    safe = jnp.maximum(parent, 0)
    valid = (tok + distance < tok_count) & (parent >= 0) & (safe // BR_DEV == tok)
    place = (starts[safe] + parents[1, child]) // WINDOW - tok * blocks
    return valid, jnp.where(valid, place, 0)


def block_state(starts, lengths, parents, tok, block):
    position = block * WINDOW
    alive, opening = jnp.bool_(False), jnp.bool_(False)
    for branch in range(BR_DEV):
        start = starts[tok * BR_DEV + branch]
        length = lengths[tok * BR_DEV + branch]
        alive = alive | ((start <= position) & (position < start + length))
        opening = opening | (start == position)
    has_tail = parents[0, tok * BR_DEV] >= 0
    return alive, opening, jnp.logical_not(opening) | has_tail


def plan_kernel(tok_count, blocks, blocks_here, starts, lengths, parents, plan_ref):
    tok, head = lax.axis_index("tok"), lax.axis_index("head")
    values = []
    for distance in range(1, LAG + 1):
        values += child_tail(starts, parents, tok, distance, tok_count, blocks)
    parent = parents[0, tok * BR_DEV]
    values.append(jnp.where(parent >= 0, tok - jnp.maximum(parent, 0) // BR_DEV, 1))
    for block in range(blocks_here):
        number = tok * blocks + head * blocks_here + block
        values += block_state(starts, lengths, parents, tok, number)
    lane = lax.broadcasted_iota(jnp.int32, plan_ref.shape, 1)
    plan = jnp.zeros(plan_ref.shape, jnp.int32)
    for place, value in enumerate(values):
        plan = jnp.where(lane == place, value.astype(jnp.int32), plan)
    plan_ref[...] = plan


def planned_tail(plan_ref, distance):
    row = plan_ref[0:1, :]
    return row[0, 2 * distance - 2] != 0, row[0, 2 * distance - 1]


def planned_source(plan_ref):
    return plan_ref[0:1, :][0, 2 * LAG]


def planned_block(plan_ref, block):
    row = plan_ref[0:1, :]
    return tuple(row[0, 2 * LAG + 1 + 3 * block + place] for place in range(3))


def take(ref, slot, width):
    if width % 128 == 0:
        return ref[:, pl.ds(pl.multiple_of(slot * width, width), width)]
    value = ref[:, :width]
    for other in range(1, ref.shape[1] // width):
        value = jnp.where(slot == other, ref[:, other * width : (other + 1) * width], value)
    return value


def pack_kernel(sink_hbm, key_hbm, value_hbm, *refs):
    *slot_refs, halo_ref, keys, values, sinks, sems = refs
    copies = [
        pltpu.make_async_copy(source, target, sems.at[place])
        for place, (source, target) in enumerate(
            ((sink_hbm, sinks), (key_hbm, keys), (value_hbm, values))
        )
    ]
    for copy in copies:
        copy.start()
    for copy in copies:
        copy.wait()
    slots, rows = len(slot_refs), keys.shape[0]
    head = lax.axis_index("head")
    width = KV_HEADS * HEAD_DIM // slots
    lane = lax.broadcasted_iota(jnp.int32, (1, 128), 1)
    sink_row = jnp.zeros((1, 128), F32)
    for place in range(sinks.shape[0]):
        sink_row = jnp.where(lane == place, sinks[place], sink_row)
    for step, slot_ref in enumerate(slot_refs):
        slot = lax.rem(head + step, slots)
        both = jnp.concatenate([take(keys, slot, width), take(values, slot, width)], axis=1)
        slot_ref[...] = with_row(both, sink_row)
    for pair in range(PAIRS):
        lanes = slice(pair * 128, (pair + 1) * 128)
        last = slice(rows - WINDOW, rows)
        halo_ref[pair] = jnp.concatenate([keys[last, lanes], values[last, lanes]], axis=1)


def choose_kernel(plan_ref, *refs):
    slots = len(refs) - LAG
    slot_refs, out_refs = refs[:slots], refs[slots:]
    head = lax.axis_index("head")
    rows = slot_refs[0].shape[0]
    blocks_here = rows // WINDOW
    for distance, out_ref in zip(range(LAG, 0, -1), out_refs):
        _, place = planned_tail(plan_ref, distance)
        begin = pl.multiple_of(place % blocks_here * WINDOW, WINDOW)
        wanted = lax.rem(head - place // blocks_here + slots, slots)
        for step, slot_ref in enumerate(slot_refs):

            @pl.when(wanted == step)
            def _(out_ref=out_ref, slot_ref=slot_ref, begin=begin):
                out_ref[...] = slot_ref[pl.ds(begin, WINDOW), :]


def sinks_kernel(*refs):
    *slot_refs, sink_ref = refs
    slots = len(slot_refs)
    head = lax.axis_index("head")
    heads = sink_ref.shape[0] // slots
    for step, slot_ref in enumerate(slot_refs):
        source = lax.rem(head - step + slots, slots)
        sink_row = row_join(slot_ref[:16])
        turned = jnp.broadcast_to(sink_row, (128, 128)).T
        sink_ref[pl.ds(pl.multiple_of(source * heads, heads), heads), :] = turned[:heads]


def arrive_kernel(plan_ref, *refs):
    *in_refs, out_ref = refs
    mine = planned_source(plan_ref)
    for distance, in_ref in zip(range(LAG, 0, -1), in_refs):

        @pl.when(mine == distance)
        def _(in_ref=in_ref):
            out_ref[...] = in_ref[...]


def stage_kernel(*refs):
    *arrays, sems = refs
    half = len(arrays) // 2
    copies = [
        pltpu.make_async_copy(source, target, sems.at[place])
        for place, (source, target) in enumerate(zip(arrays[:half], arrays[half:]))
    ]
    for copy in copies:
        copy.start()
    for copy in copies:
        copy.wait()


def attend_kernel(blocks_here, slots, steps, offset, pairs, joins, *refs):
    inputs, refs = refs[:7], refs[7:]
    tail_refs, refs = refs[: len(steps)], refs[len(steps) + joins :]
    outputs, refs = refs[:5], refs[5:]
    dtail_refs, refs = refs[: len(steps)], refs[len(steps) :]
    tails, *scratch = refs
    head = lax.axis_index("head")
    states = [planned_block(inputs[0], block) for block in range(blocks_here)]
    for step, tail_ref in zip(steps, tail_refs):
        tails[lax.rem(head + step, slots)] = tail_ref[...]

    def step(place, carry):
        pair = place // blocks_here
        if offset is not None:
            pair = lax.rem(head + pair + offset, PAIRS)
        block = place % blocks_here
        state = states[0]
        for other in range(1, blocks_here):
            state = [jnp.where(block == other, *two) for two in zip(states[other], state)]
        attend_block(
            blocks_here,
            slots,
            pair,
            block,
            [value != 0 for value in state],
            inputs,
            outputs,
            tails,
            tuple(zip(steps, dtail_refs)),
            scratch,
        )
        return carry

    lax.fori_loop(0, pairs * blocks_here, step, 0)


def attend_block(
    blocks_here, slots, pair, block, state, inputs, outputs, tails, dtails, scratch
):
    _, sink_ref, q_ref, g_ref, k_ref, v_ref, halo_ref = inputs
    o_ref, dq_ref, dk_ref, dv_ref, dhalo_ref = outputs
    tail_sum, sink_rows, prob2, slope2 = scratch
    per_slot = KV_HEADS // slots
    head = lax.axis_index("head")
    alive, opening, prev_ok = state
    here = pl.ds(pl.multiple_of(block * WINDOW, WINDOW), WINDOW)
    before = pl.ds(pl.multiple_of(jnp.maximum(block - 1, 0) * WINDOW, WINDOW), WINDOW)
    first = block == 0
    near = pl.ds(pl.multiple_of(pair * 128, 128), 128)
    big = pl.ds(pl.multiple_of(pair * 1024, 1024), 1024)
    q_ref, g_ref, o_ref, dq_ref = (ref.at[here, big] for ref in (q_ref, g_ref, o_ref, dq_ref))
    k_ref, v_ref, dk_ref, dv_ref = (ref.at[:, near] for ref in (k_ref, v_ref, dk_ref, dv_ref))
    sink_ref = sink_ref.at[pl.ds(pl.multiple_of(pair * 16, 16), 16)]
    dhalo_ref = dhalo_ref.at[pair]

    @pl.when(first)
    def _():
        tail_sum[...] = jnp.zeros_like(tail_sum)
        dhalo_ref[...] = jnp.zeros((WINDOW, 256), BF16)
        sink_rows[...] = jnp.zeros_like(sink_rows)

    @pl.when(jnp.logical_not(alive))
    def _():
        o_ref[...] = jnp.zeros((WINDOW, 1024), BF16)
        dq_ref[...] = jnp.zeros((WINDOW, 1024), BF16)
        dk_ref[here, :] = jnp.zeros((WINDOW, 128), F32)
        dv_ref[here, :] = jnp.zeros((WINDOW, 128), F32)

    @pl.when(alive)
    def _():
        if len(halo_ref.shape) == 2:
            halo = halo_ref[halo_ref.shape[0] - WINDOW :]
        else:
            halo = halo_ref[pair]
        if per_slot == 2:
            tail = tails[pair]
            tail_k, tail_v = tail[:, :128], tail[:, 128:]
        else:
            tail_a, tail_b = tails[2 * pair], tails[2 * pair + 1]
            tail_k = jnp.concatenate([tail_a[:, :64], tail_b[:, :64]], axis=1)
            tail_v = jnp.concatenate([tail_a[:, 64:], tail_b[:, 64:]], axis=1)
        near_k = jnp.where(first, halo[:, :128], k_ref[before, :])
        near_v = jnp.where(first, halo[:, 128:], v_ref[before, :])
        prev_k = jnp.where(opening, tail_k, near_k)
        prev_v = jnp.where(opening, tail_v, near_v)
        own_k, own_v = k_ref[here, :], v_ref[here, :]

        def halves(own, prev):
            return (
                jnp.concatenate([own[:HALF], prev[:HALF], prev[HALF:]], axis=0),
                jnp.concatenate([own[HALF:], prev[HALF:], own[:HALF]], axis=0),
            )

        left = lax.broadcasted_iota(jnp.int32, (1, 128), 1) < HALF
        low16 = left.astype(F32).astype(BF16)
        high16 = BF16(1) - low16

        def padded(seen):
            swapped = jnp.concatenate([seen[:, 64:], seen[:, :64]], axis=1)
            return (
                jnp.concatenate([seen * low16, swapped * high16], axis=0),
                jnp.concatenate([swapped * low16, seen * high16], axis=0),
            )

        seen_k = halves(own_k * BF16(FACTOR), prev_k * BF16(FACTOR))
        seen_v = halves(own_v, prev_v)
        padded_k = tuple(padded(value) for value in seen_k)
        padded_v = tuple(padded(value) for value in seen_v)
        turned_k = tuple(value.T for value in seen_k)
        turned_v = tuple(value.T for value in seen_v)
        bias = jnp.where(prev_ok, 0.0, LOW)
        key_place = lax.broadcasted_iota(jnp.int32, (HALF, 4 * HALF), 0)
        query_place = lax.broadcasted_iota(jnp.int32, (HALF, 4 * HALF), 1) & (HALF - 1)
        own = key_place <= query_place
        own16 = own.astype(F32).astype(BF16)
        turn = (((1,), (1,)), ((), ()))
        items = [(unit, half) for unit in range(2) for half in range(2)]
        seen = 3 * HALF

        def wide(index):
            return slice(index * 256, (index + 1) * 256)

        def feats(index):
            unit = items[index][0]
            return slice(unit * HEAD_DIM, (unit + 1) * HEAD_DIM)

        def corners(unit, half):
            rows = slice(half * HALF, (half + 1) * HALF)
            return [
                (rows, slice(unit * 512 + at * 128, unit * 512 + (at + 1) * 128)) for at in range(4)
            ]

        def stacked(ref, unit, half):
            return jnp.concatenate([ref[corner] for corner in corners(unit, half)], axis=0)

        def products(index):
            unit, half = items[index]
            score, dp = (
                lax.dot_general(
                    padded[half][unit],
                    stacked(ref, unit, half),
                    turn,
                    preferred_element_type=F32,
                )
                for padded, ref in ((padded_k, q_ref), (padded_v, g_ref))
            )
            parts = []
            for base in (0, seen):
                near, far = slice(base, base + HALF), slice(base + HALF, base + 2 * HALF)
                rest = slice(base + 2 * HALF, base + 3 * HALF)
                edge = jnp.where(own, score[near], score[far] + bias)
                whole = score[rest] + bias if half == 0 else score[rest]
                parts.append((edge, whole, jnp.where(own, dp[near], dp[far]), dp[rest]))
            return parts

        def weigh(index, odd, edge, whole, dp_edge, dp_whole):
            unit, half = items[index]
            base = odd * seen
            row = unit * GROUP + odd
            sink = jnp.concatenate(
                [
                    jnp.where(left, sink_ref[at : at + 1], sink_ref[at + 2 : at + 3])
                    for at in (row, row + 4)
                ],
                axis=1,
            )
            peak = jnp.max(jnp.maximum(edge, whole), axis=0, keepdims=True)
            peak = jnp.maximum(peak, sink)
            edge, whole = jnp.exp(edge - peak), jnp.exp(whole - peak)
            sink_weight = jnp.exp(sink - peak)
            inverse = 1.0 / (jnp.sum(edge + whole, axis=0, keepdims=True) + sink_weight)
            edge, whole = edge * inverse, whole * inverse
            term_edge, term_whole = edge * dp_edge, whole * dp_whole
            delta = jnp.sum(term_edge + term_whole, axis=0, keepdims=True)
            for target, at_edge, at_whole in (
                (prob2, edge, whole),
                (slope2, term_edge - edge * delta, term_whole - whole * delta),
            ):
                edge16 = at_edge.astype(BF16)
                edge_own = edge16 * own16
                target[base : base + HALF, wide(index)] = edge_own
                target[base + HALF : base + 2 * HALF, wide(index)] = edge16 - edge_own
                target[base + 2 * HALF : base + seen, wide(index)] = at_whole.astype(BF16)
            sink_term = sink_weight * inverse * delta
            for at, lanes in ((row, slice(0, 128)), (row + 4, slice(128, 256))):
                part = sink_term[:, lanes]
                sink_rows[at : at + 1] += jnp.where(left, part, 0.0)
                sink_rows[at + 2 : at + 3] += jnp.where(left, 0.0, part)

        def finish(index):
            unit, half = items[index]
            for source, across, out_ref in ((prob2, turned_v, o_ref), (slope2, turned_k, dq_ref)):
                out_t = [
                    jnp.dot(
                        across[half][feats(index)],
                        source[base : base + seen, wide(index)],
                        preferred_element_type=F32,
                    ).astype(BF16)
                    for base in (0, seen)
                ]
                out = jnp.concatenate(out_t, axis=0).T
                for at, corner in enumerate(corners(unit, half)):
                    out_ref[corner] = out[at * HALF : (at + 1) * HALF]

        def reduce(index):
            unit, half = items[index]
            parts = []
            for weights, ref in ((slope2, q_ref), (prob2, g_ref)):
                part = jnp.dot(
                    weights[:, wide(index)], stacked(ref, unit, half), preferred_element_type=F32
                )
                parts.append(jnp.where(left, part[:seen], part[seen:]))
            return parts

        def join(first_half, second_half):
            total = jnp.concatenate(
                [
                    first_half[:HALF] + second_half[2 * HALF :],
                    second_half[:HALF],
                    first_half[HALF : 2 * HALF],
                    first_half[2 * HALF :] + second_half[HALF : 2 * HALF],
                ],
                axis=0,
            )
            return total + pltpu.roll(total, HEAD_DIM, 1)

        ahead, parts = products(0), []
        for index in range(len(items)):
            now = ahead
            weigh(index, 0, *now[0])
            if index + 1 < len(items):
                ahead = products(index + 1)
            weigh(index, 1, *now[1])
            if index >= 1:
                finish(index - 1)
            parts.append(reduce(index))
        finish(len(items) - 1)
        grads = [
            [join(parts[2 * unit][place], parts[2 * unit + 1][place]) for place in range(2)]
            for unit in range(2)
        ]
        dk = jnp.where(left, grads[0][0], grads[1][0]) * FACTOR
        dv = jnp.where(left, grads[0][1], grads[1][1])
        dk_ref[here, :] = dk[:WINDOW]
        dv_ref[here, :] = dv[:WINDOW]

        @pl.when(opening & prev_ok)
        def _():
            tail_sum[:, :128] += dk[WINDOW:]
            tail_sum[:, 128:] += dv[WINDOW:]

        @pl.when(jnp.logical_not(opening) & first)
        def _():
            dhalo_ref[:, :128] = dk[WINDOW:].astype(BF16)
            dhalo_ref[:, 128:] = dv[WINDOW:].astype(BF16)

        @pl.when(jnp.logical_not(opening) & jnp.logical_not(first))
        def _():
            dk_ref[before, :] += dk[WINDOW:]
            dv_ref[before, :] += dv[WINDOW:]

    @pl.when(block == blocks_here - 1)
    def _():
        width = 2 * per_slot * HEAD_DIM
        heads = per_slot * GROUP
        total = tail_sum[...].astype(BF16)
        for part in range(2 // per_slot):
            feats = slice(part * width // 2, (part + 1) * width // 2)
            tail = jnp.concatenate([total[:, :128][:, feats], total[:, 128:][:, feats]], axis=1)
            rows = sink_rows[part * heads : (part + 1) * heads]
            rows = jnp.concatenate([rows, jnp.zeros((128 - heads, WINDOW), F32)], axis=0)
            sink_row = jnp.sum(rows.T, axis=0, keepdims=True)
            tail = with_row(tail, sink_row)
            wanted = lax.rem(pair * (2 // per_slot) + part - head + slots, slots)
            for step, dtail_ref in dtails:

                @pl.when(wanted == step)
                def _(dtail_ref=dtail_ref, tail=tail):
                    dtail_ref[...] = tail


def gather_kernel(*refs):
    *in_refs, out_ref = refs
    total, sink_row = 0.0, 0.0
    for in_ref in in_refs:
        total = total + in_ref[...].astype(F32)
        sink_row = sink_row + row_join(in_ref[:16])
    out_ref[...] = with_row(total.astype(BF16), sink_row)


def land_kernel(blocks, plan_ref, here_ref, *refs):
    head = lax.axis_index("head")
    in_refs, out_refs, sink_ref = refs[:LAG], refs[LAG:-1], refs[-1]
    slots = len(out_refs)
    blocks_here = blocks // slots
    for out_ref in out_refs:
        out_ref[...] = jnp.zeros_like(out_ref)
    sink_row = row_join(here_ref[:16])
    seen = lax.broadcasted_iota(jnp.int32, here_ref.shape, 0) > 0
    for distance, in_ref in enumerate(in_refs, 1):
        valid, place = planned_tail(plan_ref, distance)
        sink_row = sink_row + row_join(in_ref[:16])
        wanted = lax.rem(place // blocks_here - head + slots, slots)
        here = pl.ds(pl.multiple_of(place % blocks_here * WINDOW, WINDOW), WINDOW)
        for step, out_ref in enumerate(out_refs):

            @pl.when(valid & (wanted == step))
            def _(out_ref=out_ref, in_ref=in_ref, here=here):
                total = out_ref[here, :].astype(F32) + in_ref[...].astype(F32)
                out_ref[here, :] = jnp.where(seen, total, 0.0).astype(BF16)

    sink_ref[...] = jnp.broadcast_to(sink_row, sink_ref.shape)


def total_kernel(halo_ref, dk_ref, dv_ref, sink_ref, far_ref, *refs):
    *tail_refs, key_ref, value_ref, sink_grad, tails = refs
    slots, rows = len(tail_refs), dk_ref.shape[0]
    width = tails.shape[2] // 2
    head = lax.axis_index("head")
    for step, tail_ref in enumerate(tail_refs):
        tails[lax.rem(head - step + slots, slots)] = tail_ref[...]
    halo_k = jnp.concatenate([halo_ref[pair][:, :128] for pair in range(PAIRS)], axis=1)
    halo_v = jnp.concatenate([halo_ref[pair][:, 128:] for pair in range(PAIRS)], axis=1)
    for in_ref, halo, at, out_ref in (
        (dk_ref, halo_k, 0, key_ref),
        (dv_ref, halo_v, width, value_ref),
    ):
        for begin in range(0, rows, WINDOW):
            here = slice(begin, begin + WINDOW)
            parts = [tails[slot, here, at : at + width] for slot in range(slots)]
            total = in_ref[here, :] + jnp.concatenate(parts, axis=1).astype(F32)
            if begin == rows - WINDOW:
                total = total + halo.astype(F32)
            out_ref[here, :] = total.astype(BF16)
    sink_row = -(sink_ref[0:1] + far_ref[0:1])
    sink_grad[...] = sink_row[0, : sink_grad.shape[0]]


def swap(values, axis):
    return [values[0]] + [ring(values[step], axis, step) for step in range(1, len(values))]


def local(
    queries, key_states, value_states, out_grad, sink_logits, branch_start, branch_len, parent_list
):
    tok_count, head_count = lax.axis_size("tok"), lax.axis_size("head")
    rows = queries.shape[0]
    blocks_here = rows // WINDOW
    blocks = blocks_here * head_count
    per_slot = KV_HEADS // head_count
    width = 2 * per_slot * HEAD_DIM

    def shape(dims, kind=BF16):
        return jax.ShapeDtypeStruct(dims, kind)

    def far(value):
        return pltpu.with_memory_space_constraint(value, pltpu.HBM)

    def close(value):
        return pltpu.with_memory_space_constraint(value, pltpu.VMEM)

    *slots, halo_out, keys, values = pl.pallas_call(
        pack_kernel,
        out_shape=(shape((rows, width)),) * head_count
        + (shape((PAIRS, WINDOW, 256)),)
        + (pltpu.VMEM(key_states.shape, BF16),) * 2,
        in_specs=[HBM] * 3,
        out_specs=(VMEM,) * (head_count + 3),
        scratch_shapes=[
            pltpu.SMEM(sink_logits.shape, F32),
            pltpu.SemaphoreType.DMA((3,)),
        ],
        compiler_params=PARAMS,
        name="pack",
    )(far(sink_logits), far(key_states), far(value_states))
    spread = swap(slots, "head")
    halo = shift(halo_out, "head", 1)
    plan = pl.pallas_call(
        functools.partial(plan_kernel, tok_count, blocks, blocks_here),
        out_shape=pltpu.VMEM((8, 128), jnp.int32),
        in_specs=[SMEM] * 3,
        out_specs=VMEM,
        compiler_params=PARAMS,
        name="plan",
    )(far(branch_start), far(branch_len), far(parent_list.T))
    plan = close(plan)
    chosen = pl.pallas_call(
        choose_kernel,
        out_shape=(shape((WINDOW, width)),) * LAG,
        in_specs=[VMEM] * (1 + head_count),
        out_specs=(VMEM,) * LAG,
        compiler_params=PARAMS,
        name="choose",
    )(plan, *spread)
    late_slots = lax.optimization_barrier((*spread, *chosen))
    late_slots, chosen = late_slots[:head_count], late_slots[head_count:]
    sinks = pl.pallas_call(
        sinks_kernel,
        out_shape=shape((KV_HEADS * GROUP, 128), F32),
        in_specs=[VMEM] * head_count,
        out_specs=VMEM,
        compiler_params=PARAMS,
        name="sinks",
    )(*late_slots)
    arrived = [ring(chosen[LAG - s], "tok", s) for s in range(LAG, 0, -1)]
    queries, out_grad, _ = lax.optimization_barrier((queries, out_grad, sinks))
    near_queries, near_grad = pl.pallas_call(
        stage_kernel,
        out_shape=(pltpu.VMEM(queries.shape, BF16),) * 2,
        in_specs=[HBM] * 2,
        out_specs=(VMEM,) * 2,
        scratch_shapes=[pltpu.SemaphoreType.DMA((2,))],
        compiler_params=PARAMS,
        name="stage",
    )(far(queries), far(out_grad))
    *arrived, near_queries, near_grad = lax.optimization_barrier(
        (*arrived, near_queries, near_grad)
    )
    quarter = pl.pallas_call(
        arrive_kernel,
        out_shape=shape((WINDOW, width)),
        in_specs=[VMEM] * (1 + LAG),
        out_specs=VMEM,
        compiler_params=PARAMS,
        name="arrive",
    )(plan, *arrived)
    tails = swap([quarter] * head_count, "head")

    def attend(steps, pairs, offset, halo, joined):
        inputs = (
            sinks,
            close(near_queries),
            close(near_grad),
            close(keys),
            close(values),
            halo,
            *(tails[-step % head_count] for step in steps),
            *(close(value) for value in joined),
        )
        base = 1 + len(inputs) - len(joined)
        return pl.pallas_call(
            functools.partial(
                attend_kernel,
                blocks_here,
                head_count,
                steps,
                offset,
                pairs,
                len(joined),
            ),
            out_shape=(
                pltpu.VMEM(queries.shape, BF16),
                pltpu.VMEM(queries.shape, BF16),
                pltpu.VMEM(key_states.shape, F32),
                pltpu.VMEM(key_states.shape, F32),
                pltpu.VMEM((PAIRS, WINDOW, 256), BF16),
            )
            + (shape((WINDOW, width)),) * len(steps),
            in_specs=[VMEM] * (1 + len(inputs)),
            out_specs=(VMEM,) * (5 + len(steps)),
            scratch_shapes=[
                pltpu.VMEM((head_count, WINDOW, width), BF16),
                pltpu.VMEM((WINDOW, 256), F32),
                pltpu.VMEM((2 * GROUP, WINDOW), F32),
                pltpu.VMEM((6 * HALF, 1024), BF16),
                pltpu.VMEM((6 * HALF, 1024), BF16),
            ],
            input_output_aliases={base + place: place for place in range(len(joined))},
            compiler_params=PARAMS,
            name="attend",
        )(plan, *inputs)

    if per_slot == 2:
        *joined, own_tail = attend((0,), 1, 0, spread[1], ())
        *joined, tail_1, tail_2 = attend((1, 2), 2, 1, halo, joined)
        *results, tail_3 = attend((3,), 1, 3, halo, joined)
        dtail = [own_tail, tail_1, tail_2, tail_3]
    else:
        results = attend(tuple(range(head_count)), PAIRS, None, halo, ())
        results, dtail = results[:5], list(results[5:])
    attended, query_grad, dk, dv, dhalo = results
    parts = swap(dtail, "head")

    def gather(values):
        return pl.pallas_call(
            gather_kernel,
            out_shape=shape((WINDOW, width)),
            in_specs=[VMEM] * len(values),
            out_specs=VMEM,
            compiler_params=PARAMS,
            name="gather",
        )(*values)

    quarter_grad = gather([gather(parts[:-1]), parts[-1]])

    def flush(value):
        return pl.pallas_call(
            stage_kernel,
            out_shape=pltpu.HBM(value.shape, BF16),
            in_specs=[VMEM],
            out_specs=HBM,
            scratch_shapes=[pltpu.SemaphoreType.DMA((1,))],
            compiler_params=PARAMS,
            name="flush",
        )(close(value))

    returned = [ring(quarter_grad, "tok", -s) for s in range(LAG, 0, -1)][::-1]
    attended, _ = lax.optimization_barrier((attended, quarter_grad))
    attended = flush(attended)
    attended, *returned = lax.optimization_barrier((attended, *returned))
    halo_back = shift(dhalo, "head", -1)
    *landed, sink_near = pl.pallas_call(
        functools.partial(land_kernel, blocks),
        out_shape=(shape((rows, width)),) * head_count + (shape((8, 128), F32),),
        in_specs=[VMEM] * (LAG + 2),
        out_specs=(VMEM,) * (head_count + 1),
        compiler_params=PARAMS,
        name="land",
    )(plan, quarter_grad, *returned)
    tails_back = swap(landed, "head")
    query_grad, _ = lax.optimization_barrier((query_grad, sink_near))
    query_grad = flush(query_grad)
    span = LAG + 1
    while 2 * span < tok_count:
        sink_near = sink_near + ring(sink_near, "tok", -span)
        span *= 2
    sink_far = ring(sink_near, "tok", -span)
    key_grad, value_grad, sink_grad = pl.pallas_call(
        total_kernel,
        out_shape=(
            shape(key_states.shape),
            shape(value_states.shape),
            shape(sink_logits.shape, F32),
        ),
        in_specs=[VMEM] * (5 + head_count),
        out_specs=(VMEM,) * 3,
        scratch_shapes=[pltpu.VMEM((head_count, rows, width), BF16)],
        compiler_params=PARAMS,
        name="total",
    )(halo_back, dk, dv, sink_near, sink_far, *tails_back)
    return attended, query_grad, key_grad, value_grad, sink_grad


def solution(mesh):
    rows = P(("tok", "head"), None)
    return jax.shard_map(
        local,
        mesh=mesh,
        in_specs=(rows, rows, rows, rows, P("head"), P(), P(), P()),
        out_specs=(rows, rows, rows, rows, P("head")),
        check_vma=False,
    )
```

```python
import functools

import jax
import jax.numpy as jnp
from jax import lax
from jax.experimental import pallas as pl
from jax.experimental.pallas import tpu as pltpu
from jax.sharding import PartitionSpec as P

HEAD_DIM = 64
KV_HEADS = 8
GROUP = 8
WINDOW = 128
HALF = WINDOW // 2
LAG = 3
BR_DEV = 2
PAIRS = KV_HEADS // 2
FACTOR = 0.125
LOW = -1e30
BF16 = jnp.bfloat16
F32 = jnp.float32

SMEM = pl.BlockSpec(memory_space=pltpu.SMEM)
VMEM = pl.BlockSpec(memory_space=pltpu.VMEM)
HBM = pl.BlockSpec(memory_space=pltpu.HBM)
PARAMS = pltpu.CompilerParams(vmem_limit_bytes=24 * 1024 * 1024)


def shift(value, axis, steps):
    count = lax.axis_size(axis)
    leading, last = (max(0, -steps), min(count, count - steps))
    return lax.ppermute(value, axis, [(source, source + steps) for source in range(leading, last)])


def ring(value, axis, steps):
    count = lax.axis_size(axis)
    return lax.ppermute(value, axis, [(source, (source + steps) % count) for source in range(count)])


def with_row(tile, row):
    high = row.astype(BF16).astype(F32)
    middle = (row - high).astype(BF16).astype(F32)
    low = row - high - middle
    packed = high + pltpu.roll(middle, 32, 1) + pltpu.roll(low, 64, 1)
    place = lax.broadcasted_iota(jnp.int32, (16, 128), 0)
    top = jnp.where(place == 0, packed, tile[:16, :128].astype(F32)).astype(BF16)
    if tile.shape[1] > 128:
        top = jnp.concatenate([top, tile[:16, 128:]], axis=1)
    return jnp.concatenate([top, tile[16:]], axis=0)


def row_join(top):
    packed = top[0:1, :128].astype(F32)
    row = packed + pltpu.roll(packed, 96, 1) + pltpu.roll(packed, 64, 1)
    return jnp.where(lax.broadcasted_iota(jnp.int32, (1, 128), 1) < 32, row, 0.0)


def child_tail(starts, parents, tok, distance, tok_count, blocks):
    child = jnp.minimum(tok + distance, tok_count - 1) * BR_DEV
    parent = parents[0, child]
    safe = jnp.maximum(parent, 0)
    valid = (tok + distance < tok_count) & (parent >= 0) & (safe // BR_DEV == tok)
    place = (starts[safe] + parents[1, child]) // WINDOW - tok * blocks
    return valid, jnp.where(valid, place, 0)


def block_state(starts, lengths, parents, tok, block):
    position = block * WINDOW
    alive, opening = jnp.bool_(False), jnp.bool_(False)
    for branch in range(BR_DEV):
        start = starts[tok * BR_DEV + branch]
        length = lengths[tok * BR_DEV + branch]
        alive = alive | ((start <= position) & (position < start + length))
        opening = opening | (start == position)
    has_tail = parents[0, tok * BR_DEV] >= 0
    return alive, opening, jnp.logical_not(opening) | has_tail


def plan_kernel(tok_count, blocks, blocks_here, starts, lengths, parents, plan_ref):
    tok, head = lax.axis_index("tok"), lax.axis_index("head")
    values = []
    for distance in range(1, LAG + 1):
        values += child_tail(starts, parents, tok, distance, tok_count, blocks)
    parent = parents[0, tok * BR_DEV]
    values.append(jnp.where(parent >= 0, tok - jnp.maximum(parent, 0) // BR_DEV, 1))
    for block in range(blocks_here):
        number = tok * blocks + head * blocks_here + block
        values += block_state(starts, lengths, parents, tok, number)
    lane = lax.broadcasted_iota(jnp.int32, plan_ref.shape, 1)
    plan = jnp.zeros(plan_ref.shape, jnp.int32)
    for place, value in enumerate(values):
        plan = jnp.where(lane == place, value.astype(jnp.int32), plan)
    plan_ref[...] = plan


def planned_tail(plan_ref, distance):
    row = plan_ref[0:1, :]
    return row[0, 2 * distance - 2] != 0, row[0, 2 * distance - 1]


def planned_source(plan_ref):
    return plan_ref[0:1, :][0, 2 * LAG]


def planned_block(plan_ref, block):
    row = plan_ref[0:1, :]
    return tuple(row[0, 2 * LAG + 1 + 3 * block + place] for place in range(3))


def take(ref, slot, width):
    if width % 128 == 0:
        return ref[:, pl.ds(pl.multiple_of(slot * width, width), width)]
    value = ref[:, :width]
    for other in range(1, ref.shape[1] // width):
        value = jnp.where(slot == other, ref[:, other * width : (other + 1) * width], value)
    return value


def pack_kernel(sink_hbm, key_hbm, value_hbm, *refs):
    *slot_refs, halo_ref, keys, values, sinks, sems = refs
    copies = [
        pltpu.make_async_copy(source, target, sems.at[place])
        for place, (source, target) in enumerate(
            ((sink_hbm, sinks), (key_hbm, keys), (value_hbm, values))
        )
    ]
    for copy in copies:
        copy.start()
    for copy in copies:
        copy.wait()
    slots, rows = len(slot_refs), keys.shape[0]
    head = lax.axis_index("head")
    width = KV_HEADS * HEAD_DIM // slots
    lane = lax.broadcasted_iota(jnp.int32, (1, 128), 1)
    sink_row = jnp.zeros((1, 128), F32)
    for place in range(sinks.shape[0]):
        sink_row = jnp.where(lane == place, sinks[place], sink_row)
    for step, slot_ref in enumerate(slot_refs):
        slot = lax.rem(head + step, slots)
        both = jnp.concatenate([take(keys, slot, width), take(values, slot, width)], axis=1)
        slot_ref[...] = with_row(both, sink_row)
    for pair in range(PAIRS):
        lanes = slice(pair * 128, (pair + 1) * 128)
        last = slice(rows - WINDOW, rows)
        halo_ref[pair] = jnp.concatenate([keys[last, lanes], values[last, lanes]], axis=1)


def choose_kernel(plan_ref, *refs):
    slots = len(refs) - LAG
    slot_refs, out_refs = refs[:slots], refs[slots:]
    head = lax.axis_index("head")
    rows = slot_refs[0].shape[0]
    blocks_here = rows // WINDOW
    for distance, out_ref in zip(range(LAG, 0, -1), out_refs):
        _, place = planned_tail(plan_ref, distance)
        begin = pl.multiple_of(place % blocks_here * WINDOW, WINDOW)
        wanted = lax.rem(head - place // blocks_here + slots, slots)
        for step, slot_ref in enumerate(slot_refs):

            @pl.when(wanted == step)
            def _(out_ref=out_ref, slot_ref=slot_ref, begin=begin):
                out_ref[...] = slot_ref[pl.ds(begin, WINDOW), :]


def sinks_kernel(*refs):
    *slot_refs, sink_ref = refs
    slots = len(slot_refs)
    head = lax.axis_index("head")
    heads = sink_ref.shape[0] // slots
    for step, slot_ref in enumerate(slot_refs):
        source = lax.rem(head - step + slots, slots)
        sink_row = row_join(slot_ref[:16])
        turned = jnp.broadcast_to(sink_row, (128, 128)).T
        sink_ref[pl.ds(pl.multiple_of(source * heads, heads), heads), :] = turned[:heads]


def arrive_kernel(plan_ref, *refs):
    *in_refs, out_ref = refs
    mine = planned_source(plan_ref)
    for distance, in_ref in zip(range(LAG, 0, -1), in_refs):

        @pl.when(mine == distance)
        def _(in_ref=in_ref):
            out_ref[...] = in_ref[...]


def stage_kernel(*refs):
    *arrays, sems = refs
    half = len(arrays) // 2
    copies = [
        pltpu.make_async_copy(source, target, sems.at[place])
        for place, (source, target) in enumerate(zip(arrays[:half], arrays[half:]))
    ]
    for copy in copies:
        copy.start()
    for copy in copies:
        copy.wait()


def attend_kernel(blocks_here, slots, steps, offset, pairs, joins, *refs):
    inputs, refs = refs[:7], refs[7:]
    tail_refs, refs = refs[: len(steps)], refs[len(steps) + joins :]
    outputs, refs = refs[:5], refs[5:]
    dtail_refs, refs = refs[: len(steps)], refs[len(steps) :]
    tails, *scratch = refs
    head = lax.axis_index("head")
    states = [planned_block(inputs[0], block) for block in range(blocks_here)]
    for step, tail_ref in zip(steps, tail_refs):
        tails[lax.rem(head + step, slots)] = tail_ref[...]

    def step(place, carry):
        pair = place // blocks_here
        if offset is not None:
            pair = lax.rem(head + pair + offset, PAIRS)
        block = place % blocks_here
        state = states[0]
        for other in range(1, blocks_here):
            state = [jnp.where(block == other, *two) for two in zip(states[other], state)]
        attend_block(
            blocks_here,
            slots,
            pair,
            block,
            [value != 0 for value in state],
            inputs,
            outputs,
            tails,
            tuple(zip(steps, dtail_refs)),
            scratch,
        )
        return carry

    lax.fori_loop(0, pairs * blocks_here, step, 0)


def attend_block(
    blocks_here, slots, pair, block, state, inputs, outputs, tails, dtails, scratch
):
    _, sink_ref, q_ref, g_ref, k_ref, v_ref, halo_ref = inputs
    o_ref, dq_ref, dk_ref, dv_ref, dhalo_ref = outputs
    tail_sum, sink_rows, prob2, slope2 = scratch
    per_slot = KV_HEADS // slots
    head = lax.axis_index("head")
    alive, opening, prev_ok = state
    here = pl.ds(pl.multiple_of(block * WINDOW, WINDOW), WINDOW)
    before = pl.ds(pl.multiple_of(jnp.maximum(block - 1, 0) * WINDOW, WINDOW), WINDOW)
    first = block == 0
    near = pl.ds(pl.multiple_of(pair * 128, 128), 128)
    big = pl.ds(pl.multiple_of(pair * 1024, 1024), 1024)
    q_ref, g_ref, o_ref, dq_ref = (ref.at[here, big] for ref in (q_ref, g_ref, o_ref, dq_ref))
    k_ref, v_ref, dk_ref, dv_ref = (ref.at[:, near] for ref in (k_ref, v_ref, dk_ref, dv_ref))
    sink_ref = sink_ref.at[pl.ds(pl.multiple_of(pair * 16, 16), 16)]
    dhalo_ref = dhalo_ref.at[pair]

    @pl.when(first)
    def _():
        tail_sum[...] = jnp.zeros_like(tail_sum)
        dhalo_ref[...] = jnp.zeros((WINDOW, 256), BF16)
        sink_rows[...] = jnp.zeros_like(sink_rows)

    @pl.when(jnp.logical_not(alive))
    def _():
        o_ref[...] = jnp.zeros((WINDOW, 1024), BF16)
        dq_ref[...] = jnp.zeros((WINDOW, 1024), BF16)
        dk_ref[here, :] = jnp.zeros((WINDOW, 128), F32)
        dv_ref[here, :] = jnp.zeros((WINDOW, 128), F32)

    @pl.when(alive)
    def _():
        if len(halo_ref.shape) == 2:
            halo = halo_ref[halo_ref.shape[0] - WINDOW :]
        else:
            halo = halo_ref[pair]
        if per_slot == 2:
            tail = tails[pair]
            tail_k, tail_v = tail[:, :128], tail[:, 128:]
        else:
            tail_a, tail_b = tails[2 * pair], tails[2 * pair + 1]
            tail_k = jnp.concatenate([tail_a[:, :64], tail_b[:, :64]], axis=1)
            tail_v = jnp.concatenate([tail_a[:, 64:], tail_b[:, 64:]], axis=1)
        near_k = jnp.where(first, halo[:, :128], k_ref[before, :])
        near_v = jnp.where(first, halo[:, 128:], v_ref[before, :])
        prev_k = jnp.where(opening, tail_k, near_k)
        prev_v = jnp.where(opening, tail_v, near_v)
        own_k, own_v = k_ref[here, :], v_ref[here, :]

        def halves(own, prev):
            return (
                jnp.concatenate([own[:HALF], prev[:HALF], prev[HALF:]], axis=0),
                jnp.concatenate([own[HALF:], prev[HALF:], own[:HALF]], axis=0),
            )

        left = lax.broadcasted_iota(jnp.int32, (1, 128), 1) < HALF
        low16 = left.astype(F32).astype(BF16)
        high16 = BF16(1) - low16

        def padded(seen):
            swapped = jnp.concatenate([seen[:, 64:], seen[:, :64]], axis=1)
            return (
                jnp.concatenate([seen * low16, swapped * high16], axis=0),
                jnp.concatenate([swapped * low16, seen * high16], axis=0),
            )

        seen_k = halves(own_k * BF16(FACTOR), prev_k * BF16(FACTOR))
        seen_v = halves(own_v, prev_v)
        padded_k = tuple(padded(value) for value in seen_k)
        padded_v = tuple(padded(value) for value in seen_v)
        turned_k = tuple(value.T for value in seen_k)
        turned_v = tuple(value.T for value in seen_v)
        bias = jnp.where(prev_ok, 0.0, LOW)
        key_place = lax.broadcasted_iota(jnp.int32, (HALF, 4 * HALF), 0)
        query_place = lax.broadcasted_iota(jnp.int32, (HALF, 4 * HALF), 1) & (HALF - 1)
        own = key_place <= query_place
        own16 = own.astype(F32).astype(BF16)
        turn = (((1,), (1,)), ((), ()))
        items = [(unit, half) for unit in range(2) for half in range(2)]
        seen = 3 * HALF

        def wide(index):
            return slice(index * 256, (index + 1) * 256)

        def feats(index):
            unit = items[index][0]
            return slice(unit * HEAD_DIM, (unit + 1) * HEAD_DIM)

        def corners(unit, half):
            rows = slice(half * HALF, (half + 1) * HALF)
            return [
                (rows, slice(unit * 512 + at * 128, unit * 512 + (at + 1) * 128)) for at in range(4)
            ]

        def stacked(ref, unit, half):
            return jnp.concatenate([ref[corner] for corner in corners(unit, half)], axis=0)

        def product(padded, ref, index):
            unit, half = items[index]
            return lax.dot_general(
                padded[half][unit], stacked(ref, unit, half), turn, preferred_element_type=F32
            )

        def parts_of(odd):
            base = odd * seen
            return (
                slice(base, base + HALF),
                slice(base + HALF, base + 2 * HALF),
                slice(base + 2 * HALF, base + seen),
            )

        def scores(index):
            half = items[index][1]
            score = product(padded_k, q_ref, index)
            pairs = []
            for near, far, rest in (parts_of(0), parts_of(1)):
                edge = jnp.where(own, score[near], score[far] + bias)
                pairs.append((edge, score[rest] + bias if half == 0 else score[rest]))
            return pairs

        def weigh(index, odd, edge, whole, dp):
            near, far, rest = parts_of(odd)
            dp_edge, dp_whole = jnp.where(own, dp[near], dp[far]), dp[rest]
            unit = items[index][0]
            base = odd * seen
            row = unit * GROUP + odd
            sink = jnp.concatenate(
                [
                    jnp.where(left, sink_ref[at : at + 1], sink_ref[at + 2 : at + 3])
                    for at in (row, row + 4)
                ],
                axis=1,
            )
            peak = jnp.max(jnp.maximum(edge, whole), axis=0, keepdims=True)
            peak = jnp.maximum(peak, sink)
            edge, whole = jnp.exp(edge - peak), jnp.exp(whole - peak)
            sink_weight = jnp.exp(sink - peak)
            inverse = 1.0 / (jnp.sum(edge + whole, axis=0, keepdims=True) + sink_weight)
            edge, whole = edge * inverse, whole * inverse
            term_edge, term_whole = edge * dp_edge, whole * dp_whole
            delta = jnp.sum(term_edge + term_whole, axis=0, keepdims=True)
            for target, at_edge, at_whole in (
                (prob2, edge, whole),
                (slope2, term_edge - edge * delta, term_whole - whole * delta),
            ):
                edge16 = at_edge.astype(BF16)
                edge_own = edge16 * own16
                target[base : base + HALF, wide(index)] = edge_own
                target[base + HALF : base + 2 * HALF, wide(index)] = edge16 - edge_own
                target[base + 2 * HALF : base + seen, wide(index)] = at_whole.astype(BF16)
            sink_term = sink_weight * inverse * delta
            for at, lanes in ((row, slice(0, 128)), (row + 4, slice(128, 256))):
                part = sink_term[:, lanes]
                sink_rows[at : at + 1] += jnp.where(left, part, 0.0)
                sink_rows[at + 2 : at + 3] += jnp.where(left, 0.0, part)

        def finish(index):
            unit, half = items[index]
            for source, across, out_ref in ((prob2, turned_v, o_ref), (slope2, turned_k, dq_ref)):
                out_t = [
                    jnp.dot(
                        across[half][feats(index)],
                        source[base : base + seen, wide(index)],
                        preferred_element_type=F32,
                    ).astype(BF16)
                    for base in (0, seen)
                ]
                out = jnp.concatenate(out_t, axis=0).T
                for at, corner in enumerate(corners(unit, half)):
                    out_ref[corner] = out[at * HALF : (at + 1) * HALF]

        def reduce(index):
            unit, half = items[index]
            parts = []
            for weights, ref in ((slope2, q_ref), (prob2, g_ref)):
                part = jnp.dot(
                    weights[:, wide(index)], stacked(ref, unit, half), preferred_element_type=F32
                )
                parts.append(jnp.where(left, part[:seen], part[seen:]))
            return parts

        def join(first_half, second_half):
            total = jnp.concatenate(
                [
                    first_half[:HALF] + second_half[2 * HALF :],
                    second_half[:HALF],
                    first_half[HALF : 2 * HALF],
                    first_half[2 * HALF :] + second_half[HALF : 2 * HALF],
                ],
                axis=0,
            )
            return total + pltpu.roll(total, HEAD_DIM, 1)

        ahead, parts = scores(0), []
        for index in range(len(items)):
            now, dp = ahead, product(padded_v, g_ref, index)
            weigh(index, 0, *now[0], dp)
            if index + 1 < len(items):
                ahead = scores(index + 1)
            weigh(index, 1, *now[1], dp)
            if index >= 1:
                finish(index - 1)
            parts.append(reduce(index))
        finish(len(items) - 1)
        grads = [
            [join(parts[2 * unit][place], parts[2 * unit + 1][place]) for place in range(2)]
            for unit in range(2)
        ]
        dk = jnp.where(left, grads[0][0], grads[1][0]) * FACTOR
        dv = jnp.where(left, grads[0][1], grads[1][1])
        dk_ref[here, :] = dk[:WINDOW]
        dv_ref[here, :] = dv[:WINDOW]

        @pl.when(opening & prev_ok)
        def _():
            tail_sum[:, :128] += dk[WINDOW:]
            tail_sum[:, 128:] += dv[WINDOW:]

        @pl.when(jnp.logical_not(opening) & first)
        def _():
            dhalo_ref[:, :128] = dk[WINDOW:].astype(BF16)
            dhalo_ref[:, 128:] = dv[WINDOW:].astype(BF16)

        @pl.when(jnp.logical_not(opening) & jnp.logical_not(first))
        def _():
            dk_ref[before, :] += dk[WINDOW:]
            dv_ref[before, :] += dv[WINDOW:]

    @pl.when(block == blocks_here - 1)
    def _():
        width = 2 * per_slot * HEAD_DIM
        heads = per_slot * GROUP
        total = tail_sum[...].astype(BF16)
        for part in range(2 // per_slot):
            feats = slice(part * width // 2, (part + 1) * width // 2)
            tail = jnp.concatenate([total[:, :128][:, feats], total[:, 128:][:, feats]], axis=1)
            rows = sink_rows[part * heads : (part + 1) * heads]
            rows = jnp.concatenate([rows, jnp.zeros((128 - heads, WINDOW), F32)], axis=0)
            sink_row = jnp.sum(rows.T, axis=0, keepdims=True)
            tail = with_row(tail, sink_row)
            wanted = lax.rem(pair * (2 // per_slot) + part - head + slots, slots)
            for step, dtail_ref in dtails:

                @pl.when(wanted == step)
                def _(dtail_ref=dtail_ref, tail=tail):
                    dtail_ref[...] = tail


def gather_kernel(*refs):
    *in_refs, out_ref = refs
    total, sink_row = 0.0, 0.0
    for in_ref in in_refs:
        total = total + in_ref[...].astype(F32)
        sink_row = sink_row + row_join(in_ref[:16])
    out_ref[...] = with_row(total.astype(BF16), sink_row)


def land_kernel(blocks, plan_ref, here_ref, *refs):
    head = lax.axis_index("head")
    in_refs, out_refs, sink_ref = refs[:LAG], refs[LAG:-1], refs[-1]
    slots = len(out_refs)
    blocks_here = blocks // slots
    for out_ref in out_refs:
        out_ref[...] = jnp.zeros_like(out_ref)
    sink_row = row_join(here_ref[:16])
    seen = lax.broadcasted_iota(jnp.int32, here_ref.shape, 0) > 0
    for distance, in_ref in enumerate(in_refs, 1):
        valid, place = planned_tail(plan_ref, distance)
        sink_row = sink_row + row_join(in_ref[:16])
        wanted = lax.rem(place // blocks_here - head + slots, slots)
        here = pl.ds(pl.multiple_of(place % blocks_here * WINDOW, WINDOW), WINDOW)
        for step, out_ref in enumerate(out_refs):

            @pl.when(valid & (wanted == step))
            def _(out_ref=out_ref, in_ref=in_ref, here=here):
                total = out_ref[here, :].astype(F32) + in_ref[...].astype(F32)
                out_ref[here, :] = jnp.where(seen, total, 0.0).astype(BF16)

    sink_ref[...] = jnp.broadcast_to(sink_row, sink_ref.shape)


def total_kernel(halo_ref, dk_ref, dv_ref, sink_ref, far_ref, *refs):
    *tail_refs, key_ref, value_ref, sink_grad, tails = refs
    slots, rows = len(tail_refs), dk_ref.shape[0]
    width = tails.shape[2] // 2
    head = lax.axis_index("head")
    for step, tail_ref in enumerate(tail_refs):
        tails[lax.rem(head - step + slots, slots)] = tail_ref[...]
    halo_k = jnp.concatenate([halo_ref[pair][:, :128] for pair in range(PAIRS)], axis=1)
    halo_v = jnp.concatenate([halo_ref[pair][:, 128:] for pair in range(PAIRS)], axis=1)
    for in_ref, halo, at, out_ref in (
        (dk_ref, halo_k, 0, key_ref),
        (dv_ref, halo_v, width, value_ref),
    ):
        for begin in range(0, rows, WINDOW):
            here = slice(begin, begin + WINDOW)
            parts = [tails[slot, here, at : at + width] for slot in range(slots)]
            total = in_ref[here, :] + jnp.concatenate(parts, axis=1).astype(F32)
            if begin == rows - WINDOW:
                total = total + halo.astype(F32)
            out_ref[here, :] = total.astype(BF16)
    sink_row = -(sink_ref[0:1] + far_ref[0:1])
    sink_grad[...] = sink_row[0, : sink_grad.shape[0]]


def swap(values, axis):
    return [values[0]] + [ring(values[step], axis, step) for step in range(1, len(values))]


def local(
    queries, key_states, value_states, out_grad, sink_logits, branch_start, branch_len, parent_list
):
    tok_count, head_count = lax.axis_size("tok"), lax.axis_size("head")
    rows = queries.shape[0]
    blocks_here = rows // WINDOW
    blocks = blocks_here * head_count
    per_slot = KV_HEADS // head_count
    width = 2 * per_slot * HEAD_DIM

    def shape(dims, kind=BF16):
        return jax.ShapeDtypeStruct(dims, kind)

    def far(value):
        return pltpu.with_memory_space_constraint(value, pltpu.HBM)

    def close(value):
        return pltpu.with_memory_space_constraint(value, pltpu.VMEM)

    *slots, halo_out, keys, values = pl.pallas_call(
        pack_kernel,
        out_shape=(shape((rows, width)),) * head_count
        + (shape((PAIRS, WINDOW, 256)),)
        + (pltpu.VMEM(key_states.shape, BF16),) * 2,
        in_specs=[HBM] * 3,
        out_specs=(VMEM,) * (head_count + 3),
        scratch_shapes=[
            pltpu.SMEM(sink_logits.shape, F32),
            pltpu.SemaphoreType.DMA((3,)),
        ],
        compiler_params=PARAMS,
        name="pack",
    )(far(sink_logits), far(key_states), far(value_states))
    spread = swap(slots, "head")
    halo = shift(halo_out, "head", 1)
    plan = pl.pallas_call(
        functools.partial(plan_kernel, tok_count, blocks, blocks_here),
        out_shape=pltpu.VMEM((8, 128), jnp.int32),
        in_specs=[SMEM] * 3,
        out_specs=VMEM,
        compiler_params=PARAMS,
        name="plan",
    )(far(branch_start), far(branch_len), far(parent_list.T))
    plan = close(plan)
    chosen = pl.pallas_call(
        choose_kernel,
        out_shape=(shape((WINDOW, width)),) * LAG,
        in_specs=[VMEM] * (1 + head_count),
        out_specs=(VMEM,) * LAG,
        compiler_params=PARAMS,
        name="choose",
    )(plan, *spread)
    late_slots = lax.optimization_barrier((*spread, *chosen))
    late_slots, chosen = late_slots[:head_count], late_slots[head_count:]
    sinks = pl.pallas_call(
        sinks_kernel,
        out_shape=shape((KV_HEADS * GROUP, 128), F32),
        in_specs=[VMEM] * head_count,
        out_specs=VMEM,
        compiler_params=PARAMS,
        name="sinks",
    )(*late_slots)
    arrived = [ring(chosen[LAG - s], "tok", s) for s in range(LAG, 0, -1)]
    queries, out_grad, _ = lax.optimization_barrier((queries, out_grad, sinks))
    near_queries, near_grad = pl.pallas_call(
        stage_kernel,
        out_shape=(pltpu.VMEM(queries.shape, BF16),) * 2,
        in_specs=[HBM] * 2,
        out_specs=(VMEM,) * 2,
        scratch_shapes=[pltpu.SemaphoreType.DMA((2,))],
        compiler_params=PARAMS,
        name="stage",
    )(far(queries), far(out_grad))
    *arrived, near_queries, near_grad = lax.optimization_barrier(
        (*arrived, near_queries, near_grad)
    )
    quarter = pl.pallas_call(
        arrive_kernel,
        out_shape=shape((WINDOW, width)),
        in_specs=[VMEM] * (1 + LAG),
        out_specs=VMEM,
        compiler_params=PARAMS,
        name="arrive",
    )(plan, *arrived)
    tails = swap([quarter] * head_count, "head")

    def attend(steps, pairs, offset, halo, joined):
        inputs = (
            sinks,
            close(near_queries),
            close(near_grad),
            close(keys),
            close(values),
            halo,
            *(tails[-step % head_count] for step in steps),
            *(close(value) for value in joined),
        )
        base = 1 + len(inputs) - len(joined)
        return pl.pallas_call(
            functools.partial(
                attend_kernel,
                blocks_here,
                head_count,
                steps,
                offset,
                pairs,
                len(joined),
            ),
            out_shape=(
                pltpu.VMEM(queries.shape, BF16),
                pltpu.VMEM(queries.shape, BF16),
                pltpu.VMEM(key_states.shape, F32),
                pltpu.VMEM(key_states.shape, F32),
                pltpu.VMEM((PAIRS, WINDOW, 256), BF16),
            )
            + (shape((WINDOW, width)),) * len(steps),
            in_specs=[VMEM] * (1 + len(inputs)),
            out_specs=(VMEM,) * (5 + len(steps)),
            scratch_shapes=[
                pltpu.VMEM((head_count, WINDOW, width), BF16),
                pltpu.VMEM((WINDOW, 256), F32),
                pltpu.VMEM((2 * GROUP, WINDOW), F32),
                pltpu.VMEM((6 * HALF, 1024), BF16),
                pltpu.VMEM((6 * HALF, 1024), BF16),
            ],
            input_output_aliases={base + place: place for place in range(len(joined))},
            compiler_params=PARAMS,
            name="attend",
        )(plan, *inputs)

    if per_slot == 2:
        *joined, own_tail = attend((0,), 1, 0, spread[1], ())
        *joined, tail_1, tail_2 = attend((1, 2), 2, 1, halo, joined)
        *results, tail_3 = attend((3,), 1, 3, halo, joined)
        dtail = [own_tail, tail_1, tail_2, tail_3]
    else:
        results = attend(tuple(range(head_count)), PAIRS, None, halo, ())
        results, dtail = results[:5], list(results[5:])
    attended, query_grad, dk, dv, dhalo = results
    parts = swap(dtail, "head")

    def gather(values):
        return pl.pallas_call(
            gather_kernel,
            out_shape=shape((WINDOW, width)),
            in_specs=[VMEM] * len(values),
            out_specs=VMEM,
            compiler_params=PARAMS,
            name="gather",
        )(*values)

    quarter_grad = gather([gather(parts[:-1]), parts[-1]])

    def flush(value):
        return pl.pallas_call(
            stage_kernel,
            out_shape=pltpu.HBM(value.shape, BF16),
            in_specs=[VMEM],
            out_specs=HBM,
            scratch_shapes=[pltpu.SemaphoreType.DMA((1,))],
            compiler_params=PARAMS,
            name="flush",
        )(close(value))

    returned = [ring(quarter_grad, "tok", -s) for s in range(LAG, 0, -1)][::-1]
    attended, _ = lax.optimization_barrier((attended, quarter_grad))
    attended = flush(attended)
    attended, *returned = lax.optimization_barrier((attended, *returned))
    halo_back = shift(dhalo, "head", -1)
    *landed, sink_near = pl.pallas_call(
        functools.partial(land_kernel, blocks),
        out_shape=(shape((rows, width)),) * head_count + (shape((8, 128), F32),),
        in_specs=[VMEM] * (LAG + 2),
        out_specs=(VMEM,) * (head_count + 1),
        compiler_params=PARAMS,
        name="land",
    )(plan, quarter_grad, *returned)
    tails_back = swap(landed, "head")
    query_grad, _ = lax.optimization_barrier((query_grad, sink_near))
    query_grad = flush(query_grad)
    span = LAG + 1
    while 2 * span < tok_count:
        sink_near = sink_near + ring(sink_near, "tok", -span)
        span *= 2
    sink_far = ring(sink_near, "tok", -span)
    key_grad, value_grad, sink_grad = pl.pallas_call(
        total_kernel,
        out_shape=(
            shape(key_states.shape),
            shape(value_states.shape),
            shape(sink_logits.shape, F32),
        ),
        in_specs=[VMEM] * (5 + head_count),
        out_specs=(VMEM,) * 3,
        scratch_shapes=[pltpu.VMEM((head_count, rows, width), BF16)],
        compiler_params=PARAMS,
        name="total",
    )(halo_back, dk, dv, sink_near, sink_far, *tails_back)
    return attended, query_grad, key_grad, value_grad, sink_grad


def solution(mesh):
    rows = P(("tok", "head"), None)
    return jax.shard_map(
        local,
        mesh=mesh,
        in_specs=(rows, rows, rows, rows, P("head"), P(), P(), P()),
        out_specs=(rows, rows, rows, rows, P("head")),
        check_vma=False,
    )
```

```python
import functools

import jax
import jax.numpy as jnp
from jax import lax
from jax.experimental import pallas as pl
from jax.experimental.pallas import tpu as pltpu
from jax.sharding import PartitionSpec as P

HEAD_DIM = 64
KV_HEADS = 8
GROUP = 8
WINDOW = 128
HALF = WINDOW // 2
LAG = 3
BR_DEV = 2
PAIRS = KV_HEADS // 2
FACTOR = 0.125
LOW = -1e30
BF16 = jnp.bfloat16
F32 = jnp.float32

SMEM = pl.BlockSpec(memory_space=pltpu.SMEM)
VMEM = pl.BlockSpec(memory_space=pltpu.VMEM)
HBM = pl.BlockSpec(memory_space=pltpu.HBM)
PARAMS = pltpu.CompilerParams(vmem_limit_bytes=24 * 1024 * 1024)


def shift(value, axis, steps):
    count = lax.axis_size(axis)
    leading, last = (max(0, -steps), min(count, count - steps))
    return lax.ppermute(value, axis, [(source, source + steps) for source in range(leading, last)])


def ring(value, axis, steps):
    count = lax.axis_size(axis)
    return lax.ppermute(value, axis, [(source, (source + steps) % count) for source in range(count)])


def with_row(tile, row):
    high = row.astype(BF16).astype(F32)
    middle = (row - high).astype(BF16).astype(F32)
    low = row - high - middle
    packed = high + pltpu.roll(middle, 32, 1) + pltpu.roll(low, 64, 1)
    place = lax.broadcasted_iota(jnp.int32, (16, 128), 0)
    top = jnp.where(place == 0, packed, tile[:16, :128].astype(F32)).astype(BF16)
    if tile.shape[1] > 128:
        top = jnp.concatenate([top, tile[:16, 128:]], axis=1)
    return jnp.concatenate([top, tile[16:]], axis=0)


def row_join(top):
    packed = top[0:1, :128].astype(F32)
    row = packed + pltpu.roll(packed, 96, 1) + pltpu.roll(packed, 64, 1)
    return jnp.where(lax.broadcasted_iota(jnp.int32, (1, 128), 1) < 32, row, 0.0)


def child_tail(starts, parents, tok, distance, tok_count, blocks):
    child = jnp.minimum(tok + distance, tok_count - 1) * BR_DEV
    parent = parents[0, child]
    safe = jnp.maximum(parent, 0)
    valid = (tok + distance < tok_count) & (parent >= 0) & (safe // BR_DEV == tok)
    place = (starts[safe] + parents[1, child]) // WINDOW - tok * blocks
    return valid, jnp.where(valid, place, 0)


def block_state(starts, lengths, parents, tok, block):
    position = block * WINDOW
    alive, opening = jnp.bool_(False), jnp.bool_(False)
    for branch in range(BR_DEV):
        start = starts[tok * BR_DEV + branch]
        length = lengths[tok * BR_DEV + branch]
        alive = alive | ((start <= position) & (position < start + length))
        opening = opening | (start == position)
    has_tail = parents[0, tok * BR_DEV] >= 0
    return alive, opening, jnp.logical_not(opening) | has_tail


def plan_kernel(tok_count, blocks, blocks_here, starts, lengths, parents, plan_ref):
    tok, head = lax.axis_index("tok"), lax.axis_index("head")
    values = []
    for distance in range(1, LAG + 1):
        values += child_tail(starts, parents, tok, distance, tok_count, blocks)
    parent = parents[0, tok * BR_DEV]
    values.append(jnp.where(parent >= 0, tok - jnp.maximum(parent, 0) // BR_DEV, 1))
    for block in range(blocks_here):
        number = tok * blocks + head * blocks_here + block
        values += block_state(starts, lengths, parents, tok, number)
    lane = lax.broadcasted_iota(jnp.int32, plan_ref.shape, 1)
    plan = jnp.zeros(plan_ref.shape, jnp.int32)
    for place, value in enumerate(values):
        plan = jnp.where(lane == place, value.astype(jnp.int32), plan)
    plan_ref[...] = plan


def planned_tail(plan_ref, distance):
    row = plan_ref[0:1, :]
    return row[0, 2 * distance - 2] != 0, row[0, 2 * distance - 1]


def planned_source(plan_ref):
    return plan_ref[0:1, :][0, 2 * LAG]


def planned_block(plan_ref, block):
    row = plan_ref[0:1, :]
    return tuple(row[0, 2 * LAG + 1 + 3 * block + place] for place in range(3))


def take(ref, slot, width):
    if width % 128 == 0:
        return ref[:, pl.ds(pl.multiple_of(slot * width, width), width)]
    value = ref[:, :width]
    for other in range(1, ref.shape[1] // width):
        value = jnp.where(slot == other, ref[:, other * width : (other + 1) * width], value)
    return value


def pack_kernel(sink_hbm, key_hbm, value_hbm, *refs):
    *slot_refs, halo_ref, keys, values, sinks, sems = refs
    copies = [
        pltpu.make_async_copy(source, target, sems.at[place])
        for place, (source, target) in enumerate(
            ((sink_hbm, sinks), (key_hbm, keys), (value_hbm, values))
        )
    ]
    for copy in copies:
        copy.start()
    for copy in copies:
        copy.wait()
    slots, rows = len(slot_refs), keys.shape[0]
    head = lax.axis_index("head")
    width = KV_HEADS * HEAD_DIM // slots
    lane = lax.broadcasted_iota(jnp.int32, (1, 128), 1)
    sink_row = jnp.zeros((1, 128), F32)
    for place in range(sinks.shape[0]):
        sink_row = jnp.where(lane == place, sinks[place], sink_row)
    for step, slot_ref in enumerate(slot_refs):
        slot = lax.rem(head + step, slots)
        both = jnp.concatenate([take(keys, slot, width), take(values, slot, width)], axis=1)
        slot_ref[...] = with_row(both, sink_row)
    for pair in range(PAIRS):
        lanes = slice(pair * 128, (pair + 1) * 128)
        last = slice(rows - WINDOW, rows)
        halo_ref[pair] = jnp.concatenate([keys[last, lanes], values[last, lanes]], axis=1)


def choose_kernel(plan_ref, *refs):
    slots = len(refs) - LAG
    slot_refs, out_refs = refs[:slots], refs[slots:]
    head = lax.axis_index("head")
    rows = slot_refs[0].shape[0]
    blocks_here = rows // WINDOW
    for distance, out_ref in zip(range(LAG, 0, -1), out_refs):
        _, place = planned_tail(plan_ref, distance)
        begin = pl.multiple_of(place % blocks_here * WINDOW, WINDOW)
        wanted = lax.rem(head - place // blocks_here + slots, slots)
        for step, slot_ref in enumerate(slot_refs):

            @pl.when(wanted == step)
            def _(out_ref=out_ref, slot_ref=slot_ref, begin=begin):
                out_ref[...] = slot_ref[pl.ds(begin, WINDOW), :]


def sinks_kernel(*refs):
    *slot_refs, sink_ref = refs
    slots = len(slot_refs)
    head = lax.axis_index("head")
    heads = sink_ref.shape[0] // slots
    for step, slot_ref in enumerate(slot_refs):
        source = lax.rem(head - step + slots, slots)
        sink_row = row_join(slot_ref[:16])
        turned = jnp.broadcast_to(sink_row, (128, 128)).T
        sink_ref[pl.ds(pl.multiple_of(source * heads, heads), heads), :] = turned[:heads]


def arrive_kernel(plan_ref, *refs):
    *in_refs, out_ref = refs
    mine = planned_source(plan_ref)
    for distance, in_ref in zip(range(LAG, 0, -1), in_refs):

        @pl.when(mine == distance)
        def _(in_ref=in_ref):
            out_ref[...] = in_ref[...]


def stage_kernel(*refs):
    *arrays, sems = refs
    half = len(arrays) // 2
    copies = [
        pltpu.make_async_copy(source, target, sems.at[place])
        for place, (source, target) in enumerate(zip(arrays[:half], arrays[half:]))
    ]
    for copy in copies:
        copy.start()
    for copy in copies:
        copy.wait()


def attend_kernel(blocks_here, slots, steps, offset, pairs, joins, *refs):
    inputs, refs = refs[:7], refs[7:]
    tail_refs, refs = refs[: len(steps)], refs[len(steps) + joins :]
    outputs, refs = refs[:5], refs[5:]
    dtail_refs, refs = refs[: len(steps)], refs[len(steps) :]
    tails, *scratch = refs
    head = lax.axis_index("head")
    states = [planned_block(inputs[0], block) for block in range(blocks_here)]
    for step, tail_ref in zip(steps, tail_refs):
        tails[lax.rem(head + step, slots)] = tail_ref[...]

    def step(place, carry):
        pair = place // blocks_here
        if offset is not None:
            pair = lax.rem(head + pair + offset, PAIRS)
        block = place % blocks_here
        state = states[0]
        for other in range(1, blocks_here):
            state = [jnp.where(block == other, *two) for two in zip(states[other], state)]
        attend_block(
            blocks_here,
            slots,
            pair,
            block,
            [value != 0 for value in state],
            inputs,
            outputs,
            tails,
            tuple(zip(steps, dtail_refs)),
            scratch,
        )
        return carry

    lax.fori_loop(0, pairs * blocks_here, step, 0)


def attend_block(
    blocks_here, slots, pair, block, state, inputs, outputs, tails, dtails, scratch
):
    _, sink_ref, q_ref, g_ref, k_ref, v_ref, halo_ref = inputs
    o_ref, dq_ref, dk_ref, dv_ref, dhalo_ref = outputs
    tail_sum, sink_rows, prob2, slope2 = scratch
    per_slot = KV_HEADS // slots
    head = lax.axis_index("head")
    alive, opening, prev_ok = state
    here = pl.ds(pl.multiple_of(block * WINDOW, WINDOW), WINDOW)
    before = pl.ds(pl.multiple_of(jnp.maximum(block - 1, 0) * WINDOW, WINDOW), WINDOW)
    first = block == 0
    near = pl.ds(pl.multiple_of(pair * 128, 128), 128)
    big = pl.ds(pl.multiple_of(pair * 1024, 1024), 1024)
    q_ref, g_ref, o_ref, dq_ref = (ref.at[here, big] for ref in (q_ref, g_ref, o_ref, dq_ref))
    k_ref, v_ref, dk_ref, dv_ref = (ref.at[:, near] for ref in (k_ref, v_ref, dk_ref, dv_ref))
    sink_ref = sink_ref.at[pl.ds(pl.multiple_of(pair * 16, 16), 16)]
    dhalo_ref = dhalo_ref.at[pair]

    @pl.when(first)
    def _():
        tail_sum[...] = jnp.zeros_like(tail_sum)
        dhalo_ref[...] = jnp.zeros((WINDOW, 256), BF16)
        sink_rows[...] = jnp.zeros_like(sink_rows)

    @pl.when(jnp.logical_not(alive))
    def _():
        o_ref[...] = jnp.zeros((WINDOW, 1024), BF16)
        dq_ref[...] = jnp.zeros((WINDOW, 1024), BF16)
        dk_ref[here, :] = jnp.zeros((WINDOW, 128), F32)
        dv_ref[here, :] = jnp.zeros((WINDOW, 128), F32)

    @pl.when(alive)
    def _():
        if len(halo_ref.shape) == 2:
            halo = halo_ref[halo_ref.shape[0] - WINDOW :]
        else:
            halo = halo_ref[pair]
        if per_slot == 2:
            tail = tails[pair]
            tail_k, tail_v = tail[:, :128], tail[:, 128:]
        else:
            tail_a, tail_b = tails[2 * pair], tails[2 * pair + 1]
            tail_k = jnp.concatenate([tail_a[:, :64], tail_b[:, :64]], axis=1)
            tail_v = jnp.concatenate([tail_a[:, 64:], tail_b[:, 64:]], axis=1)
        near_k = jnp.where(first, halo[:, :128], k_ref[before, :])
        near_v = jnp.where(first, halo[:, 128:], v_ref[before, :])
        prev_k = jnp.where(opening, tail_k, near_k)
        prev_v = jnp.where(opening, tail_v, near_v)
        own_k, own_v = k_ref[here, :], v_ref[here, :]

        def halves(own, prev):
            return (
                jnp.concatenate([own[:HALF], prev[:HALF], prev[HALF:]], axis=0),
                jnp.concatenate([own[HALF:], prev[HALF:], own[:HALF]], axis=0),
            )

        left = lax.broadcasted_iota(jnp.int32, (1, 128), 1) < HALF
        low16 = left.astype(F32).astype(BF16)
        high16 = BF16(1) - low16

        def padded(seen):
            swapped = jnp.concatenate([seen[:, 64:], seen[:, :64]], axis=1)
            return (
                jnp.concatenate([seen * low16, swapped * high16], axis=0),
                jnp.concatenate([swapped * low16, seen * high16], axis=0),
            )

        seen_k = halves(own_k * BF16(FACTOR), prev_k * BF16(FACTOR))
        seen_v = halves(own_v, prev_v)
        padded_k = tuple(padded(value) for value in seen_k)
        padded_v = tuple(padded(value) for value in seen_v)
        turned_k = tuple(value.T for value in seen_k)
        turned_v = tuple(value.T for value in seen_v)
        bias = jnp.where(prev_ok, 0.0, LOW)
        key_place = lax.broadcasted_iota(jnp.int32, (HALF, 4 * HALF), 0)
        query_place = lax.broadcasted_iota(jnp.int32, (HALF, 4 * HALF), 1) & (HALF - 1)
        own = key_place <= query_place
        own16 = own.astype(F32).astype(BF16)
        turn = (((1,), (1,)), ((), ()))
        items = [(unit, half) for unit in range(2) for half in range(2)]
        seen = 3 * HALF

        def wide(index):
            return slice(index * 256, (index + 1) * 256)

        def feats(index):
            unit = items[index][0]
            return slice(unit * HEAD_DIM, (unit + 1) * HEAD_DIM)

        def corners(unit, half):
            rows = slice(half * HALF, (half + 1) * HALF)
            return [
                (rows, slice(unit * 512 + at * 128, unit * 512 + (at + 1) * 128)) for at in range(4)
            ]

        def stacked(ref, unit, half):
            return jnp.concatenate([ref[corner] for corner in corners(unit, half)], axis=0)

        def products(index):
            unit, half = items[index]
            score, dp = (
                lax.dot_general(
                    padded[half][unit],
                    stacked(ref, unit, half),
                    turn,
                    preferred_element_type=F32,
                )
                for padded, ref in ((padded_k, q_ref), (padded_v, g_ref))
            )
            parts = []
            for base in (0, seen):
                near, far = slice(base, base + HALF), slice(base + HALF, base + 2 * HALF)
                rest = slice(base + 2 * HALF, base + 3 * HALF)
                edge = jnp.where(own, score[near], score[far] + bias)
                whole = score[rest] + bias if half == 0 else score[rest]
                parts.append((edge, whole, jnp.where(own, dp[near], dp[far]), dp[rest]))
            return parts

        def weigh(index, odd, edge, whole, dp_edge, dp_whole):
            unit, half = items[index]
            base = odd * seen
            row = unit * GROUP + odd
            sink = jnp.concatenate(
                [
                    jnp.where(left, sink_ref[at : at + 1], sink_ref[at + 2 : at + 3])
                    for at in (row, row + 4)
                ],
                axis=1,
            )
            peak = jnp.max(jnp.maximum(edge, whole), axis=0, keepdims=True)
            peak = jnp.maximum(peak, sink)
            edge, whole = jnp.exp(edge - peak), jnp.exp(whole - peak)
            sink_weight = jnp.exp(sink - peak)
            inverse = 1.0 / (jnp.sum(edge + whole, axis=0, keepdims=True) + sink_weight)
            edge, whole = edge * inverse, whole * inverse
            term_edge, term_whole = edge * dp_edge, whole * dp_whole
            delta = jnp.sum(term_edge + term_whole, axis=0, keepdims=True)
            for target, at_edge, at_whole in (
                (prob2, edge, whole),
                (slope2, term_edge - edge * delta, term_whole - whole * delta),
            ):
                edge16 = at_edge.astype(BF16)
                edge_own = edge16 * own16
                target[base : base + HALF, wide(index)] = edge_own
                target[base + HALF : base + 2 * HALF, wide(index)] = edge16 - edge_own
                target[base + 2 * HALF : base + seen, wide(index)] = at_whole.astype(BF16)
            sink_term = sink_weight * inverse * delta
            for at, lanes in ((row, slice(0, 128)), (row + 4, slice(128, 256))):
                part = sink_term[:, lanes]
                sink_rows[at : at + 1] += jnp.where(left, part, 0.0)
                sink_rows[at + 2 : at + 3] += jnp.where(left, 0.0, part)

        def finish(index):
            unit, half = items[index]
            for source, across, out_ref in ((prob2, turned_v, o_ref), (slope2, turned_k, dq_ref)):
                out_t = [
                    jnp.dot(
                        across[half][feats(index)],
                        source[base : base + seen, wide(index)],
                        preferred_element_type=F32,
                    ).astype(BF16)
                    for base in (0, seen)
                ]
                out = jnp.concatenate(out_t, axis=0).T
                for at, corner in enumerate(corners(unit, half)):
                    out_ref[corner] = out[at * HALF : (at + 1) * HALF]

        def reduce(index):
            unit, half = items[index]
            parts = []
            for weights, ref in ((slope2, q_ref), (prob2, g_ref)):
                part = jnp.dot(
                    weights[:, wide(index)], stacked(ref, unit, half), preferred_element_type=F32
                )
                parts.append(jnp.where(left, part[:seen], part[seen:]))
            return parts

        def join(first_half, second_half):
            total = jnp.concatenate(
                [
                    first_half[:HALF] + second_half[2 * HALF :],
                    second_half[:HALF],
                    first_half[HALF : 2 * HALF],
                    first_half[2 * HALF :] + second_half[HALF : 2 * HALF],
                ],
                axis=0,
            )
            return total + pltpu.roll(total, HEAD_DIM, 1)

        ahead, parts = [products(0), products(1)], []
        for index in range(len(items)):
            now = ahead.pop(0)
            weigh(index, 0, *now[0])
            if index + 2 < len(items):
                ahead.append(products(index + 2))
            weigh(index, 1, *now[1])
            if index >= 1:
                finish(index - 1)
            parts.append(reduce(index))
        finish(len(items) - 1)
        grads = [
            [join(parts[2 * unit][place], parts[2 * unit + 1][place]) for place in range(2)]
            for unit in range(2)
        ]
        dk = jnp.where(left, grads[0][0], grads[1][0]) * FACTOR
        dv = jnp.where(left, grads[0][1], grads[1][1])
        dk_ref[here, :] = dk[:WINDOW]
        dv_ref[here, :] = dv[:WINDOW]

        @pl.when(opening & prev_ok)
        def _():
            tail_sum[:, :128] += dk[WINDOW:]
            tail_sum[:, 128:] += dv[WINDOW:]

        @pl.when(jnp.logical_not(opening) & first)
        def _():
            dhalo_ref[:, :128] = dk[WINDOW:].astype(BF16)
            dhalo_ref[:, 128:] = dv[WINDOW:].astype(BF16)

        @pl.when(jnp.logical_not(opening) & jnp.logical_not(first))
        def _():
            dk_ref[before, :] += dk[WINDOW:]
            dv_ref[before, :] += dv[WINDOW:]

    @pl.when(block == blocks_here - 1)
    def _():
        width = 2 * per_slot * HEAD_DIM
        heads = per_slot * GROUP
        total = tail_sum[...].astype(BF16)
        for part in range(2 // per_slot):
            feats = slice(part * width // 2, (part + 1) * width // 2)
            tail = jnp.concatenate([total[:, :128][:, feats], total[:, 128:][:, feats]], axis=1)
            rows = sink_rows[part * heads : (part + 1) * heads]
            rows = jnp.concatenate([rows, jnp.zeros((128 - heads, WINDOW), F32)], axis=0)
            sink_row = jnp.sum(rows.T, axis=0, keepdims=True)
            tail = with_row(tail, sink_row)
            wanted = lax.rem(pair * (2 // per_slot) + part - head + slots, slots)
            for step, dtail_ref in dtails:

                @pl.when(wanted == step)
                def _(dtail_ref=dtail_ref, tail=tail):
                    dtail_ref[...] = tail


def gather_kernel(*refs):
    *in_refs, out_ref = refs
    total, sink_row = 0.0, 0.0
    for in_ref in in_refs:
        total = total + in_ref[...].astype(F32)
        sink_row = sink_row + row_join(in_ref[:16])
    out_ref[...] = with_row(total.astype(BF16), sink_row)


def land_kernel(blocks, plan_ref, here_ref, *refs):
    head = lax.axis_index("head")
    in_refs, out_refs, sink_ref = refs[:LAG], refs[LAG:-1], refs[-1]
    slots = len(out_refs)
    blocks_here = blocks // slots
    for out_ref in out_refs:
        out_ref[...] = jnp.zeros_like(out_ref)
    sink_row = row_join(here_ref[:16])
    seen = lax.broadcasted_iota(jnp.int32, here_ref.shape, 0) > 0
    for distance, in_ref in enumerate(in_refs, 1):
        valid, place = planned_tail(plan_ref, distance)
        sink_row = sink_row + row_join(in_ref[:16])
        wanted = lax.rem(place // blocks_here - head + slots, slots)
        here = pl.ds(pl.multiple_of(place % blocks_here * WINDOW, WINDOW), WINDOW)
        for step, out_ref in enumerate(out_refs):

            @pl.when(valid & (wanted == step))
            def _(out_ref=out_ref, in_ref=in_ref, here=here):
                total = out_ref[here, :].astype(F32) + in_ref[...].astype(F32)
                out_ref[here, :] = jnp.where(seen, total, 0.0).astype(BF16)

    sink_ref[...] = jnp.broadcast_to(sink_row, sink_ref.shape)


def total_kernel(halo_ref, dk_ref, dv_ref, sink_ref, far_ref, *refs):
    *tail_refs, key_ref, value_ref, sink_grad, tails = refs
    slots, rows = len(tail_refs), dk_ref.shape[0]
    width = tails.shape[2] // 2
    head = lax.axis_index("head")
    for step, tail_ref in enumerate(tail_refs):
        tails[lax.rem(head - step + slots, slots)] = tail_ref[...]
    halo_k = jnp.concatenate([halo_ref[pair][:, :128] for pair in range(PAIRS)], axis=1)
    halo_v = jnp.concatenate([halo_ref[pair][:, 128:] for pair in range(PAIRS)], axis=1)
    for in_ref, halo, at, out_ref in (
        (dk_ref, halo_k, 0, key_ref),
        (dv_ref, halo_v, width, value_ref),
    ):
        for begin in range(0, rows, WINDOW):
            here = slice(begin, begin + WINDOW)
            parts = [tails[slot, here, at : at + width] for slot in range(slots)]
            total = in_ref[here, :] + jnp.concatenate(parts, axis=1).astype(F32)
            if begin == rows - WINDOW:
                total = total + halo.astype(F32)
            out_ref[here, :] = total.astype(BF16)
    sink_row = -(sink_ref[0:1] + far_ref[0:1])
    sink_grad[...] = sink_row[0, : sink_grad.shape[0]]


def swap(values, axis):
    return [values[0]] + [ring(values[step], axis, step) for step in range(1, len(values))]


def local(
    queries, key_states, value_states, out_grad, sink_logits, branch_start, branch_len, parent_list
):
    tok_count, head_count = lax.axis_size("tok"), lax.axis_size("head")
    rows = queries.shape[0]
    blocks_here = rows // WINDOW
    blocks = blocks_here * head_count
    per_slot = KV_HEADS // head_count
    width = 2 * per_slot * HEAD_DIM

    def shape(dims, kind=BF16):
        return jax.ShapeDtypeStruct(dims, kind)

    def far(value):
        return pltpu.with_memory_space_constraint(value, pltpu.HBM)

    def close(value):
        return pltpu.with_memory_space_constraint(value, pltpu.VMEM)

    *slots, halo_out, keys, values = pl.pallas_call(
        pack_kernel,
        out_shape=(shape((rows, width)),) * head_count
        + (shape((PAIRS, WINDOW, 256)),)
        + (pltpu.VMEM(key_states.shape, BF16),) * 2,
        in_specs=[HBM] * 3,
        out_specs=(VMEM,) * (head_count + 3),
        scratch_shapes=[
            pltpu.SMEM(sink_logits.shape, F32),
            pltpu.SemaphoreType.DMA((3,)),
        ],
        compiler_params=PARAMS,
        name="pack",
    )(far(sink_logits), far(key_states), far(value_states))
    spread = swap(slots, "head")
    halo = shift(halo_out, "head", 1)
    plan = pl.pallas_call(
        functools.partial(plan_kernel, tok_count, blocks, blocks_here),
        out_shape=pltpu.VMEM((8, 128), jnp.int32),
        in_specs=[SMEM] * 3,
        out_specs=VMEM,
        compiler_params=PARAMS,
        name="plan",
    )(far(branch_start), far(branch_len), far(parent_list.T))
    plan = close(plan)
    chosen = pl.pallas_call(
        choose_kernel,
        out_shape=(shape((WINDOW, width)),) * LAG,
        in_specs=[VMEM] * (1 + head_count),
        out_specs=(VMEM,) * LAG,
        compiler_params=PARAMS,
        name="choose",
    )(plan, *spread)
    late_slots = lax.optimization_barrier((*spread, *chosen))
    late_slots, chosen = late_slots[:head_count], late_slots[head_count:]
    sinks = pl.pallas_call(
        sinks_kernel,
        out_shape=shape((KV_HEADS * GROUP, 128), F32),
        in_specs=[VMEM] * head_count,
        out_specs=VMEM,
        compiler_params=PARAMS,
        name="sinks",
    )(*late_slots)
    arrived = [ring(chosen[LAG - s], "tok", s) for s in range(LAG, 0, -1)]
    queries, out_grad, _ = lax.optimization_barrier((queries, out_grad, sinks))
    near_queries, near_grad = pl.pallas_call(
        stage_kernel,
        out_shape=(pltpu.VMEM(queries.shape, BF16),) * 2,
        in_specs=[HBM] * 2,
        out_specs=(VMEM,) * 2,
        scratch_shapes=[pltpu.SemaphoreType.DMA((2,))],
        compiler_params=PARAMS,
        name="stage",
    )(far(queries), far(out_grad))
    *arrived, near_queries, near_grad = lax.optimization_barrier(
        (*arrived, near_queries, near_grad)
    )
    quarter = pl.pallas_call(
        arrive_kernel,
        out_shape=shape((WINDOW, width)),
        in_specs=[VMEM] * (1 + LAG),
        out_specs=VMEM,
        compiler_params=PARAMS,
        name="arrive",
    )(plan, *arrived)
    tails = swap([quarter] * head_count, "head")

    def attend(steps, pairs, offset, halo, joined):
        inputs = (
            sinks,
            close(near_queries),
            close(near_grad),
            close(keys),
            close(values),
            halo,
            *(tails[-step % head_count] for step in steps),
            *(close(value) for value in joined),
        )
        base = 1 + len(inputs) - len(joined)
        return pl.pallas_call(
            functools.partial(
                attend_kernel,
                blocks_here,
                head_count,
                steps,
                offset,
                pairs,
                len(joined),
            ),
            out_shape=(
                pltpu.VMEM(queries.shape, BF16),
                pltpu.VMEM(queries.shape, BF16),
                pltpu.VMEM(key_states.shape, F32),
                pltpu.VMEM(key_states.shape, F32),
                pltpu.VMEM((PAIRS, WINDOW, 256), BF16),
            )
            + (shape((WINDOW, width)),) * len(steps),
            in_specs=[VMEM] * (1 + len(inputs)),
            out_specs=(VMEM,) * (5 + len(steps)),
            scratch_shapes=[
                pltpu.VMEM((head_count, WINDOW, width), BF16),
                pltpu.VMEM((WINDOW, 256), F32),
                pltpu.VMEM((2 * GROUP, WINDOW), F32),
                pltpu.VMEM((6 * HALF, 1024), BF16),
                pltpu.VMEM((6 * HALF, 1024), BF16),
            ],
            input_output_aliases={base + place: place for place in range(len(joined))},
            compiler_params=PARAMS,
            name="attend",
        )(plan, *inputs)

    if per_slot == 2:
        *joined, own_tail = attend((0,), 1, 0, spread[1], ())
        *joined, tail_1, tail_2 = attend((1, 2), 2, 1, halo, joined)
        *results, tail_3 = attend((3,), 1, 3, halo, joined)
        dtail = [own_tail, tail_1, tail_2, tail_3]
    else:
        results = attend(tuple(range(head_count)), PAIRS, None, halo, ())
        results, dtail = results[:5], list(results[5:])
    attended, query_grad, dk, dv, dhalo = results
    parts = swap(dtail, "head")

    def gather(values):
        return pl.pallas_call(
            gather_kernel,
            out_shape=shape((WINDOW, width)),
            in_specs=[VMEM] * len(values),
            out_specs=VMEM,
            compiler_params=PARAMS,
            name="gather",
        )(*values)

    quarter_grad = gather([gather(parts[:-1]), parts[-1]])

    def flush(value):
        return pl.pallas_call(
            stage_kernel,
            out_shape=pltpu.HBM(value.shape, BF16),
            in_specs=[VMEM],
            out_specs=HBM,
            scratch_shapes=[pltpu.SemaphoreType.DMA((1,))],
            compiler_params=PARAMS,
            name="flush",
        )(close(value))

    returned = [ring(quarter_grad, "tok", -s) for s in range(LAG, 0, -1)][::-1]
    attended, _ = lax.optimization_barrier((attended, quarter_grad))
    attended = flush(attended)
    attended, *returned = lax.optimization_barrier((attended, *returned))
    halo_back = shift(dhalo, "head", -1)
    *landed, sink_near = pl.pallas_call(
        functools.partial(land_kernel, blocks),
        out_shape=(shape((rows, width)),) * head_count + (shape((8, 128), F32),),
        in_specs=[VMEM] * (LAG + 2),
        out_specs=(VMEM,) * (head_count + 1),
        compiler_params=PARAMS,
        name="land",
    )(plan, quarter_grad, *returned)
    tails_back = swap(landed, "head")
    query_grad, _ = lax.optimization_barrier((query_grad, sink_near))
    query_grad = flush(query_grad)
    span = LAG + 1
    while 2 * span < tok_count:
        sink_near = sink_near + ring(sink_near, "tok", -span)
        span *= 2
    sink_far = ring(sink_near, "tok", -span)
    key_grad, value_grad, sink_grad = pl.pallas_call(
        total_kernel,
        out_shape=(
            shape(key_states.shape),
            shape(value_states.shape),
            shape(sink_logits.shape, F32),
        ),
        in_specs=[VMEM] * (5 + head_count),
        out_specs=(VMEM,) * 3,
        scratch_shapes=[pltpu.VMEM((head_count, rows, width), BF16)],
        compiler_params=PARAMS,
        name="total",
    )(halo_back, dk, dv, sink_near, sink_far, *tails_back)
    return attended, query_grad, key_grad, value_grad, sink_grad


def solution(mesh):
    rows = P(("tok", "head"), None)
    return jax.shard_map(
        local,
        mesh=mesh,
        in_specs=(rows, rows, rows, rows, P("head"), P(), P(), P()),
        out_specs=(rows, rows, rows, rows, P("head")),
        check_vma=False,
    )
```

```python
import functools

import jax
import jax.numpy as jnp
from jax import lax
from jax.experimental import pallas as pl
from jax.experimental.pallas import tpu as pltpu
from jax.sharding import PartitionSpec as P

HEAD_DIM = 64
KV_HEADS = 8
GROUP = 8
WINDOW = 128
HALF = WINDOW // 2
LAG = 3
BR_DEV = 2
PAIRS = KV_HEADS // 2
FACTOR = 0.125
LOW = -1e30
BF16 = jnp.bfloat16
F32 = jnp.float32

SMEM = pl.BlockSpec(memory_space=pltpu.SMEM)
VMEM = pl.BlockSpec(memory_space=pltpu.VMEM)
HBM = pl.BlockSpec(memory_space=pltpu.HBM)
PARAMS = pltpu.CompilerParams(vmem_limit_bytes=24 * 1024 * 1024)


def shift(value, axis, steps):
    count = lax.axis_size(axis)
    leading, last = (max(0, -steps), min(count, count - steps))
    return lax.ppermute(value, axis, [(source, source + steps) for source in range(leading, last)])


def ring(value, axis, steps):
    count = lax.axis_size(axis)
    return lax.ppermute(value, axis, [(source, (source + steps) % count) for source in range(count)])


def with_row(tile, row):
    high = row.astype(BF16).astype(F32)
    middle = (row - high).astype(BF16).astype(F32)
    low = row - high - middle
    packed = high + pltpu.roll(middle, 32, 1) + pltpu.roll(low, 64, 1)
    place = lax.broadcasted_iota(jnp.int32, (16, 128), 0)
    top = jnp.where(place == 0, packed, tile[:16, :128].astype(F32)).astype(BF16)
    if tile.shape[1] > 128:
        top = jnp.concatenate([top, tile[:16, 128:]], axis=1)
    return jnp.concatenate([top, tile[16:]], axis=0)


def row_join(top):
    packed = top[0:1, :128].astype(F32)
    row = packed + pltpu.roll(packed, 96, 1) + pltpu.roll(packed, 64, 1)
    return jnp.where(lax.broadcasted_iota(jnp.int32, (1, 128), 1) < 32, row, 0.0)


def child_tail(starts, parents, tok, distance, tok_count, blocks):
    child = jnp.minimum(tok + distance, tok_count - 1) * BR_DEV
    parent = parents[0, child]
    safe = jnp.maximum(parent, 0)
    valid = (tok + distance < tok_count) & (parent >= 0) & (safe // BR_DEV == tok)
    place = (starts[safe] + parents[1, child]) // WINDOW - tok * blocks
    return valid, jnp.where(valid, place, 0)


def block_state(starts, lengths, parents, tok, block):
    position = block * WINDOW
    alive, opening = jnp.bool_(False), jnp.bool_(False)
    for branch in range(BR_DEV):
        start = starts[tok * BR_DEV + branch]
        length = lengths[tok * BR_DEV + branch]
        alive = alive | ((start <= position) & (position < start + length))
        opening = opening | (start == position)
    has_tail = parents[0, tok * BR_DEV] >= 0
    return alive, opening, jnp.logical_not(opening) | has_tail


def plan_kernel(tok_count, blocks, blocks_here, starts, lengths, parents, plan_ref):
    tok, head = lax.axis_index("tok"), lax.axis_index("head")
    values = []
    for distance in range(1, LAG + 1):
        values += child_tail(starts, parents, tok, distance, tok_count, blocks)
    parent = parents[0, tok * BR_DEV]
    values.append(jnp.where(parent >= 0, tok - jnp.maximum(parent, 0) // BR_DEV, 1))
    for block in range(blocks_here):
        number = tok * blocks + head * blocks_here + block
        values += block_state(starts, lengths, parents, tok, number)
    lane = lax.broadcasted_iota(jnp.int32, plan_ref.shape, 1)
    plan = jnp.zeros(plan_ref.shape, jnp.int32)
    for place, value in enumerate(values):
        plan = jnp.where(lane == place, value.astype(jnp.int32), plan)
    plan_ref[...] = plan


def planned_tail(plan_ref, distance):
    row = plan_ref[0:1, :]
    return row[0, 2 * distance - 2] != 0, row[0, 2 * distance - 1]


def planned_source(plan_ref):
    return plan_ref[0:1, :][0, 2 * LAG]


def planned_block(plan_ref, block):
    row = plan_ref[0:1, :]
    return tuple(row[0, 2 * LAG + 1 + 3 * block + place] for place in range(3))


def take(ref, slot, width):
    if width % 128 == 0:
        return ref[:, pl.ds(pl.multiple_of(slot * width, width), width)]
    value = ref[:, :width]
    for other in range(1, ref.shape[1] // width):
        value = jnp.where(slot == other, ref[:, other * width : (other + 1) * width], value)
    return value


def pack_kernel(sink_hbm, key_hbm, value_hbm, *refs):
    *slot_refs, halo_ref, keys, values, sinks, sems = refs
    copies = [
        pltpu.make_async_copy(source, target, sems.at[place])
        for place, (source, target) in enumerate(
            ((sink_hbm, sinks), (key_hbm, keys), (value_hbm, values))
        )
    ]
    for copy in copies:
        copy.start()
    for copy in copies:
        copy.wait()
    slots, rows = len(slot_refs), keys.shape[0]
    head = lax.axis_index("head")
    width = KV_HEADS * HEAD_DIM // slots
    lane = lax.broadcasted_iota(jnp.int32, (1, 128), 1)
    sink_row = jnp.zeros((1, 128), F32)
    for place in range(sinks.shape[0]):
        sink_row = jnp.where(lane == place, sinks[place], sink_row)
    for step, slot_ref in enumerate(slot_refs):
        slot = lax.rem(head + step, slots)
        both = jnp.concatenate([take(keys, slot, width), take(values, slot, width)], axis=1)
        slot_ref[...] = with_row(both, sink_row)
    for pair in range(PAIRS):
        lanes = slice(pair * 128, (pair + 1) * 128)
        last = slice(rows - WINDOW, rows)
        halo_ref[pair] = jnp.concatenate([keys[last, lanes], values[last, lanes]], axis=1)


def choose_kernel(plan_ref, *refs):
    slots = len(refs) - LAG
    slot_refs, out_refs = refs[:slots], refs[slots:]
    head = lax.axis_index("head")
    rows = slot_refs[0].shape[0]
    blocks_here = rows // WINDOW
    for distance, out_ref in zip(range(LAG, 0, -1), out_refs):
        _, place = planned_tail(plan_ref, distance)
        begin = pl.multiple_of(place % blocks_here * WINDOW, WINDOW)
        wanted = lax.rem(head - place // blocks_here + slots, slots)
        for step, slot_ref in enumerate(slot_refs):

            @pl.when(wanted == step)
            def _(out_ref=out_ref, slot_ref=slot_ref, begin=begin):
                out_ref[...] = slot_ref[pl.ds(begin, WINDOW), :]


def sinks_kernel(*refs):
    *slot_refs, sink_ref = refs
    slots = len(slot_refs)
    head = lax.axis_index("head")
    heads = sink_ref.shape[0] // slots
    for step, slot_ref in enumerate(slot_refs):
        source = lax.rem(head - step + slots, slots)
        sink_row = row_join(slot_ref[:16])
        turned = jnp.broadcast_to(sink_row, (128, 128)).T
        sink_ref[pl.ds(pl.multiple_of(source * heads, heads), heads), :] = turned[:heads]


def arrive_kernel(plan_ref, *refs):
    *in_refs, out_ref = refs
    mine = planned_source(plan_ref)
    for distance, in_ref in zip(range(LAG, 0, -1), in_refs):

        @pl.when(mine == distance)
        def _(in_ref=in_ref):
            out_ref[...] = in_ref[...]


def stage_kernel(*refs):
    *arrays, sems = refs
    half = len(arrays) // 2
    copies = [
        pltpu.make_async_copy(source, target, sems.at[place])
        for place, (source, target) in enumerate(zip(arrays[:half], arrays[half:]))
    ]
    for copy in copies:
        copy.start()
    for copy in copies:
        copy.wait()


def attend_kernel(blocks_here, slots, steps, offset, pairs, joins, *refs):
    inputs, refs = refs[:7], refs[7:]
    tail_refs, refs = refs[: len(steps)], refs[len(steps) + joins :]
    outputs, refs = refs[:5], refs[5:]
    dtail_refs, refs = refs[: len(steps)], refs[len(steps) :]
    tails, *scratch = refs
    head = lax.axis_index("head")
    states = [planned_block(inputs[0], block) for block in range(blocks_here)]
    for step, tail_ref in zip(steps, tail_refs):
        tails[lax.rem(head + step, slots)] = tail_ref[...]

    def step(place, carry):
        pair = place // blocks_here
        if offset is not None:
            pair = lax.rem(head + pair + offset, PAIRS)
        block = place % blocks_here
        state = states[0]
        for other in range(1, blocks_here):
            state = [jnp.where(block == other, *two) for two in zip(states[other], state)]
        attend_block(
            blocks_here,
            slots,
            pair,
            block,
            [value != 0 for value in state],
            inputs,
            outputs,
            tails,
            tuple(zip(steps, dtail_refs)),
            scratch,
        )
        return carry

    lax.fori_loop(0, pairs * blocks_here, step, 0)


def attend_block(
    blocks_here, slots, pair, block, state, inputs, outputs, tails, dtails, scratch
):
    _, sink_ref, q_ref, g_ref, k_ref, v_ref, halo_ref = inputs
    o_ref, dq_ref, dk_ref, dv_ref, dhalo_ref = outputs
    tail_sum, sink_rows, prob2, slope2 = scratch
    per_slot = KV_HEADS // slots
    head = lax.axis_index("head")
    alive, opening, prev_ok = state
    here = pl.ds(pl.multiple_of(block * WINDOW, WINDOW), WINDOW)
    before = pl.ds(pl.multiple_of(jnp.maximum(block - 1, 0) * WINDOW, WINDOW), WINDOW)
    first = block == 0
    near = pl.ds(pl.multiple_of(pair * 128, 128), 128)
    big = pl.ds(pl.multiple_of(pair * 1024, 1024), 1024)
    q_ref, g_ref, o_ref, dq_ref = (ref.at[here, big] for ref in (q_ref, g_ref, o_ref, dq_ref))
    k_ref, v_ref, dk_ref, dv_ref = (ref.at[:, near] for ref in (k_ref, v_ref, dk_ref, dv_ref))
    sink_ref = sink_ref.at[pl.ds(pl.multiple_of(pair * 16, 16), 16)]
    dhalo_ref = dhalo_ref.at[pair]

    @pl.when(first)
    def _():
        tail_sum[...] = jnp.zeros_like(tail_sum)
        dhalo_ref[...] = jnp.zeros((WINDOW, 256), BF16)
        sink_rows[...] = jnp.zeros_like(sink_rows)

    @pl.when(jnp.logical_not(alive))
    def _():
        o_ref[...] = jnp.zeros((WINDOW, 1024), BF16)
        dq_ref[...] = jnp.zeros((WINDOW, 1024), BF16)
        dk_ref[here, :] = jnp.zeros((WINDOW, 128), F32)
        dv_ref[here, :] = jnp.zeros((WINDOW, 128), F32)

    @pl.when(alive)
    def _():
        if len(halo_ref.shape) == 2:
            halo = halo_ref[halo_ref.shape[0] - WINDOW :]
        else:
            halo = halo_ref[pair]
        if per_slot == 2:
            tail = tails[pair]
            tail_k, tail_v = tail[:, :128], tail[:, 128:]
        else:
            tail_a, tail_b = tails[2 * pair], tails[2 * pair + 1]
            tail_k = jnp.concatenate([tail_a[:, :64], tail_b[:, :64]], axis=1)
            tail_v = jnp.concatenate([tail_a[:, 64:], tail_b[:, 64:]], axis=1)
        near_k = jnp.where(first, halo[:, :128], k_ref[before, :])
        near_v = jnp.where(first, halo[:, 128:], v_ref[before, :])
        prev_k = jnp.where(opening, tail_k, near_k)
        prev_v = jnp.where(opening, tail_v, near_v)
        own_k, own_v = k_ref[here, :], v_ref[here, :]

        def halves(own, prev):
            return (
                jnp.concatenate([own[:HALF], prev[:HALF], prev[HALF:]], axis=0),
                jnp.concatenate([own[HALF:], prev[HALF:], own[:HALF]], axis=0),
            )

        left = lax.broadcasted_iota(jnp.int32, (1, 128), 1) < HALF
        low16 = left.astype(F32).astype(BF16)
        high16 = BF16(1) - low16

        def padded(seen):
            swapped = jnp.concatenate([seen[:, 64:], seen[:, :64]], axis=1)
            return (
                jnp.concatenate([seen * low16, swapped * high16], axis=0),
                jnp.concatenate([swapped * low16, seen * high16], axis=0),
            )

        seen_k = halves(own_k * BF16(FACTOR), prev_k * BF16(FACTOR))
        seen_v = halves(own_v, prev_v)
        padded_k = tuple(padded(value) for value in seen_k)
        padded_v = tuple(padded(value) for value in seen_v)
        turned_k = tuple(value.T for value in seen_k)
        turned_v = tuple(value.T for value in seen_v)
        bias = jnp.where(prev_ok, 0.0, LOW)
        key_place = lax.broadcasted_iota(jnp.int32, (HALF, 4 * HALF), 0)
        query_place = lax.broadcasted_iota(jnp.int32, (HALF, 4 * HALF), 1) & (HALF - 1)
        own = key_place <= query_place
        own16 = own.astype(F32).astype(BF16)
        turn = (((1,), (1,)), ((), ()))
        items = [(unit, half) for unit in range(2) for half in range(2)]
        seen = 3 * HALF

        def wide(index):
            return slice(index * 256, (index + 1) * 256)

        def feats(index):
            unit = items[index][0]
            return slice(unit * HEAD_DIM, (unit + 1) * HEAD_DIM)

        def corners(unit, half):
            rows = slice(half * HALF, (half + 1) * HALF)
            return [
                (rows, slice(unit * 512 + at * 128, unit * 512 + (at + 1) * 128)) for at in range(4)
            ]

        def stacked(ref, unit, half):
            return jnp.concatenate([ref[corner] for corner in corners(unit, half)], axis=0)

        def products(index):
            unit, half = items[index]
            score, dp = (
                lax.dot_general(
                    padded[half][unit],
                    stacked(ref, unit, half),
                    turn,
                    preferred_element_type=F32,
                )
                for padded, ref in ((padded_k, q_ref), (padded_v, g_ref))
            )
            parts = []
            for base in (0, seen):
                near, far = slice(base, base + HALF), slice(base + HALF, base + 2 * HALF)
                rest = slice(base + 2 * HALF, base + 3 * HALF)
                edge = jnp.where(own, score[near], score[far] + bias)
                whole = score[rest] + bias if half == 0 else score[rest]
                parts.append((edge, whole, jnp.where(own, dp[near], dp[far]), dp[rest]))
            return parts

        def weigh(index, odd, edge, whole, dp_edge, dp_whole):
            unit, half = items[index]
            base = odd * seen
            row = unit * GROUP + odd
            sink = jnp.concatenate(
                [
                    jnp.where(left, sink_ref[at : at + 1], sink_ref[at + 2 : at + 3])
                    for at in (row, row + 4)
                ],
                axis=1,
            )
            peak = jnp.max(jnp.maximum(edge, whole), axis=0, keepdims=True)
            peak = jnp.maximum(peak, sink)
            edge, whole = jnp.exp(edge - peak), jnp.exp(whole - peak)
            sink_weight = jnp.exp(sink - peak)
            inverse = 1.0 / (jnp.sum(edge + whole, axis=0, keepdims=True) + sink_weight)
            edge, whole = edge * inverse, whole * inverse
            delta = jnp.sum(edge * dp_edge + whole * dp_whole, axis=0, keepdims=True)
            edge16, whole16 = edge.astype(BF16), whole.astype(BF16)
            edge_own = edge16 * own16
            edge_prev = edge16 - edge_own
            away_edge, away_whole = (dp_edge - delta).astype(BF16), (dp_whole - delta).astype(BF16)
            for target, rows in (
                (prob2, (edge_own, edge_prev, whole16)),
                (slope2, (edge_own * away_edge, edge_prev * away_edge, whole16 * away_whole)),
            ):
                for by, value in enumerate(rows):
                    at = base + by * HALF
                    target[at : at + HALF, wide(index)] = value
            sink_term = sink_weight * inverse * delta
            for at, lanes in ((row, slice(0, 128)), (row + 4, slice(128, 256))):
                part = sink_term[:, lanes]
                sink_rows[at : at + 1] += jnp.where(left, part, 0.0)
                sink_rows[at + 2 : at + 3] += jnp.where(left, 0.0, part)

        def finish(index):
            unit, half = items[index]
            for source, across, out_ref in ((prob2, turned_v, o_ref), (slope2, turned_k, dq_ref)):
                out_t = [
                    jnp.dot(
                        across[half][feats(index)],
                        source[base : base + seen, wide(index)],
                        preferred_element_type=F32,
                    ).astype(BF16)
                    for base in (0, seen)
                ]
                out = jnp.concatenate(out_t, axis=0).T
                for at, corner in enumerate(corners(unit, half)):
                    out_ref[corner] = out[at * HALF : (at + 1) * HALF]

        def reduce(index):
            unit, half = items[index]
            parts = []
            for weights, ref in ((slope2, q_ref), (prob2, g_ref)):
                part = jnp.dot(
                    weights[:, wide(index)], stacked(ref, unit, half), preferred_element_type=F32
                )
                parts.append(jnp.where(left, part[:seen], part[seen:]))
            return parts

        def join(first_half, second_half):
            total = jnp.concatenate(
                [
                    first_half[:HALF] + second_half[2 * HALF :],
                    second_half[:HALF],
                    first_half[HALF : 2 * HALF],
                    first_half[2 * HALF :] + second_half[HALF : 2 * HALF],
                ],
                axis=0,
            )
            return total + pltpu.roll(total, HEAD_DIM, 1)

        ahead, parts = products(0), []
        for index in range(len(items)):
            now = ahead
            weigh(index, 0, *now[0])
            if index + 1 < len(items):
                ahead = products(index + 1)
            weigh(index, 1, *now[1])
            if index >= 1:
                finish(index - 1)
            parts.append(reduce(index))
        finish(len(items) - 1)
        grads = [
            [join(parts[2 * unit][place], parts[2 * unit + 1][place]) for place in range(2)]
            for unit in range(2)
        ]
        dk = jnp.where(left, grads[0][0], grads[1][0]) * FACTOR
        dv = jnp.where(left, grads[0][1], grads[1][1])
        dk_ref[here, :] = dk[:WINDOW]
        dv_ref[here, :] = dv[:WINDOW]

        @pl.when(opening & prev_ok)
        def _():
            tail_sum[:, :128] += dk[WINDOW:]
            tail_sum[:, 128:] += dv[WINDOW:]

        @pl.when(jnp.logical_not(opening) & first)
        def _():
            dhalo_ref[:, :128] = dk[WINDOW:].astype(BF16)
            dhalo_ref[:, 128:] = dv[WINDOW:].astype(BF16)

        @pl.when(jnp.logical_not(opening) & jnp.logical_not(first))
        def _():
            dk_ref[before, :] += dk[WINDOW:]
            dv_ref[before, :] += dv[WINDOW:]

    @pl.when(block == blocks_here - 1)
    def _():
        width = 2 * per_slot * HEAD_DIM
        heads = per_slot * GROUP
        total = tail_sum[...].astype(BF16)
        for part in range(2 // per_slot):
            feats = slice(part * width // 2, (part + 1) * width // 2)
            tail = jnp.concatenate([total[:, :128][:, feats], total[:, 128:][:, feats]], axis=1)
            rows = sink_rows[part * heads : (part + 1) * heads]
            rows = jnp.concatenate([rows, jnp.zeros((128 - heads, WINDOW), F32)], axis=0)
            sink_row = jnp.sum(rows.T, axis=0, keepdims=True)
            tail = with_row(tail, sink_row)
            wanted = lax.rem(pair * (2 // per_slot) + part - head + slots, slots)
            for step, dtail_ref in dtails:

                @pl.when(wanted == step)
                def _(dtail_ref=dtail_ref, tail=tail):
                    dtail_ref[...] = tail


def gather_kernel(*refs):
    *in_refs, out_ref = refs
    total, sink_row = 0.0, 0.0
    for in_ref in in_refs:
        total = total + in_ref[...].astype(F32)
        sink_row = sink_row + row_join(in_ref[:16])
    out_ref[...] = with_row(total.astype(BF16), sink_row)


def land_kernel(blocks, plan_ref, here_ref, *refs):
    head = lax.axis_index("head")
    in_refs, out_refs, sink_ref = refs[:LAG], refs[LAG:-1], refs[-1]
    slots = len(out_refs)
    blocks_here = blocks // slots
    for out_ref in out_refs:
        out_ref[...] = jnp.zeros_like(out_ref)
    sink_row = row_join(here_ref[:16])
    seen = lax.broadcasted_iota(jnp.int32, here_ref.shape, 0) > 0
    for distance, in_ref in enumerate(in_refs, 1):
        valid, place = planned_tail(plan_ref, distance)
        sink_row = sink_row + row_join(in_ref[:16])
        wanted = lax.rem(place // blocks_here - head + slots, slots)
        here = pl.ds(pl.multiple_of(place % blocks_here * WINDOW, WINDOW), WINDOW)
        for step, out_ref in enumerate(out_refs):

            @pl.when(valid & (wanted == step))
            def _(out_ref=out_ref, in_ref=in_ref, here=here):
                total = out_ref[here, :].astype(F32) + in_ref[...].astype(F32)
                out_ref[here, :] = jnp.where(seen, total, 0.0).astype(BF16)

    sink_ref[...] = jnp.broadcast_to(sink_row, sink_ref.shape)


def total_kernel(halo_ref, dk_ref, dv_ref, sink_ref, far_ref, *refs):
    *tail_refs, key_ref, value_ref, sink_grad, tails = refs
    slots, rows = len(tail_refs), dk_ref.shape[0]
    width = tails.shape[2] // 2
    head = lax.axis_index("head")
    for step, tail_ref in enumerate(tail_refs):
        tails[lax.rem(head - step + slots, slots)] = tail_ref[...]
    halo_k = jnp.concatenate([halo_ref[pair][:, :128] for pair in range(PAIRS)], axis=1)
    halo_v = jnp.concatenate([halo_ref[pair][:, 128:] for pair in range(PAIRS)], axis=1)
    for in_ref, halo, at, out_ref in (
        (dk_ref, halo_k, 0, key_ref),
        (dv_ref, halo_v, width, value_ref),
    ):
        for begin in range(0, rows, WINDOW):
            here = slice(begin, begin + WINDOW)
            parts = [tails[slot, here, at : at + width] for slot in range(slots)]
            total = in_ref[here, :] + jnp.concatenate(parts, axis=1).astype(F32)
            if begin == rows - WINDOW:
                total = total + halo.astype(F32)
            out_ref[here, :] = total.astype(BF16)
    sink_row = -(sink_ref[0:1] + far_ref[0:1])
    sink_grad[...] = sink_row[0, : sink_grad.shape[0]]


def swap(values, axis):
    return [values[0]] + [ring(values[step], axis, step) for step in range(1, len(values))]


def local(
    queries, key_states, value_states, out_grad, sink_logits, branch_start, branch_len, parent_list
):
    tok_count, head_count = lax.axis_size("tok"), lax.axis_size("head")
    rows = queries.shape[0]
    blocks_here = rows // WINDOW
    blocks = blocks_here * head_count
    per_slot = KV_HEADS // head_count
    width = 2 * per_slot * HEAD_DIM

    def shape(dims, kind=BF16):
        return jax.ShapeDtypeStruct(dims, kind)

    def far(value):
        return pltpu.with_memory_space_constraint(value, pltpu.HBM)

    def close(value):
        return pltpu.with_memory_space_constraint(value, pltpu.VMEM)

    *slots, halo_out, keys, values = pl.pallas_call(
        pack_kernel,
        out_shape=(shape((rows, width)),) * head_count
        + (shape((PAIRS, WINDOW, 256)),)
        + (pltpu.VMEM(key_states.shape, BF16),) * 2,
        in_specs=[HBM] * 3,
        out_specs=(VMEM,) * (head_count + 3),
        scratch_shapes=[
            pltpu.SMEM(sink_logits.shape, F32),
            pltpu.SemaphoreType.DMA((3,)),
        ],
        compiler_params=PARAMS,
        name="pack",
    )(far(sink_logits), far(key_states), far(value_states))
    spread = swap(slots, "head")
    halo = shift(halo_out, "head", 1)
    plan = pl.pallas_call(
        functools.partial(plan_kernel, tok_count, blocks, blocks_here),
        out_shape=pltpu.VMEM((8, 128), jnp.int32),
        in_specs=[SMEM] * 3,
        out_specs=VMEM,
        compiler_params=PARAMS,
        name="plan",
    )(far(branch_start), far(branch_len), far(parent_list.T))
    plan = close(plan)
    chosen = pl.pallas_call(
        choose_kernel,
        out_shape=(shape((WINDOW, width)),) * LAG,
        in_specs=[VMEM] * (1 + head_count),
        out_specs=(VMEM,) * LAG,
        compiler_params=PARAMS,
        name="choose",
    )(plan, *spread)
    late_slots = lax.optimization_barrier((*spread, *chosen))
    late_slots, chosen = late_slots[:head_count], late_slots[head_count:]
    sinks = pl.pallas_call(
        sinks_kernel,
        out_shape=shape((KV_HEADS * GROUP, 128), F32),
        in_specs=[VMEM] * head_count,
        out_specs=VMEM,
        compiler_params=PARAMS,
        name="sinks",
    )(*late_slots)
    arrived = [ring(chosen[LAG - s], "tok", s) for s in range(LAG, 0, -1)]
    queries, out_grad, _ = lax.optimization_barrier((queries, out_grad, sinks))
    near_queries, near_grad = pl.pallas_call(
        stage_kernel,
        out_shape=(pltpu.VMEM(queries.shape, BF16),) * 2,
        in_specs=[HBM] * 2,
        out_specs=(VMEM,) * 2,
        scratch_shapes=[pltpu.SemaphoreType.DMA((2,))],
        compiler_params=PARAMS,
        name="stage",
    )(far(queries), far(out_grad))
    *arrived, near_queries, near_grad = lax.optimization_barrier(
        (*arrived, near_queries, near_grad)
    )
    quarter = pl.pallas_call(
        arrive_kernel,
        out_shape=shape((WINDOW, width)),
        in_specs=[VMEM] * (1 + LAG),
        out_specs=VMEM,
        compiler_params=PARAMS,
        name="arrive",
    )(plan, *arrived)
    tails = swap([quarter] * head_count, "head")

    def attend(steps, pairs, offset, halo, joined):
        inputs = (
            sinks,
            close(near_queries),
            close(near_grad),
            close(keys),
            close(values),
            halo,
            *(tails[-step % head_count] for step in steps),
            *(close(value) for value in joined),
        )
        base = 1 + len(inputs) - len(joined)
        return pl.pallas_call(
            functools.partial(
                attend_kernel,
                blocks_here,
                head_count,
                steps,
                offset,
                pairs,
                len(joined),
            ),
            out_shape=(
                pltpu.VMEM(queries.shape, BF16),
                pltpu.VMEM(queries.shape, BF16),
                pltpu.VMEM(key_states.shape, F32),
                pltpu.VMEM(key_states.shape, F32),
                pltpu.VMEM((PAIRS, WINDOW, 256), BF16),
            )
            + (shape((WINDOW, width)),) * len(steps),
            in_specs=[VMEM] * (1 + len(inputs)),
            out_specs=(VMEM,) * (5 + len(steps)),
            scratch_shapes=[
                pltpu.VMEM((head_count, WINDOW, width), BF16),
                pltpu.VMEM((WINDOW, 256), F32),
                pltpu.VMEM((2 * GROUP, WINDOW), F32),
                pltpu.VMEM((6 * HALF, 1024), BF16),
                pltpu.VMEM((6 * HALF, 1024), BF16),
            ],
            input_output_aliases={base + place: place for place in range(len(joined))},
            compiler_params=PARAMS,
            name="attend",
        )(plan, *inputs)

    if per_slot == 2:
        *joined, own_tail = attend((0,), 1, 0, spread[1], ())
        *joined, tail_1, tail_2 = attend((1, 2), 2, 1, halo, joined)
        *results, tail_3 = attend((3,), 1, 3, halo, joined)
        dtail = [own_tail, tail_1, tail_2, tail_3]
    else:
        results = attend(tuple(range(head_count)), PAIRS, None, halo, ())
        results, dtail = results[:5], list(results[5:])
    attended, query_grad, dk, dv, dhalo = results
    parts = swap(dtail, "head")

    def gather(values):
        return pl.pallas_call(
            gather_kernel,
            out_shape=shape((WINDOW, width)),
            in_specs=[VMEM] * len(values),
            out_specs=VMEM,
            compiler_params=PARAMS,
            name="gather",
        )(*values)

    quarter_grad = gather([gather(parts[:-1]), parts[-1]])

    def flush(value):
        return pl.pallas_call(
            stage_kernel,
            out_shape=pltpu.HBM(value.shape, BF16),
            in_specs=[VMEM],
            out_specs=HBM,
            scratch_shapes=[pltpu.SemaphoreType.DMA((1,))],
            compiler_params=PARAMS,
            name="flush",
        )(close(value))

    returned = [ring(quarter_grad, "tok", -s) for s in range(LAG, 0, -1)][::-1]
    attended, _ = lax.optimization_barrier((attended, quarter_grad))
    attended = flush(attended)
    attended, *returned = lax.optimization_barrier((attended, *returned))
    halo_back = shift(dhalo, "head", -1)
    *landed, sink_near = pl.pallas_call(
        functools.partial(land_kernel, blocks),
        out_shape=(shape((rows, width)),) * head_count + (shape((8, 128), F32),),
        in_specs=[VMEM] * (LAG + 2),
        out_specs=(VMEM,) * (head_count + 1),
        compiler_params=PARAMS,
        name="land",
    )(plan, quarter_grad, *returned)
    tails_back = swap(landed, "head")
    query_grad, _ = lax.optimization_barrier((query_grad, sink_near))
    query_grad = flush(query_grad)
    span = LAG + 1
    while 2 * span < tok_count:
        sink_near = sink_near + ring(sink_near, "tok", -span)
        span *= 2
    sink_far = ring(sink_near, "tok", -span)
    key_grad, value_grad, sink_grad = pl.pallas_call(
        total_kernel,
        out_shape=(
            shape(key_states.shape),
            shape(value_states.shape),
            shape(sink_logits.shape, F32),
        ),
        in_specs=[VMEM] * (5 + head_count),
        out_specs=(VMEM,) * 3,
        scratch_shapes=[pltpu.VMEM((head_count, rows, width), BF16)],
        compiler_params=PARAMS,
        name="total",
    )(halo_back, dk, dv, sink_near, sink_far, *tails_back)
    return attended, query_grad, key_grad, value_grad, sink_grad


def solution(mesh):
    rows = P(("tok", "head"), None)
    return jax.shard_map(
        local,
        mesh=mesh,
        in_specs=(rows, rows, rows, rows, P("head"), P(), P(), P()),
        out_specs=(rows, rows, rows, rows, P("head")),
        check_vma=False,
    )
```

```python
import functools

import jax
import jax.numpy as jnp
from jax import lax
from jax.experimental import pallas as pl
from jax.experimental.pallas import tpu as pltpu
from jax.sharding import PartitionSpec as P

HEAD_DIM = 64
KV_HEADS = 8
GROUP = 8
WINDOW = 128
HALF = WINDOW // 2
LAG = 3
BR_DEV = 2
PAIRS = KV_HEADS // 2
FACTOR = 0.125
LOW = -1e30
BF16 = jnp.bfloat16
F32 = jnp.float32

SMEM = pl.BlockSpec(memory_space=pltpu.SMEM)
VMEM = pl.BlockSpec(memory_space=pltpu.VMEM)
HBM = pl.BlockSpec(memory_space=pltpu.HBM)
PARAMS = pltpu.CompilerParams(vmem_limit_bytes=24 * 1024 * 1024)


def shift(value, axis, steps):
    count = lax.axis_size(axis)
    leading, last = (max(0, -steps), min(count, count - steps))
    return lax.ppermute(value, axis, [(source, source + steps) for source in range(leading, last)])


def ring(value, axis, steps):
    count = lax.axis_size(axis)
    return lax.ppermute(value, axis, [(source, (source + steps) % count) for source in range(count)])


def with_row(tile, row):
    high = row.astype(BF16).astype(F32)
    middle = (row - high).astype(BF16).astype(F32)
    low = row - high - middle
    packed = high + pltpu.roll(middle, 32, 1) + pltpu.roll(low, 64, 1)
    place = lax.broadcasted_iota(jnp.int32, (16, 128), 0)
    top = jnp.where(place == 0, packed, tile[:16, :128].astype(F32)).astype(BF16)
    if tile.shape[1] > 128:
        top = jnp.concatenate([top, tile[:16, 128:]], axis=1)
    return jnp.concatenate([top, tile[16:]], axis=0)


def row_join(top):
    packed = top[0:1, :128].astype(F32)
    row = packed + pltpu.roll(packed, 96, 1) + pltpu.roll(packed, 64, 1)
    return jnp.where(lax.broadcasted_iota(jnp.int32, (1, 128), 1) < 32, row, 0.0)


def child_tail(starts, parents, tok, distance, tok_count, blocks):
    child = jnp.minimum(tok + distance, tok_count - 1) * BR_DEV
    parent = parents[0, child]
    safe = jnp.maximum(parent, 0)
    valid = (tok + distance < tok_count) & (parent >= 0) & (safe // BR_DEV == tok)
    place = (starts[safe] + parents[1, child]) // WINDOW - tok * blocks
    return valid, jnp.where(valid, place, 0)


def block_state(starts, lengths, parents, tok, block):
    position = block * WINDOW
    alive, opening = jnp.bool_(False), jnp.bool_(False)
    for branch in range(BR_DEV):
        start = starts[tok * BR_DEV + branch]
        length = lengths[tok * BR_DEV + branch]
        alive = alive | ((start <= position) & (position < start + length))
        opening = opening | (start == position)
    has_tail = parents[0, tok * BR_DEV] >= 0
    return alive, opening, jnp.logical_not(opening) | has_tail


def plan_kernel(tok_count, blocks, blocks_here, starts, lengths, parents, plan_ref):
    tok, head = lax.axis_index("tok"), lax.axis_index("head")
    values = []
    for distance in range(1, LAG + 1):
        values += child_tail(starts, parents, tok, distance, tok_count, blocks)
    parent = parents[0, tok * BR_DEV]
    values.append(jnp.where(parent >= 0, tok - jnp.maximum(parent, 0) // BR_DEV, 1))
    for block in range(blocks_here):
        number = tok * blocks + head * blocks_here + block
        values += block_state(starts, lengths, parents, tok, number)
    lane = lax.broadcasted_iota(jnp.int32, plan_ref.shape, 1)
    plan = jnp.zeros(plan_ref.shape, jnp.int32)
    for place, value in enumerate(values):
        plan = jnp.where(lane == place, value.astype(jnp.int32), plan)
    plan_ref[...] = plan


def planned_tail(plan_ref, distance):
    row = plan_ref[0:1, :]
    return row[0, 2 * distance - 2] != 0, row[0, 2 * distance - 1]


def planned_source(plan_ref):
    return plan_ref[0:1, :][0, 2 * LAG]


def planned_block(plan_ref, block):
    row = plan_ref[0:1, :]
    return tuple(row[0, 2 * LAG + 1 + 3 * block + place] for place in range(3))


def take(ref, slot, width):
    if width % 128 == 0:
        return ref[:, pl.ds(pl.multiple_of(slot * width, width), width)]
    value = ref[:, :width]
    for other in range(1, ref.shape[1] // width):
        value = jnp.where(slot == other, ref[:, other * width : (other + 1) * width], value)
    return value


def pack_kernel(sink_hbm, key_hbm, value_hbm, *refs):
    *slot_refs, halo_ref, keys, values, sinks, sems = refs
    copies = [
        pltpu.make_async_copy(source, target, sems.at[place])
        for place, (source, target) in enumerate(
            ((sink_hbm, sinks), (key_hbm, keys), (value_hbm, values))
        )
    ]
    for copy in copies:
        copy.start()
    for copy in copies:
        copy.wait()
    slots, rows = len(slot_refs), keys.shape[0]
    head = lax.axis_index("head")
    width = KV_HEADS * HEAD_DIM // slots
    lane = lax.broadcasted_iota(jnp.int32, (1, 128), 1)
    sink_row = jnp.zeros((1, 128), F32)
    for place in range(sinks.shape[0]):
        sink_row = jnp.where(lane == place, sinks[place], sink_row)
    for step, slot_ref in enumerate(slot_refs):
        slot = lax.rem(head + step, slots)
        both = jnp.concatenate([take(keys, slot, width), take(values, slot, width)], axis=1)
        slot_ref[...] = with_row(both, sink_row)
    for pair in range(PAIRS):
        lanes = slice(pair * 128, (pair + 1) * 128)
        last = slice(rows - WINDOW, rows)
        halo_ref[pair] = jnp.concatenate([keys[last, lanes], values[last, lanes]], axis=1)


def choose_kernel(plan_ref, *refs):
    slots = len(refs) - LAG
    slot_refs, out_refs = refs[:slots], refs[slots:]
    head = lax.axis_index("head")
    rows = slot_refs[0].shape[0]
    blocks_here = rows // WINDOW
    for distance, out_ref in zip(range(LAG, 0, -1), out_refs):
        _, place = planned_tail(plan_ref, distance)
        begin = pl.multiple_of(place % blocks_here * WINDOW, WINDOW)
        wanted = lax.rem(head - place // blocks_here + slots, slots)
        for step, slot_ref in enumerate(slot_refs):

            @pl.when(wanted == step)
            def _(out_ref=out_ref, slot_ref=slot_ref, begin=begin):
                out_ref[...] = slot_ref[pl.ds(begin, WINDOW), :]


def sinks_kernel(*refs):
    *slot_refs, sink_ref = refs
    slots = len(slot_refs)
    head = lax.axis_index("head")
    heads = sink_ref.shape[0] // slots
    for step, slot_ref in enumerate(slot_refs):
        source = lax.rem(head - step + slots, slots)
        sink_row = row_join(slot_ref[:16])
        turned = jnp.broadcast_to(sink_row, (128, 128)).T
        sink_ref[pl.ds(pl.multiple_of(source * heads, heads), heads), :] = turned[:heads]


def arrive_kernel(plan_ref, *refs):
    *in_refs, out_ref = refs
    mine = planned_source(plan_ref)
    for distance, in_ref in zip(range(LAG, 0, -1), in_refs):

        @pl.when(mine == distance)
        def _(in_ref=in_ref):
            out_ref[...] = in_ref[...]


def stage_kernel(*refs):
    *arrays, sems = refs
    half = len(arrays) // 2
    copies = [
        pltpu.make_async_copy(source, target, sems.at[place])
        for place, (source, target) in enumerate(zip(arrays[:half], arrays[half:]))
    ]
    for copy in copies:
        copy.start()
    for copy in copies:
        copy.wait()


def attend_kernel(blocks_here, slots, steps, offset, pairs, joins, *refs):
    inputs, refs = refs[:7], refs[7:]
    tail_refs, refs = refs[: len(steps)], refs[len(steps) + joins :]
    outputs, refs = refs[:5], refs[5:]
    dtail_refs, refs = refs[: len(steps)], refs[len(steps) :]
    tails, *scratch = refs
    head = lax.axis_index("head")
    states = [planned_block(inputs[0], block) for block in range(blocks_here)]
    for step, tail_ref in zip(steps, tail_refs):
        tails[head ^ step] = tail_ref[...]

    def step(place, carry):
        pair = place // blocks_here
        if offset is not None:
            pair = head ^ (pair + offset)
        block = place % blocks_here
        state = states[0]
        for other in range(1, blocks_here):
            state = [jnp.where(block == other, *two) for two in zip(states[other], state)]
        attend_block(
            blocks_here,
            slots,
            pair,
            block,
            [value != 0 for value in state],
            inputs,
            outputs,
            tails,
            tuple(zip(steps, dtail_refs)),
            scratch,
        )
        return carry

    lax.fori_loop(0, pairs * blocks_here, step, 0)


def attend_block(
    blocks_here, slots, pair, block, state, inputs, outputs, tails, dtails, scratch
):
    _, sink_ref, q_ref, g_ref, k_ref, v_ref, halo_ref = inputs
    o_ref, dq_ref, dk_ref, dv_ref, dhalo_ref = outputs
    tail_sum, sink_rows, prob2, slope2 = scratch
    per_slot = KV_HEADS // slots
    head = lax.axis_index("head")
    alive, opening, prev_ok = state
    here = pl.ds(pl.multiple_of(block * WINDOW, WINDOW), WINDOW)
    before = pl.ds(pl.multiple_of(jnp.maximum(block - 1, 0) * WINDOW, WINDOW), WINDOW)
    first = block == 0
    near = pl.ds(pl.multiple_of(pair * 128, 128), 128)
    big = pl.ds(pl.multiple_of(pair * 1024, 1024), 1024)
    q_ref, g_ref, o_ref, dq_ref = (ref.at[here, big] for ref in (q_ref, g_ref, o_ref, dq_ref))
    k_ref, v_ref, dk_ref, dv_ref = (ref.at[:, near] for ref in (k_ref, v_ref, dk_ref, dv_ref))
    sink_ref = sink_ref.at[pl.ds(pl.multiple_of(pair * 16, 16), 16)]
    dhalo_ref = dhalo_ref.at[pair]

    @pl.when(first)
    def _():
        tail_sum[...] = jnp.zeros_like(tail_sum)
        dhalo_ref[...] = jnp.zeros((WINDOW, 256), BF16)
        sink_rows[...] = jnp.zeros_like(sink_rows)

    @pl.when(jnp.logical_not(alive))
    def _():
        o_ref[...] = jnp.zeros((WINDOW, 1024), BF16)
        dq_ref[...] = jnp.zeros((WINDOW, 1024), BF16)
        dk_ref[here, :] = jnp.zeros((WINDOW, 128), F32)
        dv_ref[here, :] = jnp.zeros((WINDOW, 128), F32)

    @pl.when(alive)
    def _():
        if len(halo_ref.shape) == 2:
            halo = halo_ref[halo_ref.shape[0] - WINDOW :]
        else:
            halo = halo_ref[pair]
        if per_slot == 2:
            tail = tails[pair]
            tail_k, tail_v = tail[:, :128], tail[:, 128:]
        else:
            tail_a, tail_b = tails[2 * pair], tails[2 * pair + 1]
            tail_k = jnp.concatenate([tail_a[:, :64], tail_b[:, :64]], axis=1)
            tail_v = jnp.concatenate([tail_a[:, 64:], tail_b[:, 64:]], axis=1)
        near_k = jnp.where(first, halo[:, :128], k_ref[before, :])
        near_v = jnp.where(first, halo[:, 128:], v_ref[before, :])
        prev_k = jnp.where(opening, tail_k, near_k)
        prev_v = jnp.where(opening, tail_v, near_v)
        own_k, own_v = k_ref[here, :], v_ref[here, :]

        def halves(own, prev):
            return (
                jnp.concatenate([own[:HALF], prev[:HALF], prev[HALF:]], axis=0),
                jnp.concatenate([own[HALF:], prev[HALF:], own[:HALF]], axis=0),
            )

        left = lax.broadcasted_iota(jnp.int32, (1, 128), 1) < HALF
        low16 = left.astype(F32).astype(BF16)
        high16 = BF16(1) - low16

        def padded(seen):
            swapped = jnp.concatenate([seen[:, 64:], seen[:, :64]], axis=1)
            return (
                jnp.concatenate([seen * low16, swapped * high16], axis=0),
                jnp.concatenate([swapped * low16, seen * high16], axis=0),
            )

        seen_k = halves(own_k * BF16(FACTOR), prev_k * BF16(FACTOR))
        seen_v = halves(own_v, prev_v)
        padded_k = tuple(padded(value) for value in seen_k)
        padded_v = tuple(padded(value) for value in seen_v)
        turned_k = tuple(value.T for value in seen_k)
        turned_v = tuple(value.T for value in seen_v)
        bias = jnp.where(prev_ok, 0.0, LOW)
        key_place = lax.broadcasted_iota(jnp.int32, (HALF, 4 * HALF), 0)
        query_place = lax.broadcasted_iota(jnp.int32, (HALF, 4 * HALF), 1) & (HALF - 1)
        own = key_place <= query_place
        own16 = own.astype(F32).astype(BF16)
        turn = (((1,), (1,)), ((), ()))
        items = [(unit, half) for unit in range(2) for half in range(2)]
        seen = 3 * HALF

        def wide(index):
            return slice(index * 256, (index + 1) * 256)

        def feats(index):
            unit = items[index][0]
            return slice(unit * HEAD_DIM, (unit + 1) * HEAD_DIM)

        def corners(unit, half):
            rows = slice(half * HALF, (half + 1) * HALF)
            return [
                (rows, slice(unit * 512 + at * 128, unit * 512 + (at + 1) * 128)) for at in range(4)
            ]

        def stacked(ref, unit, half):
            return jnp.concatenate([ref[corner] for corner in corners(unit, half)], axis=0)

        def products(index):
            unit, half = items[index]
            score, dp = (
                lax.dot_general(
                    padded[half][unit],
                    stacked(ref, unit, half),
                    turn,
                    preferred_element_type=F32,
                )
                for padded, ref in ((padded_k, q_ref), (padded_v, g_ref))
            )
            parts = []
            for base in (0, seen):
                near, far = slice(base, base + HALF), slice(base + HALF, base + 2 * HALF)
                rest = slice(base + 2 * HALF, base + 3 * HALF)
                edge = jnp.where(own, score[near], score[far] + bias)
                whole = score[rest] + bias if half == 0 else score[rest]
                parts.append((edge, whole, jnp.where(own, dp[near], dp[far]), dp[rest]))
            return parts

        def weigh(index, odd, edge, whole, dp_edge, dp_whole):
            unit, half = items[index]
            base = odd * seen
            row = unit * GROUP + odd
            sink = jnp.concatenate(
                [
                    jnp.where(left, sink_ref[at : at + 1], sink_ref[at + 2 : at + 3])
                    for at in (row, row + 4)
                ],
                axis=1,
            )
            peak = jnp.max(jnp.maximum(edge, whole), axis=0, keepdims=True)
            peak = jnp.maximum(peak, sink)
            edge, whole = jnp.exp(edge - peak), jnp.exp(whole - peak)
            sink_weight = jnp.exp(sink - peak)
            inverse = 1.0 / (jnp.sum(edge + whole, axis=0, keepdims=True) + sink_weight)
            edge, whole = edge * inverse, whole * inverse
            delta = jnp.sum(edge * dp_edge + whole * dp_whole, axis=0, keepdims=True)
            edge16, whole16 = edge.astype(BF16), whole.astype(BF16)
            edge_own = edge16 * own16
            edge_prev = edge16 - edge_own
            away_edge, away_whole = (dp_edge - delta).astype(BF16), (dp_whole - delta).astype(BF16)
            for target, rows in (
                (prob2, (edge_own, edge_prev, whole16)),
                (slope2, (edge_own * away_edge, edge_prev * away_edge, whole16 * away_whole)),
            ):
                for by, value in enumerate(rows):
                    at = base + by * HALF
                    target[at : at + HALF, wide(index)] = value
            sink_term = sink_weight * inverse * delta
            for at, lanes in ((row, slice(0, 128)), (row + 4, slice(128, 256))):
                part = sink_term[:, lanes]
                sink_rows[at : at + 1] += jnp.where(left, part, 0.0)
                sink_rows[at + 2 : at + 3] += jnp.where(left, 0.0, part)

        def finish(index):
            unit, half = items[index]
            for source, across, out_ref in ((prob2, turned_v, o_ref), (slope2, turned_k, dq_ref)):
                out_t = [
                    jnp.dot(
                        across[half][feats(index)],
                        source[base : base + seen, wide(index)],
                        preferred_element_type=F32,
                    ).astype(BF16)
                    for base in (0, seen)
                ]
                out = jnp.concatenate(out_t, axis=0).T
                for at, corner in enumerate(corners(unit, half)):
                    out_ref[corner] = out[at * HALF : (at + 1) * HALF]

        def reduce(index):
            unit, half = items[index]
            parts = []
            for weights, ref in ((slope2, q_ref), (prob2, g_ref)):
                part = jnp.dot(
                    weights[:, wide(index)], stacked(ref, unit, half), preferred_element_type=F32
                )
                parts.append(jnp.where(left, part[:seen], part[seen:]))
            return parts

        def join(first_half, second_half):
            total = jnp.concatenate(
                [
                    first_half[:HALF] + second_half[2 * HALF :],
                    second_half[:HALF],
                    first_half[HALF : 2 * HALF],
                    first_half[2 * HALF :] + second_half[HALF : 2 * HALF],
                ],
                axis=0,
            )
            return total + pltpu.roll(total, HEAD_DIM, 1)

        ahead, parts = products(0), []
        for index in range(len(items)):
            now = ahead
            weigh(index, 0, *now[0])
            if index + 1 < len(items):
                ahead = products(index + 1)
            weigh(index, 1, *now[1])
            if index >= 1:
                finish(index - 1)
            parts.append(reduce(index))
        finish(len(items) - 1)
        grads = [
            [join(parts[2 * unit][place], parts[2 * unit + 1][place]) for place in range(2)]
            for unit in range(2)
        ]
        dk = jnp.where(left, grads[0][0], grads[1][0]) * FACTOR
        dv = jnp.where(left, grads[0][1], grads[1][1])
        dk_ref[here, :] = dk[:WINDOW]
        dv_ref[here, :] = dv[:WINDOW]

        @pl.when(opening & prev_ok)
        def _():
            tail_sum[:, :128] += dk[WINDOW:]
            tail_sum[:, 128:] += dv[WINDOW:]

        @pl.when(jnp.logical_not(opening) & first)
        def _():
            dhalo_ref[:, :128] = dk[WINDOW:].astype(BF16)
            dhalo_ref[:, 128:] = dv[WINDOW:].astype(BF16)

        @pl.when(jnp.logical_not(opening) & jnp.logical_not(first))
        def _():
            dk_ref[before, :] += dk[WINDOW:]
            dv_ref[before, :] += dv[WINDOW:]

    @pl.when(block == blocks_here - 1)
    def _():
        width = 2 * per_slot * HEAD_DIM
        heads = per_slot * GROUP
        total = tail_sum[...].astype(BF16)
        for part in range(2 // per_slot):
            feats = slice(part * width // 2, (part + 1) * width // 2)
            tail = jnp.concatenate([total[:, :128][:, feats], total[:, 128:][:, feats]], axis=1)
            rows = sink_rows[part * heads : (part + 1) * heads]
            rows = jnp.concatenate([rows, jnp.zeros((128 - heads, WINDOW), F32)], axis=0)
            sink_row = jnp.sum(rows.T, axis=0, keepdims=True)
            tail = with_row(tail, sink_row)
            wanted = (pair * (2 // per_slot) + part) ^ head
            for step, dtail_ref in dtails:

                @pl.when(wanted == step)
                def _(dtail_ref=dtail_ref, tail=tail):
                    dtail_ref[...] = tail


def gather_kernel(*refs):
    *in_refs, out_ref = refs
    total, sink_row = 0.0, 0.0
    for in_ref in in_refs:
        total = total + in_ref[...].astype(F32)
        sink_row = sink_row + row_join(in_ref[:16])
    out_ref[...] = with_row(total.astype(BF16), sink_row)


def land_kernel(blocks, plan_ref, here_ref, *refs):
    head = lax.axis_index("head")
    in_refs, out_refs, sink_ref = refs[:LAG], refs[LAG:-1], refs[-1]
    slots = len(out_refs)
    blocks_here = blocks // slots
    for out_ref in out_refs:
        out_ref[...] = jnp.zeros_like(out_ref)
    sink_row = row_join(here_ref[:16])
    seen = lax.broadcasted_iota(jnp.int32, here_ref.shape, 0) > 0
    for distance, in_ref in enumerate(in_refs, 1):
        valid, place = planned_tail(plan_ref, distance)
        sink_row = sink_row + row_join(in_ref[:16])
        wanted = lax.rem(place // blocks_here - head + slots, slots)
        here = pl.ds(pl.multiple_of(place % blocks_here * WINDOW, WINDOW), WINDOW)
        for step, out_ref in enumerate(out_refs):

            @pl.when(valid & (wanted == step))
            def _(out_ref=out_ref, in_ref=in_ref, here=here):
                total = out_ref[here, :].astype(F32) + in_ref[...].astype(F32)
                out_ref[here, :] = jnp.where(seen, total, 0.0).astype(BF16)

    sink_ref[...] = jnp.broadcast_to(sink_row, sink_ref.shape)


def total_kernel(halo_ref, dk_ref, dv_ref, sink_ref, far_ref, *refs):
    *tail_refs, key_ref, value_ref, sink_grad, tails = refs
    slots, rows = len(tail_refs), dk_ref.shape[0]
    width = tails.shape[2] // 2
    head = lax.axis_index("head")
    for step, tail_ref in enumerate(tail_refs):
        tails[lax.rem(head - step + slots, slots)] = tail_ref[...]
    halo_k = jnp.concatenate([halo_ref[pair][:, :128] for pair in range(PAIRS)], axis=1)
    halo_v = jnp.concatenate([halo_ref[pair][:, 128:] for pair in range(PAIRS)], axis=1)
    for in_ref, halo, at, out_ref in (
        (dk_ref, halo_k, 0, key_ref),
        (dv_ref, halo_v, width, value_ref),
    ):
        for begin in range(0, rows, WINDOW):
            here = slice(begin, begin + WINDOW)
            parts = [tails[slot, here, at : at + width] for slot in range(slots)]
            total = in_ref[here, :] + jnp.concatenate(parts, axis=1).astype(F32)
            if begin == rows - WINDOW:
                total = total + halo.astype(F32)
            out_ref[here, :] = total.astype(BF16)
    sink_row = -(sink_ref[0:1] + far_ref[0:1])
    sink_grad[...] = sink_row[0, : sink_grad.shape[0]]


def swap(values, axis):
    return [values[0]] + [ring(values[step], axis, step) for step in range(1, len(values))]


def trade(values, axis):
    places = range(lax.axis_size(axis))
    return [values[0]] + [
        lax.ppermute(values[bits], axis, [(place, place ^ bits) for place in places])
        for bits in range(1, len(values))
    ]


def local(
    queries, key_states, value_states, out_grad, sink_logits, branch_start, branch_len, parent_list
):
    tok_count, head_count = lax.axis_size("tok"), lax.axis_size("head")
    rows = queries.shape[0]
    blocks_here = rows // WINDOW
    blocks = blocks_here * head_count
    per_slot = KV_HEADS // head_count
    width = 2 * per_slot * HEAD_DIM

    def shape(dims, kind=BF16):
        return jax.ShapeDtypeStruct(dims, kind)

    def far(value):
        return pltpu.with_memory_space_constraint(value, pltpu.HBM)

    def close(value):
        return pltpu.with_memory_space_constraint(value, pltpu.VMEM)

    *slots, halo_out, keys, values = pl.pallas_call(
        pack_kernel,
        out_shape=(shape((rows, width)),) * head_count
        + (shape((PAIRS, WINDOW, 256)),)
        + (pltpu.VMEM(key_states.shape, BF16),) * 2,
        in_specs=[HBM] * 3,
        out_specs=(VMEM,) * (head_count + 3),
        scratch_shapes=[
            pltpu.SMEM(sink_logits.shape, F32),
            pltpu.SemaphoreType.DMA((3,)),
        ],
        compiler_params=PARAMS,
        name="pack",
    )(far(sink_logits), far(key_states), far(value_states))
    spread = swap(slots, "head")
    halo = shift(halo_out, "head", 1)
    plan = pl.pallas_call(
        functools.partial(plan_kernel, tok_count, blocks, blocks_here),
        out_shape=pltpu.VMEM((8, 128), jnp.int32),
        in_specs=[SMEM] * 3,
        out_specs=VMEM,
        compiler_params=PARAMS,
        name="plan",
    )(far(branch_start), far(branch_len), far(parent_list.T))
    plan = close(plan)
    chosen = pl.pallas_call(
        choose_kernel,
        out_shape=(shape((WINDOW, width)),) * LAG,
        in_specs=[VMEM] * (1 + head_count),
        out_specs=(VMEM,) * LAG,
        compiler_params=PARAMS,
        name="choose",
    )(plan, *spread)
    late_slots = lax.optimization_barrier((*spread, *chosen))
    late_slots, chosen = late_slots[:head_count], late_slots[head_count:]
    sinks = pl.pallas_call(
        sinks_kernel,
        out_shape=shape((KV_HEADS * GROUP, 128), F32),
        in_specs=[VMEM] * head_count,
        out_specs=VMEM,
        compiler_params=PARAMS,
        name="sinks",
    )(*late_slots)
    arrived = [ring(chosen[LAG - s], "tok", s) for s in range(LAG, 0, -1)]
    queries, out_grad, _ = lax.optimization_barrier((queries, out_grad, sinks))
    near_queries, near_grad = pl.pallas_call(
        stage_kernel,
        out_shape=(pltpu.VMEM(queries.shape, BF16),) * 2,
        in_specs=[HBM] * 2,
        out_specs=(VMEM,) * 2,
        scratch_shapes=[pltpu.SemaphoreType.DMA((2,))],
        compiler_params=PARAMS,
        name="stage",
    )(far(queries), far(out_grad))
    *arrived, near_queries, near_grad = lax.optimization_barrier(
        (*arrived, near_queries, near_grad)
    )
    quarter = pl.pallas_call(
        arrive_kernel,
        out_shape=shape((WINDOW, width)),
        in_specs=[VMEM] * (1 + LAG),
        out_specs=VMEM,
        compiler_params=PARAMS,
        name="arrive",
    )(plan, *arrived)
    tails = trade([quarter] * head_count, "head")

    def attend(steps, pairs, offset, halo, joined):
        inputs = (
            sinks,
            close(near_queries),
            close(near_grad),
            close(keys),
            close(values),
            halo,
            *(tails[step] for step in steps),
            *(close(value) for value in joined),
        )
        base = 1 + len(inputs) - len(joined)
        return pl.pallas_call(
            functools.partial(
                attend_kernel,
                blocks_here,
                head_count,
                steps,
                offset,
                pairs,
                len(joined),
            ),
            out_shape=(
                pltpu.VMEM(queries.shape, BF16),
                pltpu.VMEM(queries.shape, BF16),
                pltpu.VMEM(key_states.shape, F32),
                pltpu.VMEM(key_states.shape, F32),
                pltpu.VMEM((PAIRS, WINDOW, 256), BF16),
            )
            + (shape((WINDOW, width)),) * len(steps),
            in_specs=[VMEM] * (1 + len(inputs)),
            out_specs=(VMEM,) * (5 + len(steps)),
            scratch_shapes=[
                pltpu.VMEM((head_count, WINDOW, width), BF16),
                pltpu.VMEM((WINDOW, 256), F32),
                pltpu.VMEM((2 * GROUP, WINDOW), F32),
                pltpu.VMEM((6 * HALF, 1024), BF16),
                pltpu.VMEM((6 * HALF, 1024), BF16),
            ],
            input_output_aliases={base + place: place for place in range(len(joined))},
            compiler_params=PARAMS,
            name="attend",
        )(plan, *inputs)

    if per_slot == 2:
        *joined, own_tail = attend((0,), 1, 0, spread[1], ())
        *joined, tail_2, tail_3 = attend((2, 3), 2, 2, halo, joined)
        *results, tail_1 = attend((1,), 1, 1, halo, joined)
        dtail = [own_tail, tail_1, tail_2, tail_3]
    else:
        results = attend(tuple(range(head_count)), PAIRS, None, halo, ())
        results, dtail = results[:5], list(results[5:])
    attended, query_grad, dk, dv, dhalo = results
    parts = trade(dtail, "head")

    def gather(values):
        return pl.pallas_call(
            gather_kernel,
            out_shape=shape((WINDOW, width)),
            in_specs=[VMEM] * len(values),
            out_specs=VMEM,
            compiler_params=PARAMS,
            name="gather",
        )(*values)

    quarter_grad = gather([gather([parts[0], *parts[2:]]), parts[1]])

    def flush(value):
        return pl.pallas_call(
            stage_kernel,
            out_shape=pltpu.HBM(value.shape, BF16),
            in_specs=[VMEM],
            out_specs=HBM,
            scratch_shapes=[pltpu.SemaphoreType.DMA((1,))],
            compiler_params=PARAMS,
            name="flush",
        )(close(value))

    returned = [ring(quarter_grad, "tok", -s) for s in range(LAG, 0, -1)][::-1]
    attended, _ = lax.optimization_barrier((attended, quarter_grad))
    attended = flush(attended)
    attended, *returned = lax.optimization_barrier((attended, *returned))
    halo_back = shift(dhalo, "head", -1)
    *landed, sink_near = pl.pallas_call(
        functools.partial(land_kernel, blocks),
        out_shape=(shape((rows, width)),) * head_count + (shape((8, 128), F32),),
        in_specs=[VMEM] * (LAG + 2),
        out_specs=(VMEM,) * (head_count + 1),
        compiler_params=PARAMS,
        name="land",
    )(plan, quarter_grad, *returned)
    tails_back = swap(landed, "head")
    query_grad, _ = lax.optimization_barrier((query_grad, sink_near))
    query_grad = flush(query_grad)
    span = LAG + 1
    while 2 * span < tok_count:
        sink_near = sink_near + ring(sink_near, "tok", -span)
        span *= 2
    sink_far = ring(sink_near, "tok", -span)
    key_grad, value_grad, sink_grad = pl.pallas_call(
        total_kernel,
        out_shape=(
            shape(key_states.shape),
            shape(value_states.shape),
            shape(sink_logits.shape, F32),
        ),
        in_specs=[VMEM] * (5 + head_count),
        out_specs=(VMEM,) * 3,
        scratch_shapes=[pltpu.VMEM((head_count, rows, width), BF16)],
        compiler_params=PARAMS,
        name="total",
    )(halo_back, dk, dv, sink_near, sink_far, *tails_back)
    return attended, query_grad, key_grad, value_grad, sink_grad


def solution(mesh):
    rows = P(("tok", "head"), None)
    return jax.shard_map(
        local,
        mesh=mesh,
        in_specs=(rows, rows, rows, rows, P("head"), P(), P(), P()),
        out_specs=(rows, rows, rows, rows, P("head")),
        check_vma=False,
    )
```

```python
import functools

import jax
import jax.numpy as jnp
from jax import lax
from jax.experimental import pallas as pl
from jax.experimental.pallas import tpu as pltpu
from jax.sharding import PartitionSpec as P

HEAD_DIM = 64
KV_HEADS = 8
GROUP = 8
WINDOW = 128
HALF = WINDOW // 2
LAG = 3
BR_DEV = 2
PAIRS = KV_HEADS // 2
FACTOR = 0.125
LOW = -1e30
BF16 = jnp.bfloat16
F32 = jnp.float32

SMEM = pl.BlockSpec(memory_space=pltpu.SMEM)
VMEM = pl.BlockSpec(memory_space=pltpu.VMEM)
HBM = pl.BlockSpec(memory_space=pltpu.HBM)
PARAMS = pltpu.CompilerParams(vmem_limit_bytes=24 * 1024 * 1024)


def shift(value, axis, steps):
    count = lax.axis_size(axis)
    leading, last = (max(0, -steps), min(count, count - steps))
    return lax.ppermute(value, axis, [(source, source + steps) for source in range(leading, last)])


def ring(value, axis, steps):
    count = lax.axis_size(axis)
    return lax.ppermute(value, axis, [(source, (source + steps) % count) for source in range(count)])


def with_row(tile, row):
    high = row.astype(BF16).astype(F32)
    middle = (row - high).astype(BF16).astype(F32)
    low = row - high - middle
    packed = high + pltpu.roll(middle, 32, 1) + pltpu.roll(low, 64, 1)
    place = lax.broadcasted_iota(jnp.int32, (16, 128), 0)
    top = jnp.where(place == 0, packed, tile[:16, :128].astype(F32)).astype(BF16)
    if tile.shape[1] > 128:
        top = jnp.concatenate([top, tile[:16, 128:]], axis=1)
    return jnp.concatenate([top, tile[16:]], axis=0)


def row_join(top):
    packed = top[0:1, :128].astype(F32)
    row = packed + pltpu.roll(packed, 96, 1) + pltpu.roll(packed, 64, 1)
    return jnp.where(lax.broadcasted_iota(jnp.int32, (1, 128), 1) < 32, row, 0.0)


def child_tail(starts, parents, tok, distance, tok_count, blocks):
    child = jnp.minimum(tok + distance, tok_count - 1) * BR_DEV
    parent = parents[0, child]
    safe = jnp.maximum(parent, 0)
    valid = (tok + distance < tok_count) & (parent >= 0) & (safe // BR_DEV == tok)
    place = (starts[safe] + parents[1, child]) // WINDOW - tok * blocks
    return valid, jnp.where(valid, place, 0)


def block_state(starts, lengths, parents, tok, block):
    position = block * WINDOW
    alive, opening = jnp.bool_(False), jnp.bool_(False)
    for branch in range(BR_DEV):
        start = starts[tok * BR_DEV + branch]
        length = lengths[tok * BR_DEV + branch]
        alive = alive | ((start <= position) & (position < start + length))
        opening = opening | (start == position)
    has_tail = parents[0, tok * BR_DEV] >= 0
    return alive, opening, jnp.logical_not(opening) | has_tail


def plan_kernel(tok_count, blocks, blocks_here, starts, lengths, parents, plan_ref):
    tok, head = lax.axis_index("tok"), lax.axis_index("head")
    values = []
    for distance in range(1, LAG + 1):
        values += child_tail(starts, parents, tok, distance, tok_count, blocks)
    parent = parents[0, tok * BR_DEV]
    values.append(jnp.where(parent >= 0, tok - jnp.maximum(parent, 0) // BR_DEV, 1))
    for block in range(blocks_here):
        number = tok * blocks + head * blocks_here + block
        values += block_state(starts, lengths, parents, tok, number)
    lane = lax.broadcasted_iota(jnp.int32, plan_ref.shape, 1)
    plan = jnp.zeros(plan_ref.shape, jnp.int32)
    for place, value in enumerate(values):
        plan = jnp.where(lane == place, value.astype(jnp.int32), plan)
    plan_ref[...] = plan


def planned_tail(plan_ref, distance):
    row = plan_ref[0:1, :]
    return row[0, 2 * distance - 2] != 0, row[0, 2 * distance - 1]


def planned_source(plan_ref):
    return plan_ref[0:1, :][0, 2 * LAG]


def planned_block(plan_ref, block):
    row = plan_ref[0:1, :]
    return tuple(row[0, 2 * LAG + 1 + 3 * block + place] for place in range(3))


def take(ref, slot, width):
    if width % 128 == 0:
        return ref[:, pl.ds(pl.multiple_of(slot * width, width), width)]
    value = ref[:, :width]
    for other in range(1, ref.shape[1] // width):
        value = jnp.where(slot == other, ref[:, other * width : (other + 1) * width], value)
    return value


def pack_kernel(sink_hbm, key_hbm, value_hbm, *refs):
    *slot_refs, halo_ref, keys, values, sinks, sems = refs
    copies = [
        pltpu.make_async_copy(source, target, sems.at[place])
        for place, (source, target) in enumerate(
            ((sink_hbm, sinks), (key_hbm, keys), (value_hbm, values))
        )
    ]
    for copy in copies:
        copy.start()
    for copy in copies:
        copy.wait()
    slots, rows = len(slot_refs), keys.shape[0]
    head = lax.axis_index("head")
    width = KV_HEADS * HEAD_DIM // slots
    lane = lax.broadcasted_iota(jnp.int32, (1, 128), 1)
    sink_row = jnp.zeros((1, 128), F32)
    for place in range(sinks.shape[0]):
        sink_row = jnp.where(lane == place, sinks[place], sink_row)
    for step, slot_ref in enumerate(slot_refs):
        slot = lax.rem(head + step, slots)
        both = jnp.concatenate([take(keys, slot, width), take(values, slot, width)], axis=1)
        slot_ref[...] = with_row(both, sink_row)
    for pair in range(PAIRS):
        lanes = slice(pair * 128, (pair + 1) * 128)
        last = slice(rows - WINDOW, rows)
        halo_ref[pair] = jnp.concatenate([keys[last, lanes], values[last, lanes]], axis=1)


def choose_kernel(plan_ref, *refs):
    slots = len(refs) - LAG
    slot_refs, out_refs = refs[:slots], refs[slots:]
    head = lax.axis_index("head")
    rows = slot_refs[0].shape[0]
    blocks_here = rows // WINDOW
    for distance, out_ref in zip(range(LAG, 0, -1), out_refs):
        _, place = planned_tail(plan_ref, distance)
        begin = pl.multiple_of(place % blocks_here * WINDOW, WINDOW)
        wanted = lax.rem(head - place // blocks_here + slots, slots)
        for step, slot_ref in enumerate(slot_refs):

            @pl.when(wanted == step)
            def _(out_ref=out_ref, slot_ref=slot_ref, begin=begin):
                out_ref[...] = slot_ref[pl.ds(begin, WINDOW), :]


def sinks_kernel(*refs):
    *slot_refs, sink_ref = refs
    slots = len(slot_refs)
    head = lax.axis_index("head")
    heads = sink_ref.shape[0] // slots
    for step, slot_ref in enumerate(slot_refs):
        source = lax.rem(head - step + slots, slots)
        sink_row = row_join(slot_ref[:16])
        turned = jnp.broadcast_to(sink_row, (128, 128)).T
        sink_ref[pl.ds(pl.multiple_of(source * heads, heads), heads), :] = turned[:heads]


def arrive_kernel(plan_ref, *refs):
    *in_refs, out_ref = refs
    mine = planned_source(plan_ref)
    for distance, in_ref in zip(range(LAG, 0, -1), in_refs):

        @pl.when(mine == distance)
        def _(in_ref=in_ref):
            out_ref[...] = in_ref[...]


def stage_kernel(*refs):
    *arrays, sems = refs
    half = len(arrays) // 2
    copies = [
        pltpu.make_async_copy(source, target, sems.at[place])
        for place, (source, target) in enumerate(zip(arrays[:half], arrays[half:]))
    ]
    for copy in copies:
        copy.start()
    for copy in copies:
        copy.wait()


def attend_kernel(blocks_here, slots, steps, offset, pairs, joins, *refs):
    inputs, refs = refs[:7], refs[7:]
    tail_refs, refs = refs[: len(steps)], refs[len(steps) + joins :]
    outputs, refs = refs[:5], refs[5:]
    dtail_refs, refs = refs[: len(steps)], refs[len(steps) :]
    tails, *scratch = refs
    head = lax.axis_index("head")
    states = [planned_block(inputs[0], block) for block in range(blocks_here)]
    for step, tail_ref in zip(steps, tail_refs):
        tails[head ^ step] = tail_ref[...]

    def step(place, carry):
        pair = place // blocks_here
        if offset is not None:
            pair = head ^ (pair + offset)
        block = place % blocks_here
        state = states[0]
        for other in range(1, blocks_here):
            state = [jnp.where(block == other, *two) for two in zip(states[other], state)]
        attend_block(
            blocks_here,
            slots,
            pair,
            block,
            [value != 0 for value in state],
            inputs,
            outputs,
            tails,
            tuple(zip(steps, dtail_refs)),
            scratch,
        )
        return carry

    lax.fori_loop(0, pairs * blocks_here, step, 0)


def attend_block(
    blocks_here, slots, pair, block, state, inputs, outputs, tails, dtails, scratch
):
    _, sink_ref, q_ref, g_ref, k_ref, v_ref, halo_ref = inputs
    o_ref, dq_ref, dk_ref, dv_ref, dhalo_ref = outputs
    tail_sum, sink_rows, prob2, slope2 = scratch
    per_slot = KV_HEADS // slots
    head = lax.axis_index("head")
    alive, opening, prev_ok = state
    here = pl.ds(pl.multiple_of(block * WINDOW, WINDOW), WINDOW)
    before = pl.ds(pl.multiple_of(jnp.maximum(block - 1, 0) * WINDOW, WINDOW), WINDOW)
    first = block == 0
    near = pl.ds(pl.multiple_of(pair * 128, 128), 128)
    big = pl.ds(pl.multiple_of(pair * 1024, 1024), 1024)
    q_ref, g_ref, o_ref, dq_ref = (ref.at[here, big] for ref in (q_ref, g_ref, o_ref, dq_ref))
    k_ref, v_ref, dk_ref, dv_ref = (ref.at[:, near] for ref in (k_ref, v_ref, dk_ref, dv_ref))
    sink_ref = sink_ref.at[pl.ds(pl.multiple_of(pair * 16, 16), 16)]
    dhalo_ref = dhalo_ref.at[pair]

    @pl.when(first)
    def _():
        tail_sum[...] = jnp.zeros_like(tail_sum)
        dhalo_ref[...] = jnp.zeros((WINDOW, 256), BF16)
        sink_rows[...] = jnp.zeros_like(sink_rows)

    @pl.when(jnp.logical_not(alive))
    def _():
        o_ref[...] = jnp.zeros((WINDOW, 1024), BF16)
        dq_ref[...] = jnp.zeros((WINDOW, 1024), BF16)
        dk_ref[here, :] = jnp.zeros((WINDOW, 128), F32)
        dv_ref[here, :] = jnp.zeros((WINDOW, 128), F32)

    @pl.when(alive)
    def _():
        if len(halo_ref.shape) == 2:
            halo = halo_ref[halo_ref.shape[0] - WINDOW :]
        else:
            halo = halo_ref[pair]
        if per_slot == 2:
            tail = tails[pair]
            tail_k, tail_v = tail[:, :128], tail[:, 128:]
        else:
            tail_a, tail_b = tails[2 * pair], tails[2 * pair + 1]
            tail_k = jnp.concatenate([tail_a[:, :64], tail_b[:, :64]], axis=1)
            tail_v = jnp.concatenate([tail_a[:, 64:], tail_b[:, 64:]], axis=1)
        near_k = jnp.where(first, halo[:, :128], k_ref[before, :])
        near_v = jnp.where(first, halo[:, 128:], v_ref[before, :])
        prev_k = jnp.where(opening, tail_k, near_k)
        prev_v = jnp.where(opening, tail_v, near_v)
        own_k, own_v = k_ref[here, :], v_ref[here, :]

        def halves(own, prev):
            return (
                jnp.concatenate([own[:HALF], prev[:HALF], prev[HALF:]], axis=0),
                jnp.concatenate([own[HALF:], prev[HALF:], own[:HALF]], axis=0),
            )

        left = lax.broadcasted_iota(jnp.int32, (1, 128), 1) < HALF
        low16 = left.astype(F32).astype(BF16)
        high16 = BF16(1) - low16

        def padded(seen):
            swapped = jnp.concatenate([seen[:, 64:], seen[:, :64]], axis=1)
            return (
                jnp.concatenate([seen * low16, swapped * high16], axis=0),
                jnp.concatenate([swapped * low16, seen * high16], axis=0),
            )

        seen_k = halves(own_k * BF16(FACTOR), prev_k * BF16(FACTOR))
        seen_v = halves(own_v, prev_v)
        padded_k = tuple(padded(value) for value in seen_k)
        padded_v = tuple(padded(value) for value in seen_v)
        turned_k = tuple(value.T for value in seen_k)
        turned_v = tuple(value.T for value in seen_v)
        bias = jnp.where(prev_ok, 0.0, LOW)
        key_place = lax.broadcasted_iota(jnp.int32, (HALF, 4 * HALF), 0)
        query_place = lax.broadcasted_iota(jnp.int32, (HALF, 4 * HALF), 1) & (HALF - 1)
        own = key_place <= query_place
        own16 = own.astype(F32).astype(BF16)
        turn = (((1,), (1,)), ((), ()))
        items = [(unit, half) for unit in range(2) for half in range(2)]
        seen = 3 * HALF

        def wide(index):
            return slice(index * 256, (index + 1) * 256)

        def feats(index):
            unit = items[index][0]
            return slice(unit * HEAD_DIM, (unit + 1) * HEAD_DIM)

        def corners(unit, half):
            rows = slice(half * HALF, (half + 1) * HALF)
            return [
                (rows, slice(unit * 512 + at * 128, unit * 512 + (at + 1) * 128)) for at in range(4)
            ]

        def stacked(ref, unit, half):
            return jnp.concatenate([ref[corner] for corner in corners(unit, half)], axis=0)

        def products(index):
            unit, half = items[index]
            score, dp = (
                lax.dot_general(
                    padded[half][unit],
                    stacked(ref, unit, half),
                    turn,
                    preferred_element_type=F32,
                )
                for padded, ref in ((padded_k, q_ref), (padded_v, g_ref))
            )
            parts = []
            for base in (0, seen):
                near, far = slice(base, base + HALF), slice(base + HALF, base + 2 * HALF)
                rest = slice(base + 2 * HALF, base + 3 * HALF)
                edge = jnp.where(own, score[near], score[far] + bias)
                whole = score[rest] + bias if half == 0 else score[rest]
                parts.append((edge, whole, jnp.where(own, dp[near], dp[far]), dp[rest]))
            return parts

        def weigh(index, odd, edge, whole, dp_edge, dp_whole):
            unit, half = items[index]
            base = odd * seen
            row = unit * GROUP + odd
            sink = jnp.concatenate(
                [
                    jnp.where(left, sink_ref[at : at + 1], sink_ref[at + 2 : at + 3])
                    for at in (row, row + 4)
                ],
                axis=1,
            )
            peak = jnp.max(jnp.maximum(edge, whole), axis=0, keepdims=True)
            peak = jnp.maximum(peak, sink)
            edge, whole = jnp.exp(edge - peak), jnp.exp(whole - peak)
            sink_weight = jnp.exp(sink - peak)
            inverse = 1.0 / (jnp.sum(edge + whole, axis=0, keepdims=True) + sink_weight)
            edge, whole = edge * inverse, whole * inverse
            delta = jnp.sum(edge * dp_edge + whole * dp_whole, axis=0, keepdims=True)
            edge16, whole16 = edge.astype(BF16), whole.astype(BF16)
            edge_own = edge16 * own16
            edge_prev = edge16 - edge_own
            away_edge, away_whole = (dp_edge - delta).astype(BF16), (dp_whole - delta).astype(BF16)
            for target, rows in (
                (prob2, (edge_own, edge_prev, whole16)),
                (slope2, (edge_own * away_edge, edge_prev * away_edge, whole16 * away_whole)),
            ):
                for by, value in enumerate(rows):
                    at = base + by * HALF
                    target[at : at + HALF, wide(index)] = value
            sink_term = sink_weight * inverse * delta
            for at, lanes in ((row, slice(0, 128)), (row + 4, slice(128, 256))):
                part = sink_term[:, lanes]
                sink_rows[at : at + 1] += jnp.where(left, part, 0.0)
                sink_rows[at + 2 : at + 3] += jnp.where(left, 0.0, part)

        def finish(index):
            unit, half = items[index]
            for source, across, out_ref in ((prob2, turned_v, o_ref), (slope2, turned_k, dq_ref)):
                out_t = [
                    jnp.dot(
                        across[half][feats(index)],
                        source[base : base + seen, wide(index)],
                        preferred_element_type=F32,
                    ).astype(BF16)
                    for base in (0, seen)
                ]
                out = jnp.concatenate(out_t, axis=0).T
                for at, corner in enumerate(corners(unit, half)):
                    out_ref[corner] = out[at * HALF : (at + 1) * HALF]

        def reduce(index):
            unit, half = items[index]
            parts = []
            for weights, ref in ((slope2, q_ref), (prob2, g_ref)):
                part = jnp.dot(
                    weights[:, wide(index)], stacked(ref, unit, half), preferred_element_type=F32
                )
                parts.append(jnp.where(left, part[:seen], part[seen:]))
            return parts

        def join(first_half, second_half):
            total = jnp.concatenate(
                [
                    first_half[:HALF] + second_half[2 * HALF :],
                    second_half[:HALF],
                    first_half[HALF : 2 * HALF],
                    first_half[2 * HALF :] + second_half[HALF : 2 * HALF],
                ],
                axis=0,
            )
            return total + pltpu.roll(total, HEAD_DIM, 1)

        ahead, parts = products(0), []
        for index in range(len(items)):
            now = ahead
            weigh(index, 0, *now[0])
            if index + 1 < len(items):
                ahead = products(index + 1)
            weigh(index, 1, *now[1])
            if index >= 1:
                finish(index - 1)
            parts.append(reduce(index))
        finish(len(items) - 1)
        grads = [
            [join(parts[2 * unit][place], parts[2 * unit + 1][place]) for place in range(2)]
            for unit in range(2)
        ]
        dk = jnp.where(left, grads[0][0], grads[1][0]) * FACTOR
        dv = jnp.where(left, grads[0][1], grads[1][1])
        dk_ref[here, :] = dk[:WINDOW]
        dv_ref[here, :] = dv[:WINDOW]

        @pl.when(opening & prev_ok)
        def _():
            tail_sum[:, :128] += dk[WINDOW:]
            tail_sum[:, 128:] += dv[WINDOW:]

        @pl.when(jnp.logical_not(opening) & first)
        def _():
            dhalo_ref[:, :128] = dk[WINDOW:].astype(BF16)
            dhalo_ref[:, 128:] = dv[WINDOW:].astype(BF16)

        @pl.when(jnp.logical_not(opening) & jnp.logical_not(first))
        def _():
            dk_ref[before, :] += dk[WINDOW:]
            dv_ref[before, :] += dv[WINDOW:]

    @pl.when(block == blocks_here - 1)
    def _():
        width = 2 * per_slot * HEAD_DIM
        heads = per_slot * GROUP
        total = tail_sum[...].astype(BF16)
        for part in range(2 // per_slot):
            feats = slice(part * width // 2, (part + 1) * width // 2)
            tail = jnp.concatenate([total[:, :128][:, feats], total[:, 128:][:, feats]], axis=1)
            rows = sink_rows[part * heads : (part + 1) * heads]
            rows = jnp.concatenate([rows, jnp.zeros((128 - heads, WINDOW), F32)], axis=0)
            sink_row = jnp.sum(rows.T, axis=0, keepdims=True)
            tail = with_row(tail, sink_row)
            wanted = (pair * (2 // per_slot) + part) ^ head
            for step, dtail_ref in dtails:

                @pl.when(wanted == step)
                def _(dtail_ref=dtail_ref, tail=tail):
                    dtail_ref[...] = tail


def gather_kernel(*refs):
    *in_refs, out_ref = refs
    total, sink_row = 0.0, 0.0
    for in_ref in in_refs:
        total = total + in_ref[...].astype(F32)
        sink_row = sink_row + row_join(in_ref[:16])
    out_ref[...] = with_row(total.astype(BF16), sink_row)


def land_kernel(blocks, plan_ref, here_ref, *refs):
    head = lax.axis_index("head")
    in_refs, out_refs, sink_ref = refs[:LAG], refs[LAG:-1], refs[-1]
    slots = len(out_refs)
    blocks_here = blocks // slots
    for out_ref in out_refs:
        out_ref[...] = jnp.zeros_like(out_ref)
    sink_row = row_join(here_ref[:16])
    seen = lax.broadcasted_iota(jnp.int32, here_ref.shape, 0) > 0
    for distance, in_ref in enumerate(in_refs, 1):
        valid, place = planned_tail(plan_ref, distance)
        sink_row = sink_row + row_join(in_ref[:16])
        wanted = (place // blocks_here) ^ head
        here = pl.ds(pl.multiple_of(place % blocks_here * WINDOW, WINDOW), WINDOW)
        for step, out_ref in enumerate(out_refs):

            @pl.when(valid & (wanted == step))
            def _(out_ref=out_ref, in_ref=in_ref, here=here):
                total = out_ref[here, :].astype(F32) + in_ref[...].astype(F32)
                out_ref[here, :] = jnp.where(seen, total, 0.0).astype(BF16)

    sink_ref[...] = jnp.broadcast_to(sink_row, sink_ref.shape)


def total_kernel(halo_ref, dk_ref, dv_ref, sink_ref, far_ref, *refs):
    *tail_refs, key_ref, value_ref, sink_grad, tails = refs
    slots, rows = len(tail_refs), dk_ref.shape[0]
    width = tails.shape[2] // 2
    head = lax.axis_index("head")
    for bits, tail_ref in zip((*range(2, slots), 1, 0), tail_refs):
        tails[head ^ bits] = tail_ref[...]
    halo_k = jnp.concatenate([halo_ref[pair][:, :128] for pair in range(PAIRS)], axis=1)
    halo_v = jnp.concatenate([halo_ref[pair][:, 128:] for pair in range(PAIRS)], axis=1)
    for in_ref, halo, at, out_ref in (
        (dk_ref, halo_k, 0, key_ref),
        (dv_ref, halo_v, width, value_ref),
    ):
        for begin in range(0, rows, WINDOW):
            here = slice(begin, begin + WINDOW)
            parts = [tails[slot, here, at : at + width] for slot in range(slots)]
            total = in_ref[here, :] + jnp.concatenate(parts, axis=1).astype(F32)
            if begin == rows - WINDOW:
                total = total + halo.astype(F32)
            out_ref[here, :] = total.astype(BF16)
    sink_row = -(sink_ref[0:1] + far_ref[0:1])
    sink_grad[...] = sink_row[0, : sink_grad.shape[0]]


def swap(values, axis):
    return [values[0]] + [ring(values[step], axis, step) for step in range(1, len(values))]


def trade(values, axis):
    places = range(lax.axis_size(axis))
    return [values[0]] + [
        lax.ppermute(values[bits], axis, [(place, place ^ bits) for place in places])
        for bits in range(1, len(values))
    ]


def local(
    queries, key_states, value_states, out_grad, sink_logits, branch_start, branch_len, parent_list
):
    tok_count, head_count = lax.axis_size("tok"), lax.axis_size("head")
    rows = queries.shape[0]
    blocks_here = rows // WINDOW
    blocks = blocks_here * head_count
    per_slot = KV_HEADS // head_count
    width = 2 * per_slot * HEAD_DIM

    def shape(dims, kind=BF16):
        return jax.ShapeDtypeStruct(dims, kind)

    def far(value):
        return pltpu.with_memory_space_constraint(value, pltpu.HBM)

    def close(value):
        return pltpu.with_memory_space_constraint(value, pltpu.VMEM)

    *slots, halo_out, keys, values = pl.pallas_call(
        pack_kernel,
        out_shape=(shape((rows, width)),) * head_count
        + (shape((PAIRS, WINDOW, 256)),)
        + (pltpu.VMEM(key_states.shape, BF16),) * 2,
        in_specs=[HBM] * 3,
        out_specs=(VMEM,) * (head_count + 3),
        scratch_shapes=[
            pltpu.SMEM(sink_logits.shape, F32),
            pltpu.SemaphoreType.DMA((3,)),
        ],
        compiler_params=PARAMS,
        name="pack",
    )(far(sink_logits), far(key_states), far(value_states))
    spread = swap(slots, "head")
    halo = shift(halo_out, "head", 1)
    plan = pl.pallas_call(
        functools.partial(plan_kernel, tok_count, blocks, blocks_here),
        out_shape=pltpu.VMEM((8, 128), jnp.int32),
        in_specs=[SMEM] * 3,
        out_specs=VMEM,
        compiler_params=PARAMS,
        name="plan",
    )(far(branch_start), far(branch_len), far(parent_list.T))
    plan = close(plan)
    chosen = pl.pallas_call(
        choose_kernel,
        out_shape=(shape((WINDOW, width)),) * LAG,
        in_specs=[VMEM] * (1 + head_count),
        out_specs=(VMEM,) * LAG,
        compiler_params=PARAMS,
        name="choose",
    )(plan, *spread)
    late_slots = lax.optimization_barrier((*spread, *chosen))
    late_slots, chosen = late_slots[:head_count], late_slots[head_count:]
    sinks = pl.pallas_call(
        sinks_kernel,
        out_shape=shape((KV_HEADS * GROUP, 128), F32),
        in_specs=[VMEM] * head_count,
        out_specs=VMEM,
        compiler_params=PARAMS,
        name="sinks",
    )(*late_slots)
    arrived = [ring(chosen[LAG - s], "tok", s) for s in range(LAG, 0, -1)]
    queries, out_grad, _ = lax.optimization_barrier((queries, out_grad, sinks))
    near_queries, near_grad = pl.pallas_call(
        stage_kernel,
        out_shape=(pltpu.VMEM(queries.shape, BF16),) * 2,
        in_specs=[HBM] * 2,
        out_specs=(VMEM,) * 2,
        scratch_shapes=[pltpu.SemaphoreType.DMA((2,))],
        compiler_params=PARAMS,
        name="stage",
    )(far(queries), far(out_grad))
    *arrived, near_queries, near_grad = lax.optimization_barrier(
        (*arrived, near_queries, near_grad)
    )
    quarter = pl.pallas_call(
        arrive_kernel,
        out_shape=shape((WINDOW, width)),
        in_specs=[VMEM] * (1 + LAG),
        out_specs=VMEM,
        compiler_params=PARAMS,
        name="arrive",
    )(plan, *arrived)
    tails = trade([quarter] * head_count, "head")

    def attend(steps, pairs, offset, halo, joined):
        inputs = (
            sinks,
            close(near_queries),
            close(near_grad),
            close(keys),
            close(values),
            halo,
            *(tails[step] for step in steps),
            *(close(value) for value in joined),
        )
        base = 1 + len(inputs) - len(joined)
        return pl.pallas_call(
            functools.partial(
                attend_kernel,
                blocks_here,
                head_count,
                steps,
                offset,
                pairs,
                len(joined),
            ),
            out_shape=(
                pltpu.VMEM(queries.shape, BF16),
                pltpu.VMEM(queries.shape, BF16),
                pltpu.VMEM(key_states.shape, F32),
                pltpu.VMEM(key_states.shape, F32),
                pltpu.VMEM((PAIRS, WINDOW, 256), BF16),
            )
            + (shape((WINDOW, width)),) * len(steps),
            in_specs=[VMEM] * (1 + len(inputs)),
            out_specs=(VMEM,) * (5 + len(steps)),
            scratch_shapes=[
                pltpu.VMEM((head_count, WINDOW, width), BF16),
                pltpu.VMEM((WINDOW, 256), F32),
                pltpu.VMEM((2 * GROUP, WINDOW), F32),
                pltpu.VMEM((6 * HALF, 1024), BF16),
                pltpu.VMEM((6 * HALF, 1024), BF16),
            ],
            input_output_aliases={base + place: place for place in range(len(joined))},
            compiler_params=PARAMS,
            name="attend",
        )(plan, *inputs)

    if per_slot == 2:
        *joined, own_tail = attend((0,), 1, 0, spread[1], ())
        *joined, tail_2, tail_3 = attend((2, 3), 2, 2, halo, joined)
        *results, tail_1 = attend((1,), 1, 1, halo, joined)
        dtail = [own_tail, tail_1, tail_2, tail_3]
    else:
        results = attend(tuple(range(head_count)), PAIRS, None, halo, ())
        results, dtail = results[:5], list(results[5:])
    attended, query_grad, dk, dv, dhalo = results
    parts = trade(dtail, "head")

    def gather(values):
        return pl.pallas_call(
            gather_kernel,
            out_shape=shape((WINDOW, width)),
            in_specs=[VMEM] * len(values),
            out_specs=VMEM,
            compiler_params=PARAMS,
            name="gather",
        )(*values)

    quarter_grad = gather([gather([parts[0], *parts[2:]]), parts[1]])

    def flush(value):
        return pl.pallas_call(
            stage_kernel,
            out_shape=pltpu.HBM(value.shape, BF16),
            in_specs=[VMEM],
            out_specs=HBM,
            scratch_shapes=[pltpu.SemaphoreType.DMA((1,))],
            compiler_params=PARAMS,
            name="flush",
        )(close(value))

    returned = [ring(quarter_grad, "tok", -s) for s in range(LAG, 0, -1)][::-1]
    attended, _ = lax.optimization_barrier((attended, quarter_grad))
    attended = flush(attended)
    attended, *returned = lax.optimization_barrier((attended, *returned))
    halo_back = shift(dhalo, "head", -1)
    *landed, sink_near = pl.pallas_call(
        functools.partial(land_kernel, blocks),
        out_shape=(shape((rows, width)),) * head_count + (shape((8, 128), F32),),
        in_specs=[VMEM] * (LAG + 2),
        out_specs=(VMEM,) * (head_count + 1),
        compiler_params=PARAMS,
        name="land",
    )(plan, quarter_grad, *returned)
    back = trade(landed, "head")
    tails_back = [*back[2:], back[1], back[0]]
    query_grad, _ = lax.optimization_barrier((query_grad, sink_near))
    query_grad = flush(query_grad)
    span = LAG + 1
    while 2 * span < tok_count:
        sink_near = sink_near + ring(sink_near, "tok", -span)
        span *= 2
    sink_far = ring(sink_near, "tok", -span)
    key_grad, value_grad, sink_grad = pl.pallas_call(
        total_kernel,
        out_shape=(
            shape(key_states.shape),
            shape(value_states.shape),
            shape(sink_logits.shape, F32),
        ),
        in_specs=[VMEM] * (5 + head_count),
        out_specs=(VMEM,) * 3,
        scratch_shapes=[pltpu.VMEM((head_count, rows, width), BF16)],
        compiler_params=PARAMS,
        name="total",
    )(halo_back, dk, dv, sink_near, sink_far, *tails_back)
    return attended, query_grad, key_grad, value_grad, sink_grad


def solution(mesh):
    rows = P(("tok", "head"), None)
    return jax.shard_map(
        local,
        mesh=mesh,
        in_specs=(rows, rows, rows, rows, P("head"), P(), P(), P()),
        out_specs=(rows, rows, rows, rows, P("head")),
        check_vma=False,
    )
```

```python
import functools

import jax
import jax.numpy as jnp
from jax import lax
from jax.experimental import pallas as pl
from jax.experimental.pallas import tpu as pltpu
from jax.sharding import PartitionSpec as P

HEAD_DIM = 64
KV_HEADS = 8
GROUP = 8
WINDOW = 128
HALF = WINDOW // 2
LAG = 3
BR_DEV = 2
PAIRS = KV_HEADS // 2
FACTOR = 0.125
LOW = -1e30
BF16 = jnp.bfloat16
F32 = jnp.float32

SMEM = pl.BlockSpec(memory_space=pltpu.SMEM)
VMEM = pl.BlockSpec(memory_space=pltpu.VMEM)
HBM = pl.BlockSpec(memory_space=pltpu.HBM)
PARAMS = pltpu.CompilerParams(vmem_limit_bytes=24 * 1024 * 1024)


def shift(value, axis, steps):
    count = lax.axis_size(axis)
    leading, last = (max(0, -steps), min(count, count - steps))
    return lax.ppermute(value, axis, [(source, source + steps) for source in range(leading, last)])


def ring(value, axis, steps):
    count = lax.axis_size(axis)
    return lax.ppermute(value, axis, [(source, (source + steps) % count) for source in range(count)])


def with_row(tile, row):
    high = row.astype(BF16).astype(F32)
    middle = (row - high).astype(BF16).astype(F32)
    low = row - high - middle
    packed = high + pltpu.roll(middle, 32, 1) + pltpu.roll(low, 64, 1)
    place = lax.broadcasted_iota(jnp.int32, (16, 128), 0)
    top = jnp.where(place == 0, packed, tile[:16, :128].astype(F32)).astype(BF16)
    if tile.shape[1] > 128:
        top = jnp.concatenate([top, tile[:16, 128:]], axis=1)
    return jnp.concatenate([top, tile[16:]], axis=0)


def row_join(top):
    packed = top[0:1, :128].astype(F32)
    row = packed + pltpu.roll(packed, 96, 1) + pltpu.roll(packed, 64, 1)
    return jnp.where(lax.broadcasted_iota(jnp.int32, (1, 128), 1) < 32, row, 0.0)


def child_tail(starts, parents, tok, distance, tok_count, blocks):
    child = jnp.minimum(tok + distance, tok_count - 1) * BR_DEV
    parent = parents[0, child]
    safe = jnp.maximum(parent, 0)
    valid = (tok + distance < tok_count) & (parent >= 0) & (safe // BR_DEV == tok)
    place = (starts[safe] + parents[1, child]) // WINDOW - tok * blocks
    return valid, jnp.where(valid, place, 0)


def block_state(starts, lengths, parents, tok, block):
    position = block * WINDOW
    alive, opening = jnp.bool_(False), jnp.bool_(False)
    for branch in range(BR_DEV):
        start = starts[tok * BR_DEV + branch]
        length = lengths[tok * BR_DEV + branch]
        alive = alive | ((start <= position) & (position < start + length))
        opening = opening | (start == position)
    has_tail = parents[0, tok * BR_DEV] >= 0
    return alive, opening, jnp.logical_not(opening) | has_tail


def plan_kernel(tok_count, blocks, blocks_here, starts, lengths, parents, plan_ref):
    tok, head = lax.axis_index("tok"), lax.axis_index("head")
    values = []
    for distance in range(1, LAG + 1):
        values += child_tail(starts, parents, tok, distance, tok_count, blocks)
    parent = parents[0, tok * BR_DEV]
    values.append(jnp.where(parent >= 0, tok - jnp.maximum(parent, 0) // BR_DEV, 1))
    for block in range(blocks_here):
        number = tok * blocks + head * blocks_here + block
        values += block_state(starts, lengths, parents, tok, number)
    lane = lax.broadcasted_iota(jnp.int32, plan_ref.shape, 1)
    plan = jnp.zeros(plan_ref.shape, jnp.int32)
    for place, value in enumerate(values):
        plan = jnp.where(lane == place, value.astype(jnp.int32), plan)
    plan_ref[...] = plan


def planned_tail(plan_ref, distance):
    row = plan_ref[0:1, :]
    return row[0, 2 * distance - 2] != 0, row[0, 2 * distance - 1]


def planned_source(plan_ref):
    return plan_ref[0:1, :][0, 2 * LAG]


def planned_block(plan_ref, block):
    row = plan_ref[0:1, :]
    return tuple(row[0, 2 * LAG + 1 + 3 * block + place] for place in range(3))


def take(ref, slot, width):
    if width % 128 == 0:
        return ref[:, pl.ds(pl.multiple_of(slot * width, width), width)]
    value = ref[:, :width]
    for other in range(1, ref.shape[1] // width):
        value = jnp.where(slot == other, ref[:, other * width : (other + 1) * width], value)
    return value


def pack_kernel(sink_hbm, key_hbm, value_hbm, *refs):
    *slot_refs, halo_ref, keys, values, sinks, sems = refs
    copies = [
        pltpu.make_async_copy(source, target, sems.at[place])
        for place, (source, target) in enumerate(
            ((sink_hbm, sinks), (key_hbm, keys), (value_hbm, values))
        )
    ]
    for copy in copies:
        copy.start()
    for copy in copies:
        copy.wait()
    slots, rows = len(slot_refs), keys.shape[0]
    head = lax.axis_index("head")
    width = KV_HEADS * HEAD_DIM // slots
    lane = lax.broadcasted_iota(jnp.int32, (1, 128), 1)
    sink_row = jnp.zeros((1, 128), F32)
    for place in range(sinks.shape[0]):
        sink_row = jnp.where(lane == place, sinks[place], sink_row)
    for step, slot_ref in enumerate(slot_refs):
        slot = lax.rem(head + step, slots)
        both = jnp.concatenate([take(keys, slot, width), take(values, slot, width)], axis=1)
        slot_ref[...] = with_row(both, sink_row)
    for pair in range(PAIRS):
        lanes = slice(pair * 128, (pair + 1) * 128)
        last = slice(rows - WINDOW, rows)
        halo_ref[pair] = jnp.concatenate([keys[last, lanes], values[last, lanes]], axis=1)


def choose_kernel(plan_ref, *refs):
    slots = len(refs) - LAG
    slot_refs, out_refs = refs[:slots], refs[slots:]
    head = lax.axis_index("head")
    rows = slot_refs[0].shape[0]
    blocks_here = rows // WINDOW
    for distance, out_ref in zip(range(LAG, 0, -1), out_refs):
        _, place = planned_tail(plan_ref, distance)
        begin = pl.multiple_of(place % blocks_here * WINDOW, WINDOW)
        wanted = lax.rem(head - place // blocks_here + slots, slots)
        for step, slot_ref in enumerate(slot_refs):

            @pl.when(wanted == step)
            def _(out_ref=out_ref, slot_ref=slot_ref, begin=begin):
                out_ref[...] = slot_ref[pl.ds(begin, WINDOW), :]


def sinks_kernel(*refs):
    *slot_refs, sink_ref = refs
    slots = len(slot_refs)
    head = lax.axis_index("head")
    heads = sink_ref.shape[0] // slots
    for step, slot_ref in enumerate(slot_refs):
        source = lax.rem(head - step + slots, slots)
        sink_row = row_join(slot_ref[:16])
        turned = jnp.broadcast_to(sink_row, (128, 128)).T
        sink_ref[pl.ds(pl.multiple_of(source * heads, heads), heads), :] = turned[:heads]


def arrive_kernel(plan_ref, *refs):
    *in_refs, out_ref = refs
    mine = planned_source(plan_ref)
    for distance, in_ref in zip(range(LAG, 0, -1), in_refs):

        @pl.when(mine == distance)
        def _(in_ref=in_ref):
            out_ref[...] = in_ref[...]


def stage_kernel(*refs):
    *arrays, sems = refs
    half = len(arrays) // 2
    copies = [
        pltpu.make_async_copy(source, target, sems.at[place])
        for place, (source, target) in enumerate(zip(arrays[:half], arrays[half:]))
    ]
    for copy in copies:
        copy.start()
    for copy in copies:
        copy.wait()


def attend_kernel(blocks_here, slots, steps, offset, pairs, joins, *refs):
    inputs, refs = refs[:7], refs[7:]
    tail_refs, refs = refs[: len(steps)], refs[len(steps) + joins :]
    outputs, refs = refs[:5], refs[5:]
    dtail_refs, refs = refs[: len(steps)], refs[len(steps) :]
    tails, *scratch = refs
    head = lax.axis_index("head")
    states = [planned_block(inputs[0], block) for block in range(blocks_here)]
    for step, tail_ref in zip(steps, tail_refs):
        tails[head ^ step] = tail_ref[...]

    def step(place, carry):
        pair = place // blocks_here
        if offset is not None:
            pair = head ^ (pair + offset)
        block = place % blocks_here
        state = states[0]
        for other in range(1, blocks_here):
            state = [jnp.where(block == other, *two) for two in zip(states[other], state)]
        attend_block(
            blocks_here,
            slots,
            pair,
            block,
            [value != 0 for value in state],
            inputs,
            outputs,
            tails,
            tuple(zip(steps, dtail_refs)),
            scratch,
        )
        return carry

    lax.fori_loop(0, pairs * blocks_here, step, 0)


def attend_block(
    blocks_here, slots, pair, block, state, inputs, outputs, tails, dtails, scratch
):
    _, sink_ref, q_ref, g_ref, k_ref, v_ref, halo_ref = inputs
    o_ref, dq_ref, dk_ref, dv_ref, dhalo_ref = outputs
    tail_sum, sink_rows, prob2, slope2 = scratch
    per_slot = KV_HEADS // slots
    head = lax.axis_index("head")
    alive, opening, prev_ok = state
    here = pl.ds(pl.multiple_of(block * WINDOW, WINDOW), WINDOW)
    before = pl.ds(pl.multiple_of(jnp.maximum(block - 1, 0) * WINDOW, WINDOW), WINDOW)
    first = block == 0
    near = pl.ds(pl.multiple_of(pair * 128, 128), 128)
    big = pl.ds(pl.multiple_of(pair * 1024, 1024), 1024)
    q_ref, g_ref, o_ref, dq_ref = (ref.at[here, big] for ref in (q_ref, g_ref, o_ref, dq_ref))
    k_ref, v_ref, dk_ref, dv_ref = (ref.at[:, near] for ref in (k_ref, v_ref, dk_ref, dv_ref))
    sink_ref = sink_ref.at[pl.ds(pl.multiple_of(pair * 16, 16), 16)]
    dhalo_ref = dhalo_ref.at[pair]

    @pl.when(first)
    def _():
        tail_sum[...] = jnp.zeros_like(tail_sum)
        dhalo_ref[...] = jnp.zeros((WINDOW, 256), BF16)
        sink_rows[...] = jnp.zeros_like(sink_rows)

    @pl.when(jnp.logical_not(alive))
    def _():
        o_ref[...] = jnp.zeros((WINDOW, 1024), BF16)
        dq_ref[...] = jnp.zeros((WINDOW, 1024), BF16)
        dk_ref[here, :] = jnp.zeros((WINDOW, 128), F32)
        dv_ref[here, :] = jnp.zeros((WINDOW, 128), F32)

    @pl.when(alive)
    def _():
        if len(halo_ref.shape) == 2:
            halo = halo_ref[halo_ref.shape[0] - WINDOW :]
        else:
            halo = halo_ref[pair]
        if per_slot == 2:
            tail = tails[pair]
            tail_k, tail_v = tail[:, :128], tail[:, 128:]
        else:
            tail_a, tail_b = tails[2 * pair], tails[2 * pair + 1]
            tail_k = jnp.concatenate([tail_a[:, :64], tail_b[:, :64]], axis=1)
            tail_v = jnp.concatenate([tail_a[:, 64:], tail_b[:, 64:]], axis=1)
        near_k = jnp.where(first, halo[:, :128], k_ref[before, :])
        near_v = jnp.where(first, halo[:, 128:], v_ref[before, :])
        prev_k = jnp.where(opening, tail_k, near_k)
        prev_v = jnp.where(opening, tail_v, near_v)
        own_k, own_v = k_ref[here, :], v_ref[here, :]

        def halves(own, prev):
            return (
                jnp.concatenate([own[:HALF], prev[:HALF], prev[HALF:]], axis=0),
                jnp.concatenate([own[HALF:], prev[HALF:], own[:HALF]], axis=0),
            )

        left = lax.broadcasted_iota(jnp.int32, (1, 128), 1) < HALF
        low16 = left.astype(F32).astype(BF16)
        high16 = BF16(1) - low16

        def padded(seen):
            swapped = jnp.concatenate([seen[:, 64:], seen[:, :64]], axis=1)
            return (
                jnp.concatenate([seen * low16, swapped * high16], axis=0),
                jnp.concatenate([swapped * low16, seen * high16], axis=0),
            )

        seen_k = halves(own_k * BF16(FACTOR), prev_k * BF16(FACTOR))
        seen_v = halves(own_v, prev_v)
        padded_k = tuple(padded(value) for value in seen_k)
        padded_v = tuple(padded(value) for value in seen_v)
        turned_k = tuple(value.T for value in seen_k)
        turned_v = tuple(value.T for value in seen_v)
        bias = jnp.where(prev_ok, 0.0, LOW)
        key_place = lax.broadcasted_iota(jnp.int32, (HALF, 4 * HALF), 0)
        query_place = lax.broadcasted_iota(jnp.int32, (HALF, 4 * HALF), 1) & (HALF - 1)
        own = key_place <= query_place
        own16 = own.astype(F32).astype(BF16)
        turn = (((1,), (1,)), ((), ()))
        items = [(unit, half) for unit in range(2) for half in range(2)]
        seen = 3 * HALF

        def wide(index):
            return slice(index * 256, (index + 1) * 256)

        def feats(index):
            unit = items[index][0]
            return slice(unit * HEAD_DIM, (unit + 1) * HEAD_DIM)

        def corners(unit, half):
            rows = slice(half * HALF, (half + 1) * HALF)
            return [
                (rows, slice(unit * 512 + at * 128, unit * 512 + (at + 1) * 128)) for at in range(4)
            ]

        def stacked(ref, unit, half):
            return jnp.concatenate([ref[corner] for corner in corners(unit, half)], axis=0)

        def products(index):
            unit, half = items[index]
            score, dp = (
                lax.dot_general(
                    padded[half][unit],
                    stacked(ref, unit, half),
                    turn,
                    preferred_element_type=F32,
                )
                for padded, ref in ((padded_k, q_ref), (padded_v, g_ref))
            )
            parts = []
            for base in (0, seen):
                near, far = slice(base, base + HALF), slice(base + HALF, base + 2 * HALF)
                rest = slice(base + 2 * HALF, base + 3 * HALF)
                edge = jnp.where(own, score[near], score[far] + bias)
                whole = score[rest] + bias if half == 0 else score[rest]
                parts.append((edge, whole, jnp.where(own, dp[near], dp[far]), dp[rest]))
            return parts

        def weigh(index, odd, edge, whole, dp_edge, dp_whole):
            unit, half = items[index]
            base = odd * seen
            row = unit * GROUP + odd
            sink = jnp.concatenate(
                [
                    jnp.where(left, sink_ref[at : at + 1], sink_ref[at + 2 : at + 3])
                    for at in (row, row + 4)
                ],
                axis=1,
            )
            peak = jnp.max(jnp.maximum(edge, whole), axis=0, keepdims=True)
            peak = jnp.maximum(peak, sink)
            edge, whole = jnp.exp(edge - peak), jnp.exp(whole - peak)
            sink_weight = jnp.exp(sink - peak)
            inverse = 1.0 / (jnp.sum(edge + whole, axis=0, keepdims=True) + sink_weight)
            edge, whole = edge * inverse, whole * inverse
            delta = jnp.sum(edge * dp_edge + whole * dp_whole, axis=0, keepdims=True)
            edge16, whole16 = edge.astype(BF16), whole.astype(BF16)
            edge_own = edge16 * own16
            edge_prev = edge16 - edge_own
            away_edge, away_whole = (dp_edge - delta).astype(BF16), (dp_whole - delta).astype(BF16)
            for target, rows in (
                (prob2, (edge_own, edge_prev, whole16)),
                (slope2, (edge_own * away_edge, edge_prev * away_edge, whole16 * away_whole)),
            ):
                for by, value in enumerate(rows):
                    at = base + by * HALF
                    target[at : at + HALF, wide(index)] = value
            sink_term = sink_weight * inverse * delta
            for at, lanes in ((row, slice(0, 128)), (row + 4, slice(128, 256))):
                part = sink_term[:, lanes]
                sink_rows[at : at + 1] += jnp.where(left, part, 0.0)
                sink_rows[at + 2 : at + 3] += jnp.where(left, 0.0, part)

        def finish(index):
            unit, half = items[index]
            for source, across, out_ref in ((prob2, turned_v, o_ref), (slope2, turned_k, dq_ref)):
                out_t = [
                    jnp.dot(
                        across[half][feats(index)],
                        source[base : base + seen, wide(index)],
                        preferred_element_type=F32,
                    ).astype(BF16)
                    for base in (0, seen)
                ]
                out = jnp.concatenate(out_t, axis=0).T
                for at, corner in enumerate(corners(unit, half)):
                    out_ref[corner] = out[at * HALF : (at + 1) * HALF]

        def reduce(index):
            unit, half = items[index]
            parts = []
            for weights, ref in ((slope2, q_ref), (prob2, g_ref)):
                part = jnp.dot(
                    weights[:, wide(index)], stacked(ref, unit, half), preferred_element_type=F32
                )
                parts.append(jnp.where(left, part[:seen], part[seen:]))
            return parts

        def join(first_half, second_half):
            total = jnp.concatenate(
                [
                    first_half[:HALF] + second_half[2 * HALF :],
                    second_half[:HALF],
                    first_half[HALF : 2 * HALF],
                    first_half[2 * HALF :] + second_half[HALF : 2 * HALF],
                ],
                axis=0,
            )
            return total + pltpu.roll(total, HEAD_DIM, 1)

        ahead, parts = products(0), []
        for index in range(len(items)):
            now = ahead
            if index + 1 < len(items):
                ahead = products(index + 1)
            weigh(index, 0, *now[0])
            if index >= 1:
                finish(index - 1)
            weigh(index, 1, *now[1])
            parts.append(reduce(index))
        finish(len(items) - 1)
        grads = [
            [join(parts[2 * unit][place], parts[2 * unit + 1][place]) for place in range(2)]
            for unit in range(2)
        ]
        dk = jnp.where(left, grads[0][0], grads[1][0]) * FACTOR
        dv = jnp.where(left, grads[0][1], grads[1][1])
        dk_ref[here, :] = dk[:WINDOW]
        dv_ref[here, :] = dv[:WINDOW]

        @pl.when(opening & prev_ok)
        def _():
            tail_sum[:, :128] += dk[WINDOW:]
            tail_sum[:, 128:] += dv[WINDOW:]

        @pl.when(jnp.logical_not(opening) & first)
        def _():
            dhalo_ref[:, :128] = dk[WINDOW:].astype(BF16)
            dhalo_ref[:, 128:] = dv[WINDOW:].astype(BF16)

        @pl.when(jnp.logical_not(opening) & jnp.logical_not(first))
        def _():
            dk_ref[before, :] += dk[WINDOW:]
            dv_ref[before, :] += dv[WINDOW:]

    @pl.when(block == blocks_here - 1)
    def _():
        width = 2 * per_slot * HEAD_DIM
        heads = per_slot * GROUP
        total = tail_sum[...].astype(BF16)
        for part in range(2 // per_slot):
            feats = slice(part * width // 2, (part + 1) * width // 2)
            tail = jnp.concatenate([total[:, :128][:, feats], total[:, 128:][:, feats]], axis=1)
            rows = sink_rows[part * heads : (part + 1) * heads]
            rows = jnp.concatenate([rows, jnp.zeros((128 - heads, WINDOW), F32)], axis=0)
            sink_row = jnp.sum(rows.T, axis=0, keepdims=True)
            tail = with_row(tail, sink_row)
            wanted = (pair * (2 // per_slot) + part) ^ head
            for step, dtail_ref in dtails:

                @pl.when(wanted == step)
                def _(dtail_ref=dtail_ref, tail=tail):
                    dtail_ref[...] = tail


def gather_kernel(*refs):
    *in_refs, out_ref = refs
    total, sink_row = 0.0, 0.0
    for in_ref in in_refs:
        total = total + in_ref[...].astype(F32)
        sink_row = sink_row + row_join(in_ref[:16])
    out_ref[...] = with_row(total.astype(BF16), sink_row)


def land_kernel(blocks, plan_ref, here_ref, *refs):
    head = lax.axis_index("head")
    in_refs, out_refs, sink_ref = refs[:LAG], refs[LAG:-1], refs[-1]
    slots = len(out_refs)
    blocks_here = blocks // slots
    for out_ref in out_refs:
        out_ref[...] = jnp.zeros_like(out_ref)
    sink_row = row_join(here_ref[:16])
    seen = lax.broadcasted_iota(jnp.int32, here_ref.shape, 0) > 0
    for distance, in_ref in enumerate(in_refs, 1):
        valid, place = planned_tail(plan_ref, distance)
        sink_row = sink_row + row_join(in_ref[:16])
        wanted = lax.rem(place // blocks_here - head + slots, slots)
        here = pl.ds(pl.multiple_of(place % blocks_here * WINDOW, WINDOW), WINDOW)
        for step, out_ref in enumerate(out_refs):

            @pl.when(valid & (wanted == step))
            def _(out_ref=out_ref, in_ref=in_ref, here=here):
                total = out_ref[here, :].astype(F32) + in_ref[...].astype(F32)
                out_ref[here, :] = jnp.where(seen, total, 0.0).astype(BF16)

    sink_ref[...] = jnp.broadcast_to(sink_row, sink_ref.shape)


def total_kernel(halo_ref, dk_ref, dv_ref, sink_ref, far_ref, *refs):
    *tail_refs, key_ref, value_ref, sink_grad, tails = refs
    slots, rows = len(tail_refs), dk_ref.shape[0]
    width = tails.shape[2] // 2
    head = lax.axis_index("head")
    for step, tail_ref in enumerate(tail_refs):
        tails[lax.rem(head - step + slots, slots)] = tail_ref[...]
    halo_k = jnp.concatenate([halo_ref[pair][:, :128] for pair in range(PAIRS)], axis=1)
    halo_v = jnp.concatenate([halo_ref[pair][:, 128:] for pair in range(PAIRS)], axis=1)
    for in_ref, halo, at, out_ref in (
        (dk_ref, halo_k, 0, key_ref),
        (dv_ref, halo_v, width, value_ref),
    ):
        for begin in range(0, rows, WINDOW):
            here = slice(begin, begin + WINDOW)
            parts = [tails[slot, here, at : at + width] for slot in range(slots)]
            total = in_ref[here, :] + jnp.concatenate(parts, axis=1).astype(F32)
            if begin == rows - WINDOW:
                total = total + halo.astype(F32)
            out_ref[here, :] = total.astype(BF16)
    sink_row = -(sink_ref[0:1] + far_ref[0:1])
    sink_grad[...] = sink_row[0, : sink_grad.shape[0]]


def swap(values, axis):
    return [values[0]] + [ring(values[step], axis, step) for step in range(1, len(values))]


def trade(values, axis):
    places = range(lax.axis_size(axis))
    return [values[0]] + [
        lax.ppermute(values[bits], axis, [(place, place ^ bits) for place in places])
        for bits in range(1, len(values))
    ]


def local(
    queries, key_states, value_states, out_grad, sink_logits, branch_start, branch_len, parent_list
):
    tok_count, head_count = lax.axis_size("tok"), lax.axis_size("head")
    rows = queries.shape[0]
    blocks_here = rows // WINDOW
    blocks = blocks_here * head_count
    per_slot = KV_HEADS // head_count
    width = 2 * per_slot * HEAD_DIM

    def shape(dims, kind=BF16):
        return jax.ShapeDtypeStruct(dims, kind)

    def far(value):
        return pltpu.with_memory_space_constraint(value, pltpu.HBM)

    def close(value):
        return pltpu.with_memory_space_constraint(value, pltpu.VMEM)

    *slots, halo_out, keys, values = pl.pallas_call(
        pack_kernel,
        out_shape=(shape((rows, width)),) * head_count
        + (shape((PAIRS, WINDOW, 256)),)
        + (pltpu.VMEM(key_states.shape, BF16),) * 2,
        in_specs=[HBM] * 3,
        out_specs=(VMEM,) * (head_count + 3),
        scratch_shapes=[
            pltpu.SMEM(sink_logits.shape, F32),
            pltpu.SemaphoreType.DMA((3,)),
        ],
        compiler_params=PARAMS,
        name="pack",
    )(far(sink_logits), far(key_states), far(value_states))
    spread = swap(slots, "head")
    halo = shift(halo_out, "head", 1)
    plan = pl.pallas_call(
        functools.partial(plan_kernel, tok_count, blocks, blocks_here),
        out_shape=pltpu.VMEM((8, 128), jnp.int32),
        in_specs=[SMEM] * 3,
        out_specs=VMEM,
        compiler_params=PARAMS,
        name="plan",
    )(far(branch_start), far(branch_len), far(parent_list.T))
    plan = close(plan)
    chosen = pl.pallas_call(
        choose_kernel,
        out_shape=(shape((WINDOW, width)),) * LAG,
        in_specs=[VMEM] * (1 + head_count),
        out_specs=(VMEM,) * LAG,
        compiler_params=PARAMS,
        name="choose",
    )(plan, *spread)
    late_slots = lax.optimization_barrier((*spread, *chosen))
    late_slots, chosen = late_slots[:head_count], late_slots[head_count:]
    sinks = pl.pallas_call(
        sinks_kernel,
        out_shape=shape((KV_HEADS * GROUP, 128), F32),
        in_specs=[VMEM] * head_count,
        out_specs=VMEM,
        compiler_params=PARAMS,
        name="sinks",
    )(*late_slots)
    arrived = [ring(chosen[LAG - s], "tok", s) for s in range(LAG, 0, -1)]
    queries, out_grad, _ = lax.optimization_barrier((queries, out_grad, sinks))
    near_queries, near_grad = pl.pallas_call(
        stage_kernel,
        out_shape=(pltpu.VMEM(queries.shape, BF16),) * 2,
        in_specs=[HBM] * 2,
        out_specs=(VMEM,) * 2,
        scratch_shapes=[pltpu.SemaphoreType.DMA((2,))],
        compiler_params=PARAMS,
        name="stage",
    )(far(queries), far(out_grad))
    *arrived, near_queries, near_grad = lax.optimization_barrier(
        (*arrived, near_queries, near_grad)
    )
    quarter = pl.pallas_call(
        arrive_kernel,
        out_shape=shape((WINDOW, width)),
        in_specs=[VMEM] * (1 + LAG),
        out_specs=VMEM,
        compiler_params=PARAMS,
        name="arrive",
    )(plan, *arrived)
    tails = trade([quarter] * head_count, "head")

    def attend(steps, pairs, offset, halo, joined):
        inputs = (
            sinks,
            close(near_queries),
            close(near_grad),
            close(keys),
            close(values),
            halo,
            *(tails[step] for step in steps),
            *(close(value) for value in joined),
        )
        base = 1 + len(inputs) - len(joined)
        return pl.pallas_call(
            functools.partial(
                attend_kernel,
                blocks_here,
                head_count,
                steps,
                offset,
                pairs,
                len(joined),
            ),
            out_shape=(
                pltpu.VMEM(queries.shape, BF16),
                pltpu.VMEM(queries.shape, BF16),
                pltpu.VMEM(key_states.shape, F32),
                pltpu.VMEM(key_states.shape, F32),
                pltpu.VMEM((PAIRS, WINDOW, 256), BF16),
            )
            + (shape((WINDOW, width)),) * len(steps),
            in_specs=[VMEM] * (1 + len(inputs)),
            out_specs=(VMEM,) * (5 + len(steps)),
            scratch_shapes=[
                pltpu.VMEM((head_count, WINDOW, width), BF16),
                pltpu.VMEM((WINDOW, 256), F32),
                pltpu.VMEM((2 * GROUP, WINDOW), F32),
                pltpu.VMEM((6 * HALF, 1024), BF16),
                pltpu.VMEM((6 * HALF, 1024), BF16),
            ],
            input_output_aliases={base + place: place for place in range(len(joined))},
            compiler_params=PARAMS,
            name="attend",
        )(plan, *inputs)

    if per_slot == 2:
        *joined, own_tail = attend((0,), 1, 0, spread[1], ())
        *joined, tail_2, tail_3 = attend((2, 3), 2, 2, halo, joined)
        *results, tail_1 = attend((1,), 1, 1, halo, joined)
        dtail = [own_tail, tail_1, tail_2, tail_3]
    else:
        results = attend(tuple(range(head_count)), PAIRS, None, halo, ())
        results, dtail = results[:5], list(results[5:])
    attended, query_grad, dk, dv, dhalo = results
    parts = trade(dtail, "head")

    def gather(values):
        return pl.pallas_call(
            gather_kernel,
            out_shape=shape((WINDOW, width)),
            in_specs=[VMEM] * len(values),
            out_specs=VMEM,
            compiler_params=PARAMS,
            name="gather",
        )(*values)

    quarter_grad = gather([gather([parts[0], *parts[2:]]), parts[1]])

    def flush(value):
        return pl.pallas_call(
            stage_kernel,
            out_shape=pltpu.HBM(value.shape, BF16),
            in_specs=[VMEM],
            out_specs=HBM,
            scratch_shapes=[pltpu.SemaphoreType.DMA((1,))],
            compiler_params=PARAMS,
            name="flush",
        )(close(value))

    returned = [ring(quarter_grad, "tok", -s) for s in range(LAG, 0, -1)][::-1]
    attended, _ = lax.optimization_barrier((attended, quarter_grad))
    attended = flush(attended)
    attended, *returned = lax.optimization_barrier((attended, *returned))
    halo_back = shift(dhalo, "head", -1)
    *landed, sink_near = pl.pallas_call(
        functools.partial(land_kernel, blocks),
        out_shape=(shape((rows, width)),) * head_count + (shape((8, 128), F32),),
        in_specs=[VMEM] * (LAG + 2),
        out_specs=(VMEM,) * (head_count + 1),
        compiler_params=PARAMS,
        name="land",
    )(plan, quarter_grad, *returned)
    tails_back = swap(landed, "head")
    query_grad, _ = lax.optimization_barrier((query_grad, sink_near))
    query_grad = flush(query_grad)
    span = LAG + 1
    while 2 * span < tok_count:
        sink_near = sink_near + ring(sink_near, "tok", -span)
        span *= 2
    sink_far = ring(sink_near, "tok", -span)
    key_grad, value_grad, sink_grad = pl.pallas_call(
        total_kernel,
        out_shape=(
            shape(key_states.shape),
            shape(value_states.shape),
            shape(sink_logits.shape, F32),
        ),
        in_specs=[VMEM] * (5 + head_count),
        out_specs=(VMEM,) * 3,
        scratch_shapes=[pltpu.VMEM((head_count, rows, width), BF16)],
        compiler_params=PARAMS,
        name="total",
    )(halo_back, dk, dv, sink_near, sink_far, *tails_back)
    return attended, query_grad, key_grad, value_grad, sink_grad


def solution(mesh):
    rows = P(("tok", "head"), None)
    return jax.shard_map(
        local,
        mesh=mesh,
        in_specs=(rows, rows, rows, rows, P("head"), P(), P(), P()),
        out_specs=(rows, rows, rows, rows, P("head")),
        check_vma=False,
    )
```
